32 devices in a mesh: tm: 8 (over z, x), head: 4 (over y, core).
Axes of the slice: x: 2, y: 2, z: 4, core: 2. Of those that a mesh axis runs over, the one named last changes fastest.
Arguments:
- frames: float32 [2, 4096, 512], P(None, 'tm'), may hold values from -6 to 6
- cotangent: float32 [2, 4096, 512], P(None, 'tm'), may hold values from -6 to 6
- seg_counts: int32 [2, 4], replicated, may hold values from 1 to 225, as said below
- query_weight: float32 [512, 512], P(None, 'head'), may hold values from -0.25 to 0.25
- query_bias: float32 [512], P('head'), may hold values from -3 to 3
- key_weight: float32 [512, 512], P(None, 'head'), may hold values from -0.25 to 0.25
- value_weight: float32 [512, 512], P(None, 'head'), may hold values from -0.25 to 0.25
- value_bias: float32 [512], P('head'), may hold values from -3 to 3
- out_weight: float32 [512, 512], P('head'), may hold values from -0.75 to 0.75
- out_bias: float32 [512], replicated, may hold values from -3 to 3
- first_gain: float32 [512], replicated, may hold values from 0.25 to 1.75
- first_shift: float32 [512], replicated, may hold values from -2 to 2
- second_gain: float32 [512], replicated, may hold values from 0.25 to 1.75
- second_shift: float32 [512], replicated, may hold values from -2 to 2
- inner_weight: float32 [512, 2048], P(None, 'head'), may hold values from -0.25 to 0.25
- inner_bias: float32 [2048], P('head'), may hold values from -3 to 3
- outer_weight: float32 [2048, 512], P('head'), may hold values from -0.1875 to 0.1875
- outer_bias: float32 [512], replicated, may hold values from -3 to 3
Outputs:
- layer_output: float32 [2, 4096, 512], P(None, 'tm')
- frames_grad: float32 [2, 4096, 512], P(None, 'tm')
- query_weight_grad: float32 [512, 512], P(None, 'head')
- query_bias_grad: float32 [512], P('head')
- key_weight_grad: float32 [512, 512], P(None, 'head')
- value_weight_grad: float32 [512, 512], P(None, 'head')
- value_bias_grad: float32 [512], P('head')
- out_weight_grad: float32 [512, 512], P('head')
- out_bias_grad: float32 [512], replicated
- first_gain_grad: float32 [512], replicated
- first_shift_grad: float32 [512], replicated
- second_gain_grad: float32 [512], replicated
- second_shift_grad: float32 [512], replicated
- inner_weight_grad: float32 [512, 2048], P(None, 'head')
- inner_bias_grad: float32 [2048], P('head')
- outer_weight_grad: float32 [2048, 512], P('head')
- outer_bias_grad: float32 [512], replicated
The draws below stay inside these ranges and needn't reach their ends.
Inputs may be any that keep to these rules, and one draw needn't show every extreme that they name: `seg_counts`: each row sums to 256; in each row exactly one utterance has 225 segments, the others at least one.
All inputs are finite; a program needn't handle non-finite values.
Results may differ from the reference program's by a relative error of at most 0.0003.
Values sent between devices are 32-bit elements; how exact they have to be, the bound alone decides.
No kernel may reach another device: no remote copies, remote signals or barrier semaphores. Data moves between devices by JAX's collectives and lax.ppermute only.
A program may use at most 128 MiB of HBM per device.

```python
import jax
import jax.numpy as jnp
from jax import lax

D = 512
HEAD_DIM = 64
FF = 2048
SEG = 16
RC = 4
LC = 30
MEM = 4
MICRO = 2
UTTS = 4
FRAMES_DEV = 512
FRAMES = 4096


def draw_seg_counts(key, part):
    key = jax.random.fold_in(key, 7)
    seg_dev = FRAMES_DEV // SEG
    longest = FRAMES // SEG - seg_dev + 1
    table = []
    for batch_index in range(MICRO):
        sub_key = jax.random.fold_in(key, batch_index)
        cut_key, place_key = jax.random.split(sub_key)
        cuts = jnp.sort(jax.random.permutation(cut_key, seg_dev - 2)[:UTTS - 2] + 1).astype(jnp.int32)
        edges = jnp.concatenate([jnp.zeros((1,), jnp.int32), cuts, jnp.full((1,), seg_dev - 1, jnp.int32)])
        shorts = edges[1:] - edges[:-1]
        place = jax.random.randint(place_key, (), 0, UTTS)
        index_row = jnp.arange(UTTS, dtype=jnp.int32)
        pick = jnp.clip(index_row - (index_row > place).astype(jnp.int32), 0, UTTS - 2)
        table.append(jnp.where(index_row == place, longest, shorts[pick]))
    return jnp.stack(table).astype(jnp.int32)


def steps_of(stream_key, dims, pieces, smallest, high):
    def one(axis_at, parts):
        heights = jax.random.uniform(jax.random.fold_in(jax.random.fold_in(stream_key, 6), axis_at), (parts,), jnp.float32, smallest / len(pieces), high / len(pieces))
        return jnp.repeat(jnp.exp(heights), dims[axis_at] // parts).reshape((-1,) + (1,) * (len(dims) - axis_at - 1))

    level = one(*pieces[0])
    for cut in pieces[1:]:
        level = level * one(*cut)
    return level


def gaussian(key, extent, scale, limit, shards=(), kind=jnp.bfloat16):
    loudness = steps_of(key, extent, shards, -0.22, 0.18) if shards else 1.0
    entries = jax.random.normal(key, extent, jnp.float32) * scale * loudness
    return jnp.minimum(jnp.maximum(entries, -limit), limit).astype(kind)


def setup_inputs(seed: int = 0) -> dict:
    key_list = jax.random.split(jax.random.key(seed), 19)
    return {
        "frames": gaussian(key_list[0], (MICRO, FRAMES, D), 1.0, 6.0, ((1, 8),), jnp.float32),
        "cotangent": gaussian(key_list[1], (MICRO, FRAMES, D), 1.0, 6.0, ((1, 8),), jnp.float32),
        "seg_counts": draw_seg_counts(jax.random.fold_in(key_list[18], 71), 0),
        "query_weight": gaussian(key_list[3], (D, D), D ** -0.5, 0.25, ((1, 4),), jnp.float32),
        "query_bias": gaussian(key_list[4], (D,), 0.5, 3.0, ((0, 4),), jnp.float32),
        "key_weight": gaussian(key_list[5], (D, D), D ** -0.5, 0.25, ((1, 4),), jnp.float32),
        "value_weight": gaussian(key_list[6], (D, D), D ** -0.5, 0.25, ((1, 4),), jnp.float32),
        "value_bias": gaussian(key_list[7], (D,), 0.5, 3.0, ((0, 4),), jnp.float32),
        "out_weight": gaussian(key_list[8], (D, D), (D // 8) ** -0.5, 0.75, ((0, 4),), jnp.float32),
        "out_bias": gaussian(key_list[9], (D,), 0.5, 3.0, (), jnp.float32),
        "first_gain": jnp.clip(1.0 + 0.15 * jax.random.normal(key_list[10], (D,), jnp.float32), 0.25, 1.75),
        "first_shift": gaussian(key_list[11], (D,), 0.3, 2.0, (), jnp.float32),
        "second_gain": jnp.clip(1.0 + 0.15 * jax.random.normal(key_list[12], (D,), jnp.float32), 0.25, 1.75),
        "second_shift": gaussian(key_list[13], (D,), 0.3, 2.0, (), jnp.float32),
        "inner_weight": gaussian(key_list[14], (D, FF), D ** -0.5, 0.25, ((1, 4),), jnp.float32),
        "inner_bias": gaussian(key_list[15], (FF,), 0.5, 3.0, ((0, 4),), jnp.float32),
        "outer_weight": gaussian(key_list[16], (FF, D), (FF // 2) ** -0.5, 0.1875, ((0, 4),), jnp.float32),
        "outer_bias": gaussian(key_list[17], (D,), 0.5, 3.0, (), jnp.float32),
    }


EPSILON = 1e-05
HIGHEST = lax.Precision.HIGHEST
MASKED = -1e+30

@jax.custom_vjp
def low(v):
    return lax.optimization_barrier(v.astype(jnp.bfloat16)).astype(jnp.float32)

@jax.custom_vjp
def low_back(v):
    return v

def low_keep(v):
    return (low(v), None)

def low_pass(kept, grad):
    return (grad,)

def back_keep(v):
    return (v, None)

def back_low(kept, grad):
    return (low(grad),)
low.defvjp(low_keep, low_pass)
low_back.defvjp(back_keep, back_low)

def product(left, right):
    return jnp.dot(left, right, precision=HIGHEST)

def layer_norm(inputs, gain, shift):
    centred = inputs - lax.optimization_barrier(jnp.mean(inputs, axis=-1, keepdims=True))
    variance = lax.optimization_barrier(jnp.mean(centred * centred, axis=-1, keepdims=True))
    return centred * lax.rsqrt(variance + EPSILON) * gain + shift

def segment_owner(counts, first_index, number, segment_total):
    bounds = jnp.cumsum(counts).astype(jnp.int32)
    segment_index = first_index + jnp.arange(number, dtype=jnp.int32)
    utterance = lax.optimization_barrier(jnp.sum((bounds[None, :] <= segment_index[:, None]).astype(jnp.int32), axis=1))
    inside = (segment_index >= 0) & (segment_index < segment_total)
    return jnp.where(inside, utterance, -1).astype(jnp.int32)

def attend(queries, extended, memory_rows, owner_ids):
    seg_count = queries.shape[0]
    feature_width = queries.shape[2]
    head_count = feature_width // HEAD_DIM
    key_span = LC + SEG + RC
    block_count = -(-key_span // SEG)
    blocks = extended.reshape(seg_count + block_count - 1, SEG, extended.shape[1])
    window = jnp.concatenate([blocks[i:i + seg_count] for i in range(block_count)], axis=1)[:, :key_span]
    memory = jnp.stack([memory_rows[j:j + seg_count] for j in range(MEM)], axis=1)
    keyset = jnp.concatenate([window, memory], axis=1)
    owners = [owner_ids[MEM + (j - LC) // SEG:MEM + (j - LC) // SEG + seg_count] for j in range(key_span)]
    owners = owners + [owner_ids[j:j + seg_count] for j in range(MEM)]
    visible = jnp.stack(owners, axis=1) == owner_ids[MEM:MEM + seg_count][:, None]
    key_rows = keyset[:, :, :feature_width].reshape(seg_count, key_span + MEM, head_count, HEAD_DIM)
    value_rows = keyset[:, :, feature_width:].reshape(seg_count, key_span + MEM, head_count, HEAD_DIM)
    query_rows = queries.reshape(seg_count, SEG, head_count, HEAD_DIM)
    scores = jnp.einsum('nqhd,nkhd->nhqk', query_rows, key_rows, precision=HIGHEST) * HEAD_DIM ** (-0.5)
    scores = jnp.where(visible[:, None, None, :], scores, MASKED)
    scores = scores - lax.optimization_barrier(jnp.max(scores, axis=-1, keepdims=True))
    weights = jnp.exp(scores)
    weights = weights / lax.optimization_barrier(jnp.sum(weights, axis=-1, keepdims=True))
    mixture = jnp.einsum('nhqk,nkhd->nqhd', weights, value_rows, precision=HIGHEST)
    return mixture.reshape(seg_count * SEG, feature_width)

def project(normed, query_weight, query_bias, key_weight, value_weight, value_bias):
    queries = product(normed, query_weight) + query_bias
    keyvals = jnp.concatenate([product(normed, key_weight), product(normed, value_weight) + value_bias], axis=1)
    summary = lax.optimization_barrier(jnp.mean(keyvals.reshape(-1, SEG, keyvals.shape[1]), axis=1))
    return (queries, keyvals, summary)

def feed(normed, inner_weight, inner_bias, outer_weight):
    return product(jax.nn.gelu(product(normed, inner_weight) + inner_bias, approximate=False), outer_weight)

def forward_layer(inputs, counts, query_weight, query_bias, key_weight, value_weight, value_bias, out_weight, out_bias, first_gain, first_shift, second_gain, second_shift, inner_weight, inner_bias, outer_weight, outer_bias):
    seg_total = FRAMES // SEG
    owner_ids = segment_owner(counts, -MEM, seg_total + MEM + 2, seg_total)
    normed = layer_norm(inputs, first_gain, first_shift)
    queries, keyvals, summary = project(normed, query_weight, query_bias, key_weight, value_weight, value_bias)
    key_span = LC + SEG + RC
    block_count = -(-key_span // SEG)
    padding = (seg_total + block_count - 1) * SEG - (LC + FRAMES + RC)
    kv_width = keyvals.shape[1]
    extended = jnp.concatenate([jnp.zeros((LC, kv_width), jnp.float32), keyvals, jnp.zeros((RC + padding, kv_width), jnp.float32)], axis=0)
    memory_rows = jnp.concatenate([jnp.zeros((MEM, kv_width), jnp.float32), summary], axis=0)
    mixture = attend(queries.reshape(seg_total, SEG, queries.shape[1]), extended, memory_rows, owner_ids)
    middle = inputs + product(mixture, out_weight) + out_bias
    normed_two = layer_norm(middle, second_gain, second_shift)
    return middle + feed(normed_two, inner_weight, inner_bias, outer_weight) + outer_bias

def reference(frames, cotangent, seg_counts, query_weight, query_bias, key_weight, value_weight, value_bias, out_weight, out_bias, first_gain, first_shift, second_gain, second_shift, inner_weight, inner_bias, outer_weight, outer_bias):
    params = (query_weight, query_bias, key_weight, value_weight, value_bias, out_weight, out_bias, first_gain, first_shift, second_gain, second_shift, inner_weight, inner_bias, outer_weight, outer_bias)
    results = []
    input_grads = []
    totals = [jnp.zeros_like(p) for p in params]
    for batch_index in range(MICRO):
        counts = seg_counts[batch_index]

        def run_layer(inputs, *weights):
            return forward_layer(inputs, counts, *weights)
        result, pullback = jax.vjp(run_layer, frames[batch_index], *params)
        grads = pullback(cotangent[batch_index])
        results.append(result)
        input_grads.append(grads[0])
        totals = [t + g for t, g in zip(totals, grads[1:])]
    return (jnp.stack(results), jnp.stack(input_grads), totals[0], totals[1], totals[2], totals[3], totals[4], totals[5], totals[6], totals[7], totals[8], totals[9], totals[10], totals[11], totals[12], totals[13], totals[14])
```

```python
import functools

import jax
import jax.numpy as jnp
from jax import lax
from jax.experimental import pallas as pl
from jax.experimental.pallas import tpu as pltpu
from jax.sharding import PartitionSpec as P

HEAD_DIM = 64
SEG = 16
RC = 4
LC = 30
MEM = 4

EPSILON = 1e-05
MASKED = -1e30
F32 = jnp.float32

CACHE = 32
SUMS = 8
AHEAD = 8
BLOCK = 64
WIN = CACHE + BLOCK + AHEAD
SWIN = 16
KEYS = 128
MIB = 1 << 20


def mm(left, right, left_dim=1, right_dim=0):
    return lax.dot_general(
        left,
        right,
        (((left_dim,), (right_dim,)), ((), ())),
        precision=lax.Precision.HIGH,
        preferred_element_type=F32,
    )


def normalise(values):
    centred = values - jnp.mean(values, axis=-1, keepdims=True)
    variance = jnp.mean(centred * centred, axis=-1, keepdims=True)
    rate = lax.rsqrt(variance + EPSILON)
    return centred * rate, rate


def norm_back(grad, gain, xhat, rate):
    scaled = grad * gain
    first = jnp.mean(scaled, axis=-1, keepdims=True)
    second = jnp.mean(scaled * xhat, axis=-1, keepdims=True)
    return rate * (scaled - first - xhat * second)


def column_sums(values):
    return jnp.sum(values, axis=0, keepdims=True)


def seg_means(values):
    rows, width = values.shape
    return jnp.sum(values.reshape(rows // SEG, SEG, width), axis=1) * (1.0 / SEG)


def core_bit():
    return lax.axis_index("head") % 2


def full(shape):
    return pl.BlockSpec(shape, lambda *_: (0,) * len(shape))


def micro_block(shape, index):
    return pl.BlockSpec((1,) + shape, lambda *_: (index,) + (0,) * len(shape))


def call(kernel, name, outs, in_specs, args, scratch=(), vmem=40, grid=(1,), out_specs=None):
    return pl.pallas_call(
        kernel,
        name=name,
        grid=grid,
        in_specs=in_specs,
        out_specs=out_specs if out_specs is not None else [full(s) for s in outs],
        out_shape=[jax.ShapeDtypeStruct(s, F32) for s in outs],
        scratch_shapes=[pltpu.VMEM(s, F32) for s in scratch],
        compiler_params=pltpu.CompilerParams(vmem_limit_bytes=vmem * MIB),
    )(*args)


def project_kernel(x_ref, gain, shift, wq, bq, wk, wv, bv, q_ref, kv_ref, tail_ref, head_ref):
    xhat, _ = normalise(x_ref[0])
    normed = xhat * gain[...] + shift[...]
    width = wq.shape[1]
    q_ref[0] = mm(normed, wq[...]) + bq[...]
    kv_ref[0, :, :width] = mm(normed, wk[...])
    kv_ref[0, :, width:] = mm(normed, wv[...]) + bv[...]
    length = kv_ref.shape[1]
    tail_ref[0, :CACHE] = kv_ref[0, length - CACHE :]
    tail_ref[0, CACHE:] = seg_means(kv_ref[0, length - SUMS * SEG :])
    head_ref[0] = kv_ref[0, :AHEAD]


def fill_keys(kv, cache, ahead, kx, sx):
    length = kv.shape[0]
    kx[:CACHE] = cache[:CACHE]
    kx[CACHE : CACHE + length] = kv
    kx[CACHE + length :] = ahead
    segs = length // SEG
    sx[:SUMS] = cache[CACHE:]
    sx[SUMS : SUMS + segs] = seg_means(kv)
    sx[SUMS + segs :] = jnp.zeros((SUMS, kv.shape[1]), F32)


def summary_start(block):
    return (block * (BLOCK // SEG) + SUMS - MEM) // SUMS * SUMS


def key_window(kx, sx, block):
    start = summary_start(block)
    rows = [kx[block * BLOCK : block * BLOCK + WIN], sx[start : start + SWIN]]
    return jnp.concatenate(rows + [jnp.zeros((KEYS - WIN - SWIN, kx.shape[1]), F32)], axis=0)


def by_head(values):
    first = lax.broadcasted_iota(jnp.int32, values.shape, 1) < HEAD_DIM
    return jnp.concatenate([jnp.where(first, values, 0.0), jnp.where(first, 0.0, values)], axis=0)


def side_by_side(values):
    rows = values.shape[0] // 2
    first = lax.broadcasted_iota(jnp.int32, (rows, values.shape[1]), 1) < HEAD_DIM
    return jnp.where(first, values[:rows], values[rows:])


def owner_of(segment, bounds):
    owner = jnp.where(segment < 0, -1, 0)
    for bound in bounds:
        owner = owner + (segment >= bound).astype(jnp.int32)
    return owner


def visible(block, base, bounds):
    row = lax.broadcasted_iota(jnp.int32, (2 * BLOCK, 1), 0) % BLOCK
    column = lax.broadcasted_iota(jnp.int32, (1, KEYS), 1)
    query_seg = block * (BLOCK // SEG) + row // SEG
    frame = block * BLOCK - CACHE + column
    is_frame = column < WIN
    summary = summary_start(block) - SUMS + column - WIN
    key_seg = jnp.where(is_frame, (frame + CACHE) // SEG - CACHE // SEG, summary)
    key_seg = jnp.where(column < WIN + SWIN, key_seg, -(1 << 20))
    low = jnp.where(is_frame, frame, key_seg * SEG + SEG - LC)
    inside = (low >= query_seg * SEG - LC) & (low < query_seg * SEG + SEG + RC)
    near = (key_seg >= query_seg - MEM) & (key_seg < query_seg)
    seen = (is_frame & inside) | ((column >= WIN) & near)
    return seen & (owner_of(key_seg + base, bounds) == owner_of(query_seg + base, bounds))


def bounds_of(counts, micro):
    bounds, total = [], 0
    for utterance in range(counts.shape[1]):
        total = total + counts[micro, utterance]
        bounds.append(total)
    return bounds


def attend_kernel(micro, counts, q_ref, kv_ref, cache, ahead, mix_ref, p_ref, kx, sx):
    length = q_ref.shape[1]
    fill_keys(kv_ref[0], cache[0], ahead[0], kx, sx)
    base = lax.axis_index("tm") * (length // SEG)
    bounds = bounds_of(counts, micro)
    width = q_ref.shape[2]
    for block in range(length // BLOCK):
        rows = slice(block * BLOCK, (block + 1) * BLOCK)
        window = key_window(kx, sx, block)
        query = by_head(q_ref[0, rows] * HEAD_DIM ** (-0.5))
        scores = mm(query, window[:, :width], 1, 1)
        scores = jnp.where(visible(block, base, bounds), scores, MASKED)
        weights = jnp.exp(scores - jnp.max(scores, axis=-1, keepdims=True))
        weights = weights / jnp.sum(weights, axis=-1, keepdims=True)
        p_ref[block] = weights
        mix_ref[rows] = side_by_side(mm(weights, window[:, width:]))


def attend_back_kernel(
    dmine, dtheirs, wo, mix, q_ref, kv_ref, cache, ahead, p_ref,
    dq_ref, dkv_ref, dsum_ref, back_ref, fore_ref, dwo_ref,
    kx, sx, dkx, dsx, dmid, dmix,
):
    length, width = mix.shape
    half = length // 2
    bit = core_bit()
    dmid[pl.ds(bit * half, half)] = dmine[...]
    dmid[pl.ds((1 - bit) * half, half)] = dtheirs[...]
    dmix[...] = mm(dmid[...], wo[...], 1, 1)
    dwo_ref[...] = mm(dmid[...], mix[...], 0, 0)
    fill_keys(kv_ref[0], cache[0], ahead[0], kx, sx)
    dkx[...] = jnp.zeros_like(dkx)
    dsx[...] = jnp.zeros_like(dsx)
    for block in range(length // BLOCK):
        rows = slice(block * BLOCK, (block + 1) * BLOCK)
        window = key_window(kx, sx, block)
        query = by_head(q_ref[0, rows] * HEAD_DIM ** (-0.5))
        grad = by_head(dmix[rows])
        weights = p_ref[block]
        dweights = mm(grad, window[:, width:], 1, 1)
        dscores = weights * (dweights - jnp.sum(dweights * weights, axis=-1, keepdims=True))
        dq_ref[rows] = side_by_side(mm(dscores, window[:, :width])) * HEAD_DIM ** (-0.5)
        dkeys = mm(dscores, query, 0, 0)
        dvalues = mm(weights, grad, 0, 0)
        frames = slice(block * BLOCK, block * BLOCK + WIN)
        sums = slice(summary_start(block), summary_start(block) + SWIN)
        dkx[frames, :width] += dkeys[:WIN]
        dkx[frames, width:] += dvalues[:WIN]
        dsx[sums, :width] += dkeys[WIN : WIN + SWIN]
        dsx[sums, width:] += dvalues[WIN : WIN + SWIN]
    dkv_ref[...] = dkx[CACHE : CACHE + length]
    dsum_ref[...] = dsx[SUMS : SUMS + length // SEG]
    back_ref[:CACHE] = dkx[:CACHE]
    back_ref[CACHE:] = dsx[:SUMS]
    fore_ref[...] = dkx[CACHE + length :]


def gather_heads(parts, put):
    head = lax.axis_index("head")
    for number, part in enumerate(parts):
        low = (head % 2 + number % 2) % 2
        high = (head // 2 + number // 2) % 2
        put(high * 2 + low, part)


def feed_kernel(
    mix_own, mix_core, mix_far, wo_own, wo_core, wo_far, x_ref, g_ref, bo, gain, shift, wi, bi, wu,
    n2_ref, h_ref, dpre_ref, mid_ref, mine_ref, theirs_ref,
    mix, wo, work,
):
    length, width = mix_own.shape
    half = length // 2
    bit = core_bit()

    def put_mix(at, part):
        mix[:, pl.ds(pl.multiple_of(at * width, width), width)] = part

    def put_wo(at, part):
        wo[pl.ds(pl.multiple_of(at * width, width), width), :] = part

    gather_heads([mix_own[...], mix_core[0], mix_far[...], mix_core[1]], put_mix)
    gather_heads([wo_own[...], wo_core[0], wo_far[...], wo_core[1]], put_wo)
    middle = x_ref[0] + mm(mix[...], wo[...]) + bo[...]
    work[...] = middle
    mid_ref[...] = work[pl.ds(bit * half, half)]
    xhat, _ = normalise(middle)
    normed = xhat * gain[...] + shift[...]
    n2_ref[...] = normed
    pre = mm(normed, wi[...]) + bi[...]
    phi = 0.5 + 0.5 * lax.erf(pre * (0.5**0.5))
    h_ref[...] = pre * phi
    slope = phi + pre * (jnp.exp(-0.5 * pre * pre) * 0.3989422804014327)
    dpre = mm(g_ref[0], wu[...], 1, 1) * slope
    dpre_ref[...] = dpre
    work[...] = mm(dpre, wi[...], 1, 1)
    mine_ref[...] = work[pl.ds(bit * half, half)]
    theirs_ref[...] = work[pl.ds((1 - bit) * half, half)]


def split_rows(work, bit, mine_ref, theirs_ref):
    half = work.shape[0] // 2
    mine_ref[...] = work[pl.ds(bit * half, half)]
    theirs_ref[...] = work[pl.ds((1 - bit) * half, half)]


def feed_weights_kernel(
    n2_0, n2_1, h_0, h_1, d_0, d_1, g_ref, wu,
    im_ref, it_ref, om_ref, ot_ref, pm_ref, pt_ref, db_ref, gb_ref,
    work,
):
    tm_bit = lax.axis_index("tm") % 2
    work[...] = mm(n2_0[...], d_0[...], 0, 0) + mm(n2_1[...], d_1[...], 0, 0)
    split_rows(work, tm_bit, im_ref, it_ref)
    work[...] = mm(h_0[...], g_ref[0], 0, 0) + mm(h_1[...], g_ref[1], 0, 0)
    split_rows(work, tm_bit, om_ref, ot_ref)
    for micro, hidden in enumerate((h_0, h_1)):
        work[...] = mm(hidden[...], wu[...])
        split_rows(work, core_bit(), pm_ref.at[micro], pt_ref.at[micro])
    db_ref[...] = column_sums(d_0[...]) + column_sums(d_1[...])
    gb_ref[...] = column_sums(g_ref[0]) + column_sums(g_ref[1])


def middle_back_kernel(a_ref, b_ref, mid_ref, g_ref, gain, dmid_ref, vec_ref):
    half = mid_ref.shape[0]
    grad = a_ref[...] + b_ref[...]
    xhat, rate = normalise(mid_ref[...])
    dmid = g_ref[0, pl.ds(core_bit() * half, half)] + norm_back(grad, gain[...], xhat, rate)
    dmid_ref[...] = dmid
    vec_ref[0:1] = column_sums(dmid)
    vec_ref[1:2] = column_sums(grad * xhat)
    vec_ref[2:3] = column_sums(grad)


def project_back_kernel(
    dq, dkv, dsum, cache_back, ahead_back, x_ref, wq, wk, wv,
    dqkv_ref, mine_ref, theirs_ref, vec_ref, dkx, dsx, work,
):
    length, width = dq.shape
    segs = length // SEG
    dkx[...] = dkv[...]
    dkx[length - CACHE :] += cache_back[:CACHE]
    dkx[:AHEAD] += ahead_back[...]
    dsx[...] = dsum[...]
    dsx[segs - SUMS :] += cache_back[CACHE:]
    spread = jnp.broadcast_to((dsx[...] * (1.0 / SEG))[:, None, :], (segs, SEG, 2 * width))
    dkx[...] += spread.reshape(length, 2 * width)
    dqkv_ref[:, :width] = dq[...]
    dqkv_ref[:, width:] = dkx[...]
    part = mm(dq[...], wq[...], 1, 1)
    part = part + mm(dkx[:, :width], wk[...], 1, 1) + mm(dkx[:, width:], wv[...], 1, 1)
    work[...] = part
    split_rows(work, core_bit(), mine_ref, theirs_ref)
    xhat, _ = normalise(x_ref[0])
    vec_ref[0:1] = column_sums(part * xhat)
    vec_ref[1:2] = column_sums(part)


def project_weights_kernel(x_ref, gain, shift, d_0, d_1, w_0, w_1, mine_ref, theirs_ref, vec_ref, work):
    width = w_0.shape[1]
    wide = d_0.shape[1]
    total = None
    for micro, grads in enumerate((d_0, d_1)):
        xhat, _ = normalise(x_ref[micro])
        step = mm(xhat * gain[...] + shift[...], grads[...], 0, 0)
        total = step if total is None else total + step
    work[:, :wide] = total
    work[:, wide:] = w_0[...] + w_1[...]
    split_rows(work, lax.axis_index("tm") % 2, mine_ref, theirs_ref)
    vec_ref[...] = column_sums(d_0[...]) + column_sums(d_1[...])
    del width


def frames_back_kernel(a_ref, b_ref, x_ref, dmid_ref, gain, out_ref):
    half = dmid_ref.shape[0]
    xhat, rate = normalise(x_ref[0, pl.ds(core_bit() * half, half)])
    out_ref[...] = dmid_ref[...] + norm_back(a_ref[...] + b_ref[...], gain[...], xhat, rate)


def swap(value, axis, bit):
    size = lax.axis_size(axis)
    return lax.ppermute(value, axis, [(i, i ^ bit) for i in range(size)])


def shift_along(value, axis, by):
    size = lax.axis_size(axis)
    return lax.ppermute(value, axis, [(i, i + by) for i in range(size) if 0 <= i + by < size])


def ordered(bit, mine, theirs, axis):
    return jnp.where(
        bit == 0,
        jnp.concatenate([mine, theirs], axis=axis),
        jnp.concatenate([theirs, mine], axis=axis),
    )


def sum_over_tm(mine, theirs):
    size = lax.axis_size("tm")
    index = lax.axis_index("tm")
    bits = []
    bit = 1
    while bit < size:
        bits.append(bit)
        bit *= 2
    for number, bit in enumerate(bits):
        mine = mine + swap(theirs, "tm", bit)
        if number + 1 < len(bits):
            place = (index // bits[number + 1]) % 2
            half = mine.shape[0] // 2
            theirs = lax.dynamic_slice_in_dim(mine, (1 - place) * half, half, 0)
            mine = lax.dynamic_slice_in_dim(mine, place * half, half, 0)
    for bit in reversed(bits):
        mine = ordered((index // bit) % 2, mine, swap(mine, "tm", bit), 0)
    return mine


def per_device(
    frames, cotangent, seg_counts, query_weight, query_bias, key_weight, value_weight, value_bias,
    out_weight, out_bias, first_gain, first_shift, second_gain, second_shift,
    inner_weight, inner_bias, outer_weight, outer_bias,
):
    micro_count, length, features = frames.shape
    width = query_weight.shape[1]
    hidden = inner_weight.shape[1]
    half = length // 2
    segs = length // SEG
    blocks = length // BLOCK
    bit = core_bit()
    row = lambda v: v.reshape(1, v.shape[0])
    bq, bv, bo, bi, bu = map(row, (query_bias, value_bias, out_bias, inner_bias, outer_bias))
    g1, s1, g2, s2 = map(row, (first_gain, first_shift, second_gain, second_shift))
    big = (length, features)
    halfs = (half, features)

    wo_far = swap(out_weight, "head", 2)
    wo_core = swap(jnp.stack([out_weight, wo_far]), "head", 1)

    each = lambda shape: pl.BlockSpec((1,) + shape, lambda m: (m,) + (0,) * len(shape))
    q, kv, tail, ahead = call(
        project_kernel, "project",
        [(micro_count, length, width), (micro_count, length, 2 * width),
         (micro_count, CACHE + SUMS, 2 * width), (micro_count, AHEAD, 2 * width)],
        [each(big)] + [full(v.shape) for v in (g1, s1, query_weight, bq, key_weight, value_weight, bv)],
        (frames, g1, s1, query_weight, bq, key_weight, value_weight, bv),
        grid=(micro_count,),
        out_specs=[each((length, width)), each((length, 2 * width)), each((CACHE + SUMS, 2 * width)), each((AHEAD, 2 * width))],
    )
    cache = shift_along(tail, "tm", 1)
    ahead = shift_along(ahead, "tm", -1)

    key_scratch = [(CACHE + length + AHEAD, 2 * width), (SUMS + segs + SUMS, 2 * width)]
    attn_specs = lambda m: [
        micro_block((length, width), m), micro_block((length, 2 * width), m),
        micro_block((CACHE + SUMS, 2 * width), m), micro_block((AHEAD, 2 * width), m),
    ]
    mix, probs, feed = [], [], []
    for m in range(micro_count):
        mix_m, p_m = call(
            functools.partial(attend_kernel, m), "attend",
            [(length, width), (blocks, 2 * BLOCK, KEYS)],
            [pl.BlockSpec(memory_space=pltpu.SMEM)] + attn_specs(m),
            (seg_counts, q, kv, cache, ahead), key_scratch,
        )
        mix.append(mix_m)
        probs.append(p_m)
    for m in range(micro_count):
        mix_far = swap(mix[m], "head", 2)
        mix_core = swap(jnp.stack([mix[m], mix_far]), "head", 1)
        feed.append(call(
            feed_kernel, "feed",
            [big, (length, hidden), (length, hidden), halfs, halfs, halfs],
            [full(v.shape) for v in (mix[m], mix_core, mix_far, out_weight, wo_core, wo_far)]
            + [micro_block(big, m), micro_block(big, m)]
            + [full(v.shape) for v in (bo, g2, s2, inner_weight, bi, outer_weight)],
            (mix[m], mix_core, mix_far, out_weight, wo_core, wo_far, frames, cotangent,
             bo, g2, s2, inner_weight, bi, outer_weight),
            [big, (features, features), big],
        ))
    dn_sum = []
    for m in range(micro_count):
        _, _, _, _, mine, theirs = feed[m]
        mine = mine + swap(theirs, "head", 1)
        dn_sum.append((mine, swap(mine, "head", 2)))

    quarter = (features // 2, features)
    n2s, hs, dpres = ([f[i] for f in feed] for i in range(3))
    im, it, om, ot, pm, pt, ib_grad, ub_grad = call(
        feed_weights_kernel, "feed_weights",
        [(features // 2, hidden)] * 2 + [(hidden // 2, features)] * 2
        + [(micro_count,) + halfs] * 2 + [(1, hidden), (1, features)],
        [full(v.shape) for v in (*n2s, *hs, *dpres, cotangent, outer_weight)],
        (*n2s, *hs, *dpres, cotangent, outer_weight),
        [big],
    )
    inner_grad = sum_over_tm(im, it)
    outer_grad = sum_over_tm(om, ot)

    dmids, back, vec2 = [], [], []
    for m in range(micro_count):
        a, b = dn_sum[m]
        dmid, vec = call(
            middle_back_kernel, "middle_back", [halfs, (3, features)],
            [full(halfs)] * 3 + [micro_block(big, m), full(g2.shape)],
            (a, b, feed[m][3], cotangent, g2),
        )
        dmids.append(dmid)
        vec2.append(vec)
        theirs = swap(dmid, "head", 1)
        back.append(call(
            attend_back_kernel, "attend_back",
            [(length, width), (length, 2 * width), (segs, 2 * width), (CACHE + SUMS, 2 * width),
             (AHEAD, 2 * width), (features, width)],
            [full(halfs), full(halfs), full(out_weight.shape), full((length, width))] + attn_specs(m)
            + [full(probs[m].shape)],
            (dmid, theirs, out_weight, mix[m], q, kv, cache, ahead, probs[m]),
            key_scratch * 2 + [big, (length, width)],
        ))
    pm = pm + swap(pt, "head", 1)
    inner_total = pm + swap(pm, "head", 2)
    out_half = jnp.stack([f[3] for f in feed]) + inner_total + bu
    layer_output = ordered(bit, out_half, swap(out_half, "head", 1), 1)

    fronts = []
    for m in range(micro_count):
        dq, dkv, dsum, to_left, to_right, _ = back[m]
        cache_back = shift_along(to_left, "tm", -1)
        ahead_back = shift_along(to_right, "tm", 1)
        fronts.append(call(
            project_back_kernel, "project_back",
            [(length, 3 * width), halfs, halfs, (2, features)],
            [full(v.shape) for v in (dq, dkv, dsum, cache_back, ahead_back)] + [micro_block(big, m)]
            + [full(query_weight.shape)] * 3,
            (dq, dkv, dsum, cache_back, ahead_back, frames, query_weight, key_weight, value_weight),
            [(length, 2 * width), (segs, 2 * width), big],
        ))
    halves = []
    for m in range(micro_count):
        _, mine, theirs, _ = fronts[m]
        mine = mine + swap(theirs, "head", 1)
        far = swap(mine, "head", 2)
        (half_grad,) = call(
            frames_back_kernel, "frames_back", [halfs],
            [full(halfs), full(halfs), micro_block(big, m), full(halfs), full(g1.shape)],
            (mine, far, frames, dmids[m], g1),
        )
        halves.append(half_grad)
    half_grads = jnp.stack(halves)
    frames_grad = ordered(bit, half_grads, swap(half_grads, "head", 1), 1)

    dqkvs, dwos = [f[0] for f in fronts], [b[5] for b in back]
    qm, qt, bias_grads = call(
        project_weights_kernel, "project_weights",
        [(features // 2, 4 * width)] * 2 + [(1, 3 * width)],
        [full(frames.shape), full(g1.shape), full(s1.shape)] + [full(v.shape) for v in (*dqkvs, *dwos)],
        (frames, g1, s1, *dqkvs, *dwos),
        [(features, 4 * width)],
    )
    weights_grad = sum_over_tm(qm, qt)

    vec2 = vec2[0] + vec2[1]
    vec1 = fronts[0][3] + fronts[1][3]
    shared = jnp.concatenate([vec2 * 0.5, vec1, ub_grad * 0.25], axis=0)
    shared = shared + swap(shared, "head", 1)
    shared = shared + swap(shared, "head", 2)
    own = jnp.concatenate([bias_grads, ib_grad[:, : features - 3 * width], ib_grad[:, features - 3 * width :], jnp.zeros((1, 2 * features - 3 * width - hidden), F32)], axis=1).reshape(2, features)
    small = jnp.concatenate([shared, own], axis=0)
    reach = 1
    while reach < lax.axis_size("tm"):
        small = small + swap(small, "tm", reach)
        reach *= 2
    own = small[6:].reshape(2 * features)
    return (
        layer_output,
        frames_grad,
        weights_grad[:, :width],
        own[:width],
        weights_grad[:, width : 2 * width],
        weights_grad[:, 2 * width : 3 * width],
        own[2 * width : 3 * width],
        weights_grad[:, 3 * width :].T,
        small[0],
        small[3],
        small[4],
        small[1],
        small[2],
        inner_grad,
        own[3 * width : 3 * width + hidden],
        outer_grad,
        small[5],
    )


def solution(mesh):
    in_specs = (
        P(None, "tm", None),
        P(None, "tm", None),
        P(),
        P(None, "head"),
        P("head"),
        P(None, "head"),
        P(None, "head"),
        P("head"),
        P("head", None),
        P(),
        P(),
        P(),
        P(),
        P(),
        P(None, "head"),
        P("head"),
        P("head", None),
        P(),
    )
    out_specs = (
        P(None, "tm", None),
        P(None, "tm", None),
        P(None, "head"),
        P("head"),
        P(None, "head"),
        P(None, "head"),
        P("head"),
        P("head", None),
        P(),
        P(),
        P(),
        P(),
        P(),
        P(None, "head"),
        P("head"),
        P("head", None),
        P(),
    )
    return jax.shard_map(
        per_device, mesh=mesh, in_specs=in_specs, out_specs=out_specs, check_vma=False
    )
```

```python
import functools

import jax
import jax.numpy as jnp
from jax import lax
from jax.experimental import pallas as pl
from jax.experimental.pallas import tpu as pltpu
from jax.sharding import PartitionSpec as P

HEAD_DIM = 64
SEG = 16
RC = 4
LC = 30
MEM = 4

EPSILON = 1e-05
MASKED = -1e30
F32 = jnp.float32

CACHE = 32
SUMS = 8
AHEAD = 8
BLOCK = 64
WIN = CACHE + BLOCK + AHEAD
SWIN = 16
KEYS = 128
FIRST_GAIN, SECOND_GAIN, SECOND_SHIFT, OUT_BIAS, INNER_BIAS, OUTER_BIAS = range(6)
PAIR = 2 * HEAD_DIM
MIB = 1 << 20


def mm(left, right, left_dim=1, right_dim=0):
    return lax.dot_general(
        left,
        right,
        (((left_dim,), (right_dim,)), ((), ())),
        precision=lax.Precision.HIGH,
        preferred_element_type=F32,
    )


def normalise(values):
    centred = values - jnp.mean(values, axis=-1, keepdims=True)
    variance = jnp.mean(centred * centred, axis=-1, keepdims=True)
    rate = lax.rsqrt(variance + EPSILON)
    return centred * rate, rate


def norm_back(grad, gain, xhat, rate):
    scaled = grad * gain
    first = jnp.mean(scaled, axis=-1, keepdims=True)
    second = jnp.mean(scaled * xhat, axis=-1, keepdims=True)
    return rate * (scaled - first - xhat * second)


def column_sums(values):
    return jnp.sum(values, axis=0, keepdims=True)


def seg_means(values):
    rows, width = values.shape
    return jnp.sum(values.reshape(rows // SEG, SEG, width), axis=1) * (1.0 / SEG)


def near_bit():
    return lax.axis_index("head") % 2


def far_bit():
    return lax.axis_index("head") // 2


def my_rows(rows):
    half = rows // 2
    return pl.ds(pl.multiple_of(near_bit() * half, half), half)


def lanes_of(place, width, start=0):
    at = place + near_bit() - 2 * place * near_bit()
    return pl.ds(pl.multiple_of(start + at * width, width), width)


def full(shape):
    return pl.BlockSpec(shape, lambda *_: (0,) * len(shape))


def micro_block(shape, index):
    return pl.BlockSpec((1,) + shape, lambda *_: (index,) + (0,) * len(shape))


class Steps:
    def __init__(self):
        self.held = []

    def hold(self, *values):
        self.held.extend(values)

    def call(self, kernel, name, us, outs, args, specs=None, scratch=(), vmem=32, copies=0, far=(), far_outs=()):
        specs = dict(specs or {})
        given, made, held = len(args), len(outs), tuple(self.held)
        token = bool(far_outs)
        somewhere = pl.BlockSpec(memory_space=pl.ANY)
        in_hbm = pl.BlockSpec(memory_space=pltpu.HBM)

        def body(*refs):
            ins, rest = refs[:given], refs[given + len(held) :]
            if token:
                rest[made][...] = jnp.zeros(rest[made].shape, F32)
            kernel(*ins, *rest[:made], *rest[made + token :])

        args = [pltpu.with_memory_space_constraint(a, pltpu.HBM) if i in far else a for i, a in enumerate(args)]
        out_specs = [in_hbm if i in far_outs else full(shape) for i, shape in enumerate(outs)]
        out_shape = [
            pltpu.HBM(shape, F32) if i in far_outs else jax.ShapeDtypeStruct(shape, F32) for i, shape in enumerate(outs)
        ]
        if token:
            out_specs.append(full((1, 128)))
            out_shape.append(jax.ShapeDtypeStruct((1, 128), F32))
        out = pl.pallas_call(
            body,
            name=name,
            grid=(1,),
            in_specs=[in_hbm if i in far else specs.get(i, full(a.shape)) for i, a in enumerate(args)]
            + [somewhere] * len(held),
            out_specs=out_specs,
            out_shape=out_shape,
            scratch_shapes=[pltpu.VMEM(shape, F32) for shape in scratch]
            + ([pltpu.SemaphoreType.DMA((copies,))] if copies else []),
            compiler_params=pltpu.CompilerParams(vmem_limit_bytes=vmem * MIB),
            cost_estimate=pl.CostEstimate(flops=int(us * 5.18e8), bytes_accessed=0, transcendentals=0),
        )(*args, *held)
        self.held = [out[-1]]
        return out[:made]


def copy_all(pairs, sems):
    copies = [pltpu.make_async_copy(a, b, sems.at[i]) for i, (a, b) in enumerate(pairs)]
    for copy in copies:
        copy.start()
    return copies


def norm_kernel(frames, gain, shift, wq, wk, wv, bq, bv, x_ref, xhat_ref, rate_ref, normed_ref, w_ref, b_ref, params, sems):
    micros, half, _ = x_ref.shape
    rows = frames.shape[1]
    width = wq.shape[1]
    pairs = [(gain, params.at[pl.ds(0, 1)]), (shift, params.at[pl.ds(8, 1)])]
    pairs += [(frames.at[m, my_rows(rows)], x_ref.at[m]) for m in range(micros)]
    pairs += [(w, w_ref.at[:, pl.ds(i * width, width)]) for i, w in enumerate((wq, wk, wv))]
    pairs += [(b, b_ref.at[:, pl.ds(i * width, width)]) for i, b in enumerate((bq, bv))]
    copies = copy_all(pairs, sems)
    for copy in copies[:2]:
        copy.wait()
    for micro in range(micros):
        copies[2 + micro].wait()
        xhat, rate = normalise(x_ref[micro])
        xhat_ref[micro] = xhat
        rate_ref[micro] = jnp.broadcast_to(rate, (half, rate_ref.shape[2]))
        normed_ref[micro] = xhat * params[0:1] + params[8:9]
    for copy in copies[micros + 2 :]:
        copy.wait()


def project_kernel(
    normed, own, b_own, q_pair, k_pair, v_pair, bq_pair, bv_pair, wi, wu, wo, cotangent, g1, g2, s2, bo, bi, bu,
    q_ref, kv_ref, tail_ref, head_ref, w_ref, wi_ref, wu_ref, wo_ref, g_ref, rows_ref,
    bias, sems,
):
    micros, half, _ = normed.shape
    width = q_pair.shape[1]
    pairs = [(wi, wi_ref), (wu, wu_ref), (wo, wo_ref)]
    pairs += [(cotangent.at[m, my_rows(cotangent.shape[1])], g_ref.at[m]) for m in range(micros)]
    pairs += [(v, rows_ref.at[i]) for i, v in enumerate((g1, g2, s2, bo, bi, bu))]
    copies = copy_all(pairs, sems)
    for number, pair in enumerate((q_pair, k_pair, v_pair)):
        at = 2 * number * width
        w_ref[:, lanes_of(0, width, at)] = own[:, number * width : (number + 1) * width]
        w_ref[:, lanes_of(1, width, at)] = pair[...]
    bias[...] = jnp.zeros_like(bias)
    bias[:, lanes_of(0, width)] = b_own[:, :width]
    bias[:, lanes_of(1, width)] = bq_pair[...]
    bias[:, lanes_of(0, width, 4 * width)] = b_own[:, width:]
    bias[:, lanes_of(1, width, 4 * width)] = bv_pair[...]
    for micro in range(micros):
        out = mm(normed[micro], w_ref[...]) + bias[...]
        q_ref[micro] = out[:, : 2 * width]
        kv_ref[micro] = out[:, 2 * width :]
        tail_ref[micro, :CACHE] = kv_ref[micro, half - CACHE :]
        tail_ref[micro, CACHE:] = seg_means(kv_ref[micro, half - SUMS * SEG :])
        head_ref[micro] = kv_ref[micro, :AHEAD]
    for copy in copies:
        copy.wait()


def fill_keys(kv, cache, ahead, kx, sx):
    length = kv.shape[0]
    segs = length // SEG
    kx[CACHE : CACHE + length] = kv
    sx[SUMS : SUMS + segs] = seg_means(kv)
    if cache is not None:
        kx[:CACHE] = cache[:CACHE]
        kx[CACHE + length :] = ahead
        sx[:SUMS] = cache[CACHE:]
        sx[SUMS + segs :] = jnp.zeros((SUMS, kv.shape[1]), F32)


def summary_start(block):
    return (block * (BLOCK // SEG) + SUMS - MEM) // SUMS * SUMS


def key_window(kx, sx, block, lanes):
    start = summary_start(block)
    rows = [kx[block * BLOCK : block * BLOCK + WIN, lanes], sx[start : start + SWIN, lanes]]
    return jnp.concatenate(rows + [jnp.zeros((KEYS - WIN - SWIN, PAIR), F32)], axis=0)


def by_head(values):
    first = lax.broadcasted_iota(jnp.int32, values.shape, 1) < HEAD_DIM
    return jnp.concatenate([jnp.where(first, values, 0.0), jnp.where(first, 0.0, values)], axis=0)


def side_by_side(values):
    rows = values.shape[0] // 2
    first = lax.broadcasted_iota(jnp.int32, (rows, values.shape[1]), 1) < HEAD_DIM
    return jnp.where(first, values[:rows], values[rows:])


def owner_of(segment, bounds):
    owner = jnp.where(segment < 0, -1, 0)
    for bound in bounds:
        owner = owner + (segment >= bound).astype(jnp.int32)
    return owner


def visible(block, base, bounds):
    row = lax.broadcasted_iota(jnp.int32, (2 * BLOCK, 1), 0) % BLOCK
    column = lax.broadcasted_iota(jnp.int32, (1, KEYS), 1)
    query_seg = block * (BLOCK // SEG) + row // SEG
    frame = block * BLOCK - CACHE + column
    is_frame = column < WIN
    summary = summary_start(block) - SUMS + column - WIN
    key_seg = jnp.where(is_frame, (frame + CACHE) // SEG - CACHE // SEG, summary)
    key_seg = jnp.where(column < WIN + SWIN, key_seg, -(1 << 20))
    inside = (frame >= query_seg * SEG - LC) & (frame < query_seg * SEG + SEG + RC)
    near = (key_seg >= query_seg - MEM) & (key_seg < query_seg)
    seen = (is_frame & inside) | ((column >= WIN) & near)
    return seen & (owner_of(key_seg + base, bounds) == owner_of(query_seg + base, bounds))


def bounds_of(counts, micro):
    bounds, total = [], 0
    for utterance in range(counts.shape[1]):
        total = total + counts[micro, utterance]
        bounds.append(total)
    return bounds


def first_segment(length):
    return (lax.axis_index("tm") * 2 + near_bit()) * (length // SEG)


def attend_block(block, seen, query, kx, sx, keep, put):
    width = query.shape[1]
    for pair in range(width // PAIR):
        lanes = slice(pair * PAIR, (pair + 1) * PAIR)
        value_lanes = slice(width + pair * PAIR, width + (pair + 1) * PAIR)
        scores = mm(by_head(query[:, lanes] * HEAD_DIM ** (-0.5)), key_window(kx, sx, block, lanes), 1, 1)
        scores = jnp.where(seen, scores, MASKED)
        weights = jnp.exp(scores - jnp.max(scores, axis=-1, keepdims=True))
        weights = weights / jnp.sum(weights, axis=-1, keepdims=True)
        keep(pair, weights)
        put(lanes, side_by_side(mm(weights, key_window(kx, sx, block, value_lanes))))


def block_rows(block):
    return slice(block * BLOCK, (block + 1) * BLOCK)


def attend_inner_kernel(counts, q_ref, kv_ref, mix_ref, p_ref, kx, sx):
    micros, length, _ = q_ref.shape
    blocks = length // BLOCK
    base = first_segment(length)
    for micro in range(micros):
        fill_keys(kv_ref[micro], None, None, kx, sx)
        bounds = bounds_of(counts, micro)
        for number, block in enumerate(range(1, blocks - 1)):
            def keep(pair, weights):
                p_ref[micro, number, pair] = weights

            def put(lanes, values):
                mix_ref[micro, block_rows(number), lanes] = values

            seen = visible(block, base, bounds)
            attend_block(block, seen, q_ref[micro, block_rows(block)], kx, sx, keep, put)


def attend_outer_kernel(micro, counts, q_ref, kv_ref, cache, ahead, inner, *refs):
    *refs, kx, sx = refs
    passed = len(refs) // 2 - 1
    mix_ref, p_ref = refs[passed : passed + 2]
    for source, target in zip(refs[:passed], refs[passed + 2 :], strict=True):
        target[...] = source[...]
    _, length, _ = q_ref.shape
    blocks = length // BLOCK
    base = first_segment(length)
    fill_keys(kv_ref[0], cache[0], ahead[0], kx, sx)
    bounds = bounds_of(counts, micro)
    mix_ref[BLOCK : length - BLOCK] = inner[0]
    for number, block in enumerate((0, blocks - 1)):
        def keep(pair, weights):
            p_ref[number, pair] = weights

        def put(lanes, values):
            mix_ref[block_rows(block), lanes] = values

        seen = visible(block, base, bounds)
        attend_block(block, seen, q_ref[0, block_rows(block)], kx, sx, keep, put)


def back_block(block, weights_of, query, grads, kx, sx, dq_ref, dkx, dsx):
    width = query.shape[1]
    start = summary_start(block)
    frames = slice(block * BLOCK, block * BLOCK + WIN)
    for pair in range(width // PAIR):
        lanes = slice(pair * PAIR, (pair + 1) * PAIR)
        value_lanes = slice(width + pair * PAIR, width + (pair + 1) * PAIR)
        weights = weights_of(pair)
        grad = by_head(grads[:, lanes])
        dweights = mm(grad, key_window(kx, sx, block, value_lanes), 1, 1)
        dscores = weights * (dweights - jnp.sum(dweights * weights, axis=-1, keepdims=True))
        dquery = side_by_side(mm(dscores, key_window(kx, sx, block, lanes)))
        dq_ref[block_rows(block), lanes] = dquery * HEAD_DIM ** (-0.5)
        dkeys = mm(dscores, by_head(query[:, lanes] * HEAD_DIM ** (-0.5)), 0, 0)
        dvalues = mm(weights, grad, 0, 0)
        dkx[frames, lanes] += dkeys[:WIN]
        dkx[frames, value_lanes] += dvalues[:WIN]
        dsx[start : start + SWIN, lanes] += dkeys[WIN : WIN + SWIN]
        dsx[start : start + SWIN, value_lanes] += dvalues[WIN : WIN + SWIN]


def back_outer_kernel(
    a_ref, b_ref, mid_ref, g_ref, params, wo_own, wo_pair, q_ref, kv_ref, cache, ahead, p_ref,
    dmid_ref, dmix_ref, dq_ref, back_ref, fore_ref, vec_ref, dkx, dsx,
    kx, sx,
):
    length, features = mid_ref.shape
    width = wo_own.shape[0]
    blocks = length // BLOCK
    grad = a_ref[...] + b_ref[...]
    xhat, rate = normalise(mid_ref[...])
    dmid = g_ref[0] + norm_back(grad, params[SECOND_GAIN], xhat, rate)
    dmid_ref[...] = dmid
    vec_ref[0:1] = column_sums(dmid)
    vec_ref[1:2] = column_sums(grad * xhat)
    vec_ref[2:3] = column_sums(grad)
    dmix_ref[:, lanes_of(0, width)] = mm(dmid, wo_own[...], 1, 1)
    dmix_ref[:, lanes_of(1, width)] = mm(dmid, wo_pair[...], 1, 1)
    fill_keys(kv_ref[0], cache[0], ahead[0], kx, sx)
    dkx[...] = jnp.zeros_like(dkx)
    dsx[...] = jnp.zeros_like(dsx)
    for number, block in enumerate((0, blocks - 1)):
        rows = block_rows(block)
        back_block(
            block, lambda pair: p_ref[number, pair], q_ref[0, rows], dmix_ref[rows], kx, sx, dq_ref, dkx, dsx
        )
    dq_ref[BLOCK : length - BLOCK] = jnp.zeros((length - 2 * BLOCK, dq_ref.shape[1]), F32)
    back_ref[:CACHE] = dkx[:CACHE]
    back_ref[CACHE:] = dsx[:SUMS]
    fore_ref[...] = dkx[CACHE + length :]


def back_inner_kernel(
    dmid, dmix, mix, q_ref, kv_ref, p_ref, dq_in, dkx_in, dsx_in,
    dq_ref, dkv_ref, dsum_ref, dwo_own, dwo_pair,
    kx, sx, dkx, dsx, dwo,
):
    length = dmid.shape[0]
    width = dwo_own.shape[1]
    blocks = length // BLOCK
    dwo[...] = mm(dmid[...], mix[...], 0, 0)
    dwo_own[...] = dwo[:, lanes_of(0, width)]
    dwo_pair[...] = dwo[:, lanes_of(1, width)]
    fill_keys(kv_ref[0], None, None, kx, sx)
    dq_ref[...] = dq_in[...]
    dkx[...] = dkx_in[...]
    dsx[...] = dsx_in[...]
    for number, block in enumerate(range(1, blocks - 1)):
        rows = block_rows(block)
        back_block(
            block, lambda pair: p_ref[0, number, pair], q_ref[0, rows], dmix[rows], kx, sx, dq_ref, dkx, dsx
        )
    dkv_ref[...] = dkx[CACHE : CACHE + length]
    dsum_ref[...] = dsx[SUMS : SUMS + length // SEG]


def feed_kernel(
    mix_own, mix_far, wo_own, wo_pair, wo_far, wo_far_pair, x_ref, g_ref, params,
    wi_own, wi_pair, bi_pair, wu_own, wu_pair,
    n2_ref, h_ref, dpre_ref, mid_ref, part_ref,
    mix, wo,
):
    width = wo_own.shape[0]
    hidden = wi_own.shape[1]
    far = far_bit()
    here = pl.multiple_of(far * 2 * width, 2 * width)
    there = pl.multiple_of((1 - far) * 2 * width, 2 * width)
    mix[:, pl.ds(here, 2 * width)] = mix_own[...]
    mix[:, pl.ds(there, 2 * width)] = mix_far[...]
    wo[lanes_of(0, width, here)] = wo_own[...]
    wo[lanes_of(1, width, here)] = wo_pair[...]
    wo[lanes_of(0, width, there)] = wo_far[...]
    wo[lanes_of(1, width, there)] = wo_far_pair[...]
    middle = x_ref[0] + mm(mix[...], wo[...]) + params[OUT_BIAS]
    mid_ref[...] = middle
    xhat, _ = normalise(middle)
    normed = xhat * params[SECOND_GAIN] + params[SECOND_SHIFT]
    n2_ref[...] = normed
    part = None
    for place, (wi, wu, bias) in enumerate(((wi_own, wu_own, params[INNER_BIAS]), (wi_pair, wu_pair, bi_pair[...]))):
        at = slice(place * hidden, (place + 1) * hidden)
        pre = mm(normed, wi[...]) + bias
        phi = 0.5 + 0.5 * lax.erf(pre * (0.5**0.5))
        h_ref[:, at] = pre * phi
        slope = phi + pre * (jnp.exp(-0.5 * pre * pre) * 0.3989422804014327)
        dpre = mm(g_ref[0], wu[...], 1, 1) * slope
        dpre_ref[:, at] = dpre
        step = mm(dpre, wi[...], 1, 1)
        part = step if part is None else part + step
    part_ref[...] = part


def put_rows(value, outs):
    at = 0
    for out in outs:
        count = out.shape[0]
        out[...] = value[at : at + count]
        at += count


def inner_weights_kernel(n2_0, n2_1, d_0, d_1, own_ref, *rest):
    *pair, vec_ref = rest
    hidden = own_ref.shape[1]
    for place, outs in enumerate(((own_ref,), pair)):
        at = slice(place * hidden, (place + 1) * hidden)
        put_rows(mm(n2_0[...], d_0[:, at], 0, 0) + mm(n2_1[...], d_1[:, at], 0, 0), outs)
        vec_ref[place : place + 1] = column_sums(d_0[:, at]) + column_sums(d_1[:, at])


def outer_weights_kernel(h_0, h_1, g_ref, own_ref, *rest):
    *pair, vec_ref = rest
    hidden = own_ref.shape[0]
    for place, outs in enumerate(((own_ref,), pair)):
        at = slice(place * hidden, (place + 1) * hidden)
        put_rows(mm(h_0[:, at], g_ref[0], 0, 0) + mm(h_1[:, at], g_ref[1], 0, 0), outs)
    vec_ref[...] = column_sums(g_ref[0]) + column_sums(g_ref[1])


def out_half_kernel(mid_ref, part, far, params, *outs):
    put_rows(mid_ref[...] + (part[...] + far[...]) + params[OUTER_BIAS], outs)


def feed_out_kernel(h_ref, wu_own, wu_pair, out_ref):
    hidden = wu_own.shape[0]
    out_ref[...] = mm(h_ref[:, :hidden], wu_own[...]) + mm(h_ref[:, hidden:], wu_pair[...])


def project_back_kernel(
    dq, dkv, dsum, cache_back, ahead_back, xhat, w_ref,
    dqkv_ref, part_ref, vec_ref, dsx,
):
    length, wide = dq.shape
    segs = length // SEG
    dsx[...] = dsum[...]
    dsx[segs - SUMS :] += cache_back[0, CACHE:]
    spread = jnp.broadcast_to((dsx[...] * (1.0 / SEG))[:, None, :], (segs, SEG, 2 * wide))
    dqkv_ref[:, :wide] = dq[...]
    dqkv_ref[:, wide:] = dkv[...] + spread.reshape(length, 2 * wide)
    dqkv_ref[length - CACHE :, wide:] += cache_back[0, :CACHE]
    dqkv_ref[:AHEAD, wide:] += ahead_back[0]
    part = mm(dqkv_ref[...], w_ref[...], 1, 1)
    part_ref[...] = part
    vec_ref[0:1] = column_sums(part * xhat[0])
    vec_ref[1:2] = column_sums(part)


def project_weights_kernel(
    normed, d_0, d_1, wo_own_0, wo_own_1, wo_pair_0, wo_pair_1, mid_0, mid_1, first_0, first_1, vec_outer, vec_inner,
    own_0, own_1, rows_ref, pair_rows, *rest,
):
    *pair, message, sums, row = rest
    features = normed.shape[2]
    width = wo_own_0.shape[1]
    hidden = vec_inner.shape[1]
    total = None
    for micro, grads in enumerate((d_0, d_1)):
        step = mm(normed[micro], grads[...], 0, 0)
        total = step if total is None else total + step
    sums[...] = total
    row[...] = column_sums(d_0[...]) + column_sums(d_1[...])
    rows_ref[0:3] = (mid_0[...] + mid_1[...]) * 0.5
    rows_ref[3:5] = first_0[...] + first_1[...]
    rows_ref[5:6] = vec_outer[...] * 0.5
    rows_ref[6:] = jnp.zeros((2, features), F32)
    pair_rows[0:6] = rows_ref[0:6]
    pair_rows[6:] = jnp.zeros((2, features), F32)
    for place, out_ref in enumerate((rows_ref, pair_rows)):
        for number in range(3):
            lanes = slice(number * width, (number + 1) * width)
            out_ref[6:7, lanes] = row[:, lanes_of(place, width, 2 * number * width)]
        out_ref[7:8, :hidden] = vec_inner[place : place + 1]
    for place, (outs, wo_0, wo_1) in enumerate((((own_0, own_1), wo_own_0, wo_own_1), (pair, wo_pair_0, wo_pair_1))):
        for number in range(3):
            lanes = slice(number * width, (number + 1) * width)
            message[:, lanes] = sums[:, lanes_of(place, width, 2 * number * width)]
        message[:, 3 * width :] = wo_0[...] + wo_1[...]
        put_rows(message, outs)


def frames_back_kernel(a_ref, b_ref, xhat, rate, dmid_ref, params, *outs):
    grad = norm_back(a_ref[...] + b_ref[...], params[FIRST_GAIN], xhat[0], rate[0, :, :1])
    put_rows(dmid_ref[...] + grad, outs)


def place_kernel(*refs):
    *pieces, out, sems = refs
    half = out.shape[1] // 2
    near = near_bit()
    pairs = []
    at = 0
    for piece in pieces:
        count = piece.shape[0]
        micro, at_half = at // (2 * half), at // half % 2
        start = (near + at_half * (1 - 2 * near)) * half + at % half
        pairs.append((piece, out.at[micro, pl.ds(pl.multiple_of(start, count), count)]))
        at += count
    for copy in copy_all(pairs, sems):
        copy.wait()


def place_of(bit):
    return lax.axis_index("tm") // bit % 2


def add_pieces(work, a_ref, pieces):
    at = 0
    for piece in pieces:
        count = piece.shape[0]
        work[at : at + count] = a_ref[at : at + count] + piece[...]
        at += count


def add_split_kernel(bit, rows, a_ref, *refs):
    if rows:
        rows_ref, *pieces, got_rows, mine_ref, theirs_ref, new_rows, work = refs
        new_rows[...] = rows_ref[...] + got_rows[...]
    else:
        *pieces, mine_ref, theirs_ref, work = refs
    half = mine_ref.shape[0]
    add_pieces(work, a_ref, pieces)
    place = place_of(bit)
    mine_ref[...] = work[pl.ds(pl.multiple_of(place * half, half), half)]
    theirs_ref[...] = work[pl.ds(pl.multiple_of((1 - place) * half, half), half)]


def add_kernel(rows, a_ref, *refs):
    if rows:
        rows_ref, *pieces, got_rows, out_ref, new_rows = refs
        new_rows[...] = rows_ref[...] + got_rows[...]
    else:
        *pieces, out_ref = refs
    add_pieces(out_ref, a_ref, pieces)


def join_kernel(bit, a_ref, b_ref, out_ref):
    half = a_ref.shape[0]
    place = place_of(bit)
    out_ref[pl.ds(pl.multiple_of(place * half, half), half)] = a_ref[...]
    out_ref[pl.ds(pl.multiple_of((1 - place) * half, half), half)] = b_ref[...]


def join_out_kernel(bit, a_ref, b_ref, out, sems):
    half = a_ref.shape[0]
    place = place_of(bit)
    pairs = [
        (a_ref, out.at[pl.ds(pl.multiple_of(place * half, half), half)]),
        (b_ref, out.at[pl.ds(pl.multiple_of((1 - place) * half, half), half)]),
    ]
    for copy in copy_all(pairs, sems):
        copy.wait()


def join_heads_kernel(bits, *refs):
    *parts, wq, wk, wv, wo = refs
    width = wq.shape[1]
    at = 0
    for number, bit in enumerate(bits):
        mine, theirs = parts[2 * number : 2 * number + 2]
        half = mine.shape[0]
        place = place_of(bit)
        for where, part in ((place, mine), (1 - place, theirs)):
            rows = pl.ds(pl.multiple_of(at + where * half, half), half)
            for heads, out in enumerate((wq, wk, wv)):
                out[rows, :] = part[:, heads * width : (heads + 1) * width]
            wo[:, rows] = part[:, 3 * width :].T
        at += 2 * half


def small_kernel(rows, far, *outs):
    width = outs[-3].shape[1]
    for number, out in enumerate(outs[:6]):
        out[...] = rows[number : number + 1] + far[number : number + 1]
    outs[6][...] = rows[6:7, :width]
    outs[7][...] = rows[6:7, 2 * width : 3 * width]
    outs[8][...] = rows[7:8, : outs[8].shape[1]]


def swap(value, axis, bit):
    size = lax.axis_size(axis)
    return lax.ppermute(value, axis, [(i, i ^ bit) for i in range(size)])


def swap_near(parts):
    return [swap(part, "head", 1) for part in parts]


def shift_halves(value, by):
    group = lax.axis_size("head")
    halves = 2 * lax.axis_size("tm")
    pairs = []
    for source in range(halves):
        target = source + by
        if 0 <= target < halves:
            for far in range(group // 2):
                place = lambda at: at // 2 * group + far * 2 + at % 2
                pairs.append((place(source), place(target)))
    return lax.ppermute(value, ("tm", "head"), pairs)


class SumOverTm:
    def __init__(self, run, a, b, first, rows=None):
        bits = [1 << i for i in range(lax.axis_size("tm").bit_length() - 1)]
        if first in bits:
            bits.remove(first)
            bits.insert(0, first)
        self.run, self.value, self.got = run, a, list(b)
        self.rows = [] if rows is None else [rows]
        self.down, self.last, self.up, self.place = bits[:-1], bits[-1:], bits[-2::-1], None
        self.step()

    def step(self):
        run, value = self.run, self.value
        count, features = value.shape
        has_rows = bool(self.rows)
        extra = [v.shape for v in self.rows]
        if self.down:
            bit = self.down.pop(0)
            half = (count // 2, features)
            self.value, message, *self.rows = run.call(
                functools.partial(add_split_kernel, bit, has_rows), "add_split", 0.1, [half, half] + extra,
                (value, *self.rows, *self.got), scratch=[value.shape],
            )
            self.got = [swap(v, "tm", bit) for v in (message, *self.rows)]
            return
        if self.place is None:
            self.value, *self.rows = run.call(
                functools.partial(add_kernel, has_rows), "add", 0.05, [value.shape] + extra,
                (value, *self.rows, *self.got),
            )
            if self.last:
                bit = self.last.pop()
                self.got = [swap(v, "tm", bit) for v in (self.value, *self.rows)]
                return
        else:
            (self.value,) = run.call(
                functools.partial(join_kernel, self.place), "join", 0.05, [(2 * count, features)], (value, *self.got)
            )
        self.place = self.up.pop(0)
        self.got = [swap(self.value, "tm", self.place)]

    @property
    def joined(self):
        return not self.up

    def halves(self):
        return (self.value, *self.got)


def per_device(
    frames, cotangent, seg_counts, query_weight, query_bias, key_weight, value_weight, value_bias,
    out_weight, out_bias, first_gain, first_shift, second_gain, second_shift,
    inner_weight, inner_bias, outer_weight, outer_bias,
):
    micro_count, shard, features = frames.shape
    width = query_weight.shape[1]
    hidden = inner_weight.shape[1]
    length = shard // 2
    segs = length // SEG
    blocks = length // BLOCK
    pairs = 2 * width // PAIR
    row = lambda v: v.reshape(1, v.shape[0])
    bq, bv, bo, bi, bu = map(row, (query_bias, value_bias, out_bias, inner_bias, outer_bias))
    g1, s1, g2, s2 = map(row, (first_gain, first_shift, second_gain, second_shift))
    big = (length, features)
    quarter = (length // 2, features)
    each = (micro_count, length)
    run = Steps()
    smem = pl.BlockSpec(memory_space=pltpu.SMEM)

    wq_pair, wk_pair, wv_pair, bq_pair, bv_pair = (
        swap(v, "head", 1) for v in (query_weight, key_weight, value_weight, bq, bv)
    )
    wo_far = swap(out_weight, "head", 2)

    x, xhat, rate, normed, w_own, b_own = run.call(
        norm_kernel, "norm", 0.8,
        [each + (features,)] * 2 + [each + (128,), each + (features,), (features, 3 * width), (1, 2 * width)],
        (frames, g1, s1, query_weight, key_weight, value_weight, bq, bv),
        scratch=[(16, features)], copies=micro_count + 7, far=range(8),
    )
    q, kv, tail, ahead, w_all, wi, wu, wo, g, params = run.call(
        project_kernel, "project", 2.2,
        [each + (2 * width,), each + (4 * width,),
         (micro_count, CACHE + SUMS, 4 * width), (micro_count, AHEAD, 4 * width), (features, 6 * width),
         inner_weight.shape, outer_weight.shape, out_weight.shape, each + (features,), (6, 1, features)],
        (normed, w_own, b_own, wq_pair, wk_pair, wv_pair, bq_pair, bv_pair,
         inner_weight, outer_weight, out_weight, cotangent, g1, g2, s2, bo, bi, bu),
        scratch=[(1, 6 * width)], copies=micro_count + 9, far=range(8, 18),
    )
    cache = shift_halves(tail, 1)
    ahead = shift_halves(ahead, -1)
    wo_pair, wi_pair, wu_pair, bi_pair = (swap(v, "head", 1) for v in (wo, wi, wu, params[INNER_BIAS]))

    key_scratch = [(CACHE + length + AHEAD, 4 * width), (SUMS + segs + SUMS, 4 * width)]
    q_spec = lambda m: micro_block((length, 2 * width), m)
    kv_spec = lambda m: micro_block((length, 4 * width), m)
    cache_spec = lambda m: micro_block((CACHE + SUMS, 4 * width), m)
    ahead_spec = lambda m: micro_block((AHEAD, 4 * width), m)
    square = (2 * BLOCK, KEYS)
    mix_inner, p_inner = run.call(
        attend_inner_kernel, "attend_inner", 3.7,
        [(micro_count, length - 2 * BLOCK, 2 * width), (micro_count, blocks - 2, pairs) + square],
        (seg_counts, q, kv), {0: smem}, key_scratch,
    )
    mix, mix_far, p_outer = [], [], []
    for m in range(micro_count):
        passed = [] if m else [wo_far]
        mix_m, p_m, *passed = run.call(
            functools.partial(attend_outer_kernel, m), "attend_outer", 2.05,
            [(length, 2 * width), (2, pairs) + square] + [v.shape for v in passed],
            (seg_counts, q, kv, cache, ahead, mix_inner, *passed),
            {0: smem, 1: q_spec(m), 2: kv_spec(m), 3: cache_spec(m), 4: ahead_spec(m),
             5: micro_block((length - 2 * BLOCK, 2 * width), m)},
            key_scratch,
        )
        mix.append(mix_m)
        mix_far.append(swap(mix_m, "head", 2))
        p_outer.append(p_m)
        if passed:
            wo_far_pair = swap(passed[0], "head", 1)
    feed, dn2 = [], []
    for m in range(micro_count):
        feed.append(run.call(
            feed_kernel, "feed", 3.9,
            [big, (length, 2 * hidden), (length, 2 * hidden), big, big],
            (mix[m], mix_far[m], wo, wo_pair, wo_far, wo_far_pair, x, g, params, wi, wi_pair, bi_pair, wu, wu_pair),
            {6: micro_block(big, m), 7: micro_block(big, m)},
            [(length, features), (features, features)],
        ))
        dn2.append((feed[m][4], swap(feed[m][4], "head", 2)))

    def feed_out(m):
        (part,) = run.call(feed_out_kernel, "feed_out", 1.1, [big], (feed[m][1], wu, wu_pair))
        return part, swap(part, "head", 2)

    def out_half(m):
        half = run.call(out_half_kernel, "out_half", 0.1, [quarter] * 2, (feed[m][3], *parts[m], params))
        return [*half, *swap_near(half)]

    def back_outer(m):
        return run.call(
            back_outer_kernel, "back_outer", 2.7,
            [big, (length, 2 * width), (length, 2 * width), (CACHE + SUMS, 4 * width), (AHEAD, 4 * width), (3, features)]
            + key_scratch,
            (*dn2[m], feed[m][3], g, params, wo, wo_pair, q, kv, cache, ahead, p_outer[m]),
            {3: micro_block(big, m), 7: q_spec(m), 8: kv_spec(m), 9: cache_spec(m), 10: ahead_spec(m)},
            key_scratch,
        )

    def back_inner(m):
        dmid, dmix, dq, _, _, _, dkx, dsx = outers[m]
        return run.call(
            back_inner_kernel, "back_inner", 1.9,
            [(length, 2 * width), (length, 4 * width), (segs, 4 * width), (features, width), (features, width)],
            (dmid, dmix, mix[m], q, kv, p_inner, dq, dkx, dsx),
            {3: q_spec(m), 4: kv_spec(m), 5: micro_block((blocks - 2, pairs) + square, m)},
            key_scratch * 2 + [(features, 2 * width)],
        )

    def project_back(m):
        dq, dkv, dsum, _, _ = inners[m]
        return run.call(
            project_back_kernel, "project_back", 0.9,
            [(length, 6 * width), big, (2, features)],
            (dq, dkv, dsum, cache_back, ahead_back, xhat, w_all),
            {3: cache_spec(m), 4: ahead_spec(m), 5: micro_block(big, m)},
            [(segs, 4 * width)],
        )

    def frames_back(m):
        half = run.call(
            frames_back_kernel, "frames_back", 0.3, [quarter] * 2,
            (*dn1[m], xhat, rate, outers[m][0], params),
            {2: micro_block(big, m), 3: micro_block((length, 128), m)},
        )
        return [*half, *swap_near(half)]

    def place(halves):
        args = [half for both in halves for half in both]
        (out,) = run.call(
            place_kernel, "place", 1.3, [(micro_count, 2 * length, features)], args, copies=len(args), far_outs=[0],
        )
        return out

    inner_own, *inner_pair, vec_inner = run.call(
        inner_weights_kernel, "inner_weights", 2.0,
        [(features, hidden)] + [(features // 4, hidden)] * 4 + [(2, hidden)],
        (feed[0][0], feed[1][0], feed[0][2], feed[1][2]),
    )
    inner_pair = swap_near(inner_pair)
    outer_own, *outer_pair, vec_outer = run.call(
        outer_weights_kernel, "outer_weights", 1.95,
        [(hidden, features)] + [(hidden // 4, features)] * 4 + [(1, features)],
        (feed[0][1], feed[1][1], g),
    )
    outer_pair = swap_near(outer_pair)
    parts, outers, inners, fronts, dn1, outs, halves = [], [], [], [], [], [], []
    parts.append(feed_out(0))
    inner = SumOverTm(run, inner_own, inner_pair, 2)
    outer = SumOverTm(run, outer_own, outer_pair, 1)
    outers.append(back_outer(0))
    inners.append(back_inner(0))
    outers.append(back_outer(1))
    cache_back = shift_halves(jnp.stack([outers[0][3], outers[1][3]]), -1)
    ahead_back = shift_halves(jnp.stack([outers[0][4], outers[1][4]]), 1)
    inners.append(back_inner(1))
    parts.append(feed_out(1))
    inner.step()
    outer.step()
    outs.append(out_half(0))
    for m in range(micro_count):
        fronts.append(project_back(m))
        dn1.append((fronts[m][1], swap(fronts[m][1], "head", 2)))
    attn_0, attn_1, rows, pair_rows, *attn_pair = run.call(
        project_weights_kernel, "project_weights", 1.8,
        [(features // 2, 4 * width)] * 2 + [(8, features)] * 2 + [(features // 4, 4 * width)] * 4,
        (normed, fronts[0][0], fronts[1][0], inners[0][3], inners[1][3], inners[0][4], inners[1][4],
         outers[0][5], outers[1][5], fronts[0][2], fronts[1][2], vec_outer, vec_inner),
        scratch=[(features, 4 * width), (features, 6 * width), (1, 6 * width)],
    )
    *attn_pair, pair_rows = swap_near([*attn_pair, pair_rows])
    inner.step()
    outer.step()
    attn_0 = SumOverTm(run, attn_0, [*attn_pair[:2], pair_rows], 1, rows)
    attn_1 = SumOverTm(run, attn_1, attn_pair[2:], 2)
    outs.append(out_half(1))
    attn_0.step()
    attn_1.step()
    layer_output = place(outs)
    halves.append(frames_back(0))
    inner.step()
    outer.step()
    attn_0.step()
    attn_1.step()
    halves.append(frames_back(1))
    inner.step()
    outer.step()
    frames_grad = place(halves)
    chains = (attn_0, attn_1, inner, outer)
    while not all(chain.joined for chain in chains):
        for chain in chains:
            if not chain.joined:
                chain.step()
    square_out = dict(copies=2, far_outs=[0])
    (inner_grad,) = run.call(
        functools.partial(join_out_kernel, inner.place), "join_out", 1.0, [inner_weight.shape], inner.halves(), **square_out
    )
    (outer_grad,) = run.call(
        functools.partial(join_out_kernel, outer.place), "join_out", 1.0, [outer_weight.shape], outer.halves(), **square_out
    )
    small = run.call(
        small_kernel, "small", 0.6, [(1, features)] * 6 + [(1, width)] * 2 + [(1, hidden)],
        (attn_0.rows[0], swap(attn_0.rows[0], "head", 2)),
    )
    weights = run.call(
        functools.partial(join_heads_kernel, (attn_0.place, attn_1.place)), "join_heads", 1.0,
        [(features, width)] * 3 + [(width, features)], (*attn_0.halves(), *attn_1.halves()),
    )
    bo, g2, s2, g1, s1, bu, bq, bv, bi = (v.reshape(v.shape[1]) for v in small)
    return (
        layer_output, frames_grad, weights[0], bq, weights[1], weights[2], bv, weights[3], bo,
        g1, s1, g2, s2, inner_grad, bi, outer_grad, bu,
    )


def solution(mesh):
    in_specs = (
        P(None, "tm", None),
        P(None, "tm", None),
        P(),
        P(None, "head"),
        P("head"),
        P(None, "head"),
        P(None, "head"),
        P("head"),
        P("head", None),
        P(),
        P(),
        P(),
        P(),
        P(),
        P(None, "head"),
        P("head"),
        P("head", None),
        P(),
    )
    out_specs = (
        P(None, "tm", None),
        P(None, "tm", None),
        P(None, "head"),
        P("head"),
        P(None, "head"),
        P(None, "head"),
        P("head"),
        P("head", None),
        P(),
        P(),
        P(),
        P(),
        P(),
        P(None, "head"),
        P("head"),
        P("head", None),
        P(),
    )
    return jax.shard_map(
        per_device, mesh=mesh, in_specs=in_specs, out_specs=out_specs, check_vma=False
    )
```

```python
import functools

import jax
import jax.numpy as jnp
from jax import lax
from jax.experimental import pallas as pl
from jax.experimental.pallas import tpu as pltpu
from jax.sharding import PartitionSpec as P

HEAD_DIM = 64
SEG = 16
RC = 4
LC = 30
MEM = 4

EPSILON = 1e-05
MASKED = -1e30
F32 = jnp.float32

BEFORE = MEM * SEG
AHEAD = 8
CACHE = 32
SUMS = 8
BLOCK = 64
WIN = CACHE + BLOCK + AHEAD
SWIN = 16
KEYS = 128
FIRST_GAIN, FIRST_SHIFT, SECOND_GAIN, SECOND_SHIFT, OUT_BIAS, INNER_BIAS, OUTER_BIAS = range(7)
PAIR = 2 * HEAD_DIM
MIB = 1 << 20


def mm(left, right, left_dim=1, right_dim=0):
    return lax.dot_general(
        left,
        right,
        (((left_dim,), (right_dim,)), ((), ())),
        precision=lax.Precision.HIGH,
        preferred_element_type=F32,
    )


def normalise(values):
    centred = values - jnp.mean(values, axis=-1, keepdims=True)
    variance = jnp.mean(centred * centred, axis=-1, keepdims=True)
    rate = lax.rsqrt(variance + EPSILON)
    return centred * rate, rate


def norm_back(grad, gain, xhat, rate):
    scaled = grad * gain
    first = jnp.mean(scaled, axis=-1, keepdims=True)
    second = jnp.mean(scaled * xhat, axis=-1, keepdims=True)
    return rate * (scaled - first - xhat * second)


def column_sums(values):
    return jnp.sum(values, axis=0, keepdims=True)


def seg_means(values):
    rows, width = values.shape
    return jnp.sum(values.reshape(rows // SEG, SEG, width), axis=1) * (1.0 / SEG)


def near_bit():
    return lax.axis_index("head") % 2


def far_bit():
    return lax.axis_index("head") // 2


def my_rows(rows):
    half = rows // 2
    return pl.ds(pl.multiple_of(near_bit() * half, half), half)


def lanes_of(place, width, start=0):
    at = place + near_bit() - 2 * place * near_bit()
    return pl.ds(pl.multiple_of(start + at * width, width), width)


def half_rows(place, half):
    return pl.ds(pl.multiple_of(place * half, half), half)


def full(shape):
    return pl.BlockSpec(shape, lambda *_: (0,) * len(shape))


class Steps:
    def __init__(self):
        self.held = []
        self.us = 0.1

    def call(self, kernel, name, outs, args, specs=None, scratch=(), vmem=32, copies=0, far=(), far_outs=()):
        specs = dict(specs or {})
        given, made, held = len(args), len(outs), tuple(self.held)
        token = bool(far_outs)
        somewhere = pl.BlockSpec(memory_space=pl.ANY)
        in_hbm = pl.BlockSpec(memory_space=pltpu.HBM)

        def body(*refs):
            ins, rest = refs[:given], refs[given + len(held) :]
            if token:
                rest[made][...] = jnp.zeros(rest[made].shape, F32)
            kernel(*ins, *rest[:made], *rest[made + token :])

        args = [pltpu.with_memory_space_constraint(a, pltpu.HBM) if i in far else a for i, a in enumerate(args)]
        out_specs = [in_hbm if i in far_outs else full(shape) for i, shape in enumerate(outs)]
        out_shape = [
            pltpu.HBM(shape, F32) if i in far_outs else jax.ShapeDtypeStruct(shape, F32) for i, shape in enumerate(outs)
        ]
        if token:
            out_specs.append(full((1, 128)))
            out_shape.append(jax.ShapeDtypeStruct((1, 128), F32))
        out = pl.pallas_call(
            body,
            name=name,
            grid=(1,),
            in_specs=[in_hbm if i in far else specs.get(i, full(a.shape)) for i, a in enumerate(args)]
            + [somewhere] * len(held),
            out_specs=out_specs,
            out_shape=out_shape,
            scratch_shapes=[pltpu.VMEM(shape, F32) for shape in scratch]
            + ([pltpu.SemaphoreType.DMA((copies,))] if copies else []),
            compiler_params=pltpu.CompilerParams(vmem_limit_bytes=vmem * MIB),
            cost_estimate=pl.CostEstimate(flops=int(self.us * 5.18e8), bytes_accessed=0, transcendentals=0),
        )(*args, *held)
        self.held = [out[-1]]
        return out[:made]


def copy_all(pairs, sems):
    copies = [pltpu.make_async_copy(a, b, sems.at[i]) for i, (a, b) in enumerate(pairs)]
    for copy in copies:
        copy.start()
    return copies


def pack_kernel(wq, wk, wv, wo, bq, bv, bi, frames, out, edge, sems):
    rows, width = wq.shape
    out[rows:] = jnp.zeros((out.shape[0] - rows, out.shape[1]), F32)
    pairs = [(w, out.at[pl.ds(0, rows), pl.ds(i * width, width)]) for i, w in enumerate((wq, wk, wv))]
    for at in range(0, wo.shape[1], width):
        pairs.append((wo.at[:, pl.ds(at, width)], out.at[pl.ds(at, width), pl.ds(3 * width, width)]))
    pairs += [(b, out.at[pl.ds(rows, 1), pl.ds(i * width, width)]) for i, b in ((0, bq), (2, bv))]
    pairs.append((bi, out.at[pl.ds(rows + 1, 1), pl.ds(0, bi.shape[1])]))
    start = pl.multiple_of((1 - near_bit()) * (frames.shape[1] - BEFORE), BEFORE)
    pairs += [(frames.at[m, pl.ds(start, BEFORE)], edge.at[m]) for m in range(frames.shape[0])]
    for copy in copy_all(pairs, sems):
        copy.wait()


def norm_kernel(
    frames, gain, shift, wi, wu, wo, cotangent,
    x_ref, xhat_ref, rate_ref, normed_ref, wi_ref, wu_ref, wo_ref, g_0, g_1, before, ahead, params, sems,
):
    micros, half, _ = x_ref.shape
    rows = frames.shape[1]
    pairs = [(gain, params.at[pl.ds(0, 1)]), (shift, params.at[pl.ds(8, 1)])]
    pairs += [(frames.at[m, my_rows(rows)], x_ref.at[m]) for m in range(micros)]
    pairs += [(frames.at[m, pl.ds(half - BEFORE, BEFORE)], before.at[m]) for m in range(micros)]
    pairs += [(frames.at[m, pl.ds(half, AHEAD)], ahead.at[m]) for m in range(micros)]
    pairs += [(wo, wo_ref), (wi, wi_ref), (wu, wu_ref)]
    pairs += [(cotangent.at[m, my_rows(rows)], g) for m, g in enumerate((g_0, g_1))]
    copies = copy_all(pairs, sems)
    for copy in copies[:2]:
        copy.wait()
    for micro in range(micros):
        copies[2 + micro].wait()
        xhat, rate = normalise(x_ref[micro])
        xhat_ref[micro] = xhat
        normed_ref[micro] = xhat * params[0:1] + params[8:9]
        rate_ref[micro] = jnp.broadcast_to(rate, (half, rate_ref.shape[2]))
    for copy in copies[2 + micros :]:
        copy.wait()


def project_kernel(normed, own, pair, g1, s1, g2, s2, bo, bi, bu, q_ref, kv_ref, w_ref, bias, rows_ref, sems):
    micros, half, wide = q_ref.shape
    features = normed.shape[2]
    width = own.shape[1] // 4
    copies = copy_all([(v, rows_ref.at[i]) for i, v in enumerate((g1, s1, g2, s2, bo, bi, bu))], sems)
    for number in range(3):
        at = slice(number * width, (number + 1) * width)
        for place, source in enumerate((own, pair)):
            lanes = lanes_of(place, width, 2 * number * width)
            w_ref[:, lanes] = source[:features, at]
            bias[:, lanes] = source[features : features + 1, at]
    for micro in range(micros):
        out = mm(normed[micro], w_ref[...]) + bias[...]
        q_ref[micro] = out[:, :wide]
        kv_ref[micro] = out[:, wide:]
    for copy in copies:
        copy.wait()


def edges_kernel(edge, before, ahead, params, w_ref, bias, xhat_ref, normed_ref, kv_ref):
    near = near_bit()
    wide = w_ref.shape[1] // 3
    for micro in range(edge.shape[0]):
        first = jnp.where(near == 0, edge[micro], before[micro])
        last = jnp.where(near == 0, ahead[micro], edge[micro, :AHEAD])
        xhat, _ = normalise(jnp.concatenate([first, last], axis=0))
        normed = xhat * params[FIRST_GAIN] + params[FIRST_SHIFT]
        xhat_ref[micro] = xhat
        normed_ref[micro] = normed
        kv_ref[micro] = mm(normed, w_ref[:, wide:]) + bias[:, wide:]


def fill_keys(kv, edge, kx, sx):
    length = kv.shape[0]
    kx[BEFORE : BEFORE + length] = kv
    segs = length // SEG
    sx[SUMS : SUMS + segs] = seg_means(kv)
    if edge is not None:
        kx[:BEFORE] = edge[:BEFORE]
        kx[BEFORE + length :] = edge[BEFORE:]
        sx[: SUMS - MEM] = jnp.zeros((SUMS - MEM, kv.shape[1]), F32)
        sx[SUMS - MEM : SUMS] = seg_means(edge[:BEFORE])
        sx[SUMS + segs :] = jnp.zeros((sx.shape[0] - SUMS - segs, kv.shape[1]), F32)


def summary_start(block):
    return (block * (BLOCK // SEG) + SUMS - MEM) // SUMS * SUMS


def frame_rows(block):
    start = BEFORE - CACHE + block * BLOCK
    return slice(start, start + WIN)


def key_window(kx, sx, block, lanes):
    start = summary_start(block)
    rows = [kx[frame_rows(block), lanes], sx[start : start + SWIN, lanes]]
    return jnp.concatenate(rows + [jnp.zeros((KEYS - WIN - SWIN, PAIR), F32)], axis=0)


def by_head(values):
    first = lax.broadcasted_iota(jnp.int32, values.shape, 1) < HEAD_DIM
    return jnp.concatenate([jnp.where(first, values, 0.0), jnp.where(first, 0.0, values)], axis=0)


def side_by_side(values):
    rows = values.shape[0] // 2
    first = lax.broadcasted_iota(jnp.int32, (rows, values.shape[1]), 1) < HEAD_DIM
    return jnp.where(first, values[:rows], values[rows:])


def owner_of(segment, bounds):
    owner = jnp.where(segment < 0, -1, 0)
    for bound in bounds:
        owner = owner + (segment >= bound).astype(jnp.int32)
    return owner


def visible(block, base, bounds):
    row = lax.broadcasted_iota(jnp.int32, (2 * BLOCK, 1), 0) % BLOCK
    column = lax.broadcasted_iota(jnp.int32, (1, KEYS), 1)
    query_seg = block * (BLOCK // SEG) + row // SEG
    frame = block * BLOCK - CACHE + column
    is_frame = column < WIN
    summary = summary_start(block) - SUMS + column - WIN
    key_seg = jnp.where(is_frame, (frame + CACHE) // SEG - CACHE // SEG, summary)
    key_seg = jnp.where(column < WIN + SWIN, key_seg, -(1 << 20))
    inside = (frame >= query_seg * SEG - LC) & (frame < query_seg * SEG + SEG + RC)
    near = (key_seg >= query_seg - MEM) & (key_seg < query_seg)
    seen = (is_frame & inside) | ((column >= WIN) & near)
    return seen & (owner_of(key_seg + base, bounds) == owner_of(query_seg + base, bounds))


def bounds_of(counts, micro):
    bounds, total = [], 0
    for utterance in range(counts.shape[1]):
        total = total + counts[micro, utterance]
        bounds.append(total)
    return bounds


def first_segment(length):
    return (lax.axis_index("tm") * 2 + near_bit()) * (length // SEG)


def block_rows(block):
    return slice(block * BLOCK, (block + 1) * BLOCK)


def attend_block(block, seen, query, kx, sx, keep, put):
    width = query.shape[1]
    for pair in range(width // PAIR):
        lanes = slice(pair * PAIR, (pair + 1) * PAIR)
        value_lanes = slice(width + pair * PAIR, width + (pair + 1) * PAIR)
        scores = mm(by_head(query[:, lanes] * HEAD_DIM ** (-0.5)), key_window(kx, sx, block, lanes), 1, 1)
        scores = jnp.where(seen, scores, MASKED)
        weights = jnp.exp(scores - jnp.max(scores, axis=-1, keepdims=True))
        weights = weights / jnp.sum(weights, axis=-1, keepdims=True)
        keep(pair, weights)
        put(lanes, side_by_side(mm(weights, key_window(kx, sx, block, value_lanes))))


def attend_inner_kernel(counts, q_ref, kv_ref, mix_ref, p_ref, kx, sx):
    micros, length, _ = q_ref.shape
    base = first_segment(length)
    for micro in range(micros):
        fill_keys(kv_ref[micro], None, kx, sx)
        bounds = bounds_of(counts, micro)
        for number, block in enumerate(range(1, length // BLOCK - 1)):
            def keep(pair, weights):
                p_ref[micro, number, pair] = weights

            def put(lanes, values):
                mix_ref[micro, block_rows(number), lanes] = values

            seen = visible(block, base, bounds)
            attend_block(block, seen, q_ref[micro, block_rows(block)], kx, sx, keep, put)


def attend_outer_kernel(micro, counts, q_ref, kv_ref, edge, inner, mix_ref, p_ref, kx, sx):
    _, length, _ = q_ref.shape
    base = first_segment(length)
    fill_keys(kv_ref[micro], edge[micro], kx, sx)
    bounds = bounds_of(counts, micro)
    mix_ref[BLOCK : length - BLOCK] = inner[micro]
    for number, block in enumerate((0, length // BLOCK - 1)):
        def keep(pair, weights):
            p_ref[number, pair] = weights

        def put(lanes, values):
            mix_ref[block_rows(block), lanes] = values

        seen = visible(block, base, bounds)
        attend_block(block, seen, q_ref[micro, block_rows(block)], kx, sx, keep, put)


def back_kernel(
    micro, grad_ref, mid_ref, g_ref, params, wo_here, mix, q_ref, kv_ref, edge, p_inner, p_outer,
    dmid_ref, dq_ref, dkv_ref, dwo_own, dwo_pair, vec_ref,
    kx, sx, dsx, dmix, dwo,
):
    _, length, width = q_ref.shape
    near_width = dwo_own.shape[1]
    grad = grad_ref[...]
    xhat, rate = normalise(mid_ref[...])
    dmid = g_ref[...] + norm_back(grad, params[SECOND_GAIN], xhat, rate)
    dmid_ref[...] = dmid
    vec_ref[0:1] = column_sums(dmid)
    vec_ref[1:2] = column_sums(grad * xhat)
    vec_ref[2:3] = column_sums(grad)
    dmix[...] = mm(dmid, wo_here[...], 1, 1)
    dwo[...] = mm(dmid, mix[...], 0, 0)
    dwo_own[...] = dwo[:, lanes_of(0, near_width)]
    dwo_pair[...] = dwo[:, lanes_of(1, near_width)]
    fill_keys(kv_ref[micro], edge[micro], kx, sx)
    dkv_ref[...] = jnp.zeros_like(dkv_ref)
    dsx[...] = jnp.zeros_like(dsx)
    for block in range(length // BLOCK):
        start = summary_start(block)
        rows, frames, sums = block_rows(block), frame_rows(block), slice(start, start + SWIN)
        for pair in range(width // PAIR):
            lanes = slice(pair * PAIR, (pair + 1) * PAIR)
            value_lanes = slice(width + pair * PAIR, width + (pair + 1) * PAIR)
            inside = 0 < block < length // BLOCK - 1
            weights = p_inner[micro, block - 1, pair] if inside else p_outer[min(block, 1), pair]
            grad = by_head(dmix[rows, lanes])
            dweights = mm(grad, key_window(kx, sx, block, value_lanes), 1, 1)
            dscores = weights * (dweights - jnp.sum(dweights * weights, axis=-1, keepdims=True))
            dquery = side_by_side(mm(dscores, key_window(kx, sx, block, lanes)))
            dq_ref[rows, lanes] = dquery * HEAD_DIM ** (-0.5)
            dkeys = mm(dscores, by_head(q_ref[micro, rows, lanes] * HEAD_DIM ** (-0.5)), 0, 0)
            dvalues = mm(weights, grad, 0, 0)
            dkv_ref[frames, lanes] += dkeys[:WIN]
            dkv_ref[frames, value_lanes] += dvalues[:WIN]
            dsx[sums, lanes] += dkeys[WIN : WIN + SWIN]
            dsx[sums, value_lanes] += dvalues[WIN : WIN + SWIN]
    count = BEFORE + length
    segs = count // SEG
    spread = dsx[SUMS - MEM : SUMS - MEM + segs] * (1.0 / SEG)
    spread = jnp.broadcast_to(spread[:, None, :], (segs, SEG, 2 * width))
    dkv_ref[:count] += spread.reshape(count, 2 * width)


def feed_kernel(
    micro, mix_own, mix_far, wo_here, wo_far, wo_far_pair, x_ref, g_ref, params, pair, wi_own, wi_pair, wu_own, wu_pair,
    n2_ref, h_ref, dpre_ref, mid_ref, part_ref,
    mix, wo,
):
    width = mix_own.shape[1] // 2
    features, hidden = wi_own.shape
    far = far_bit()
    here = pl.multiple_of(far * 2 * width, 2 * width)
    there = pl.multiple_of((1 - far) * 2 * width, 2 * width)
    mix[:, pl.ds(here, 2 * width)] = mix_own[...]
    mix[:, pl.ds(there, 2 * width)] = mix_far[...]
    wo[pl.ds(here, 2 * width)] = wo_here[...]
    wo[lanes_of(0, width, there)] = wo_far[...]
    wo[lanes_of(1, width, there)] = wo_far_pair[...]
    middle = x_ref[micro] + mm(mix[...], wo[...]) + params[OUT_BIAS]
    mid_ref[...] = middle
    xhat, _ = normalise(middle)
    normed = xhat * params[SECOND_GAIN] + params[SECOND_SHIFT]
    n2_ref[...] = normed
    part = None
    for place, (wi, wu, bias) in enumerate(((wi_own, wu_own, params[INNER_BIAS][:, :hidden]), (wi_pair, wu_pair, pair[features + 1 : features + 2, :hidden]))):
        at = slice(place * hidden, (place + 1) * hidden)
        pre = mm(normed, wi[...]) + bias
        phi = 0.5 + 0.5 * lax.erf(pre * (0.5**0.5))
        h_ref[:, at] = pre * phi
        slope = phi + pre * (jnp.exp(-0.5 * pre * pre) * 0.3989422804014327)
        dpre = mm(g_ref[...], wu[...], 1, 1) * slope
        dpre_ref[:, at] = dpre
        step = mm(dpre, wi[...], 1, 1)
        part = step if part is None else part + step
    part_ref[...] = part


def put_rows(value, outs):
    at = 0
    for out in outs:
        count = out.shape[0]
        out[...] = value[at : at + count]
        at += count


def inner_weights_kernel(n2_0, n2_1, d_0, d_1, own_ref, *rest):
    *pair, vec_ref = rest
    hidden = own_ref.shape[1]
    for place, outs in enumerate(((own_ref,), pair)):
        at = slice(place * hidden, (place + 1) * hidden)
        put_rows(mm(n2_0[...], d_0[:, at], 0, 0) + mm(n2_1[...], d_1[:, at], 0, 0), outs)
        vec_ref[place : place + 1] = column_sums(d_0[:, at]) + column_sums(d_1[:, at])


def outer_weights_kernel(h_0, h_1, g_0, g_1, own_ref, *rest):
    *pair, vec_ref = rest
    hidden = own_ref.shape[0]
    for place, outs in enumerate(((own_ref,), pair)):
        at = slice(place * hidden, (place + 1) * hidden)
        put_rows(mm(h_0[:, at], g_0[...], 0, 0) + mm(h_1[:, at], g_1[...], 0, 0), outs)
    vec_ref[...] = column_sums(g_0[...]) + column_sums(g_1[...])


def feed_out_kernel(h_0, h_1, wu_own, wu_pair, out_ref):
    hidden = wu_own.shape[0]
    rows = h_0.shape[0]
    for micro, h_ref in enumerate((h_0, h_1)):
        part = mm(h_ref[:, :hidden], wu_own[...]) + mm(h_ref[:, hidden:], wu_pair[...])
        out_ref[micro * rows : (micro + 1) * rows] = part


def out_half_kernel(mid_0, mid_1, part, far, params, out):
    rows = mid_0.shape[0]
    for micro, mid_ref in enumerate((mid_0, mid_1)):
        at = slice(micro * rows, (micro + 1) * rows)
        out[at] = mid_ref[...] + (part[at] + far[at]) + params[OUTER_BIAS]


def project_back_kernel(
    dq_0, dkv_0, dq_1, dkv_1, xhat, xhat_edge, w_ref, part_ref, pair_ref, beyond_ref, vec_ref, work
):
    near = near_bit()
    length, wide = dq_0.shape
    own = slice(BEFORE, BEFORE + length)
    gain, shift = 0.0, 0.0
    for micro, (dq, dkv) in enumerate(((dq_0, dkv_0), (dq_1, dkv_1))):
        work[...] = mm(dkv[...], w_ref[:, wide:], 1, 1)
        work[own] += mm(dq[...], w_ref[:, :wide], 1, 1)
        part_ref[micro * length : (micro + 1) * length] = work[own]
        before = work[:BEFORE]
        ahead = jnp.concatenate([work[BEFORE + length :], jnp.zeros((BEFORE - AHEAD, work.shape[1]), F32)], axis=0)
        pair_ref[micro] = jnp.where(near == 0, ahead, before)
        beyond_ref[micro] = jnp.where(near == 0, before, ahead)
        gain = gain + column_sums(work[own] * xhat[micro]) + column_sums(work[:BEFORE] * xhat_edge[micro, :BEFORE])
        gain = gain + column_sums(work[BEFORE + length :] * xhat_edge[micro, BEFORE:])
        shift = shift + column_sums(work[...])
    vec_ref[0:1] = gain
    vec_ref[1:2] = shift


def edge_add_kernel(part, pair, beyond, out):
    out[...] = part[...]
    near = near_bit()
    micros = pair.shape[0]
    length = part.shape[0] // micros
    for micro in range(micros):
        end = (micro + 1) * length
        out[end - BEFORE : end] += jnp.where(near == 0, pair[micro], beyond[micro])
        out[end - length : end - length + AHEAD] += jnp.where(near == 0, beyond[micro, :AHEAD], pair[micro, :AHEAD])


def project_weights_kernel(
    normed, normed_edge, dq_0, dq_1, dkv_0, dkv_1, wo_own_0, wo_own_1, wo_pair_0, wo_pair_1, mid_0, mid_1, first, vec_outer, vec_inner,
    own_0, own_1, rows_ref, pair_0, pair_1, message, sums, row,
):
    features = normed.shape[2]
    width = wo_own_0.shape[1]
    hidden = vec_inner.shape[1]
    length, wide = dq_0.shape
    queries, keyvals = 0.0, 0.0
    for micro, (dq, dkv) in enumerate(((dq_0, dkv_0), (dq_1, dkv_1))):
        own = slice(BEFORE, BEFORE + length)
        edges = jnp.concatenate([dkv[:BEFORE], dkv[BEFORE + length :]], axis=0)
        queries = queries + mm(normed[micro], dq[...], 0, 0)
        keyvals = keyvals + mm(normed[micro], dkv[own], 0, 0) + mm(normed_edge[micro], edges, 0, 0)
    sums[:, :wide] = queries
    sums[:, wide:] = keyvals
    row[:, :wide] = column_sums(dq_0[...]) + column_sums(dq_1[...])
    row[:, wide:] = column_sums(dkv_0[...]) + column_sums(dkv_1[...])
    rows_ref[0:3] = (mid_0[...] + mid_1[...]) * 0.5
    rows_ref[3:5] = first[...]
    rows_ref[5:6] = vec_outer[...] * 0.5
    rows_ref[6:] = jnp.zeros((2, features), F32)
    half = own_0.shape[0]
    pair_0[half : half + 6] = rows_ref[0:6]
    pair_0[half + 6 :] = jnp.zeros((2, features), F32)
    for place, (out_ref, at) in enumerate(((rows_ref, 6), (pair_0, half + 6))):
        for number in range(3):
            lanes = slice(number * width, (number + 1) * width)
            out_ref[at : at + 1, lanes] = row[:, lanes_of(place, width, 2 * number * width)]
        out_ref[at + 1 : at + 2, :hidden] = vec_inner[place : place + 1]
    for place, (outs, wo_0, wo_1) in enumerate((((own_0, own_1), wo_own_0, wo_own_1), ((pair_0, pair_1), wo_pair_0, wo_pair_1))):
        for number in range(3):
            lanes = slice(number * width, (number + 1) * width)
            message[:, lanes] = sums[:, lanes_of(place, width, 2 * number * width)]
        message[:, 3 * width :] = wo_0[...] + wo_1[...]
        for number, out_ref in enumerate(outs):
            out_ref[:half] = message[number * half : (number + 1) * half]


def frames_back_kernel(a_ref, b_ref, xhat, rate, dmid_0, dmid_1, params, out):
    rows = dmid_0.shape[0]
    for micro, dmid_ref in enumerate((dmid_0, dmid_1)):
        at = slice(micro * rows, (micro + 1) * rows)
        grad = norm_back(a_ref[at] + b_ref[at], params[FIRST_GAIN], xhat[micro], rate[micro, :, :1])
        out[at] = dmid_ref[...] + grad


def place_kernel(own, pair, out, sems):
    micros, half = out.shape[0], out.shape[1] // 2
    near = near_bit()
    pairs = []
    for micro in range(micros):
        rows = pl.ds(micro * half, half)
        pairs.append((own.at[rows], out.at[micro, half_rows(near, half)]))
        pairs.append((pair.at[rows], out.at[micro, half_rows(1 - near, half)]))
    for copy in copy_all(pairs, sems):
        copy.wait()


def place_of(bit):
    return lax.axis_index("tm") // bit % 2


def add_pieces(out, a_ref, pieces, rows_ref=None, new_rows=None):
    count, at = a_ref.shape[0], 0
    for piece in pieces:
        take = min(piece.shape[0], count - at)
        if take:
            out[at : at + take] = a_ref[at : at + take] + piece[:take]
        if take < piece.shape[0]:
            new_rows[...] = rows_ref[...] + piece[take:]
        at += take


def add_split_kernel(bits, counts, rows, *refs):
    total = len(bits)
    values, refs = refs[:total], refs[total:]
    rows_ref, refs = (refs[0], refs[1:]) if rows else (None, refs)
    pieces = []
    for count in counts:
        pieces.append(refs[:count])
        refs = refs[count:]
    kept, sent, refs = refs[:total], refs[total : 2 * total], refs[2 * total :]
    new_rows, work = (refs[0], refs[1]) if rows else (None, refs[0])
    for number, bit in enumerate(bits):
        small = (rows_ref, new_rows) if rows and number == 0 else ()
        half = kept[number].shape[0]
        add_pieces(work, values[number], pieces[number], *small)
        place = place_of(bit)
        kept[number][...] = work[half_rows(place, half)]
        sent[number][:half] = work[half_rows(1 - place, half)]
        if small:
            sent[number][half:] = new_rows[...]


def last_kernel(rows, a_ref, *refs):
    rows_ref, refs = (refs[0], refs[1:]) if rows else (None, refs)
    b_ref, out_ref = refs
    half = a_ref.shape[0]
    out_ref[:half] = a_ref[...] + b_ref[:half]
    if rows:
        out_ref[half:] = rows_ref[...] + b_ref[half:]


def stack_kernel(rows, a_0, a_1, *refs):
    rows_ref, refs = (refs[0], refs[1:]) if rows else (None, refs)
    b_0, b_1, out_ref = refs
    half = a_0.shape[0]
    out_ref[:half] = a_0[...] + b_0[:half]
    out_ref[half : 2 * half] = a_1[...] + b_1[...]
    if rows:
        out_ref[2 * half :] = rows_ref[...] + b_0[half:]


def add_whole_kernel(a_ref, b_ref, *outs):
    at = 0
    for out in outs:
        count = out.shape[0]
        out[...] = a_ref[at : at + count] + b_ref[at : at + count]
        at += count


def join_kernel(bits, *refs):
    total = len(bits)
    for bit, mine, theirs, out in zip(bits, refs[:total], refs[total : 2 * total], refs[2 * total :], strict=True):
        half = mine.shape[0]
        place = place_of(bit)
        out[half_rows(place, half)] = mine[...]
        out[half_rows(1 - place, half)] = theirs[...]


def join_out_kernel(bit, mine, theirs, out, sems):
    half = mine.shape[0]
    place = place_of(bit)
    for copy in copy_all([(mine, out.at[half_rows(place, half)]), (theirs, out.at[half_rows(1 - place, half)])], sems):
        copy.wait()


def join_heads_kernel(bits, *refs):
    *parts, wq, wk, wv, wo = refs
    width = wq.shape[1]
    at = 0
    for number, bit in enumerate(bits):
        mine, theirs = parts[2 * number : 2 * number + 2]
        half = mine.shape[0]
        place = place_of(bit)
        for where, part in ((place, mine), (1 - place, theirs)):
            rows = pl.ds(pl.multiple_of(at + where * half, half), half)
            for heads, out in enumerate((wq, wk, wv)):
                out[rows, :] = part[:, heads * width : (heads + 1) * width]
            wo[:, rows] = part[:, 3 * width :].T
        at += 2 * half


def small_kernel(rows, far, outs):
    width = outs[-3].shape[1]
    for number, out in enumerate(outs[:6]):
        out[...] = rows[number : number + 1] + far[number : number + 1]
    outs[6][...] = rows[6:7, :width]
    outs[7][...] = rows[6:7, 2 * width : 3 * width]
    outs[8][...] = rows[7:8, : outs[8].shape[1]]


def finish_kernel(bits, rows, far, *refs):
    count = 2 * len(bits)
    small_kernel(rows, far, refs[count : count + 9])
    join_heads_kernel(bits, *refs[:count], *refs[count + 9 :])


def swap(value, axis, bit):
    size = lax.axis_size(axis)
    return lax.ppermute(value, axis, [(i, i ^ bit) for i in range(size)])


def swap_near(parts):
    return [swap(part, "head", 1) for part in parts]


def swap_edges(value, back):
    size, group = lax.axis_size("tm"), lax.axis_size("head")
    pairs = []
    for source in range(size):
        for place in range(group):
            target = source + (1 - 2 * (place % 2)) * (-1 if back else 1)
            if 0 <= target < size:
                pairs.append((source * group + place, target * group + (place ^ 1 if back else place)))
    return lax.ppermute(value, ("tm", "head"), pairs)


class SumsOverTm:
    def __init__(self, run, a, b, rows=None):
        bits = [1 << i for i in range(lax.axis_size("tm").bit_length() - 1)]
        self.run, self.values, self.got = run, list(a), [list(v) for v in b]
        self.rows = [] if rows is None else [rows]
        self.apart = [(bits[0], bits[1]), (bits[1], bits[0])]
        self.together, self.last = bits[2:-1], bits[-1]
        self.todo = [("split", pair) for pair in self.apart]
        self.todo.append(("stack",))
        self.todo += [("split", (bit,)) for bit in self.together] + [("last",)] * bool(self.together)
        self.todo.append(("add",))
        self.todo += [("join", (bit,)) for bit in reversed(self.together)] + [("part",)] * bool(self.together)
        self.todo.append(("join", self.apart[1]))
        self.step()

    def step(self):
        run, values = self.run, self.values
        kind, *rest = self.todo.pop(0)
        features = values[0].shape[1]
        count = values[0].shape[0]
        more = sum(v.shape[0] for v in self.rows)
        has_rows = bool(self.rows)
        shape = lambda rows: (rows, features)
        got = [piece for pieces in self.got for piece in pieces]
        if kind == "split":
            (bits,) = rest
            half = count // 2
            extra = [more] + [0] * (len(bits) - 1)
            out = run.call(
                functools.partial(add_split_kernel, bits, [len(v) for v in self.got], has_rows), "add_split",
                [shape(half)] * len(bits) + [shape(half + e) for e in extra] + [v.shape for v in self.rows],
                (*values, *self.rows, *got), scratch=[shape(count)],
            )
            self.values, messages, self.rows = out[: len(bits)], out[len(bits) : 2 * len(bits)], out[2 * len(bits) :]
            self.got = [[swap(v, "tm", bit)] for v, bit in zip(messages, bits, strict=True)]
            return
        if kind in ("stack", "last"):
            if kind == "stack":
                (value,) = run.call(
                    functools.partial(stack_kernel, has_rows), "stack", [shape(2 * count + more)], (*values, *self.rows, *got)
                )
                count = 2 * count
            else:
                (value,) = run.call(
                    functools.partial(last_kernel, has_rows), "stack", [shape(count + more)], (*values, *self.rows, *got)
                )
            if kind == "stack" and self.together:
                self.values, self.rows = [value[:count]], [value[count:]] * has_rows
                self.values, self.got = self.values, [[]]
                return self.step()
            self.values, self.count = [value], count
            self.got = [[swap(value, "tm", self.last)]]
            return
        if kind == "add":
            parts = [self.count] if self.together else [self.count // 2] * 2
            out = run.call(
                add_whole_kernel, "add", [shape(n) for n in parts] + [v.shape for v in self.rows], (*values, *got)
            )
            self.values, self.rows = out[: len(parts)], out[len(parts) :]
        elif kind == "join":
            (bits,) = rest
            self.values = run.call(
                functools.partial(join_kernel, bits), "join", [shape(2 * count)] * len(bits), (*values, *got)
            )
        elif kind == "part":
            self.values = [values[0][: count // 2], values[0][count // 2 :]]
        following = self.todo[0] if self.todo else ("join", self.apart[0])
        if following[0] == "part":
            return self.step()
        self.got = [[swap(v, "tm", bit)] for v, bit in zip(self.values, following[1], strict=True)]

    @property
    def joined(self):
        return not self.todo

    def halves(self, number):
        return self.apart[0][number], (self.values[number], *self.got[number])


ORDER = (
    ("pack", 8), ("norm", 4.8), ("project", 2.2), ("attend_inner", 11), ("edges", 1), ("hand_on", 0.5),
    ("attend_outer0", 24), ("attend_outer1", 1), ("feed0", 18), ("feed1", 14), ("outer_weights", 6),
    ("inner_weights", 11), ("feed_out", 0.6), ("grad_sum0", 18), ("ffn", 11), ("back0", 6), ("grad_sum1", 18),
    ("back1", 0.5), ("ffn", 0.1), ("project_back", 1.8), ("project_weights", 2), ("ffn", 0.1), ("edge_add", 11),
    ("out_half", 6), ("heads", 1), ("heads", 0.1), ("ffn", 11), ("heads", 0.1), ("frames_back", 6), ("ffn", 0.1),
    ("out_send", 0.05), ("heads", 18), ("heads", 0.1), ("place_out", 3), ("place_frames", 1.3), ("join_outer", 1),
    ("join_inner", 3), ("finish", 3),
)
PIECES = 1


def copy_kernel(source, target):
    target[...] = source[...]


def hand_on_kernel(own, pair, far, here, far_copy):
    far_copy[...] = far[...]
    width = far.shape[0]
    for near, source in enumerate((own, pair)):
        for at in range(0, far.shape[1], width):
            lanes = slice(3 * width, 4 * width)
            here[lanes_of(near, width), at : at + width] = source[at : at + width, lanes]


class Layer:
    def __init__(
        self, frames, cotangent, seg_counts, query_weight, query_bias, key_weight, value_weight, value_bias,
        out_weight, out_bias, first_gain, first_shift, second_gain, second_shift,
        inner_weight, inner_bias, outer_weight, outer_bias,
    ):
        self.frames, self.cotangent, self.counts = frames, cotangent, seg_counts
        self.projections = (query_weight, key_weight, value_weight)
        self.weights = (inner_weight, outer_weight, out_weight)
        row = lambda v: v.reshape(1, v.shape[0])
        self.bq, self.bv, self.bo, self.bi, self.bu = map(row, (query_bias, value_bias, out_bias, inner_bias, outer_bias))
        self.g1, self.s1, self.g2, self.s2 = map(row, (first_gain, first_shift, second_gain, second_shift))
        micros, shard, features = frames.shape
        self.micros, self.features = micros, features
        self.width, self.hidden = query_weight.shape[1], inner_weight.shape[1]
        self.length = shard // 2
        self.segs, self.blocks, self.pairs = self.length // SEG, self.length // BLOCK, 2 * self.width // PAIR
        self.big = (self.length, features)
        self.each = (micros, self.length)
        self.quarter = (self.length // 2, features)
        self.square = (2 * BLOCK, KEYS)
        self.around = BEFORE + self.length + AHEAD
        self.key_scratch = [(self.around, 4 * self.width), (SUMS + self.segs + SUMS, 4 * self.width)]
        self.run = Steps()
        self.smem = pl.BlockSpec(memory_space=pltpu.SMEM)
        pairs = [None] * micros
        self.mix, self.mix_far, self.p_outer, self.fed, self.dn2 = (list(pairs) for _ in range(5))
        self.back_of = list(pairs)
        self.sums = {}

    def pack(self):
        args = (*self.projections, self.weights[2], self.bq, self.bv, self.bi, self.frames)
        self.own, edge = self.run.call(
            pack_kernel, "pack", [(self.features + 8, 4 * self.width), (self.micros, BEFORE, self.features)], args,
            copies=6 + self.features // self.width + self.micros, far=range(8),
        )
        self.pair = swap(self.own, "head", 1)
        self.edge = swap_edges(edge, False)

    def norm(self):
        each, features, micros = self.each, self.features, self.micros
        wi, wu, wo = self.weights
        (self.x, self.xhat, self.rate, self.normed, self.wi, self.wu, self.wo, *self.g, self.before, self.ahead) = self.run.call(
            norm_kernel, "norm",
            [each + (features,)] * 2 + [each + (128,), each + (features,), wi.shape, wu.shape, wo.shape, self.big, self.big,
             (micros, BEFORE, features), (micros, AHEAD, features)],
            (self.frames, self.g1, self.s1, wi, wu, wo, self.cotangent),
            scratch=[(16, features)], copies=4 * micros + 5, far=range(7),
        )
        self.wo_far = swap(self.wo, "head", 2)
        self.wi_pair, self.wu_pair = (swap(v, "head", 1) for v in (self.wi, self.wu))

    def project(self):
        each, features, width = self.each, self.features, self.width
        args = (self.normed, self.own, self.pair, self.g1, self.s1, self.g2, self.s2, self.bo, self.bi, self.bu)
        self.q, self.kv, self.w_all, self.bias, self.params = self.run.call(
            project_kernel, "project",
            [each + (2 * width,), each + (4 * width,), (features, 6 * width), (1, 6 * width), (7, 1, features)],
            args, copies=7, far=range(3, 10),
        )

    def edges(self):
        shape = (self.micros, BEFORE + AHEAD)
        self.xhat_edge, self.normed_edge, self.kv_edge = self.run.call(
            edges_kernel, "edges", [shape + (self.features,)] * 2 + [shape + (4 * self.width,)],
            (self.edge, self.before, self.ahead, self.params, self.w_all, self.bias),
        )

    def attend_inner(self):
        self.mix_inner, self.p_inner = self.run.call(
            attend_inner_kernel, "attend_inner",
            [(self.micros, self.length - 2 * BLOCK, 2 * self.width),
             (self.micros, self.blocks - 2, self.pairs) + self.square],
            (self.counts, self.q, self.kv), {0: self.smem}, self.key_scratch,
        )

    def attend_outer(self, m):
        self.mix[m], self.p_outer[m] = self.run.call(
            functools.partial(attend_outer_kernel, m), "attend_outer",
            [(self.length, 2 * self.width), (2, self.pairs) + self.square],
            (self.counts, self.q, self.kv, self.kv_edge, self.mix_inner),
            {0: self.smem}, self.key_scratch,
        )
        self.mix_far[m] = swap(self.mix[m], "head", 2)

    def hand_on(self):
        shape = self.wo_far.shape
        self.wo_here, far = self.run.call(
            hand_on_kernel, "hand_on", [(2 * shape[0], shape[1]), shape], (self.own, self.pair, self.wo_far)
        )
        self.wo_far_pair = swap(far, "head", 1)

    def feed(self, m):
        big, features, hidden = self.big, self.features, self.hidden
        *self.fed[m], part = self.run.call(
            functools.partial(feed_kernel, m), "feed", [big, (self.length, 2 * hidden), (self.length, 2 * hidden), big, big],
            (self.mix[m], self.mix_far[m], self.wo_here, self.wo_far, self.wo_far_pair, self.x, self.g[m], self.params,
             self.pair, self.wi, self.wi_pair, self.wu, self.wu_pair),
            scratch=[big, (features, features)],
        )
        self.dn2[m] = (part, swap(part, "head", 2))

    def inner_weights(self):
        features, hidden = self.features, self.hidden
        self.inner_own, *pair, self.vec_inner = self.run.call(
            inner_weights_kernel, "inner_weights",
            [(features, hidden)] + [(features // PIECES, hidden)] * PIECES + [(2, hidden)],
            (self.fed[0][0], self.fed[1][0], self.fed[0][2], self.fed[1][2]),
        )
        self.inner_pair = swap_near(pair)

    def outer_weights(self):
        features, hidden = self.features, self.hidden
        self.outer_own, *pair, self.vec_outer = self.run.call(
            outer_weights_kernel, "outer_weights",
            [(hidden, features)] + [(hidden // PIECES, features)] * PIECES + [(1, features)],
            (self.fed[0][1], self.fed[1][1], *self.g),
        )
        self.outer_pair = swap_near(pair)

    def feed_out(self):
        (part,) = self.run.call(
            feed_out_kernel, "feed_out", [(self.micros * self.length, self.features)],
            (self.fed[0][1], self.fed[1][1], self.wu, self.wu_pair),
        )
        self.part = (part, swap(part, "head", 2))

    def out_half(self):
        (half,) = self.run.call(
            out_half_kernel, "out_half", [(self.micros * self.length, self.features)],
            (self.fed[0][3], self.fed[1][3], *self.part, self.params),
        )
        self.out = half

    def out_send(self):
        (half,) = self.run.call(copy_kernel, "out_send", [self.out.shape], (self.out,))
        self.out = (half, swap(half, "head", 1))

    def grad_sum(self, m):
        (self.dn2[m],) = self.run.call(add_whole_kernel, "grad_sum", [self.big], self.dn2[m])

    def back(self, m):
        length, width, features = self.length, self.width, self.features
        self.back_of[m] = self.run.call(
            functools.partial(back_kernel, m), "back",
            [self.big, (length, 2 * width), (self.around, 4 * width), (features, width), (features, width), (3, features)],
            (self.dn2[m], self.fed[m][3], self.g[m], self.params, self.wo_here, self.mix[m], self.q, self.kv,
             self.kv_edge, self.p_inner, self.p_outer[m]),
            scratch=self.key_scratch + self.key_scratch[1:] + [(length, 2 * width), (features, 2 * width)],
        )

    def pick(self, number):
        return [v[number] for v in self.back_of]

    def project_back(self):
        features, micros = self.features, self.micros
        (dq_0, dq_1), (dkv_0, dkv_1) = self.pick(1), self.pick(2)
        part, pair, beyond, self.vec_first = self.run.call(
            project_back_kernel, "project_back",
            [(micros * self.length, features)] + [(micros, BEFORE, features)] * 2 + [(2, features)],
            (dq_0, dkv_0, dq_1, dkv_1, self.xhat, self.xhat_edge, self.w_all), scratch=[(self.around, features)],
        )
        self.edges_back = (part, swap(pair, "head", 1), swap_edges(beyond, True))

    def edge_add(self):
        part = self.edges_back[0]
        (part,) = self.run.call(edge_add_kernel, "edge_add", [part.shape], self.edges_back)
        self.dn1 = (part, swap(part, "head", 2))

    def project_weights(self):
        features, width = self.features, self.width
        *self.heads_own, self.rows, a, b = self.run.call(
            project_weights_kernel, "project_weights",
            [(features // 2, 4 * width)] * 2 + [(8, features), (features // 2 + 8, 4 * width), (features // 2, 4 * width)],
            (self.normed, self.normed_edge, *self.pick(1), *self.pick(2), *self.pick(3), *self.pick(4), *self.pick(5),
             self.vec_first, self.vec_outer, self.vec_inner),
            scratch=[(features, 4 * width), (features, 6 * width), (1, 6 * width)],
        )
        self.heads_pair = swap_near((a, b))

    def begin(self, name):
        if name == "heads":
            a, b = self.heads_pair
            return SumsOverTm(self.run, self.heads_own, ((a,), (b,)), self.rows)
        return SumsOverTm(self.run, (self.outer_own, self.inner_own), (self.outer_pair, self.inner_pair))

    def sum(self, name):
        if name not in self.sums:
            self.sums[name] = self.begin(name)
        elif not self.sums[name].joined:
            self.sums[name].step()

    def ffn(self):
        self.sum("ffn")

    def heads(self):
        self.sum("heads")

    def frames_back(self):
        (half,) = self.run.call(
            frames_back_kernel, "frames_back", [(self.micros * self.length, self.features)],
            (*self.dn1, self.xhat, self.rate, *self.pick(0), self.params),
        )
        self.grad = (half, swap(half, "head", 1))

    def place(self, name, halves):
        (out,) = self.run.call(
            place_kernel, name, [(self.micros, 2 * self.length, self.features)], halves, copies=2 * self.micros, far_outs=[0]
        )
        return out

    def place_out(self):
        self.layer_output = self.place("place_out", self.out)

    def place_frames(self):
        self.frames_grad = self.place("place_frames", self.grad)

    def join(self, name, number, shape):
        bit, parts = self.sums["ffn"].halves(number)
        (out,) = self.run.call(
            functools.partial(join_out_kernel, bit), name, [shape], parts, copies=2, far_outs=[0]
        )
        return out

    def settle(self, *names):
        while not all(self.sums[name].joined for name in names):
            for name in names:
                self.sum(name)

    def join_outer(self):
        self.settle("ffn", "heads")
        self.outer_grad = self.join("join_outer", 0, self.weights[1].shape)

    def join_inner(self):
        self.inner_grad = self.join("join_inner", 1, self.weights[0].shape)

    def finish(self):
        features, width, hidden = self.features, self.width, self.hidden
        sums = self.sums["heads"]
        rows = sums.rows[0]
        bits, parts = zip(*(sums.halves(i) for i in range(2)), strict=True)
        out = self.run.call(
            functools.partial(finish_kernel, list(bits)), "finish",
            [(1, features)] * 6 + [(1, width)] * 2 + [(1, hidden)] + [(features, width)] * 3 + [(width, features)],
            (rows, swap(rows, "head", 2), *parts[0], *parts[1]),
        )
        bo, g2, s2, g1, s1, bu, bq, bv, bi = (v.reshape(v.shape[1]) for v in out[:9])
        wq, wk, wv, wo = out[9:]
        return (
            self.layer_output, self.frames_grad, wq, bq, wk, wv, bv, wo, bo, g1, s1, g2, s2, self.inner_grad, bi,
            self.outer_grad, bu,
        )


def per_device(*args):
    layer = Layer(*args)
    for step, us in ORDER:
        layer.run.us = us
        name = step.rstrip("0123456789")
        result = getattr(layer, name)(*(int(digit) for digit in step[len(name) :]))
    return result


def solution(mesh):
    in_specs = (
        P(None, "tm", None),
        P(None, "tm", None),
        P(),
        P(None, "head"),
        P("head"),
        P(None, "head"),
        P(None, "head"),
        P("head"),
        P("head", None),
        P(),
        P(),
        P(),
        P(),
        P(),
        P(None, "head"),
        P("head"),
        P("head", None),
        P(),
    )
    out_specs = (
        P(None, "tm", None),
        P(None, "tm", None),
        P(None, "head"),
        P("head"),
        P(None, "head"),
        P(None, "head"),
        P("head"),
        P("head", None),
        P(),
        P(),
        P(),
        P(),
        P(),
        P(None, "head"),
        P("head"),
        P("head", None),
        P(),
    )
    return jax.shard_map(
        per_device, mesh=mesh, in_specs=in_specs, out_specs=out_specs, check_vma=False
    )
```

```python
import functools

import jax
import jax.numpy as jnp
from jax import lax
from jax.experimental import pallas as pl
from jax.experimental.pallas import tpu as pltpu
from jax.sharding import PartitionSpec as P

HEAD_DIM = 64
SEG = 16
RC = 4
LC = 30
MEM = 4

EPSILON = 1e-05
MASKED = -1e30
F32 = jnp.float32

BEFORE = MEM * SEG
AHEAD = 8
CACHE = 32
SUMS = 8
BLOCK = 64
WIN = CACHE + BLOCK + AHEAD
SWIN = 16
KEYS = 128
FIRST_GAIN, FIRST_SHIFT, SECOND_GAIN, SECOND_SHIFT, OUT_BIAS, INNER_BIAS, OUTER_BIAS = range(7)
PAIR = 2 * HEAD_DIM
MIB = 1 << 20


def mm(left, right, left_dim=1, right_dim=0):
    return lax.dot_general(
        left,
        right,
        (((left_dim,), (right_dim,)), ((), ())),
        precision=lax.Precision.HIGH,
        preferred_element_type=F32,
    )


def normalise(values):
    centred = values - jnp.mean(values, axis=-1, keepdims=True)
    variance = jnp.mean(centred * centred, axis=-1, keepdims=True)
    rate = lax.rsqrt(variance + EPSILON)
    return centred * rate, rate


def norm_back(grad, gain, xhat, rate):
    scaled = grad * gain
    first = jnp.mean(scaled, axis=-1, keepdims=True)
    second = jnp.mean(scaled * xhat, axis=-1, keepdims=True)
    return rate * (scaled - first - xhat * second)


def column_sums(values):
    return jnp.sum(values, axis=0, keepdims=True)


def seg_means(values):
    rows, width = values.shape
    return jnp.sum(values.reshape(rows // SEG, SEG, width), axis=1) * (1.0 / SEG)


def near_bit():
    return lax.axis_index("head") % 2


def far_bit():
    return lax.axis_index("head") // 2


def my_rows(rows):
    half = rows // 2
    return pl.ds(pl.multiple_of(near_bit() * half, half), half)


def lanes_of(place, width, start=0):
    at = place + near_bit() - 2 * place * near_bit()
    return pl.ds(pl.multiple_of(start + at * width, width), width)


def half_rows(place, half):
    return pl.ds(pl.multiple_of(place * half, half), half)


def full(shape):
    return pl.BlockSpec(shape, lambda *_: (0,) * len(shape))


class Steps:
    def __init__(self):
        self.held = []
        self.us = 0.1

    def call(self, kernel, name, outs, args, specs=None, scratch=(), vmem=32, copies=0, far=(), far_outs=()):
        specs = dict(specs or {})
        given, made, held = len(args), len(outs), tuple(self.held)
        token = bool(far_outs)
        somewhere = pl.BlockSpec(memory_space=pl.ANY)
        in_hbm = pl.BlockSpec(memory_space=pltpu.HBM)

        def body(*refs):
            ins, rest = refs[:given], refs[given + len(held) :]
            if token:
                rest[made][...] = jnp.zeros(rest[made].shape, F32)
            kernel(*ins, *rest[:made], *rest[made + token :])

        args = [pltpu.with_memory_space_constraint(a, pltpu.HBM) if i in far else a for i, a in enumerate(args)]
        out_specs = [in_hbm if i in far_outs else full(shape) for i, shape in enumerate(outs)]
        out_shape = [
            pltpu.HBM(shape, F32) if i in far_outs else jax.ShapeDtypeStruct(shape, F32) for i, shape in enumerate(outs)
        ]
        if token:
            out_specs.append(full((1, 128)))
            out_shape.append(jax.ShapeDtypeStruct((1, 128), F32))
        out = pl.pallas_call(
            body,
            name=name,
            grid=(1,),
            in_specs=[in_hbm if i in far else specs.get(i, full(a.shape)) for i, a in enumerate(args)]
            + [somewhere] * len(held),
            out_specs=out_specs,
            out_shape=out_shape,
            scratch_shapes=[pltpu.VMEM(shape, F32) for shape in scratch]
            + ([pltpu.SemaphoreType.DMA((copies,))] if copies else []),
            compiler_params=pltpu.CompilerParams(vmem_limit_bytes=vmem * MIB),
            cost_estimate=pl.CostEstimate(flops=int(self.us * 5.18e8), bytes_accessed=0, transcendentals=0),
        )(*args, *held)
        self.held = [out[-1]]
        return out[:made]


def copy_all(pairs, sems):
    copies = [pltpu.make_async_copy(a, b, sems.at[i]) for i, (a, b) in enumerate(pairs)]
    for copy in copies:
        copy.start()
    return copies


def pack_kernel(wq, wk, wv, wo, bq, bv, bi, frames, out, edge, sems):
    rows, width = wq.shape
    out[rows:] = jnp.zeros((out.shape[0] - rows, out.shape[1]), F32)
    pairs = [(w, out.at[pl.ds(0, rows), pl.ds(i * width, width)]) for i, w in enumerate((wq, wk, wv))]
    for at in range(0, wo.shape[1], width):
        pairs.append((wo.at[:, pl.ds(at, width)], out.at[pl.ds(at, width), pl.ds(3 * width, width)]))
    pairs += [(b, out.at[pl.ds(rows, 1), pl.ds(i * width, width)]) for i, b in ((0, bq), (2, bv))]
    pairs.append((bi, out.at[pl.ds(rows + 1, 1), pl.ds(0, bi.shape[1])]))
    start = pl.multiple_of((1 - near_bit()) * (frames.shape[1] - BEFORE), BEFORE)
    pairs += [(frames.at[m, pl.ds(start, BEFORE)], edge.at[m]) for m in range(frames.shape[0])]
    for copy in copy_all(pairs, sems):
        copy.wait()


def norm_kernel(
    frames, gain, shift, wi, wu, wo, cotangent,
    x_ref, xhat_ref, rate_ref, normed_ref, wi_ref, wu_ref, wo_ref, g_0, g_1, before, ahead, params, sems,
):
    micros, half, _ = x_ref.shape
    rows = frames.shape[1]
    pairs = [(gain, params.at[pl.ds(0, 1)]), (shift, params.at[pl.ds(8, 1)])]
    pairs += [(frames.at[m, my_rows(rows)], x_ref.at[m]) for m in range(micros)]
    pairs += [(frames.at[m, pl.ds(half - BEFORE, BEFORE)], before.at[m]) for m in range(micros)]
    pairs += [(frames.at[m, pl.ds(half, AHEAD)], ahead.at[m]) for m in range(micros)]
    pairs += [(wo, wo_ref), (wi, wi_ref), (wu, wu_ref)]
    pairs += [(cotangent.at[m, my_rows(rows)], g) for m, g in enumerate((g_0, g_1))]
    copies = copy_all(pairs, sems)
    for copy in copies[:2]:
        copy.wait()
    for micro in range(micros):
        copies[2 + micro].wait()
        xhat, rate = normalise(x_ref[micro])
        xhat_ref[micro] = xhat
        normed_ref[micro] = xhat * params[0:1] + params[8:9]
        rate_ref[micro] = jnp.broadcast_to(rate, (half, rate_ref.shape[2]))
    for copy in copies[2 + micros :]:
        copy.wait()


def project_kernel(normed, own, pair, g1, s1, g2, s2, bo, bi, bu, q_ref, kv_ref, w_ref, bias, rows_ref, sems):
    micros, half, wide = q_ref.shape
    features = normed.shape[2]
    width = own.shape[1] // 4
    copies = copy_all([(v, rows_ref.at[i]) for i, v in enumerate((g1, s1, g2, s2, bo, bi, bu))], sems)
    for number in range(3):
        at = slice(number * width, (number + 1) * width)
        for place, source in enumerate((own, pair)):
            lanes = lanes_of(place, width, 2 * number * width)
            w_ref[:, lanes] = source[:features, at]
            bias[:, lanes] = source[features : features + 1, at]
    for micro in range(micros):
        out = mm(normed[micro], w_ref[...]) + bias[...]
        q_ref[micro] = out[:, :wide]
        kv_ref[micro] = out[:, wide:]
    for copy in copies:
        copy.wait()


def edges_kernel(edge, before, ahead, params, w_ref, bias, xhat_ref, normed_ref, kv_ref):
    near = near_bit()
    wide = w_ref.shape[1] // 3
    for micro in range(edge.shape[0]):
        first = jnp.where(near == 0, edge[micro], before[micro])
        last = jnp.where(near == 0, ahead[micro], edge[micro, :AHEAD])
        xhat, _ = normalise(jnp.concatenate([first, last], axis=0))
        normed = xhat * params[FIRST_GAIN] + params[FIRST_SHIFT]
        xhat_ref[micro] = xhat
        normed_ref[micro] = normed
        kv_ref[micro] = mm(normed, w_ref[:, wide:]) + bias[:, wide:]


def fill_keys(kv, edge, kx, sx):
    length = kv.shape[0]
    kx[BEFORE : BEFORE + length] = kv
    segs = length // SEG
    sx[SUMS : SUMS + segs] = seg_means(kv)
    if edge is not None:
        kx[:BEFORE] = edge[:BEFORE]
        kx[BEFORE + length :] = edge[BEFORE:]
        sx[: SUMS - MEM] = jnp.zeros((SUMS - MEM, kv.shape[1]), F32)
        sx[SUMS - MEM : SUMS] = seg_means(edge[:BEFORE])
        sx[SUMS + segs :] = jnp.zeros((sx.shape[0] - SUMS - segs, kv.shape[1]), F32)


def summary_start(block):
    return (block * (BLOCK // SEG) + SUMS - MEM) // SUMS * SUMS


def frame_rows(block):
    start = BEFORE - CACHE + block * BLOCK
    return slice(start, start + WIN)


def key_window(kx, sx, block, lanes):
    start = summary_start(block)
    rows = [kx[frame_rows(block), lanes], sx[start : start + SWIN, lanes]]
    return jnp.concatenate(rows + [jnp.zeros((KEYS - WIN - SWIN, PAIR), F32)], axis=0)


def by_head(values):
    first = lax.broadcasted_iota(jnp.int32, values.shape, 1) < HEAD_DIM
    return jnp.concatenate([jnp.where(first, values, 0.0), jnp.where(first, 0.0, values)], axis=0)


def side_by_side(values):
    rows = values.shape[0] // 2
    first = lax.broadcasted_iota(jnp.int32, (rows, values.shape[1]), 1) < HEAD_DIM
    return jnp.where(first, values[:rows], values[rows:])


def owner_of(segment, bounds):
    owner = jnp.where(segment < 0, -1, 0)
    for bound in bounds:
        owner = owner + (segment >= bound).astype(jnp.int32)
    return owner


def visible(block, base, bounds):
    row = lax.broadcasted_iota(jnp.int32, (2 * BLOCK, 1), 0) % BLOCK
    column = lax.broadcasted_iota(jnp.int32, (1, KEYS), 1)
    query_seg = block * (BLOCK // SEG) + row // SEG
    frame = block * BLOCK - CACHE + column
    is_frame = column < WIN
    summary = summary_start(block) - SUMS + column - WIN
    key_seg = jnp.where(is_frame, (frame + CACHE) // SEG - CACHE // SEG, summary)
    key_seg = jnp.where(column < WIN + SWIN, key_seg, -(1 << 20))
    inside = (frame >= query_seg * SEG - LC) & (frame < query_seg * SEG + SEG + RC)
    near = (key_seg >= query_seg - MEM) & (key_seg < query_seg)
    seen = (is_frame & inside) | ((column >= WIN) & near)
    return seen & (owner_of(key_seg + base, bounds) == owner_of(query_seg + base, bounds))


def bounds_of(counts, micro):
    bounds, total = [], 0
    for utterance in range(counts.shape[1]):
        total = total + counts[micro, utterance]
        bounds.append(total)
    return bounds


def first_segment(length):
    return (lax.axis_index("tm") * 2 + near_bit()) * (length // SEG)


def block_rows(block):
    return slice(block * BLOCK, (block + 1) * BLOCK)


def attend_block(block, seen, query, kx, sx, keep, put):
    width = query.shape[1]
    for pair in range(width // PAIR):
        lanes = slice(pair * PAIR, (pair + 1) * PAIR)
        value_lanes = slice(width + pair * PAIR, width + (pair + 1) * PAIR)
        scores = mm(by_head(query[:, lanes] * HEAD_DIM ** (-0.5)), key_window(kx, sx, block, lanes), 1, 1)
        scores = jnp.where(seen, scores, MASKED)
        weights = jnp.exp(scores - jnp.max(scores, axis=-1, keepdims=True))
        weights = weights / jnp.sum(weights, axis=-1, keepdims=True)
        keep(pair, weights)
        put(lanes, side_by_side(mm(weights, key_window(kx, sx, block, value_lanes))))


def attend_inner_kernel(counts, q_ref, kv_ref, mix_ref, p_ref, kx, sx):
    micros, length, _ = q_ref.shape
    base = first_segment(length)
    for micro in range(micros):
        fill_keys(kv_ref[micro], None, kx, sx)
        bounds = bounds_of(counts, micro)
        for number, block in enumerate(range(1, length // BLOCK - 1)):
            def keep(pair, weights):
                p_ref[micro, number, pair] = weights

            def put(lanes, values):
                mix_ref[micro, block_rows(number), lanes] = values

            seen = visible(block, base, bounds)
            attend_block(block, seen, q_ref[micro, block_rows(block)], kx, sx, keep, put)


def attend_outer_kernel(micro, counts, q_ref, kv_ref, edge, inner, mix_ref, p_ref, kx, sx):
    _, length, _ = q_ref.shape
    base = first_segment(length)
    fill_keys(kv_ref[micro], edge[micro], kx, sx)
    bounds = bounds_of(counts, micro)
    mix_ref[BLOCK : length - BLOCK] = inner[micro]
    for number, block in enumerate((0, length // BLOCK - 1)):
        def keep(pair, weights):
            p_ref[number, pair] = weights

        def put(lanes, values):
            mix_ref[block_rows(block), lanes] = values

        seen = visible(block, base, bounds)
        attend_block(block, seen, q_ref[micro, block_rows(block)], kx, sx, keep, put)


def back_kernel(
    micro, grad_ref, mid_ref, g_ref, params, wo_here, mix, q_ref, kv_ref, edge, p_inner, p_outer,
    dmid_ref, dq_ref, dkv_ref, dwo_own, dwo_pair, vec_ref,
    kx, sx, dsx, dmix, dwo,
):
    _, length, width = q_ref.shape
    near_width = dwo_own.shape[1]
    grad = grad_ref[...]
    xhat, rate = normalise(mid_ref[...])
    dmid = g_ref[...] + norm_back(grad, params[SECOND_GAIN], xhat, rate)
    dmid_ref[...] = dmid
    vec_ref[0:1] = column_sums(dmid)
    vec_ref[1:2] = column_sums(grad * xhat)
    vec_ref[2:3] = column_sums(grad)
    dmix[...] = mm(dmid, wo_here[...], 1, 1)
    dwo[...] = mm(dmid, mix[...], 0, 0)
    dwo_own[...] = dwo[:, lanes_of(0, near_width)]
    dwo_pair[...] = dwo[:, lanes_of(1, near_width)]
    fill_keys(kv_ref[micro], edge[micro], kx, sx)
    dkv_ref[...] = jnp.zeros_like(dkv_ref)
    dsx[...] = jnp.zeros_like(dsx)
    for block in range(length // BLOCK):
        start = summary_start(block)
        rows, frames, sums = block_rows(block), frame_rows(block), slice(start, start + SWIN)
        for pair in range(width // PAIR):
            lanes = slice(pair * PAIR, (pair + 1) * PAIR)
            value_lanes = slice(width + pair * PAIR, width + (pair + 1) * PAIR)
            inside = 0 < block < length // BLOCK - 1
            weights = p_inner[micro, block - 1, pair] if inside else p_outer[min(block, 1), pair]
            grad = by_head(dmix[rows, lanes])
            dweights = mm(grad, key_window(kx, sx, block, value_lanes), 1, 1)
            dscores = weights * (dweights - jnp.sum(dweights * weights, axis=-1, keepdims=True))
            dquery = side_by_side(mm(dscores, key_window(kx, sx, block, lanes)))
            dq_ref[rows, lanes] = dquery * HEAD_DIM ** (-0.5)
            dkeys = mm(dscores, by_head(q_ref[micro, rows, lanes] * HEAD_DIM ** (-0.5)), 0, 0)
            dvalues = mm(weights, grad, 0, 0)
            dkv_ref[frames, lanes] += dkeys[:WIN]
            dkv_ref[frames, value_lanes] += dvalues[:WIN]
            dsx[sums, lanes] += dkeys[WIN : WIN + SWIN]
            dsx[sums, value_lanes] += dvalues[WIN : WIN + SWIN]
    count = BEFORE + length
    segs = count // SEG
    spread = dsx[SUMS - MEM : SUMS - MEM + segs] * (1.0 / SEG)
    spread = jnp.broadcast_to(spread[:, None, :], (segs, SEG, 2 * width))
    dkv_ref[:count] += spread.reshape(count, 2 * width)


def feed_kernel(
    micro, mix_own, mix_far, wo_here, wo_far, wo_far_pair, x_ref, g_ref, params, pair, wi_own, wi_pair, wu_own, wu_pair,
    n2_ref, h_ref, dpre_ref, mid_ref, part_ref,
    mix, wo,
):
    width = mix_own.shape[1] // 2
    features, hidden = wi_own.shape
    far = far_bit()
    here = pl.multiple_of(far * 2 * width, 2 * width)
    there = pl.multiple_of((1 - far) * 2 * width, 2 * width)
    mix[:, pl.ds(here, 2 * width)] = mix_own[...]
    mix[:, pl.ds(there, 2 * width)] = mix_far[...]
    wo[pl.ds(here, 2 * width)] = wo_here[...]
    wo[lanes_of(0, width, there)] = wo_far[...]
    wo[lanes_of(1, width, there)] = wo_far_pair[...]
    middle = x_ref[micro] + mm(mix[...], wo[...]) + params[OUT_BIAS]
    mid_ref[...] = middle
    xhat, _ = normalise(middle)
    normed = xhat * params[SECOND_GAIN] + params[SECOND_SHIFT]
    n2_ref[...] = normed
    part = None
    for place, (wi, wu, bias) in enumerate(((wi_own, wu_own, params[INNER_BIAS][:, :hidden]), (wi_pair, wu_pair, pair[features + 1 : features + 2, :hidden]))):
        at = slice(place * hidden, (place + 1) * hidden)
        pre = mm(normed, wi[...]) + bias
        phi = 0.5 + 0.5 * lax.erf(pre * (0.5**0.5))
        h_ref[:, at] = pre * phi
        slope = phi + pre * (jnp.exp(-0.5 * pre * pre) * 0.3989422804014327)
        dpre = mm(g_ref[...], wu[...], 1, 1) * slope
        dpre_ref[:, at] = dpre
        step = mm(dpre, wi[...], 1, 1)
        part = step if part is None else part + step
    part_ref[...] = part


def put_rows(value, outs):
    at = 0
    for out in outs:
        count = out.shape[0]
        out[...] = value[at : at + count]
        at += count


def inner_weights_kernel(n2_0, n2_1, d_0, d_1, own_ref, *rest):
    *pair, vec_ref = rest
    hidden = own_ref.shape[1]
    for place, outs in enumerate(((own_ref,), pair)):
        at = slice(place * hidden, (place + 1) * hidden)
        put_rows(mm(n2_0[...], d_0[:, at], 0, 0) + mm(n2_1[...], d_1[:, at], 0, 0), outs)
        vec_ref[place : place + 1] = column_sums(d_0[:, at]) + column_sums(d_1[:, at])


def outer_weights_kernel(h_0, h_1, g_0, g_1, own_ref, *rest):
    *pair, vec_ref = rest
    hidden = own_ref.shape[0]
    for place, outs in enumerate(((own_ref,), pair)):
        at = slice(place * hidden, (place + 1) * hidden)
        put_rows(mm(h_0[:, at], g_0[...], 0, 0) + mm(h_1[:, at], g_1[...], 0, 0), outs)
    vec_ref[...] = column_sums(g_0[...]) + column_sums(g_1[...])


def feed_out_kernel(h_0, h_1, wu_own, wu_pair, out_ref):
    hidden = wu_own.shape[0]
    rows = h_0.shape[0]
    for micro, h_ref in enumerate((h_0, h_1)):
        part = mm(h_ref[:, :hidden], wu_own[...]) + mm(h_ref[:, hidden:], wu_pair[...])
        out_ref[micro * rows : (micro + 1) * rows] = part


def out_half_kernel(mid_0, mid_1, part, far, params, out):
    rows = mid_0.shape[0]
    for micro, mid_ref in enumerate((mid_0, mid_1)):
        at = slice(micro * rows, (micro + 1) * rows)
        out[at] = mid_ref[...] + (part[at] + far[at]) + params[OUTER_BIAS]


def project_back_kernel(
    dq_0, dkv_0, dq_1, dkv_1, xhat, xhat_edge, w_ref, part_ref, pair_ref, beyond_ref, vec_ref, work
):
    near = near_bit()
    length, wide = dq_0.shape
    own = slice(BEFORE, BEFORE + length)
    gain, shift = 0.0, 0.0
    for micro, (dq, dkv) in enumerate(((dq_0, dkv_0), (dq_1, dkv_1))):
        work[...] = mm(dkv[...], w_ref[:, wide:], 1, 1)
        work[own] += mm(dq[...], w_ref[:, :wide], 1, 1)
        part_ref[micro * length : (micro + 1) * length] = work[own]
        before = work[:BEFORE]
        ahead = jnp.concatenate([work[BEFORE + length :], jnp.zeros((BEFORE - AHEAD, work.shape[1]), F32)], axis=0)
        pair_ref[micro] = jnp.where(near == 0, ahead, before)
        beyond_ref[micro] = jnp.where(near == 0, before, ahead)
        gain = gain + column_sums(work[own] * xhat[micro]) + column_sums(work[:BEFORE] * xhat_edge[micro, :BEFORE])
        gain = gain + column_sums(work[BEFORE + length :] * xhat_edge[micro, BEFORE:])
        shift = shift + column_sums(work[...])
    vec_ref[0:1] = gain
    vec_ref[1:2] = shift


def edge_add_kernel(part, pair, beyond, out):
    out[...] = part[...]
    near = near_bit()
    micros = pair.shape[0]
    length = part.shape[0] // micros
    for micro in range(micros):
        end = (micro + 1) * length
        out[end - BEFORE : end] += jnp.where(near == 0, pair[micro], beyond[micro])
        out[end - length : end - length + AHEAD] += jnp.where(near == 0, beyond[micro, :AHEAD], pair[micro, :AHEAD])


def project_weights_kernel(
    normed, normed_edge, dq_0, dq_1, dkv_0, dkv_1, wo_own_0, wo_own_1, wo_pair_0, wo_pair_1, mid_0, mid_1, first, vec_outer, vec_inner,
    own_0, own_1, rows_ref, pair_0, pair_1, message, sums, row,
):
    features = normed.shape[2]
    width = wo_own_0.shape[1]
    hidden = vec_inner.shape[1]
    length, wide = dq_0.shape
    own, after = slice(BEFORE, BEFORE + length), slice(BEFORE + length, None)
    edges = jnp.concatenate([dkv_0[:BEFORE], dkv_0[after], dkv_1[:BEFORE], dkv_1[after]], axis=0)
    normed_edges = jnp.concatenate([normed_edge[0], normed_edge[1]], axis=0)
    queries = mm(normed[0], dq_0[...], 0, 0) + mm(normed[1], dq_1[...], 0, 0)
    keyvals = mm(normed[0], dkv_0[own], 0, 0) + mm(normed[1], dkv_1[own], 0, 0) + mm(normed_edges, edges, 0, 0)
    sums[:, :wide] = queries
    sums[:, wide:] = keyvals
    row[:, :wide] = column_sums(dq_0[...]) + column_sums(dq_1[...])
    row[:, wide:] = column_sums(dkv_0[...]) + column_sums(dkv_1[...])
    rows_ref[0:3] = (mid_0[...] + mid_1[...]) * 0.5
    rows_ref[3:5] = first[...]
    rows_ref[5:6] = vec_outer[...] * 0.5
    rows_ref[6:] = jnp.zeros((2, features), F32)
    half = own_0.shape[0]
    pair_0[half : half + 6] = rows_ref[0:6]
    pair_0[half + 6 :] = jnp.zeros((2, features), F32)
    for place, (out_ref, at) in enumerate(((rows_ref, 6), (pair_0, half + 6))):
        for number in range(3):
            lanes = slice(number * width, (number + 1) * width)
            out_ref[at : at + 1, lanes] = row[:, lanes_of(place, width, 2 * number * width)]
        out_ref[at + 1 : at + 2, :hidden] = vec_inner[place : place + 1]
    for place, (outs, wo_0, wo_1) in enumerate((((own_0, own_1), wo_own_0, wo_own_1), ((pair_0, pair_1), wo_pair_0, wo_pair_1))):
        for number in range(3):
            lanes = slice(number * width, (number + 1) * width)
            message[:, lanes] = sums[:, lanes_of(place, width, 2 * number * width)]
        message[:, 3 * width :] = wo_0[...] + wo_1[...]
        for number, out_ref in enumerate(outs):
            out_ref[:half] = message[number * half : (number + 1) * half]


def frames_back_kernel(a_ref, b_ref, xhat, rate, dmid_0, dmid_1, params, out):
    rows = dmid_0.shape[0]
    for micro, dmid_ref in enumerate((dmid_0, dmid_1)):
        at = slice(micro * rows, (micro + 1) * rows)
        grad = norm_back(a_ref[at] + b_ref[at], params[FIRST_GAIN], xhat[micro], rate[micro, :, :1])
        out[at] = dmid_ref[...] + grad


def place_kernel(own, pair, out, sems):
    micros, half = out.shape[0], out.shape[1] // 2
    near = near_bit()
    pairs = []
    for micro in range(micros):
        rows = pl.ds(micro * half, half)
        pairs.append((own.at[rows], out.at[micro, half_rows(near, half)]))
        pairs.append((pair.at[rows], out.at[micro, half_rows(1 - near, half)]))
    for copy in copy_all(pairs, sems):
        copy.wait()


def place_of(bit):
    return lax.axis_index("tm") // bit % 2


def add_pieces(out, a_ref, pieces, rows_ref=None, new_rows=None):
    count, at = a_ref.shape[0], 0
    if not pieces:
        out[...] = a_ref[...]
        if new_rows is not None:
            new_rows[...] = rows_ref[...]
    for piece in pieces:
        take = min(piece.shape[0], count - at)
        if take:
            out[at : at + take] = a_ref[at : at + take] + piece[:take]
        if take < piece.shape[0]:
            new_rows[...] = rows_ref[...] + piece[take:]
        at += take


def add_split_kernel(bits, counts, rows, *refs):
    total = len(bits)
    values, refs = refs[:total], refs[total:]
    rows_ref, refs = (refs[0], refs[1:]) if rows else (None, refs)
    pieces = []
    for count in counts:
        pieces.append(refs[:count])
        refs = refs[count:]
    kept, sent, refs = refs[:total], refs[total : 2 * total], refs[2 * total :]
    new_rows, work = (refs[0], refs[1]) if rows else (None, refs[0])
    for number, bit in enumerate(bits):
        small = (rows_ref, new_rows) if rows and number == 0 else ()
        half = kept[number].shape[0]
        add_pieces(work, values[number], pieces[number], *small)
        place = place_of(bit)
        kept[number][...] = work[half_rows(place, half)]
        sent[number][:half] = work[half_rows(1 - place, half)]
        if small:
            sent[number][half:] = new_rows[...]


def last_kernel(rows, a_ref, *refs):
    rows_ref, refs = (refs[0], refs[1:]) if rows else (None, refs)
    b_ref, out_ref = refs
    half = a_ref.shape[0]
    out_ref[:half] = a_ref[...] + b_ref[:half]
    if rows:
        out_ref[half:] = rows_ref[...] + b_ref[half:]


def stack_kernel(rows, a_0, a_1, *refs):
    rows_ref, refs = (refs[0], refs[1:]) if rows else (None, refs)
    b_0, b_1, out_ref = refs
    half = a_0.shape[0]
    out_ref[:half] = a_0[...] + b_0[:half]
    out_ref[half : 2 * half] = a_1[...] + b_1[...]
    if rows:
        out_ref[2 * half :] = rows_ref[...] + b_0[half:]


def add_whole_kernel(a_ref, b_ref, *outs):
    at = 0
    for out in outs:
        count = out.shape[0]
        out[...] = a_ref[at : at + count] + b_ref[at : at + count]
        at += count


def join_kernel(bits, *refs):
    total = len(bits)
    for bit, mine, theirs, out in zip(bits, refs[:total], refs[total : 2 * total], refs[2 * total :], strict=True):
        half = mine.shape[0]
        place = place_of(bit)
        out[half_rows(place, half)] = mine[...]
        out[half_rows(1 - place, half)] = theirs[...]


def join_out_kernel(bit, mine, theirs, out, sems):
    half = mine.shape[0]
    place = place_of(bit)
    for copy in copy_all([(mine, out.at[half_rows(place, half)]), (theirs, out.at[half_rows(1 - place, half)])], sems):
        copy.wait()


def join_heads_kernel(bits, *refs):
    *parts, wq, wk, wv, wo = refs
    width = wq.shape[1]
    at = 0
    for number, bit in enumerate(bits):
        mine, theirs = parts[2 * number : 2 * number + 2]
        half = mine.shape[0]
        place = place_of(bit)
        for where, part in ((place, mine), (1 - place, theirs)):
            rows = pl.ds(pl.multiple_of(at + where * half, half), half)
            for heads, out in enumerate((wq, wk, wv)):
                out[rows, :] = part[:, heads * width : (heads + 1) * width]
            wo[:, rows] = part[:, 3 * width :].T
        at += 2 * half


def small_kernel(rows, far, outs):
    width = outs[-3].shape[1]
    for number, out in enumerate(outs[:6]):
        out[...] = rows[number : number + 1] + far[number : number + 1]
    outs[6][...] = rows[6:7, :width]
    outs[7][...] = rows[6:7, 2 * width : 3 * width]
    outs[8][...] = rows[7:8, : outs[8].shape[1]]


def finish_kernel(bits, rows, far, *refs):
    count = 2 * len(bits)
    small_kernel(rows, far, refs[count : count + 9])
    join_heads_kernel(bits, *refs[:count], *refs[count + 9 :])


def swap(value, axis, bit):
    size = lax.axis_size(axis)
    return lax.ppermute(value, axis, [(i, i ^ bit) for i in range(size)])


def swap_near(parts):
    return [swap(part, "head", 1) for part in parts]


def swap_edges(value, back):
    size, group = lax.axis_size("tm"), lax.axis_size("head")
    pairs = []
    for source in range(size):
        for place in range(group):
            target = source + (1 - 2 * (place % 2)) * (-1 if back else 1)
            if 0 <= target < size:
                pairs.append((source * group + place, target * group + (place ^ 1 if back else place)))
    return lax.ppermute(value, ("tm", "head"), pairs)


class SumsOverTm:
    def __init__(self, run, a, b, rows=None):
        bits = [1 << i for i in range(lax.axis_size("tm").bit_length() - 1)]
        self.run, self.values, self.got = run, list(a), [list(v) for v in b]
        self.rows = [] if rows is None else [rows]
        self.apart = [(bits[1], bits[0]), (bits[0], bits[1])]
        self.together, self.last = bits[2:-1], bits[-1]
        self.todo = [("split", pair) for pair in self.apart]
        self.todo.append(("stack",))
        self.todo += [("split", (bit,)) for bit in self.together] + [("last",)] * bool(self.together)
        self.todo.append(("add",))
        self.todo += [("join", (bit,)) for bit in reversed(self.together)] + [("part",)] * bool(self.together)
        self.todo.append(("join", self.apart[1]))
        self.step()

    def step(self):
        run, values = self.run, self.values
        kind, *rest = self.todo.pop(0)
        features = values[0].shape[1]
        count = values[0].shape[0]
        more = sum(v.shape[0] for v in self.rows)
        has_rows = bool(self.rows)
        shape = lambda rows: (rows, features)
        got = [piece for pieces in self.got for piece in pieces]
        if kind == "split":
            (bits,) = rest
            half = count // 2
            extra = [more] + [0] * (len(bits) - 1)
            out = run.call(
                functools.partial(add_split_kernel, bits, [len(v) for v in self.got], has_rows), "add_split",
                [shape(half)] * len(bits) + [shape(half + e) for e in extra] + [v.shape for v in self.rows],
                (*values, *self.rows, *got), scratch=[shape(count)],
            )
            self.values, messages, self.rows = out[: len(bits)], out[len(bits) : 2 * len(bits)], out[2 * len(bits) :]
            self.got = [[swap(v, "tm", bit)] for v, bit in zip(messages, bits, strict=True)]
            return
        if kind in ("stack", "last"):
            if kind == "stack":
                (value,) = run.call(
                    functools.partial(stack_kernel, has_rows), "stack", [shape(2 * count + more)], (*values, *self.rows, *got)
                )
                count = 2 * count
            else:
                (value,) = run.call(
                    functools.partial(last_kernel, has_rows), "stack", [shape(count + more)], (*values, *self.rows, *got)
                )
            if kind == "stack" and self.together:
                self.values, self.rows = [value[:count]], [value[count:]] * has_rows
                self.values, self.got = self.values, [[]]
                return self.step()
            self.values, self.count = [value], count
            self.got = [[swap(value, "tm", self.last)]]
            return
        if kind == "add":
            parts = [self.count] if self.together else [self.count // 2] * 2
            out = run.call(
                add_whole_kernel, "add", [shape(n) for n in parts] + [v.shape for v in self.rows], (*values, *got)
            )
            self.values, self.rows = out[: len(parts)], out[len(parts) :]
        elif kind == "join":
            (bits,) = rest
            self.values = run.call(
                functools.partial(join_kernel, bits), "join", [shape(2 * count)] * len(bits), (*values, *got)
            )
        elif kind == "part":
            self.values = [values[0][: count // 2], values[0][count // 2 :]]
        following = self.todo[0] if self.todo else ("join", self.apart[0])
        if following[0] == "part":
            return self.step()
        self.got = [[swap(v, "tm", bit)] for v, bit in zip(self.values, following[1], strict=True)]

    @property
    def joined(self):
        return not self.todo

    def halves(self, number):
        return self.apart[0][number], (self.values[number], *self.got[number])


ORDER = (
    ("pack", 8), ("norm", 4.8), ("project", 2.2), ("attend_inner", 11), ("edges", 1), ("hand_on", 0.5),
    ("attend_outer0", 24), ("attend_outer1", 1), ("feed0", 18), ("feed1", 14), ("outer_weights", 6),
    ("inner_weights", 11), ("feed_out", 0.6), ("grad_sum0", 18), ("ffn", 11), ("back0", 6), ("grad_sum1", 18),
    ("back1", 0.5), ("ffn", 0.1), ("project_back", 1.8), ("project_weights", 2), ("ffn", 0.1), ("edge_add", 5),
    ("out_half", 5), ("out_send", 6), ("heads", 20), ("place_out", 1.3), ("heads", 0.1), ("ffn", 0.1), ("heads", 3),
    ("frames_back", 0.6), ("ffn", 20), ("place_frames", 0.1), ("heads", 0.1), ("heads", 0.1), ("join_outer", 0.1),
    ("join_inner", 0.1), ("finish", 1.3),
)
PIECES = 1


def copy_kernel(source, target):
    target[...] = source[...]


def hand_on_kernel(own, pair, far, here, far_copy):
    far_copy[...] = far[...]
    width = far.shape[0]
    for near, source in enumerate((own, pair)):
        for at in range(0, far.shape[1], width):
            lanes = slice(3 * width, 4 * width)
            here[lanes_of(near, width), at : at + width] = source[at : at + width, lanes]


class Layer:
    def __init__(
        self, frames, cotangent, seg_counts, query_weight, query_bias, key_weight, value_weight, value_bias,
        out_weight, out_bias, first_gain, first_shift, second_gain, second_shift,
        inner_weight, inner_bias, outer_weight, outer_bias,
    ):
        self.frames, self.cotangent, self.counts = frames, cotangent, seg_counts
        self.projections = (query_weight, key_weight, value_weight)
        self.weights = (inner_weight, outer_weight, out_weight)
        row = lambda v: v.reshape(1, v.shape[0])
        self.bq, self.bv, self.bo, self.bi, self.bu = map(row, (query_bias, value_bias, out_bias, inner_bias, outer_bias))
        self.g1, self.s1, self.g2, self.s2 = map(row, (first_gain, first_shift, second_gain, second_shift))
        micros, shard, features = frames.shape
        self.micros, self.features = micros, features
        self.width, self.hidden = query_weight.shape[1], inner_weight.shape[1]
        self.length = shard // 2
        self.segs, self.blocks, self.pairs = self.length // SEG, self.length // BLOCK, 2 * self.width // PAIR
        self.big = (self.length, features)
        self.each = (micros, self.length)
        self.quarter = (self.length // 2, features)
        self.square = (2 * BLOCK, KEYS)
        self.around = BEFORE + self.length + AHEAD
        self.key_scratch = [(self.around, 4 * self.width), (SUMS + self.segs + SUMS, 4 * self.width)]
        self.run = Steps()
        self.smem = pl.BlockSpec(memory_space=pltpu.SMEM)
        pairs = [None] * micros
        self.mix, self.mix_far, self.p_outer, self.fed, self.dn2 = (list(pairs) for _ in range(5))
        self.back_of = list(pairs)
        self.sums = {}

    def pack(self):
        args = (*self.projections, self.weights[2], self.bq, self.bv, self.bi, self.frames)
        self.own, edge = self.run.call(
            pack_kernel, "pack", [(self.features + 8, 4 * self.width), (self.micros, BEFORE, self.features)], args,
            copies=6 + self.features // self.width + self.micros, far=range(8),
        )
        self.pair = swap(self.own, "head", 1)
        self.edge = swap_edges(edge, False)

    def norm(self):
        each, features, micros = self.each, self.features, self.micros
        wi, wu, wo = self.weights
        (self.x, self.xhat, self.rate, self.normed, self.wi, self.wu, self.wo, *self.g, self.before, self.ahead) = self.run.call(
            norm_kernel, "norm",
            [each + (features,)] * 2 + [each + (128,), each + (features,), wi.shape, wu.shape, wo.shape, self.big, self.big,
             (micros, BEFORE, features), (micros, AHEAD, features)],
            (self.frames, self.g1, self.s1, wi, wu, wo, self.cotangent),
            scratch=[(16, features)], copies=4 * micros + 5, far=range(7),
        )
        self.wo_far = swap(self.wo, "head", 2)
        self.wi_pair, self.wu_pair = (swap(v, "head", 1) for v in (self.wi, self.wu))

    def project(self):
        each, features, width = self.each, self.features, self.width
        args = (self.normed, self.own, self.pair, self.g1, self.s1, self.g2, self.s2, self.bo, self.bi, self.bu)
        self.q, self.kv, self.w_all, self.bias, self.params = self.run.call(
            project_kernel, "project",
            [each + (2 * width,), each + (4 * width,), (features, 6 * width), (1, 6 * width), (7, 1, features)],
            args, copies=7, far=range(3, 10),
        )

    def edges(self):
        shape = (self.micros, BEFORE + AHEAD)
        self.xhat_edge, self.normed_edge, self.kv_edge = self.run.call(
            edges_kernel, "edges", [shape + (self.features,)] * 2 + [shape + (4 * self.width,)],
            (self.edge, self.before, self.ahead, self.params, self.w_all, self.bias),
        )

    def attend_inner(self):
        self.mix_inner, self.p_inner = self.run.call(
            attend_inner_kernel, "attend_inner",
            [(self.micros, self.length - 2 * BLOCK, 2 * self.width),
             (self.micros, self.blocks - 2, self.pairs) + self.square],
            (self.counts, self.q, self.kv), {0: self.smem}, self.key_scratch,
        )

    def attend_outer(self, m):
        self.mix[m], self.p_outer[m] = self.run.call(
            functools.partial(attend_outer_kernel, m), "attend_outer",
            [(self.length, 2 * self.width), (2, self.pairs) + self.square],
            (self.counts, self.q, self.kv, self.kv_edge, self.mix_inner),
            {0: self.smem}, self.key_scratch,
        )
        self.mix_far[m] = swap(self.mix[m], "head", 2)

    def hand_on(self):
        shape = self.wo_far.shape
        self.wo_here, far = self.run.call(
            hand_on_kernel, "hand_on", [(2 * shape[0], shape[1]), shape], (self.own, self.pair, self.wo_far)
        )
        self.wo_far_pair = swap(far, "head", 1)

    def feed(self, m):
        big, features, hidden = self.big, self.features, self.hidden
        *self.fed[m], part = self.run.call(
            functools.partial(feed_kernel, m), "feed", [big, (self.length, 2 * hidden), (self.length, 2 * hidden), big, big],
            (self.mix[m], self.mix_far[m], self.wo_here, self.wo_far, self.wo_far_pair, self.x, self.g[m], self.params,
             self.pair, self.wi, self.wi_pair, self.wu, self.wu_pair),
            scratch=[big, (features, features)],
        )
        self.dn2[m] = (part, swap(part, "head", 2))

    def inner_weights(self):
        features, hidden = self.features, self.hidden
        self.inner_own, *pair, self.vec_inner = self.run.call(
            inner_weights_kernel, "inner_weights",
            [(features, hidden)] + [(features // PIECES, hidden)] * PIECES + [(2, hidden)],
            (self.fed[0][0], self.fed[1][0], self.fed[0][2], self.fed[1][2]),
        )
        self.inner_pair = swap_near(pair)

    def outer_weights(self):
        features, hidden = self.features, self.hidden
        self.outer_own, *pair, self.vec_outer = self.run.call(
            outer_weights_kernel, "outer_weights",
            [(hidden, features)] + [(hidden // PIECES, features)] * PIECES + [(1, features)],
            (self.fed[0][1], self.fed[1][1], *self.g),
        )
        self.outer_pair = swap_near(pair)

    def feed_out(self):
        (part,) = self.run.call(
            feed_out_kernel, "feed_out", [(self.micros * self.length, self.features)],
            (self.fed[0][1], self.fed[1][1], self.wu, self.wu_pair),
        )
        self.part = (part, swap(part, "head", 2))

    def out_half(self):
        (half,) = self.run.call(
            out_half_kernel, "out_half", [(self.micros * self.length, self.features)],
            (self.fed[0][3], self.fed[1][3], *self.part, self.params),
        )
        self.out = half

    def out_send(self):
        (half,) = self.run.call(copy_kernel, "out_send", [self.out.shape], (self.out,))
        self.out = (half, swap(half, "head", 1))

    def grad_sum(self, m):
        (self.dn2[m],) = self.run.call(add_whole_kernel, "grad_sum", [self.big], self.dn2[m])

    def back(self, m):
        length, width, features = self.length, self.width, self.features
        self.back_of[m] = self.run.call(
            functools.partial(back_kernel, m), "back",
            [self.big, (length, 2 * width), (self.around, 4 * width), (features, width), (features, width), (3, features)],
            (self.dn2[m], self.fed[m][3], self.g[m], self.params, self.wo_here, self.mix[m], self.q, self.kv,
             self.kv_edge, self.p_inner, self.p_outer[m]),
            scratch=self.key_scratch + self.key_scratch[1:] + [(length, 2 * width), (features, 2 * width)],
        )

    def pick(self, number):
        return [v[number] for v in self.back_of]

    def project_back(self):
        features, micros = self.features, self.micros
        (dq_0, dq_1), (dkv_0, dkv_1) = self.pick(1), self.pick(2)
        part, pair, beyond, self.vec_first = self.run.call(
            project_back_kernel, "project_back",
            [(micros * self.length, features)] + [(micros, BEFORE, features)] * 2 + [(2, features)],
            (dq_0, dkv_0, dq_1, dkv_1, self.xhat, self.xhat_edge, self.w_all), scratch=[(self.around, features)],
        )
        self.edges_back = (part, swap(pair, "head", 1), swap_edges(beyond, True))

    def edge_add(self):
        part = self.edges_back[0]
        (part,) = self.run.call(edge_add_kernel, "edge_add", [part.shape], self.edges_back)
        self.dn1 = (part, swap(part, "head", 2))

    def project_weights(self):
        features, width = self.features, self.width
        *self.heads_own, self.rows, a, b = self.run.call(
            project_weights_kernel, "project_weights",
            [(features // 2, 4 * width)] * 2 + [(8, features), (features // 2 + 8, 4 * width), (features // 2, 4 * width)],
            (self.normed, self.normed_edge, *self.pick(1), *self.pick(2), *self.pick(3), *self.pick(4), *self.pick(5),
             self.vec_first, self.vec_outer, self.vec_inner),
            scratch=[(features, 4 * width), (features, 6 * width), (1, 6 * width)],
        )
        self.heads_pair = swap_near((a, b))

    def begin(self, name):
        if name == "heads":
            a, b = self.heads_pair
            return SumsOverTm(self.run, self.heads_own, ((a,), (b,)), self.rows)
        return SumsOverTm(self.run, (self.outer_own, self.inner_own), (self.outer_pair, self.inner_pair))

    def sum(self, name):
        if name not in self.sums:
            self.sums[name] = self.begin(name)
        elif not self.sums[name].joined:
            self.sums[name].step()

    def ffn(self):
        self.sum("ffn")

    def heads(self):
        self.sum("heads")

    def frames_back(self):
        (half,) = self.run.call(
            frames_back_kernel, "frames_back", [(self.micros * self.length, self.features)],
            (*self.dn1, self.xhat, self.rate, *self.pick(0), self.params),
        )
        self.grad = (half, swap(half, "head", 1))

    def place(self, name, halves):
        (out,) = self.run.call(
            place_kernel, name, [(self.micros, 2 * self.length, self.features)], halves, copies=2 * self.micros, far_outs=[0]
        )
        return out

    def place_out(self):
        self.layer_output = self.place("place_out", self.out)

    def place_frames(self):
        self.frames_grad = self.place("place_frames", self.grad)

    def join(self, name, number, shape):
        bit, parts = self.sums["ffn"].halves(number)
        (out,) = self.run.call(
            functools.partial(join_out_kernel, bit), name, [shape], parts, copies=2, far_outs=[0]
        )
        return out

    def settle(self, *names):
        while not all(self.sums[name].joined for name in names):
            for name in names:
                self.sum(name)

    def join_outer(self):
        self.settle("ffn", "heads")
        self.outer_grad = self.join("join_outer", 0, self.weights[1].shape)

    def join_inner(self):
        self.inner_grad = self.join("join_inner", 1, self.weights[0].shape)

    def finish(self):
        features, width, hidden = self.features, self.width, self.hidden
        sums = self.sums["heads"]
        rows = sums.rows[0]
        bits, parts = zip(*(sums.halves(i) for i in range(2)), strict=True)
        out = self.run.call(
            functools.partial(finish_kernel, list(bits)), "finish",
            [(1, features)] * 6 + [(1, width)] * 2 + [(1, hidden)] + [(features, width)] * 3 + [(width, features)],
            (rows, swap(rows, "head", 2), *parts[0], *parts[1]),
        )
        bo, g2, s2, g1, s1, bu, bq, bv, bi = (v.reshape(v.shape[1]) for v in out[:9])
        wq, wk, wv, wo = out[9:]
        return (
            self.layer_output, self.frames_grad, wq, bq, wk, wv, bv, wo, bo, g1, s1, g2, s2, self.inner_grad, bi,
            self.outer_grad, bu,
        )


def per_device(*args):
    layer = Layer(*args)
    for step, us in ORDER:
        layer.run.us = us
        name = step.rstrip("0123456789")
        result = getattr(layer, name)(*(int(digit) for digit in step[len(name) :]))
    return result


def solution(mesh):
    in_specs = (
        P(None, "tm", None),
        P(None, "tm", None),
        P(),
        P(None, "head"),
        P("head"),
        P(None, "head"),
        P(None, "head"),
        P("head"),
        P("head", None),
        P(),
        P(),
        P(),
        P(),
        P(),
        P(None, "head"),
        P("head"),
        P("head", None),
        P(),
    )
    out_specs = (
        P(None, "tm", None),
        P(None, "tm", None),
        P(None, "head"),
        P("head"),
        P(None, "head"),
        P(None, "head"),
        P("head"),
        P("head", None),
        P(),
        P(),
        P(),
        P(),
        P(),
        P(None, "head"),
        P("head"),
        P("head", None),
        P(),
    )
    return jax.shard_map(
        per_device, mesh=mesh, in_specs=in_specs, out_specs=out_specs, check_vma=False
    )
```

```python
import functools

import jax
import jax.numpy as jnp
from jax import lax
from jax.experimental import pallas as pl
from jax.experimental.pallas import tpu as pltpu
from jax.sharding import PartitionSpec as P

HEAD_DIM = 64
SEG = 16
RC = 4
LC = 30
MEM = 4

EPSILON = 1e-05
MASKED = -1e30
F32 = jnp.float32

BEFORE = MEM * SEG
AHEAD = 8
CACHE = 32
SUMS = 8
BLOCK = 64
WIN = CACHE + BLOCK + AHEAD
SWIN = 16
KEYS = 128
FIRST_GAIN, FIRST_SHIFT, SECOND_GAIN, SECOND_SHIFT, OUT_BIAS, INNER_BIAS, OUTER_BIAS = range(7)
PAIR = 2 * HEAD_DIM
MIB = 1 << 20


def mm(left, right, left_dim=1, right_dim=0):
    return lax.dot_general(
        left,
        right,
        (((left_dim,), (right_dim,)), ((), ())),
        precision=lax.Precision.HIGH,
        preferred_element_type=F32,
    )


def normalise(values):
    centred = values - jnp.mean(values, axis=-1, keepdims=True)
    variance = jnp.mean(centred * centred, axis=-1, keepdims=True)
    rate = lax.rsqrt(variance + EPSILON)
    return centred * rate, rate


def norm_back(grad, gain, xhat, rate):
    scaled = grad * gain
    first = jnp.mean(scaled, axis=-1, keepdims=True)
    second = jnp.mean(scaled * xhat, axis=-1, keepdims=True)
    return rate * (scaled - first - xhat * second)


def column_sums(values):
    return jnp.sum(values, axis=0, keepdims=True)


def seg_means(values):
    rows, width = values.shape
    return jnp.sum(values.reshape(rows // SEG, SEG, width), axis=1) * (1.0 / SEG)


def near_bit():
    return lax.axis_index("head") % 2


def far_bit():
    return lax.axis_index("head") // 2


def my_rows(rows):
    half = rows // 2
    return pl.ds(pl.multiple_of(near_bit() * half, half), half)


def lanes_of(place, width, start=0):
    at = place + near_bit() - 2 * place * near_bit()
    return pl.ds(pl.multiple_of(start + at * width, width), width)


def half_rows(place, half):
    return pl.ds(pl.multiple_of(place * half, half), half)


def full(shape):
    return pl.BlockSpec(shape, lambda *_: (0,) * len(shape))


class Steps:
    def __init__(self):
        self.held = []
        self.us = 0.1

    def call(self, kernel, name, outs, args, specs=None, scratch=(), vmem=32, copies=0, far=(), far_outs=()):
        specs = dict(specs or {})
        given, made, held = len(args), len(outs), tuple(self.held)
        token = bool(far_outs)
        somewhere = pl.BlockSpec(memory_space=pl.ANY)
        in_hbm = pl.BlockSpec(memory_space=pltpu.HBM)

        def body(*refs):
            ins, rest = refs[:given], refs[given + len(held) :]
            if token:
                rest[made][...] = jnp.zeros(rest[made].shape, F32)
            kernel(*ins, *rest[:made], *rest[made + token :])

        args = [pltpu.with_memory_space_constraint(a, pltpu.HBM) if i in far else a for i, a in enumerate(args)]
        out_specs = [in_hbm if i in far_outs else full(shape) for i, shape in enumerate(outs)]
        out_shape = [
            pltpu.HBM(shape, F32) if i in far_outs else jax.ShapeDtypeStruct(shape, F32) for i, shape in enumerate(outs)
        ]
        if token:
            out_specs.append(full((1, 128)))
            out_shape.append(jax.ShapeDtypeStruct((1, 128), F32))
        out = pl.pallas_call(
            body,
            name=name,
            grid=(1,),
            in_specs=[in_hbm if i in far else specs.get(i, full(a.shape)) for i, a in enumerate(args)]
            + [somewhere] * len(held),
            out_specs=out_specs,
            out_shape=out_shape,
            scratch_shapes=[pltpu.VMEM(shape, F32) for shape in scratch]
            + ([pltpu.SemaphoreType.DMA((copies,))] if copies else []),
            compiler_params=pltpu.CompilerParams(vmem_limit_bytes=vmem * MIB),
            cost_estimate=pl.CostEstimate(flops=int(self.us * 5.18e8), bytes_accessed=0, transcendentals=0),
        )(*args, *held)
        self.held = [out[-1]]
        return out[:made]


def copy_all(pairs, sems):
    copies = [pltpu.make_async_copy(a, b, sems.at[i]) for i, (a, b) in enumerate(pairs)]
    for copy in copies:
        copy.start()
    return copies


def pack_kernel(wq, wk, wv, wo, bq, bv, bi, frames, out, edge, sems):
    rows, width = wq.shape
    out[rows:] = jnp.zeros((out.shape[0] - rows, out.shape[1]), F32)
    pairs = [(w, out.at[pl.ds(0, rows), pl.ds(i * width, width)]) for i, w in enumerate((wq, wk, wv))]
    for at in range(0, wo.shape[1], width):
        pairs.append((wo.at[:, pl.ds(at, width)], out.at[pl.ds(at, width), pl.ds(3 * width, width)]))
    pairs += [(b, out.at[pl.ds(rows, 1), pl.ds(i * width, width)]) for i, b in ((0, bq), (2, bv))]
    pairs.append((bi, out.at[pl.ds(rows + 1, 1), pl.ds(0, bi.shape[1])]))
    start = pl.multiple_of((1 - near_bit()) * (frames.shape[1] - BEFORE), BEFORE)
    pairs += [(frames.at[m, pl.ds(start, BEFORE)], edge.at[m]) for m in range(frames.shape[0])]
    for copy in copy_all(pairs, sems):
        copy.wait()


def norm_kernel(
    frames, gain, shift, wi, wu, wo, cotangent,
    x_ref, xhat_ref, rate_ref, normed_ref, wi_ref, wu_ref, wo_ref, g_0, g_1, before, ahead, params, sems,
):
    micros, half, _ = x_ref.shape
    rows = frames.shape[1]
    pairs = [(gain, params.at[pl.ds(0, 1)]), (shift, params.at[pl.ds(8, 1)])]
    pairs += [(frames.at[m, my_rows(rows)], x_ref.at[m]) for m in range(micros)]
    pairs += [(frames.at[m, pl.ds(half - BEFORE, BEFORE)], before.at[m]) for m in range(micros)]
    pairs += [(frames.at[m, pl.ds(half, AHEAD)], ahead.at[m]) for m in range(micros)]
    pairs += [(wo, wo_ref), (wi, wi_ref), (wu, wu_ref)]
    pairs += [(cotangent.at[m, my_rows(rows)], g) for m, g in enumerate((g_0, g_1))]
    copies = copy_all(pairs, sems)
    for copy in copies[:2]:
        copy.wait()
    for micro in range(micros):
        copies[2 + micro].wait()
        xhat, rate = normalise(x_ref[micro])
        xhat_ref[micro] = xhat
        normed_ref[micro] = xhat * params[0:1] + params[8:9]
        rate_ref[micro] = jnp.broadcast_to(rate, (half, rate_ref.shape[2]))
    for copy in copies[2 + micros :]:
        copy.wait()


def project_kernel(normed, own, pair, g1, s1, g2, s2, bo, bi, bu, q_ref, kv_ref, w_ref, bias, rows_ref, sems):
    micros, half, wide = q_ref.shape
    features = normed.shape[2]
    width = own.shape[1] // 4
    copies = copy_all([(v, rows_ref.at[i]) for i, v in enumerate((g1, s1, g2, s2, bo, bi, bu))], sems)
    for number in range(3):
        at = slice(number * width, (number + 1) * width)
        for place, source in enumerate((own, pair)):
            lanes = lanes_of(place, width, 2 * number * width)
            w_ref[:, lanes] = source[:features, at]
            bias[:, lanes] = source[features : features + 1, at]
    for micro in range(micros):
        out = mm(normed[micro], w_ref[...]) + bias[...]
        q_ref[micro] = out[:, :wide]
        kv_ref[micro] = out[:, wide:]
    for copy in copies:
        copy.wait()


def edges_kernel(edge, before, ahead, params, w_ref, bias, xhat_ref, normed_ref, kv_ref):
    near = near_bit()
    wide = w_ref.shape[1] // 3
    for micro in range(edge.shape[0]):
        first = jnp.where(near == 0, edge[micro], before[micro])
        last = jnp.where(near == 0, ahead[micro], edge[micro, :AHEAD])
        xhat, _ = normalise(jnp.concatenate([first, last], axis=0))
        normed = xhat * params[FIRST_GAIN] + params[FIRST_SHIFT]
        xhat_ref[micro] = xhat
        normed_ref[micro] = normed
        kv_ref[micro] = mm(normed, w_ref[:, wide:]) + bias[:, wide:]


def fill_keys(kv, edge, kx, sx):
    length = kv.shape[0]
    kx[BEFORE : BEFORE + length] = kv
    segs = length // SEG
    sx[SUMS : SUMS + segs] = seg_means(kv)
    if edge is not None:
        kx[:BEFORE] = edge[:BEFORE]
        kx[BEFORE + length :] = edge[BEFORE:]
        sx[: SUMS - MEM] = jnp.zeros((SUMS - MEM, kv.shape[1]), F32)
        sx[SUMS - MEM : SUMS] = seg_means(edge[:BEFORE])
        sx[SUMS + segs :] = jnp.zeros((sx.shape[0] - SUMS - segs, kv.shape[1]), F32)


def summary_start(block):
    return (block * (BLOCK // SEG) + SUMS - MEM) // SUMS * SUMS


def frame_rows(block):
    start = BEFORE - CACHE + block * BLOCK
    return slice(start, start + WIN)


def key_window(kx, sx, block, lanes):
    start = summary_start(block)
    rows = [kx[frame_rows(block), lanes], sx[start : start + SWIN, lanes]]
    return jnp.concatenate(rows + [jnp.zeros((KEYS - WIN - SWIN, PAIR), F32)], axis=0)


def by_head(values):
    first = lax.broadcasted_iota(jnp.int32, values.shape, 1) < HEAD_DIM
    return jnp.concatenate([jnp.where(first, values, 0.0), jnp.where(first, 0.0, values)], axis=0)


def side_by_side(values):
    rows = values.shape[0] // 2
    first = lax.broadcasted_iota(jnp.int32, (rows, values.shape[1]), 1) < HEAD_DIM
    return jnp.where(first, values[:rows], values[rows:])


def owner_of(segment, bounds):
    owner = jnp.where(segment < 0, -1, 0)
    for bound in bounds:
        owner = owner + (segment >= bound).astype(jnp.int32)
    return owner


def visible(block, base, bounds):
    row = lax.broadcasted_iota(jnp.int32, (2 * BLOCK, 1), 0) % BLOCK
    column = lax.broadcasted_iota(jnp.int32, (1, KEYS), 1)
    query_seg = block * (BLOCK // SEG) + row // SEG
    frame = block * BLOCK - CACHE + column
    is_frame = column < WIN
    summary = summary_start(block) - SUMS + column - WIN
    key_seg = jnp.where(is_frame, (frame + CACHE) // SEG - CACHE // SEG, summary)
    key_seg = jnp.where(column < WIN + SWIN, key_seg, -(1 << 20))
    inside = (frame >= query_seg * SEG - LC) & (frame < query_seg * SEG + SEG + RC)
    near = (key_seg >= query_seg - MEM) & (key_seg < query_seg)
    seen = (is_frame & inside) | ((column >= WIN) & near)
    return seen & (owner_of(key_seg + base, bounds) == owner_of(query_seg + base, bounds))


def bounds_of(counts, micro):
    bounds, total = [], 0
    for utterance in range(counts.shape[1]):
        total = total + counts[micro, utterance]
        bounds.append(total)
    return bounds


def first_segment(length):
    return (lax.axis_index("tm") * 2 + near_bit()) * (length // SEG)


def block_rows(block):
    return slice(block * BLOCK, (block + 1) * BLOCK)


def attend_block(block, seen, query, kx, sx, keep, put):
    width = query.shape[1]
    for pair in range(width // PAIR):
        lanes = slice(pair * PAIR, (pair + 1) * PAIR)
        value_lanes = slice(width + pair * PAIR, width + (pair + 1) * PAIR)
        scores = mm(by_head(query[:, lanes] * HEAD_DIM ** (-0.5)), key_window(kx, sx, block, lanes), 1, 1)
        scores = jnp.where(seen, scores, MASKED)
        weights = jnp.exp(scores - jnp.max(scores, axis=-1, keepdims=True))
        weights = weights / jnp.sum(weights, axis=-1, keepdims=True)
        keep(pair, weights)
        put(lanes, side_by_side(mm(weights, key_window(kx, sx, block, value_lanes))))


def attend_inner_kernel(counts, q_ref, kv_ref, mix_0, mix_1, p_ref, kx, sx):
    _, length, _ = q_ref.shape
    base = first_segment(length)
    for micro, mix_ref in enumerate((mix_0, mix_1)):
        fill_keys(kv_ref[micro], None, kx, sx)
        bounds = bounds_of(counts, micro)
        for number, block in enumerate(range(1, length // BLOCK - 1)):
            def keep(pair, weights):
                p_ref[micro, number, pair] = weights

            def put(lanes, values):
                mix_ref[block_rows(number), lanes] = values

            seen = visible(block, base, bounds)
            attend_block(block, seen, q_ref[micro, block_rows(block)], kx, sx, keep, put)


def attend_outer_kernel(micro, counts, q_ref, kv_ref, edge, mix_ref, p_ref, kx, sx):
    _, length, _ = q_ref.shape
    base = first_segment(length)
    fill_keys(kv_ref[micro], edge[micro], kx, sx)
    bounds = bounds_of(counts, micro)
    for number, block in enumerate((0, length // BLOCK - 1)):
        def keep(pair, weights):
            p_ref[number, pair] = weights

        def put(lanes, values):
            mix_ref[block_rows(number), lanes] = values

        seen = visible(block, base, bounds)
        attend_block(block, seen, q_ref[micro, block_rows(block)], kx, sx, keep, put)


def fill_rows(target, lanes, inner, outer):
    length = inner.shape[0] + outer.shape[0]
    target[:BLOCK, lanes] = outer[:BLOCK]
    target[BLOCK : length - BLOCK, lanes] = inner[...]
    target[length - BLOCK : length, lanes] = outer[BLOCK:]


def back_kernel(
    micro, grad_ref, mid_ref, g_ref, params, wo_here, mix_inner, mix_outer, q_ref, kv_ref, edge, p_inner, p_outer,
    dmid_ref, dq_ref, dkv_ref, dwo_own, dwo_pair, vec_ref,
    kx, sx, dsx, dmix, mix, dwo,
):
    _, length, width = q_ref.shape
    near_width = dwo_own.shape[1]
    grad = grad_ref[...]
    xhat, rate = normalise(mid_ref[...])
    dmid = g_ref[...] + norm_back(grad, params[SECOND_GAIN], xhat, rate)
    dmid_ref[...] = dmid
    vec_ref[0:1] = column_sums(dmid)
    vec_ref[1:2] = column_sums(grad * xhat)
    vec_ref[2:3] = column_sums(grad)
    dmix[...] = mm(dmid, wo_here[...], 1, 1)
    fill_rows(mix, slice(None), mix_inner, mix_outer)
    dwo[...] = mm(dmid, mix[...], 0, 0)
    dwo_own[...] = dwo[:, lanes_of(0, near_width)]
    dwo_pair[...] = dwo[:, lanes_of(1, near_width)]
    fill_keys(kv_ref[micro], edge[micro], kx, sx)
    dkv_ref[...] = jnp.zeros_like(dkv_ref)
    dsx[...] = jnp.zeros_like(dsx)
    for block in range(length // BLOCK):
        start = summary_start(block)
        rows, frames, sums = block_rows(block), frame_rows(block), slice(start, start + SWIN)
        for pair in range(width // PAIR):
            lanes = slice(pair * PAIR, (pair + 1) * PAIR)
            value_lanes = slice(width + pair * PAIR, width + (pair + 1) * PAIR)
            inside = 0 < block < length // BLOCK - 1
            weights = p_inner[micro, block - 1, pair] if inside else p_outer[min(block, 1), pair]
            grad = by_head(dmix[rows, lanes])
            dweights = mm(grad, key_window(kx, sx, block, value_lanes), 1, 1)
            dscores = weights * (dweights - jnp.sum(dweights * weights, axis=-1, keepdims=True))
            dquery = side_by_side(mm(dscores, key_window(kx, sx, block, lanes)))
            dq_ref[rows, lanes] = dquery * HEAD_DIM ** (-0.5)
            dkeys = mm(dscores, by_head(q_ref[micro, rows, lanes] * HEAD_DIM ** (-0.5)), 0, 0)
            dvalues = mm(weights, grad, 0, 0)
            dkv_ref[frames, lanes] += dkeys[:WIN]
            dkv_ref[frames, value_lanes] += dvalues[:WIN]
            dsx[sums, lanes] += dkeys[WIN : WIN + SWIN]
            dsx[sums, value_lanes] += dvalues[WIN : WIN + SWIN]
    count = BEFORE + length
    segs = count // SEG
    spread = dsx[SUMS - MEM : SUMS - MEM + segs] * (1.0 / SEG)
    spread = jnp.broadcast_to(spread[:, None, :], (segs, SEG, 2 * width))
    dkv_ref[:count] += spread.reshape(count, 2 * width)


def feed_kernel(
    micro, own_inner, own_outer, far_inner, far_outer, wo_here, wo_far, wo_far_pair, x_ref, g_ref, params, pair, wi_own, wi_pair, wu_own, wu_pair,
    n2_ref, h_ref, dpre_ref, mid_ref, part_ref,
    mix, wo,
):
    width = own_inner.shape[1] // 2
    features, hidden = wi_own.shape
    far = far_bit()
    here = pl.multiple_of(far * 2 * width, 2 * width)
    there = pl.multiple_of((1 - far) * 2 * width, 2 * width)
    fill_rows(mix, pl.ds(here, 2 * width), own_inner, own_outer)
    fill_rows(mix, pl.ds(there, 2 * width), far_inner, far_outer)
    wo[pl.ds(here, 2 * width)] = wo_here[...]
    wo[lanes_of(0, width, there)] = wo_far[...]
    wo[lanes_of(1, width, there)] = wo_far_pair[...]
    middle = x_ref[micro] + mm(mix[...], wo[...]) + params[OUT_BIAS]
    mid_ref[...] = middle
    xhat, _ = normalise(middle)
    normed = xhat * params[SECOND_GAIN] + params[SECOND_SHIFT]
    n2_ref[...] = normed
    part = None
    for place, (wi, wu, bias) in enumerate(((wi_own, wu_own, params[INNER_BIAS][:, :hidden]), (wi_pair, wu_pair, pair[features + 1 : features + 2, :hidden]))):
        at = slice(place * hidden, (place + 1) * hidden)
        pre = mm(normed, wi[...]) + bias
        phi = 0.5 + 0.5 * lax.erf(pre * (0.5**0.5))
        h_ref[:, at] = pre * phi
        slope = phi + pre * (jnp.exp(-0.5 * pre * pre) * 0.3989422804014327)
        dpre = mm(g_ref[...], wu[...], 1, 1) * slope
        dpre_ref[:, at] = dpre
        step = mm(dpre, wi[...], 1, 1)
        part = step if part is None else part + step
    part_ref[...] = part


def put_rows(value, outs):
    at = 0
    for out in outs:
        count = out.shape[0]
        out[...] = value[at : at + count]
        at += count


def inner_weights_kernel(n2_0, n2_1, d_0, d_1, own_ref, *rest):
    *pair, vec_ref = rest
    hidden = own_ref.shape[1]
    for place, outs in enumerate(((own_ref,), pair)):
        at = slice(place * hidden, (place + 1) * hidden)
        put_rows(mm(n2_0[...], d_0[:, at], 0, 0) + mm(n2_1[...], d_1[:, at], 0, 0), outs)
        vec_ref[place : place + 1] = column_sums(d_0[:, at]) + column_sums(d_1[:, at])


def outer_weights_kernel(h_0, h_1, g_0, g_1, own_ref, *rest):
    *pair, vec_ref = rest
    hidden = own_ref.shape[0]
    for place, outs in enumerate(((own_ref,), pair)):
        at = slice(place * hidden, (place + 1) * hidden)
        put_rows(mm(h_0[:, at], g_0[...], 0, 0) + mm(h_1[:, at], g_1[...], 0, 0), outs)
    vec_ref[...] = column_sums(g_0[...]) + column_sums(g_1[...])


def feed_out_kernel(h_0, h_1, wu_own, wu_pair, out_ref):
    hidden = wu_own.shape[0]
    rows = h_0.shape[0]
    for micro, h_ref in enumerate((h_0, h_1)):
        part = mm(h_ref[:, :hidden], wu_own[...]) + mm(h_ref[:, hidden:], wu_pair[...])
        out_ref[micro * rows : (micro + 1) * rows] = part


def out_half_kernel(mid_0, mid_1, part, far, params, out):
    rows = mid_0.shape[0]
    for micro, mid_ref in enumerate((mid_0, mid_1)):
        at = slice(micro * rows, (micro + 1) * rows)
        out[at] = mid_ref[...] + (part[at] + far[at]) + params[OUTER_BIAS]


def project_back_kernel(
    dq_0, dkv_0, dq_1, dkv_1, xhat, xhat_edge, w_ref, part_ref, pair_ref, beyond_ref, vec_ref, work
):
    near = near_bit()
    length, wide = dq_0.shape
    own = slice(BEFORE, BEFORE + length)
    gain, shift = 0.0, 0.0
    for micro, (dq, dkv) in enumerate(((dq_0, dkv_0), (dq_1, dkv_1))):
        work[...] = mm(dkv[...], w_ref[:, wide:], 1, 1)
        work[own] += mm(dq[...], w_ref[:, :wide], 1, 1)
        part_ref[micro * length : (micro + 1) * length] = work[own]
        before = work[:BEFORE]
        ahead = jnp.concatenate([work[BEFORE + length :], jnp.zeros((BEFORE - AHEAD, work.shape[1]), F32)], axis=0)
        pair_ref[micro] = jnp.where(near == 0, ahead, before)
        beyond_ref[micro] = jnp.where(near == 0, before, ahead)
        gain = gain + column_sums(work[own] * xhat[micro]) + column_sums(work[:BEFORE] * xhat_edge[micro, :BEFORE])
        gain = gain + column_sums(work[BEFORE + length :] * xhat_edge[micro, BEFORE:])
        shift = shift + column_sums(work[...])
    vec_ref[0:1] = gain
    vec_ref[1:2] = shift


def edge_add_kernel(part, pair, beyond, out):
    out[...] = part[...]
    near = near_bit()
    micros = pair.shape[0]
    length = part.shape[0] // micros
    for micro in range(micros):
        end = (micro + 1) * length
        out[end - BEFORE : end] += jnp.where(near == 0, pair[micro], beyond[micro])
        out[end - length : end - length + AHEAD] += jnp.where(near == 0, beyond[micro, :AHEAD], pair[micro, :AHEAD])


def project_weights_kernel(
    normed, normed_edge, dq_0, dq_1, dkv_0, dkv_1, wo_own_0, wo_own_1, wo_pair_0, wo_pair_1, mid_0, mid_1, first, vec_outer, vec_inner,
    own_0, own_1, rows_ref, pair_0, pair_1, message, sums, row,
):
    features = normed.shape[2]
    width = wo_own_0.shape[1]
    hidden = vec_inner.shape[1]
    length, wide = dq_0.shape
    own, after = slice(BEFORE, BEFORE + length), slice(BEFORE + length, None)
    edges = jnp.concatenate([dkv_0[:BEFORE], dkv_0[after], dkv_1[:BEFORE], dkv_1[after]], axis=0)
    normed_edges = jnp.concatenate([normed_edge[0], normed_edge[1]], axis=0)
    queries = mm(normed[0], dq_0[...], 0, 0) + mm(normed[1], dq_1[...], 0, 0)
    keyvals = mm(normed[0], dkv_0[own], 0, 0) + mm(normed[1], dkv_1[own], 0, 0) + mm(normed_edges, edges, 0, 0)
    sums[:, :wide] = queries
    sums[:, wide:] = keyvals
    row[:, :wide] = column_sums(dq_0[...]) + column_sums(dq_1[...])
    row[:, wide:] = column_sums(dkv_0[...]) + column_sums(dkv_1[...])
    rows_ref[0:3] = (mid_0[...] + mid_1[...]) * 0.5
    rows_ref[3:5] = first[...]
    rows_ref[5:6] = vec_outer[...] * 0.5
    rows_ref[6:] = jnp.zeros((2, features), F32)
    half = own_0.shape[0]
    pair_0[half : half + 6] = rows_ref[0:6]
    pair_0[half + 6 :] = jnp.zeros((2, features), F32)
    for place, (out_ref, at) in enumerate(((rows_ref, 6), (pair_0, half + 6))):
        for number in range(3):
            lanes = slice(number * width, (number + 1) * width)
            out_ref[at : at + 1, lanes] = row[:, lanes_of(place, width, 2 * number * width)]
        out_ref[at + 1 : at + 2, :hidden] = vec_inner[place : place + 1]
    for place, (outs, wo_0, wo_1) in enumerate((((own_0, own_1), wo_own_0, wo_own_1), ((pair_0, pair_1), wo_pair_0, wo_pair_1))):
        for number in range(3):
            lanes = slice(number * width, (number + 1) * width)
            message[:, lanes] = sums[:, lanes_of(place, width, 2 * number * width)]
        message[:, 3 * width :] = wo_0[...] + wo_1[...]
        for number, out_ref in enumerate(outs):
            out_ref[:half] = message[number * half : (number + 1) * half]


def frames_back_kernel(a_ref, b_ref, xhat, rate, dmid_0, dmid_1, params, out):
    rows = dmid_0.shape[0]
    for micro, dmid_ref in enumerate((dmid_0, dmid_1)):
        at = slice(micro * rows, (micro + 1) * rows)
        grad = norm_back(a_ref[at] + b_ref[at], params[FIRST_GAIN], xhat[micro], rate[micro, :, :1])
        out[at] = dmid_ref[...] + grad


def place_kernel(own, pair, out, sems):
    micros, half = out.shape[0], out.shape[1] // 2
    near = near_bit()
    pairs = []
    for micro in range(micros):
        rows = pl.ds(micro * half, half)
        pairs.append((own.at[rows], out.at[micro, half_rows(near, half)]))
        pairs.append((pair.at[rows], out.at[micro, half_rows(1 - near, half)]))
    for copy in copy_all(pairs, sems):
        copy.wait()


def place_of(bit):
    return lax.axis_index("tm") // bit % 2


def add_pieces(out, a_ref, pieces, rows_ref=None, new_rows=None):
    count, at = a_ref.shape[0], 0
    if not pieces:
        out[...] = a_ref[...]
        if new_rows is not None:
            new_rows[...] = rows_ref[...]
    for piece in pieces:
        take = min(piece.shape[0], count - at)
        if take:
            out[at : at + take] = a_ref[at : at + take] + piece[:take]
        if take < piece.shape[0]:
            new_rows[...] = rows_ref[...] + piece[take:]
        at += take


def add_split_kernel(bits, counts, rows, *refs):
    total = len(bits)
    values, refs = refs[:total], refs[total:]
    rows_ref, refs = (refs[0], refs[1:]) if rows else (None, refs)
    pieces = []
    for count in counts:
        pieces.append(refs[:count])
        refs = refs[count:]
    kept, sent, refs = refs[:total], refs[total : 2 * total], refs[2 * total :]
    new_rows, work = (refs[0], refs[1]) if rows else (None, refs[0])
    for number, bit in enumerate(bits):
        small = (rows_ref, new_rows) if rows and number == 0 else ()
        half = kept[number].shape[0]
        add_pieces(work, values[number], pieces[number], *small)
        place = place_of(bit)
        kept[number][...] = work[half_rows(place, half)]
        sent[number][:half] = work[half_rows(1 - place, half)]
        if small:
            sent[number][half:] = new_rows[...]


def last_kernel(rows, a_ref, *refs):
    rows_ref, refs = (refs[0], refs[1:]) if rows else (None, refs)
    b_ref, out_ref = refs
    half = a_ref.shape[0]
    out_ref[:half] = a_ref[...] + b_ref[:half]
    if rows:
        out_ref[half:] = rows_ref[...] + b_ref[half:]


def stack_kernel(rows, a_0, a_1, *refs):
    rows_ref, refs = (refs[0], refs[1:]) if rows else (None, refs)
    b_0, b_1, out_ref = refs
    half = a_0.shape[0]
    out_ref[:half] = a_0[...] + b_0[:half]
    out_ref[half : 2 * half] = a_1[...] + b_1[...]
    if rows:
        out_ref[2 * half :] = rows_ref[...] + b_0[half:]


def add_whole_kernel(a_ref, b_ref, *outs):
    at = 0
    for out in outs:
        count = out.shape[0]
        out[...] = a_ref[at : at + count] + b_ref[at : at + count]
        at += count


def join_kernel(bits, *refs):
    total = len(bits)
    for bit, mine, theirs, out in zip(bits, refs[:total], refs[total : 2 * total], refs[2 * total :], strict=True):
        half = mine.shape[0]
        place = place_of(bit)
        out[half_rows(place, half)] = mine[...]
        out[half_rows(1 - place, half)] = theirs[...]


def join_out_kernel(bit, mine, theirs, out, sems):
    half = mine.shape[0]
    place = place_of(bit)
    for copy in copy_all([(mine, out.at[half_rows(place, half)]), (theirs, out.at[half_rows(1 - place, half)])], sems):
        copy.wait()


def join_heads_kernel(bits, *refs):
    *parts, wq, wk, wv, wo = refs
    width = wq.shape[1]
    at = 0
    for number, bit in enumerate(bits):
        mine, theirs = parts[2 * number : 2 * number + 2]
        half = mine.shape[0]
        place = place_of(bit)
        for where, part in ((place, mine), (1 - place, theirs)):
            rows = pl.ds(pl.multiple_of(at + where * half, half), half)
            for heads, out in enumerate((wq, wk, wv)):
                out[rows, :] = part[:, heads * width : (heads + 1) * width]
            wo[:, rows] = part[:, 3 * width :].T
        at += 2 * half


def small_kernel(rows, far, outs):
    width = outs[-3].shape[1]
    for number, out in enumerate(outs[:6]):
        out[...] = rows[number : number + 1] + far[number : number + 1]
    outs[6][...] = rows[6:7, :width]
    outs[7][...] = rows[6:7, 2 * width : 3 * width]
    outs[8][...] = rows[7:8, : outs[8].shape[1]]


def finish_kernel(bits, rows, far, *refs):
    count = 2 * len(bits)
    small_kernel(rows, far, refs[count : count + 9])
    join_heads_kernel(bits, *refs[:count], *refs[count + 9 :])


def swap(value, axis, bit):
    size = lax.axis_size(axis)
    return lax.ppermute(value, axis, [(i, i ^ bit) for i in range(size)])


def swap_near(parts):
    return [swap(part, "head", 1) for part in parts]


def swap_edges(value, back):
    size, group = lax.axis_size("tm"), lax.axis_size("head")
    pairs = []
    for source in range(size):
        for place in range(group):
            target = source + (1 - 2 * (place % 2)) * (-1 if back else 1)
            if 0 <= target < size:
                pairs.append((source * group + place, target * group + (place ^ 1 if back else place)))
    return lax.ppermute(value, ("tm", "head"), pairs)


class SumsOverTm:
    def __init__(self, run, a, b, rows=None):
        bits = [1 << i for i in range(lax.axis_size("tm").bit_length() - 1)]
        self.run, self.values, self.got = run, list(a), [list(v) for v in b]
        self.rows = [] if rows is None else [rows]
        self.apart = [(bits[1], bits[0]), (bits[0], bits[1])]
        self.together, self.last = bits[2:-1], bits[-1]
        self.todo = [("split", pair) for pair in self.apart]
        self.todo.append(("stack",))
        self.todo += [("split", (bit,)) for bit in self.together] + [("last",)] * bool(self.together)
        self.todo.append(("add",))
        self.todo += [("join", (bit,)) for bit in reversed(self.together)] + [("part",)] * bool(self.together)
        self.todo.append(("join", self.apart[1]))
        self.step()

    def step(self):
        run, values = self.run, self.values
        kind, *rest = self.todo.pop(0)
        features = values[0].shape[1]
        count = values[0].shape[0]
        more = sum(v.shape[0] for v in self.rows)
        has_rows = bool(self.rows)
        shape = lambda rows: (rows, features)
        got = [piece for pieces in self.got for piece in pieces]
        if kind == "split":
            (bits,) = rest
            half = count // 2
            extra = [more] + [0] * (len(bits) - 1)
            out = run.call(
                functools.partial(add_split_kernel, bits, [len(v) for v in self.got], has_rows), "add_split",
                [shape(half)] * len(bits) + [shape(half + e) for e in extra] + [v.shape for v in self.rows],
                (*values, *self.rows, *got), scratch=[shape(count)],
            )
            self.values, messages, self.rows = out[: len(bits)], out[len(bits) : 2 * len(bits)], out[2 * len(bits) :]
            self.got = [[swap(v, "tm", bit)] for v, bit in zip(messages, bits, strict=True)]
            return
        if kind in ("stack", "last"):
            if kind == "stack":
                (value,) = run.call(
                    functools.partial(stack_kernel, has_rows), "stack", [shape(2 * count + more)], (*values, *self.rows, *got)
                )
                count = 2 * count
            else:
                (value,) = run.call(
                    functools.partial(last_kernel, has_rows), "stack", [shape(count + more)], (*values, *self.rows, *got)
                )
            if kind == "stack" and self.together:
                self.values, self.rows = [value[:count]], [value[count:]] * has_rows
                self.values, self.got = self.values, [[]]
                return self.step()
            self.values, self.count = [value], count
            self.got = [[swap(value, "tm", self.last)]]
            return
        if kind == "add":
            parts = [self.count] if self.together else [self.count // 2] * 2
            out = run.call(
                add_whole_kernel, "add", [shape(n) for n in parts] + [v.shape for v in self.rows], (*values, *got)
            )
            self.values, self.rows = out[: len(parts)], out[len(parts) :]
        elif kind == "join":
            (bits,) = rest
            self.values = run.call(
                functools.partial(join_kernel, bits), "join", [shape(2 * count)] * len(bits), (*values, *got)
            )
        elif kind == "part":
            self.values = [values[0][: count // 2], values[0][count // 2 :]]
        following = self.todo[0] if self.todo else ("join", self.apart[0])
        if following[0] == "part":
            return self.step()
        self.got = [[swap(v, "tm", bit)] for v, bit in zip(self.values, following[1], strict=True)]

    @property
    def joined(self):
        return not self.todo

    def halves(self, number):
        return self.apart[0][number], (self.values[number], *self.got[number])


ORDER = (
    ("pack", 8), ("norm", 4.8), ("project", 2.2), ("attend_inner", 11), ("edges", 1), ("hand_on", 0.5),
    ("attend_outer0", 24), ("attend_outer1", 1), ("feed0", 18), ("feed1", 14), ("outer_weights", 6),
    ("inner_weights", 11), ("feed_out", 0.6), ("grad_sum0", 18), ("ffn", 11), ("back0", 6), ("grad_sum1", 18),
    ("back1", 0.5), ("ffn", 0.1), ("project_back", 1.8), ("project_weights", 2), ("ffn", 0.1), ("edge_add", 5),
    ("out_half", 5), ("out_send", 6), ("heads", 20), ("place_out", 1.3), ("heads", 0.1), ("ffn", 0.1), ("heads", 3),
    ("frames_back", 0.6), ("ffn", 20), ("place_frames", 0.1), ("heads", 0.1), ("heads", 0.1), ("join_outer", 0.1),
    ("join_inner", 0.1), ("finish", 1.3),
)
PIECES = 1


def copy_kernel(source, target):
    target[...] = source[...]


def hand_on_kernel(own, pair, far, here, far_copy):
    far_copy[...] = far[...]
    width = far.shape[0]
    for near, source in enumerate((own, pair)):
        for at in range(0, far.shape[1], width):
            lanes = slice(3 * width, 4 * width)
            here[lanes_of(near, width), at : at + width] = source[at : at + width, lanes]


class Layer:
    def __init__(
        self, frames, cotangent, seg_counts, query_weight, query_bias, key_weight, value_weight, value_bias,
        out_weight, out_bias, first_gain, first_shift, second_gain, second_shift,
        inner_weight, inner_bias, outer_weight, outer_bias,
    ):
        self.frames, self.cotangent, self.counts = frames, cotangent, seg_counts
        self.projections = (query_weight, key_weight, value_weight)
        self.weights = (inner_weight, outer_weight, out_weight)
        row = lambda v: v.reshape(1, v.shape[0])
        self.bq, self.bv, self.bo, self.bi, self.bu = map(row, (query_bias, value_bias, out_bias, inner_bias, outer_bias))
        self.g1, self.s1, self.g2, self.s2 = map(row, (first_gain, first_shift, second_gain, second_shift))
        micros, shard, features = frames.shape
        self.micros, self.features = micros, features
        self.width, self.hidden = query_weight.shape[1], inner_weight.shape[1]
        self.length = shard // 2
        self.segs, self.blocks, self.pairs = self.length // SEG, self.length // BLOCK, 2 * self.width // PAIR
        self.big = (self.length, features)
        self.each = (micros, self.length)
        self.quarter = (self.length // 2, features)
        self.square = (2 * BLOCK, KEYS)
        self.around = BEFORE + self.length + AHEAD
        self.key_scratch = [(self.around, 4 * self.width), (SUMS + self.segs + SUMS, 4 * self.width)]
        self.run = Steps()
        self.smem = pl.BlockSpec(memory_space=pltpu.SMEM)
        pairs = [None] * micros
        self.mix_outer, self.far_outer, self.p_outer, self.fed, self.dn2 = (list(pairs) for _ in range(5))
        self.back_of = list(pairs)
        self.sums = {}

    def pack(self):
        args = (*self.projections, self.weights[2], self.bq, self.bv, self.bi, self.frames)
        self.own, edge = self.run.call(
            pack_kernel, "pack", [(self.features + 8, 4 * self.width), (self.micros, BEFORE, self.features)], args,
            copies=6 + self.features // self.width + self.micros, far=range(8),
        )
        self.pair = swap(self.own, "head", 1)
        self.edge = swap_edges(edge, False)

    def norm(self):
        each, features, micros = self.each, self.features, self.micros
        wi, wu, wo = self.weights
        (self.x, self.xhat, self.rate, self.normed, self.wi, self.wu, self.wo, *self.g, self.before, self.ahead) = self.run.call(
            norm_kernel, "norm",
            [each + (features,)] * 2 + [each + (128,), each + (features,), wi.shape, wu.shape, wo.shape, self.big, self.big,
             (micros, BEFORE, features), (micros, AHEAD, features)],
            (self.frames, self.g1, self.s1, wi, wu, wo, self.cotangent),
            scratch=[(16, features)], copies=4 * micros + 5, far=range(7),
        )
        self.wo_far = swap(self.wo, "head", 2)
        self.wi_pair, self.wu_pair = (swap(v, "head", 1) for v in (self.wi, self.wu))

    def project(self):
        each, features, width = self.each, self.features, self.width
        args = (self.normed, self.own, self.pair, self.g1, self.s1, self.g2, self.s2, self.bo, self.bi, self.bu)
        self.q, self.kv, self.w_all, self.bias, self.params = self.run.call(
            project_kernel, "project",
            [each + (2 * width,), each + (4 * width,), (features, 6 * width), (1, 6 * width), (7, 1, features)],
            args, copies=7, far=range(3, 10),
        )

    def edges(self):
        shape = (self.micros, BEFORE + AHEAD)
        self.xhat_edge, self.normed_edge, self.kv_edge = self.run.call(
            edges_kernel, "edges", [shape + (self.features,)] * 2 + [shape + (4 * self.width,)],
            (self.edge, self.before, self.ahead, self.params, self.w_all, self.bias),
        )

    def attend_inner(self):
        *self.mix_inner, self.p_inner = self.run.call(
            attend_inner_kernel, "attend_inner",
            [(self.length - 2 * BLOCK, 2 * self.width)] * 2 + [(self.micros, self.blocks - 2, self.pairs) + self.square],
            (self.counts, self.q, self.kv), {0: self.smem}, self.key_scratch,
        )
        self.far_inner = [swap(v, "head", 2) for v in self.mix_inner]

    def attend_outer(self, m):
        if m:
            self.run.held.append(self.far_inner[0])
        self.mix_outer[m], self.p_outer[m] = self.run.call(
            functools.partial(attend_outer_kernel, m), "attend_outer",
            [(2 * BLOCK, 2 * self.width), (2, self.pairs) + self.square],
            (self.counts, self.q, self.kv, self.kv_edge),
            {0: self.smem}, self.key_scratch,
        )
        self.far_outer[m] = swap(self.mix_outer[m], "head", 2)

    def hand_on(self):
        shape = self.wo_far.shape
        self.wo_here, far = self.run.call(
            hand_on_kernel, "hand_on", [(2 * shape[0], shape[1]), shape], (self.own, self.pair, self.wo_far)
        )
        self.wo_far_pair = swap(far, "head", 1)

    def feed(self, m):
        big, features, hidden = self.big, self.features, self.hidden
        *self.fed[m], part = self.run.call(
            functools.partial(feed_kernel, m), "feed", [big, (self.length, 2 * hidden), (self.length, 2 * hidden), big, big],
            (self.mix_inner[m], self.mix_outer[m], self.far_inner[m], self.far_outer[m], self.wo_here, self.wo_far, self.wo_far_pair, self.x, self.g[m], self.params,
             self.pair, self.wi, self.wi_pair, self.wu, self.wu_pair),
            scratch=[big, (features, features)],
        )
        self.dn2[m] = (part, swap(part, "head", 2))

    def inner_weights(self):
        features, hidden = self.features, self.hidden
        self.inner_own, *pair, self.vec_inner = self.run.call(
            inner_weights_kernel, "inner_weights",
            [(features, hidden)] + [(features // PIECES, hidden)] * PIECES + [(2, hidden)],
            (self.fed[0][0], self.fed[1][0], self.fed[0][2], self.fed[1][2]),
        )
        self.inner_pair = swap_near(pair)

    def outer_weights(self):
        features, hidden = self.features, self.hidden
        self.outer_own, *pair, self.vec_outer = self.run.call(
            outer_weights_kernel, "outer_weights",
            [(hidden, features)] + [(hidden // PIECES, features)] * PIECES + [(1, features)],
            (self.fed[0][1], self.fed[1][1], *self.g),
        )
        self.outer_pair = swap_near(pair)

    def feed_out(self):
        (part,) = self.run.call(
            feed_out_kernel, "feed_out", [(self.micros * self.length, self.features)],
            (self.fed[0][1], self.fed[1][1], self.wu, self.wu_pair),
        )
        self.part = (part, swap(part, "head", 2))

    def out_half(self):
        (half,) = self.run.call(
            out_half_kernel, "out_half", [(self.micros * self.length, self.features)],
            (self.fed[0][3], self.fed[1][3], *self.part, self.params),
        )
        self.out = half

    def out_send(self):
        (half,) = self.run.call(copy_kernel, "out_send", [self.out.shape], (self.out,))
        self.out = (half, swap(half, "head", 1))

    def grad_sum(self, m):
        (self.dn2[m],) = self.run.call(add_whole_kernel, "grad_sum", [self.big], self.dn2[m])

    def back(self, m):
        length, width, features = self.length, self.width, self.features
        self.back_of[m] = self.run.call(
            functools.partial(back_kernel, m), "back",
            [self.big, (length, 2 * width), (self.around, 4 * width), (features, width), (features, width), (3, features)],
            (self.dn2[m], self.fed[m][3], self.g[m], self.params, self.wo_here, self.mix_inner[m], self.mix_outer[m], self.q, self.kv,
             self.kv_edge, self.p_inner, self.p_outer[m]),
            scratch=self.key_scratch + self.key_scratch[1:] + [(length, 2 * width)] * 2 + [(features, 2 * width)],
        )

    def pick(self, number):
        return [v[number] for v in self.back_of]

    def project_back(self):
        features, micros = self.features, self.micros
        (dq_0, dq_1), (dkv_0, dkv_1) = self.pick(1), self.pick(2)
        part, pair, beyond, self.vec_first = self.run.call(
            project_back_kernel, "project_back",
            [(micros * self.length, features)] + [(micros, BEFORE, features)] * 2 + [(2, features)],
            (dq_0, dkv_0, dq_1, dkv_1, self.xhat, self.xhat_edge, self.w_all), scratch=[(self.around, features)],
        )
        self.edges_back = (part, swap(pair, "head", 1), swap_edges(beyond, True))

    def edge_add(self):
        part = self.edges_back[0]
        (part,) = self.run.call(edge_add_kernel, "edge_add", [part.shape], self.edges_back)
        self.dn1 = (part, swap(part, "head", 2))

    def project_weights(self):
        features, width = self.features, self.width
        *self.heads_own, self.rows, a, b = self.run.call(
            project_weights_kernel, "project_weights",
            [(features // 2, 4 * width)] * 2 + [(8, features), (features // 2 + 8, 4 * width), (features // 2, 4 * width)],
            (self.normed, self.normed_edge, *self.pick(1), *self.pick(2), *self.pick(3), *self.pick(4), *self.pick(5),
             self.vec_first, self.vec_outer, self.vec_inner),
            scratch=[(features, 4 * width), (features, 6 * width), (1, 6 * width)],
        )
        self.heads_pair = swap_near((a, b))

    def begin(self, name):
        if name == "heads":
            a, b = self.heads_pair
            return SumsOverTm(self.run, self.heads_own, ((a,), (b,)), self.rows)
        return SumsOverTm(self.run, (self.outer_own, self.inner_own), (self.outer_pair, self.inner_pair))

    def sum(self, name):
        if name not in self.sums:
            self.sums[name] = self.begin(name)
        elif not self.sums[name].joined:
            self.sums[name].step()

    def ffn(self):
        self.sum("ffn")

    def heads(self):
        self.sum("heads")

    def frames_back(self):
        (half,) = self.run.call(
            frames_back_kernel, "frames_back", [(self.micros * self.length, self.features)],
            (*self.dn1, self.xhat, self.rate, *self.pick(0), self.params),
        )
        self.grad = (half, swap(half, "head", 1))

    def place(self, name, halves):
        (out,) = self.run.call(
            place_kernel, name, [(self.micros, 2 * self.length, self.features)], halves, copies=2 * self.micros, far_outs=[0]
        )
        return out

    def place_out(self):
        self.layer_output = self.place("place_out", self.out)

    def place_frames(self):
        self.frames_grad = self.place("place_frames", self.grad)

    def join(self, name, number, shape):
        bit, parts = self.sums["ffn"].halves(number)
        (out,) = self.run.call(
            functools.partial(join_out_kernel, bit), name, [shape], parts, copies=2, far_outs=[0]
        )
        return out

    def settle(self, *names):
        while not all(self.sums[name].joined for name in names):
            for name in names:
                self.sum(name)

    def join_outer(self):
        self.settle("ffn", "heads")
        self.outer_grad = self.join("join_outer", 0, self.weights[1].shape)

    def join_inner(self):
        self.inner_grad = self.join("join_inner", 1, self.weights[0].shape)

    def finish(self):
        features, width, hidden = self.features, self.width, self.hidden
        sums = self.sums["heads"]
        rows = sums.rows[0]
        bits, parts = zip(*(sums.halves(i) for i in range(2)), strict=True)
        out = self.run.call(
            functools.partial(finish_kernel, list(bits)), "finish",
            [(1, features)] * 6 + [(1, width)] * 2 + [(1, hidden)] + [(features, width)] * 3 + [(width, features)],
            (rows, swap(rows, "head", 2), *parts[0], *parts[1]),
        )
        bo, g2, s2, g1, s1, bu, bq, bv, bi = (v.reshape(v.shape[1]) for v in out[:9])
        wq, wk, wv, wo = out[9:]
        return (
            self.layer_output, self.frames_grad, wq, bq, wk, wv, bv, wo, bo, g1, s1, g2, s2, self.inner_grad, bi,
            self.outer_grad, bu,
        )


def per_device(*args):
    layer = Layer(*args)
    for step, us in ORDER:
        layer.run.us = us
        name = step.rstrip("0123456789")
        result = getattr(layer, name)(*(int(digit) for digit in step[len(name) :]))
    return result


def solution(mesh):
    in_specs = (
        P(None, "tm", None),
        P(None, "tm", None),
        P(),
        P(None, "head"),
        P("head"),
        P(None, "head"),
        P(None, "head"),
        P("head"),
        P("head", None),
        P(),
        P(),
        P(),
        P(),
        P(),
        P(None, "head"),
        P("head"),
        P("head", None),
        P(),
    )
    out_specs = (
        P(None, "tm", None),
        P(None, "tm", None),
        P(None, "head"),
        P("head"),
        P(None, "head"),
        P(None, "head"),
        P("head"),
        P("head", None),
        P(),
        P(),
        P(),
        P(),
        P(),
        P(None, "head"),
        P("head"),
        P("head", None),
        P(),
    )
    return jax.shard_map(
        per_device, mesh=mesh, in_specs=in_specs, out_specs=out_specs, check_vma=False
    )
```

```python
import functools

import jax
import jax.numpy as jnp
from jax import lax
from jax.experimental import pallas as pl
from jax.experimental.pallas import tpu as pltpu
from jax.sharding import PartitionSpec as P

HEAD_DIM = 64
SEG = 16
RC = 4
LC = 30
MEM = 4

EPSILON = 1e-05
MASKED = -1e30
F32 = jnp.float32

BEFORE = MEM * SEG
AHEAD = 8
CACHE = 32
SUMS = 8
BLOCK = 64
WIN = CACHE + BLOCK + AHEAD
SWIN = 16
KEYS = 128
FIRST_GAIN, FIRST_SHIFT, SECOND_GAIN, SECOND_SHIFT, OUT_BIAS, INNER_BIAS, OUTER_BIAS = range(7)
PAIR = 2 * HEAD_DIM
MIB = 1 << 20


def mm(left, right, left_dim=1, right_dim=0):
    return lax.dot_general(
        left,
        right,
        (((left_dim,), (right_dim,)), ((), ())),
        precision=lax.Precision.HIGH,
        preferred_element_type=F32,
    )


def normalise(values):
    centred = values - jnp.mean(values, axis=-1, keepdims=True)
    variance = jnp.mean(centred * centred, axis=-1, keepdims=True)
    rate = lax.rsqrt(variance + EPSILON)
    return centred * rate, rate


def norm_back(grad, gain, xhat, rate):
    scaled = grad * gain
    first = jnp.mean(scaled, axis=-1, keepdims=True)
    second = jnp.mean(scaled * xhat, axis=-1, keepdims=True)
    return rate * (scaled - first - xhat * second)


def column_sums(values):
    return jnp.sum(values, axis=0, keepdims=True)


def seg_means(values):
    rows, width = values.shape
    return jnp.sum(values.reshape(rows // SEG, SEG, width), axis=1) * (1.0 / SEG)


def near_bit():
    return lax.axis_index("head") % 2


def far_bit():
    return lax.axis_index("head") // 2


def my_rows(rows):
    half = rows // 2
    return pl.ds(pl.multiple_of(near_bit() * half, half), half)


def lanes_of(place, width, start=0):
    at = place + near_bit() - 2 * place * near_bit()
    return pl.ds(pl.multiple_of(start + at * width, width), width)


def half_rows(place, half):
    return pl.ds(pl.multiple_of(place * half, half), half)


def full(shape):
    return pl.BlockSpec(shape, lambda *_: (0,) * len(shape))


class Steps:
    def __init__(self):
        self.held = []
        self.us = 0.1

    def call(self, kernel, name, outs, args, specs=None, scratch=(), vmem=32, copies=0, far=(), far_outs=()):
        specs = dict(specs or {})
        given, made, held = len(args), len(outs), tuple(self.held)
        token = bool(far_outs)
        somewhere = pl.BlockSpec(memory_space=pl.ANY)
        in_hbm = pl.BlockSpec(memory_space=pltpu.HBM)

        def body(*refs):
            ins, rest = refs[:given], refs[given + len(held) :]
            if token:
                rest[made][...] = jnp.zeros(rest[made].shape, F32)
            kernel(*ins, *rest[:made], *rest[made + token :])

        args = [pltpu.with_memory_space_constraint(a, pltpu.HBM) if i in far else a for i, a in enumerate(args)]
        out_specs = [in_hbm if i in far_outs else full(shape) for i, shape in enumerate(outs)]
        out_shape = [
            pltpu.HBM(shape, F32) if i in far_outs else jax.ShapeDtypeStruct(shape, F32) for i, shape in enumerate(outs)
        ]
        if token:
            out_specs.append(full((1, 128)))
            out_shape.append(jax.ShapeDtypeStruct((1, 128), F32))
        out = pl.pallas_call(
            body,
            name=name,
            grid=(1,),
            in_specs=[in_hbm if i in far else specs.get(i, full(a.shape)) for i, a in enumerate(args)]
            + [somewhere] * len(held),
            out_specs=out_specs,
            out_shape=out_shape,
            scratch_shapes=[pltpu.VMEM(shape, F32) for shape in scratch]
            + ([pltpu.SemaphoreType.DMA((copies,))] if copies else []),
            compiler_params=pltpu.CompilerParams(vmem_limit_bytes=vmem * MIB),
            cost_estimate=pl.CostEstimate(flops=int(self.us * 5.18e8), bytes_accessed=0, transcendentals=0),
        )(*args, *held)
        self.held = [out[-1]]
        return out[:made]


def copy_all(pairs, sems):
    copies = [pltpu.make_async_copy(a, b, sems.at[i]) for i, (a, b) in enumerate(pairs)]
    for copy in copies:
        copy.start()
    return copies


def pack_kernel(wq, wk, wv, wo, bq, bv, bi, frames, out, edge, sems):
    rows, width = wq.shape
    out[rows:] = jnp.zeros((out.shape[0] - rows, out.shape[1]), F32)
    pairs = [(w, out.at[pl.ds(0, rows), pl.ds(i * width, width)]) for i, w in enumerate((wq, wk, wv))]
    for at in range(0, wo.shape[1], width):
        pairs.append((wo.at[:, pl.ds(at, width)], out.at[pl.ds(at, width), pl.ds(3 * width, width)]))
    pairs += [(b, out.at[pl.ds(rows, 1), pl.ds(i * width, width)]) for i, b in ((0, bq), (2, bv))]
    pairs.append((bi, out.at[pl.ds(rows + 1, 1), pl.ds(0, bi.shape[1])]))
    start = pl.multiple_of((1 - near_bit()) * (frames.shape[1] - BEFORE), BEFORE)
    pairs += [(frames.at[m, pl.ds(start, BEFORE)], edge.at[m]) for m in range(frames.shape[0])]
    for copy in copy_all(pairs, sems):
        copy.wait()


def norm_kernel(
    frames, gain, shift, wi, wu, wo, cotangent,
    x_ref, xhat_ref, rate_ref, normed_ref, wi_ref, wu_ref, wo_ref, g_0, g_1, before, ahead, params, sems,
):
    micros, half, _ = x_ref.shape
    rows = frames.shape[1]
    pairs = [(gain, params.at[pl.ds(0, 1)]), (shift, params.at[pl.ds(8, 1)])]
    pairs += [(frames.at[m, my_rows(rows)], x_ref.at[m]) for m in range(micros)]
    pairs += [(frames.at[m, pl.ds(half - BEFORE, BEFORE)], before.at[m]) for m in range(micros)]
    pairs += [(frames.at[m, pl.ds(half, AHEAD)], ahead.at[m]) for m in range(micros)]
    pairs += [(wo, wo_ref), (wi, wi_ref), (wu, wu_ref)]
    pairs += [(cotangent.at[m, my_rows(rows)], g) for m, g in enumerate((g_0, g_1))]
    copies = copy_all(pairs, sems)
    for copy in copies[:2]:
        copy.wait()
    for micro in range(micros):
        copies[2 + micro].wait()
        xhat, rate = normalise(x_ref[micro])
        xhat_ref[micro] = xhat
        normed_ref[micro] = xhat * params[0:1] + params[8:9]
        rate_ref[micro] = jnp.broadcast_to(rate, (half, rate_ref.shape[2]))
    for copy in copies[2 + micros :]:
        copy.wait()


def project_kernel(normed, own, pair, g1, s1, g2, s2, bo, bi, bu, q_ref, kv_ref, w_ref, bias, rows_ref, sems):
    micros, half, wide = q_ref.shape
    features = normed.shape[2]
    width = own.shape[1] // 4
    copies = copy_all([(v, rows_ref.at[i]) for i, v in enumerate((g1, s1, g2, s2, bo, bi, bu))], sems)
    for number in range(3):
        at = slice(number * width, (number + 1) * width)
        for place, source in enumerate((own, pair)):
            lanes = lanes_of(place, width, 2 * number * width)
            w_ref[:, lanes] = source[:features, at]
            bias[:, lanes] = source[features : features + 1, at]
    for micro in range(micros):
        out = mm(normed[micro], w_ref[...]) + bias[...]
        q_ref[micro] = out[:, :wide]
        kv_ref[micro] = out[:, wide:]
    for copy in copies:
        copy.wait()


def edges_kernel(edge, before, ahead, params, w_ref, bias, xhat_ref, normed_ref, kv_ref):
    near = near_bit()
    wide = w_ref.shape[1] // 3
    for micro in range(edge.shape[0]):
        first = jnp.where(near == 0, edge[micro], before[micro])
        last = jnp.where(near == 0, ahead[micro], edge[micro, :AHEAD])
        xhat, _ = normalise(jnp.concatenate([first, last], axis=0))
        normed = xhat * params[FIRST_GAIN] + params[FIRST_SHIFT]
        xhat_ref[micro] = xhat
        normed_ref[micro] = normed
        kv_ref[micro] = mm(normed, w_ref[:, wide:]) + bias[:, wide:]


def fill_keys(kv, edge, kx, sx):
    length = kv.shape[0]
    kx[BEFORE : BEFORE + length] = kv
    segs = length // SEG
    sx[SUMS : SUMS + segs] = seg_means(kv)
    if edge is not None:
        kx[:BEFORE] = edge[:BEFORE]
        kx[BEFORE + length :] = edge[BEFORE:]
        sx[: SUMS - MEM] = jnp.zeros((SUMS - MEM, kv.shape[1]), F32)
        sx[SUMS - MEM : SUMS] = seg_means(edge[:BEFORE])
        sx[SUMS + segs :] = jnp.zeros((sx.shape[0] - SUMS - segs, kv.shape[1]), F32)


def summary_start(block):
    return (block * (BLOCK // SEG) + SUMS - MEM) // SUMS * SUMS


def frame_rows(block):
    start = BEFORE - CACHE + block * BLOCK
    return slice(start, start + WIN)


def key_window(kx, sx, block, lanes):
    start = summary_start(block)
    rows = [kx[frame_rows(block), lanes], sx[start : start + SWIN, lanes]]
    return jnp.concatenate(rows + [jnp.zeros((KEYS - WIN - SWIN, PAIR), F32)], axis=0)


def by_head(values):
    first = lax.broadcasted_iota(jnp.int32, values.shape, 1) < HEAD_DIM
    return jnp.concatenate([jnp.where(first, values, 0.0), jnp.where(first, 0.0, values)], axis=0)


def side_by_side(values):
    rows = values.shape[0] // 2
    first = lax.broadcasted_iota(jnp.int32, (rows, values.shape[1]), 1) < HEAD_DIM
    return jnp.where(first, values[:rows], values[rows:])


def owner_of(segment, bounds):
    owner = jnp.where(segment < 0, -1, 0)
    for bound in bounds:
        owner = owner + (segment >= bound).astype(jnp.int32)
    return owner


def visible(block, base, bounds):
    row = lax.broadcasted_iota(jnp.int32, (2 * BLOCK, 1), 0) % BLOCK
    column = lax.broadcasted_iota(jnp.int32, (1, KEYS), 1)
    query_seg = block * (BLOCK // SEG) + row // SEG
    frame = block * BLOCK - CACHE + column
    is_frame = column < WIN
    summary = summary_start(block) - SUMS + column - WIN
    key_seg = jnp.where(is_frame, (frame + CACHE) // SEG - CACHE // SEG, summary)
    key_seg = jnp.where(column < WIN + SWIN, key_seg, -(1 << 20))
    inside = (frame >= query_seg * SEG - LC) & (frame < query_seg * SEG + SEG + RC)
    near = (key_seg >= query_seg - MEM) & (key_seg < query_seg)
    seen = (is_frame & inside) | ((column >= WIN) & near)
    return seen & (owner_of(key_seg + base, bounds) == owner_of(query_seg + base, bounds))


def bounds_of(counts, micro):
    bounds, total = [], 0
    for utterance in range(counts.shape[1]):
        total = total + counts[micro, utterance]
        bounds.append(total)
    return bounds


def first_segment(length):
    return (lax.axis_index("tm") * 2 + near_bit()) * (length // SEG)


def block_rows(block):
    return slice(block * BLOCK, (block + 1) * BLOCK)


def attend_block(block, seen, query, kx, sx, keep, put):
    width = query.shape[1]
    for pair in range(width // PAIR):
        lanes = slice(pair * PAIR, (pair + 1) * PAIR)
        value_lanes = slice(width + pair * PAIR, width + (pair + 1) * PAIR)
        scores = mm(by_head(query[:, lanes] * HEAD_DIM ** (-0.5)), key_window(kx, sx, block, lanes), 1, 1)
        scores = jnp.where(seen, scores, MASKED)
        weights = jnp.exp(scores - jnp.max(scores, axis=-1, keepdims=True))
        weights = weights / jnp.sum(weights, axis=-1, keepdims=True)
        keep(pair, weights)
        put(lanes, side_by_side(mm(weights, key_window(kx, sx, block, value_lanes))))


def attend_inner_kernel(counts, q_ref, kv_ref, mix_0, mix_1, p_ref, kx, sx):
    _, length, _ = q_ref.shape
    base = first_segment(length)
    for micro, mix_ref in enumerate((mix_0, mix_1)):
        fill_keys(kv_ref[micro], None, kx, sx)
        bounds = bounds_of(counts, micro)
        for number, block in enumerate(range(1, length // BLOCK - 1)):
            def keep(pair, weights):
                p_ref[micro, number, pair] = weights

            def put(lanes, values):
                mix_ref[block_rows(number), lanes] = values

            seen = visible(block, base, bounds)
            attend_block(block, seen, q_ref[micro, block_rows(block)], kx, sx, keep, put)


def attend_outer_kernel(micro, counts, q_ref, kv_ref, edge, mix_ref, p_ref, kx, sx):
    _, length, _ = q_ref.shape
    base = first_segment(length)
    fill_keys(kv_ref[micro], edge[micro], kx, sx)
    bounds = bounds_of(counts, micro)
    for number, block in enumerate((0, length // BLOCK - 1)):
        def keep(pair, weights):
            p_ref[number, pair] = weights

        def put(lanes, values):
            mix_ref[block_rows(number), lanes] = values

        seen = visible(block, base, bounds)
        attend_block(block, seen, q_ref[micro, block_rows(block)], kx, sx, keep, put)


def fill_rows(target, lanes, inner, outer):
    length = inner.shape[0] + outer.shape[0]
    target[:BLOCK, lanes] = outer[:BLOCK]
    target[BLOCK : length - BLOCK, lanes] = inner[...]
    target[length - BLOCK : length, lanes] = outer[BLOCK:]


def back_kernel(
    micro, grad_ref, mid_ref, g_ref, params, wo_here, mix_inner, mix_outer, q_ref, kv_ref, edge, p_inner, p_outer,
    dmid_ref, dq_ref, dkv_ref, dwo_own, dwo_pair, vec_ref,
    kx, sx, dsx, dmix, mix, dwo,
):
    _, length, width = q_ref.shape
    near_width = dwo_own.shape[1]
    grad = grad_ref[...]
    xhat, rate = normalise(mid_ref[...])
    dmid = g_ref[...] + norm_back(grad, params[SECOND_GAIN], xhat, rate)
    dmid_ref[...] = dmid
    vec_ref[0:1] = column_sums(dmid)
    vec_ref[1:2] = column_sums(grad * xhat)
    vec_ref[2:3] = column_sums(grad)
    dmix[...] = mm(dmid, wo_here[...], 1, 1)
    fill_rows(mix, slice(None), mix_inner, mix_outer)
    dwo[...] = mm(dmid, mix[...], 0, 0)
    dwo_own[...] = dwo[:, lanes_of(0, near_width)]
    dwo_pair[...] = dwo[:, lanes_of(1, near_width)]
    fill_keys(kv_ref[micro], edge[micro], kx, sx)
    dkv_ref[...] = jnp.zeros_like(dkv_ref)
    dsx[...] = jnp.zeros_like(dsx)
    for block in range(length // BLOCK):
        start = summary_start(block)
        rows, frames, sums = block_rows(block), frame_rows(block), slice(start, start + SWIN)
        for pair in range(width // PAIR):
            lanes = slice(pair * PAIR, (pair + 1) * PAIR)
            value_lanes = slice(width + pair * PAIR, width + (pair + 1) * PAIR)
            inside = 0 < block < length // BLOCK - 1
            weights = p_inner[micro, block - 1, pair] if inside else p_outer[min(block, 1), pair]
            grad = by_head(dmix[rows, lanes])
            dweights = mm(grad, key_window(kx, sx, block, value_lanes), 1, 1)
            dscores = weights * (dweights - jnp.sum(dweights * weights, axis=-1, keepdims=True))
            dquery = side_by_side(mm(dscores, key_window(kx, sx, block, lanes)))
            dq_ref[rows, lanes] = dquery * HEAD_DIM ** (-0.5)
            dkeys = mm(dscores, by_head(q_ref[micro, rows, lanes] * HEAD_DIM ** (-0.5)), 0, 0)
            dvalues = mm(weights, grad, 0, 0)
            dkv_ref[frames, lanes] += dkeys[:WIN]
            dkv_ref[frames, value_lanes] += dvalues[:WIN]
            dsx[sums, lanes] += dkeys[WIN : WIN + SWIN]
            dsx[sums, value_lanes] += dvalues[WIN : WIN + SWIN]
    count = BEFORE + length
    segs = count // SEG
    spread = dsx[SUMS - MEM : SUMS - MEM + segs] * (1.0 / SEG)
    spread = jnp.broadcast_to(spread[:, None, :], (segs, SEG, 2 * width))
    dkv_ref[:count] += spread.reshape(count, 2 * width)


def feed_kernel(
    micro, own_inner, own_outer, far_inner, far_outer, wo_here, wo_far, wo_far_pair, x_ref, g_ref, params, pair, wi_own, wi_pair, wu_own, wu_pair,
    n2_ref, h_ref, dpre_ref, mid_ref, part_ref,
    mix, wo,
):
    width = own_inner.shape[1] // 2
    features, hidden = wi_own.shape
    far = far_bit()
    here = pl.multiple_of(far * 2 * width, 2 * width)
    there = pl.multiple_of((1 - far) * 2 * width, 2 * width)
    fill_rows(mix, pl.ds(here, 2 * width), own_inner, own_outer)
    fill_rows(mix, pl.ds(there, 2 * width), far_inner, far_outer)
    wo[pl.ds(here, 2 * width)] = wo_here[...]
    wo[lanes_of(0, width, there)] = wo_far[...]
    wo[lanes_of(1, width, there)] = wo_far_pair[...]
    middle = x_ref[micro] + mm(mix[...], wo[...]) + params[OUT_BIAS]
    mid_ref[...] = middle
    xhat, _ = normalise(middle)
    normed = xhat * params[SECOND_GAIN] + params[SECOND_SHIFT]
    n2_ref[...] = normed
    part = None
    for place, (wi, wu, bias) in enumerate(((wi_own, wu_own, params[INNER_BIAS][:, :hidden]), (wi_pair, wu_pair, pair[features + 1 : features + 2, :hidden]))):
        at = slice(place * hidden, (place + 1) * hidden)
        pre = mm(normed, wi[...]) + bias
        phi = 0.5 + 0.5 * lax.erf(pre * (0.5**0.5))
        h_ref[:, at] = pre * phi
        slope = phi + pre * (jnp.exp(-0.5 * pre * pre) * 0.3989422804014327)
        dpre = mm(g_ref[...], wu[...], 1, 1) * slope
        dpre_ref[:, at] = dpre
        step = mm(dpre, wi[...], 1, 1)
        part = step if part is None else part + step
    part_ref[...] = part


def put_rows(value, outs):
    at = 0
    for out in outs:
        count = out.shape[0]
        out[...] = value[at : at + count]
        at += count


def inner_weights_kernel(n2_0, n2_1, d_0, d_1, own_ref, *rest):
    *pair, vec_ref = rest
    hidden = own_ref.shape[1]
    for place, outs in enumerate(((own_ref,), pair)):
        at = slice(place * hidden, (place + 1) * hidden)
        put_rows(mm(n2_0[...], d_0[:, at], 0, 0) + mm(n2_1[...], d_1[:, at], 0, 0), outs)
        vec_ref[place : place + 1] = column_sums(d_0[:, at]) + column_sums(d_1[:, at])


def outer_weights_kernel(h_0, h_1, g_0, g_1, own_ref, *rest):
    *pair, vec_ref = rest
    hidden = own_ref.shape[0]
    for place, outs in enumerate(((own_ref,), pair)):
        at = slice(place * hidden, (place + 1) * hidden)
        put_rows(mm(h_0[:, at], g_0[...], 0, 0) + mm(h_1[:, at], g_1[...], 0, 0), outs)
    vec_ref[...] = column_sums(g_0[...]) + column_sums(g_1[...])


def feed_out_kernel(h_0, h_1, wu_own, wu_pair, out_ref):
    hidden = wu_own.shape[0]
    rows = h_0.shape[0]
    for micro, h_ref in enumerate((h_0, h_1)):
        part = mm(h_ref[:, :hidden], wu_own[...]) + mm(h_ref[:, hidden:], wu_pair[...])
        out_ref[micro * rows : (micro + 1) * rows] = part


def out_half_kernel(mid_0, mid_1, part, far, params, out):
    rows = mid_0.shape[0]
    for micro, mid_ref in enumerate((mid_0, mid_1)):
        at = slice(micro * rows, (micro + 1) * rows)
        out[at] = mid_ref[...] + (part[at] + far[at]) + params[OUTER_BIAS]


def project_back_kernel(
    dq_0, dkv_0, dq_1, dkv_1, xhat, xhat_edge, w_ref, part_ref, pair_ref, beyond_ref, vec_ref, work
):
    near = near_bit()
    length, wide = dq_0.shape
    own = slice(BEFORE, BEFORE + length)
    gain, shift = 0.0, 0.0
    for micro, (dq, dkv) in enumerate(((dq_0, dkv_0), (dq_1, dkv_1))):
        work[...] = mm(dkv[...], w_ref[:, wide:], 1, 1)
        work[own] += mm(dq[...], w_ref[:, :wide], 1, 1)
        part_ref[micro * length : (micro + 1) * length] = work[own]
        before = work[:BEFORE]
        ahead = jnp.concatenate([work[BEFORE + length :], jnp.zeros((BEFORE - AHEAD, work.shape[1]), F32)], axis=0)
        pair_ref[micro] = jnp.where(near == 0, ahead, before)
        beyond_ref[micro] = jnp.where(near == 0, before, ahead)
        gain = gain + column_sums(work[own] * xhat[micro]) + column_sums(work[:BEFORE] * xhat_edge[micro, :BEFORE])
        gain = gain + column_sums(work[BEFORE + length :] * xhat_edge[micro, BEFORE:])
        shift = shift + column_sums(work[...])
    vec_ref[0:1] = gain
    vec_ref[1:2] = shift


def edge_add_kernel(part, pair, beyond, out):
    out[...] = part[...]
    near = near_bit()
    micros = pair.shape[0]
    length = part.shape[0] // micros
    for micro in range(micros):
        end = (micro + 1) * length
        out[end - BEFORE : end] += jnp.where(near == 0, pair[micro], beyond[micro])
        out[end - length : end - length + AHEAD] += jnp.where(near == 0, beyond[micro, :AHEAD], pair[micro, :AHEAD])


def project_weights_kernel(
    normed, normed_edge, dq_0, dq_1, dkv_0, dkv_1, wo_own_0, wo_own_1, wo_pair_0, wo_pair_1, mid_0, mid_1, first, vec_outer, vec_inner,
    own_0, own_1, rows_ref, pair_0, pair_1, message, sums, row,
):
    features = normed.shape[2]
    width = wo_own_0.shape[1]
    hidden = vec_inner.shape[1]
    length, wide = dq_0.shape
    own, after = slice(BEFORE, BEFORE + length), slice(BEFORE + length, None)
    edges = jnp.concatenate([dkv_0[:BEFORE], dkv_0[after], dkv_1[:BEFORE], dkv_1[after]], axis=0)
    normed_edges = jnp.concatenate([normed_edge[0], normed_edge[1]], axis=0)
    queries = mm(normed[0], dq_0[...], 0, 0) + mm(normed[1], dq_1[...], 0, 0)
    keyvals = mm(normed[0], dkv_0[own], 0, 0) + mm(normed[1], dkv_1[own], 0, 0) + mm(normed_edges, edges, 0, 0)
    sums[:, :wide] = queries
    sums[:, wide:] = keyvals
    row[:, :wide] = column_sums(dq_0[...]) + column_sums(dq_1[...])
    row[:, wide:] = column_sums(dkv_0[...]) + column_sums(dkv_1[...])
    rows_ref[0:3] = (mid_0[...] + mid_1[...]) * 0.5
    rows_ref[3:5] = first[...]
    rows_ref[5:6] = vec_outer[...] * 0.5
    rows_ref[6:] = jnp.zeros((2, features), F32)
    half = own_0.shape[0]
    pair_0[half : half + 6] = rows_ref[0:6]
    pair_0[half + 6 :] = jnp.zeros((2, features), F32)
    for place, (out_ref, at) in enumerate(((rows_ref, 6), (pair_0, half + 6))):
        for number in range(3):
            lanes = slice(number * width, (number + 1) * width)
            out_ref[at : at + 1, lanes] = row[:, lanes_of(place, width, 2 * number * width)]
        out_ref[at + 1 : at + 2, :hidden] = vec_inner[place : place + 1]
    for place, (outs, wo_0, wo_1) in enumerate((((own_0, own_1), wo_own_0, wo_own_1), ((pair_0, pair_1), wo_pair_0, wo_pair_1))):
        for number in range(3):
            lanes = slice(number * width, (number + 1) * width)
            message[:, lanes] = sums[:, lanes_of(place, width, 2 * number * width)]
        message[:, 3 * width :] = wo_0[...] + wo_1[...]
        for number, out_ref in enumerate(outs):
            out_ref[:half] = message[number * half : (number + 1) * half]


def frames_back_kernel(a_ref, b_ref, xhat, rate, dmid_0, dmid_1, params, out):
    rows = dmid_0.shape[0]
    for micro, dmid_ref in enumerate((dmid_0, dmid_1)):
        at = slice(micro * rows, (micro + 1) * rows)
        grad = norm_back(a_ref[at] + b_ref[at], params[FIRST_GAIN], xhat[micro], rate[micro, :, :1])
        out[at] = dmid_ref[...] + grad


def place_kernel(own, pair, out, sems):
    micros, half = out.shape[0], out.shape[1] // 2
    near = near_bit()
    pairs = []
    for micro in range(micros):
        rows = pl.ds(micro * half, half)
        pairs.append((own.at[rows], out.at[micro, half_rows(near, half)]))
        pairs.append((pair.at[rows], out.at[micro, half_rows(1 - near, half)]))
    for copy in copy_all(pairs, sems):
        copy.wait()


def place_of(bit):
    return lax.axis_index("tm") // bit % 2


def add_pieces(out, a_ref, pieces, rows_ref=None, new_rows=None):
    count, at = a_ref.shape[0], 0
    if not pieces:
        out[...] = a_ref[...]
        if new_rows is not None:
            new_rows[...] = rows_ref[...]
    for piece in pieces:
        take = min(piece.shape[0], count - at)
        if take:
            out[at : at + take] = a_ref[at : at + take] + piece[:take]
        if take < piece.shape[0]:
            new_rows[...] = rows_ref[...] + piece[take:]
        at += take


def add_split_kernel(bits, counts, rows, *refs):
    total = len(bits)
    values, refs = refs[:total], refs[total:]
    rows_ref, refs = (refs[0], refs[1:]) if rows else (None, refs)
    pieces = []
    for count in counts:
        pieces.append(refs[:count])
        refs = refs[count:]
    kept, sent, refs = refs[:total], refs[total : 2 * total], refs[2 * total :]
    new_rows, work = (refs[0], refs[1]) if rows else (None, refs[0])
    for number, bit in enumerate(bits):
        small = (rows_ref, new_rows) if rows and number == 0 else ()
        half = kept[number].shape[0]
        add_pieces(work, values[number], pieces[number], *small)
        place = place_of(bit)
        kept[number][...] = work[half_rows(place, half)]
        sent[number][:half] = work[half_rows(1 - place, half)]
        if small:
            sent[number][half:] = new_rows[...]


def last_kernel(rows, a_ref, *refs):
    rows_ref, refs = (refs[0], refs[1:]) if rows else (None, refs)
    b_ref, out_ref = refs
    half = a_ref.shape[0]
    out_ref[:half] = a_ref[...] + b_ref[:half]
    if rows:
        out_ref[half:] = rows_ref[...] + b_ref[half:]


def stack_kernel(rows, a_0, a_1, *refs):
    rows_ref, refs = (refs[0], refs[1:]) if rows else (None, refs)
    b_0, b_1, out_ref = refs
    half = a_0.shape[0]
    out_ref[:half] = a_0[...] + b_0[:half]
    out_ref[half : 2 * half] = a_1[...] + b_1[...]
    if rows:
        out_ref[2 * half :] = rows_ref[...] + b_0[half:]


def add_whole_kernel(a_ref, b_ref, *outs):
    at = 0
    for out in outs:
        count = out.shape[0]
        out[...] = a_ref[at : at + count] + b_ref[at : at + count]
        at += count


def join_kernel(bits, *refs):
    total = len(bits)
    for bit, mine, theirs, out in zip(bits, refs[:total], refs[total : 2 * total], refs[2 * total :], strict=True):
        half = mine.shape[0]
        place = place_of(bit)
        out[half_rows(place, half)] = mine[...]
        out[half_rows(1 - place, half)] = theirs[...]


def join_out_kernel(bit, mine, theirs, out, sems):
    half = mine.shape[0]
    place = place_of(bit)
    for copy in copy_all([(mine, out.at[half_rows(place, half)]), (theirs, out.at[half_rows(1 - place, half)])], sems):
        copy.wait()


def join_heads_kernel(bits, *refs):
    *parts, wq, wk, wv, wo = refs
    width = wq.shape[1]
    at = 0
    for number, bit in enumerate(bits):
        mine, theirs = parts[2 * number : 2 * number + 2]
        half = mine.shape[0]
        place = place_of(bit)
        for where, part in ((place, mine), (1 - place, theirs)):
            rows = pl.ds(pl.multiple_of(at + where * half, half), half)
            for heads, out in enumerate((wq, wk, wv)):
                out[rows, :] = part[:, heads * width : (heads + 1) * width]
            wo[:, rows] = part[:, 3 * width :].T
        at += 2 * half


def small_kernel(rows, far, outs):
    width = outs[-3].shape[1]
    for number, out in enumerate(outs[:6]):
        out[...] = rows[number : number + 1] + far[number : number + 1]
    outs[6][...] = rows[6:7, :width]
    outs[7][...] = rows[6:7, 2 * width : 3 * width]
    outs[8][...] = rows[7:8, : outs[8].shape[1]]


def finish_kernel(bits, rows, far, *refs):
    count = 2 * len(bits)
    small_kernel(rows, far, refs[count : count + 9])
    join_heads_kernel(bits, *refs[:count], *refs[count + 9 :])


def swap(value, axis, bit):
    size = lax.axis_size(axis)
    return lax.ppermute(value, axis, [(i, i ^ bit) for i in range(size)])


def swap_near(parts):
    return [swap(part, "head", 1) for part in parts]


def swap_edges(value, back):
    size, group = lax.axis_size("tm"), lax.axis_size("head")
    pairs = []
    for source in range(size):
        for place in range(group):
            target = source + (1 - 2 * (place % 2)) * (-1 if back else 1)
            if 0 <= target < size:
                pairs.append((source * group + place, target * group + (place ^ 1 if back else place)))
    return lax.ppermute(value, ("tm", "head"), pairs)


class SumsOverTm:
    def __init__(self, run, a, b, rows=None):
        bits = [1 << i for i in range(lax.axis_size("tm").bit_length() - 1)]
        self.run, self.values, self.got, self.ones = run, list(a), [list(v) for v in b], []
        self.rows = [] if rows is None else [rows]
        self.apart = [(bits[1], bits[0]), (bits[0], bits[1])]
        self.together, self.last = bits[2:-1], bits[-1]
        self.todo = [("split", pair) for pair in self.apart]
        self.todo.append(("stack",))
        self.todo += [("split", (bit,)) for bit in self.together] + [("last",)] * bool(self.together)
        self.todo.append(("add",))
        self.todo += [("join", (bit,)) for bit in reversed(self.together)] + [("part",)] * bool(self.together)
        self.todo.append(("join", self.apart[1]))
        self.step()

    def step(self):
        run, values = self.run, self.values
        kind, *rest = self.todo.pop(0)
        features = values[0].shape[1]
        count = values[0].shape[0]
        more = sum(v.shape[0] for v in self.rows)
        has_rows = bool(self.rows)
        shape = lambda rows: (rows, features)
        got = [piece for pieces in self.got for piece in pieces]
        if kind == "split":
            (bits,) = rest
            half = count // 2
            extra = [more] + [0] * (len(bits) - 1)
            out = run.call(
                functools.partial(add_split_kernel, bits, [len(v) for v in self.got], has_rows), "add_split",
                [shape(half)] * len(bits) + [shape(half + e) for e in extra] + [v.shape for v in self.rows],
                (*values, *self.rows, *got), scratch=[shape(count)],
            )
            self.values, messages, self.rows = out[: len(bits)], out[len(bits) : 2 * len(bits)], out[2 * len(bits) :]
            self.got = [[swap(v, "tm", bit)] for v, bit in zip(messages, bits, strict=True)]
            return
        if kind in ("stack", "last"):
            if kind == "stack":
                (value,) = run.call(
                    functools.partial(stack_kernel, has_rows), "stack", [shape(2 * count + more)], (*values, *self.rows, *got)
                )
                count = 2 * count
            else:
                (value,) = run.call(
                    functools.partial(last_kernel, has_rows), "stack", [shape(count + more)], (*values, *self.rows, *got)
                )
            if kind == "stack" and self.together:
                self.values, self.rows = [value[:count]], [value[count:]] * has_rows
                self.values, self.got = self.values, [[]]
                return self.step()
            self.values, self.count = [value], count
            self.got = [[swap(value, "tm", self.last)]]
            return
        if kind == "add":
            parts = [self.count] if self.together else [self.count // 2] * 2
            out = run.call(
                add_whole_kernel, "add", [shape(n) for n in parts] + [v.shape for v in self.rows], (*values, *got)
            )
            self.values, self.rows = out[: len(parts)], out[len(parts) :]
        elif kind == "join":
            (bits,) = rest
            self.values = run.call(
                functools.partial(join_kernel, bits), "join", [shape(2 * count)] * len(bits), (*values, *got)
            )
        elif kind == "part":
            self.values = [values[0][: count // 2], values[0][count // 2 :]]
        following = self.todo[0] if self.todo else ("join", self.apart[0])
        if following[0] == "part":
            return self.step()
        self.got = [[swap(v, "tm", bit)] for v, bit in zip(self.values, following[1], strict=True)]

    def join_one(self, number):
        if len(self.todo) != 1:
            return
        bits = self.todo[0][1]
        value = self.values[number]
        values, got = list(self.values), list(self.got)
        (values[number],) = self.run.call(
            functools.partial(join_kernel, bits[number : number + 1]), "join", [(2 * value.shape[0], value.shape[1])],
            (value, *got[number]),
        )
        got[number] = [swap(values[number], "tm", self.apart[0][number])]
        self.values, self.got = values, got
        self.ones.append(number)
        if len(self.ones) == 2:
            self.todo.pop()

    @property
    def joined(self):
        return not self.todo

    def halves(self, number):
        return self.apart[0][number], (self.values[number], *self.got[number])


ORDER = (
    ("pack", 8), ("norm", 4.8), ("project", 2.2), ("attend_inner", 11), ("edges", 1), ("hand_on", 0.5),
    ("attend_outer0", 24), ("attend_outer1", 1), ("feed0", 18), ("feed1", 14), ("outer_weights", 6),
    ("inner_weights", 11), ("feed_out", 0.6), ("grad_sum0", 18), ("ffn", 11), ("back0", 6), ("grad_sum1", 18),
    ("back1", 0.5), ("ffn", 0.1), ("project_back", 1.8), ("project_weights", 2), ("ffn", 0.1), ("edge_add", 5),
    ("out_half", 5), ("out_send", 6), ("heads", 20), ("place_out", 1.3), ("heads", 0.1), ("ffn", 0.1), ("heads", 3),
    ("frames_back", 0.6), ("ffn_last0", 0.1), ("ffn_last1", 20), ("place_frames", 0.1), ("heads", 0.1),
    ("heads", 0.1), ("join_outer", 0.1), ("join_inner", 0.1), ("finish", 1.3),
)
PIECES = 1


def copy_kernel(source, target):
    target[...] = source[...]


def hand_on_kernel(own, pair, far, here, far_copy):
    far_copy[...] = far[...]
    width = far.shape[0]
    for near, source in enumerate((own, pair)):
        for at in range(0, far.shape[1], width):
            lanes = slice(3 * width, 4 * width)
            here[lanes_of(near, width), at : at + width] = source[at : at + width, lanes]


class Layer:
    def __init__(
        self, frames, cotangent, seg_counts, query_weight, query_bias, key_weight, value_weight, value_bias,
        out_weight, out_bias, first_gain, first_shift, second_gain, second_shift,
        inner_weight, inner_bias, outer_weight, outer_bias,
    ):
        self.frames, self.cotangent, self.counts = frames, cotangent, seg_counts
        self.projections = (query_weight, key_weight, value_weight)
        self.weights = (inner_weight, outer_weight, out_weight)
        row = lambda v: v.reshape(1, v.shape[0])
        self.bq, self.bv, self.bo, self.bi, self.bu = map(row, (query_bias, value_bias, out_bias, inner_bias, outer_bias))
        self.g1, self.s1, self.g2, self.s2 = map(row, (first_gain, first_shift, second_gain, second_shift))
        micros, shard, features = frames.shape
        self.micros, self.features = micros, features
        self.width, self.hidden = query_weight.shape[1], inner_weight.shape[1]
        self.length = shard // 2
        self.segs, self.blocks, self.pairs = self.length // SEG, self.length // BLOCK, 2 * self.width // PAIR
        self.big = (self.length, features)
        self.each = (micros, self.length)
        self.quarter = (self.length // 2, features)
        self.square = (2 * BLOCK, KEYS)
        self.around = BEFORE + self.length + AHEAD
        self.key_scratch = [(self.around, 4 * self.width), (SUMS + self.segs + SUMS, 4 * self.width)]
        self.run = Steps()
        self.smem = pl.BlockSpec(memory_space=pltpu.SMEM)
        pairs = [None] * micros
        self.mix_outer, self.far_outer, self.p_outer, self.fed, self.dn2 = (list(pairs) for _ in range(5))
        self.back_of = list(pairs)
        self.sums = {}

    def pack(self):
        args = (*self.projections, self.weights[2], self.bq, self.bv, self.bi, self.frames)
        self.own, edge = self.run.call(
            pack_kernel, "pack", [(self.features + 8, 4 * self.width), (self.micros, BEFORE, self.features)], args,
            copies=6 + self.features // self.width + self.micros, far=range(8),
        )
        self.pair = swap(self.own, "head", 1)
        self.edge = swap_edges(edge, False)

    def norm(self):
        each, features, micros = self.each, self.features, self.micros
        wi, wu, wo = self.weights
        (self.x, self.xhat, self.rate, self.normed, self.wi, self.wu, self.wo, *self.g, self.before, self.ahead) = self.run.call(
            norm_kernel, "norm",
            [each + (features,)] * 2 + [each + (128,), each + (features,), wi.shape, wu.shape, wo.shape, self.big, self.big,
             (micros, BEFORE, features), (micros, AHEAD, features)],
            (self.frames, self.g1, self.s1, wi, wu, wo, self.cotangent),
            scratch=[(16, features)], copies=4 * micros + 5, far=range(7),
        )
        self.wo_far = swap(self.wo, "head", 2)
        self.wi_pair, self.wu_pair = (swap(v, "head", 1) for v in (self.wi, self.wu))

    def project(self):
        each, features, width = self.each, self.features, self.width
        args = (self.normed, self.own, self.pair, self.g1, self.s1, self.g2, self.s2, self.bo, self.bi, self.bu)
        self.q, self.kv, self.w_all, self.bias, self.params = self.run.call(
            project_kernel, "project",
            [each + (2 * width,), each + (4 * width,), (features, 6 * width), (1, 6 * width), (7, 1, features)],
            args, copies=7, far=range(3, 10),
        )

    def edges(self):
        shape = (self.micros, BEFORE + AHEAD)
        self.xhat_edge, self.normed_edge, self.kv_edge = self.run.call(
            edges_kernel, "edges", [shape + (self.features,)] * 2 + [shape + (4 * self.width,)],
            (self.edge, self.before, self.ahead, self.params, self.w_all, self.bias),
        )

    def attend_inner(self):
        *self.mix_inner, self.p_inner = self.run.call(
            attend_inner_kernel, "attend_inner",
            [(self.length - 2 * BLOCK, 2 * self.width)] * 2 + [(self.micros, self.blocks - 2, self.pairs) + self.square],
            (self.counts, self.q, self.kv), {0: self.smem}, self.key_scratch,
        )
        self.far_inner = [swap(v, "head", 2) for v in self.mix_inner]

    def attend_outer(self, m):
        if m:
            self.run.held.append(self.far_inner[0])
        self.mix_outer[m], self.p_outer[m] = self.run.call(
            functools.partial(attend_outer_kernel, m), "attend_outer",
            [(2 * BLOCK, 2 * self.width), (2, self.pairs) + self.square],
            (self.counts, self.q, self.kv, self.kv_edge),
            {0: self.smem}, self.key_scratch,
        )
        self.far_outer[m] = swap(self.mix_outer[m], "head", 2)

    def hand_on(self):
        shape = self.wo_far.shape
        self.wo_here, far = self.run.call(
            hand_on_kernel, "hand_on", [(2 * shape[0], shape[1]), shape], (self.own, self.pair, self.wo_far)
        )
        self.wo_far_pair = swap(far, "head", 1)

    def feed(self, m):
        big, features, hidden = self.big, self.features, self.hidden
        *self.fed[m], part = self.run.call(
            functools.partial(feed_kernel, m), "feed", [big, (self.length, 2 * hidden), (self.length, 2 * hidden), big, big],
            (self.mix_inner[m], self.mix_outer[m], self.far_inner[m], self.far_outer[m], self.wo_here, self.wo_far, self.wo_far_pair, self.x, self.g[m], self.params,
             self.pair, self.wi, self.wi_pair, self.wu, self.wu_pair),
            scratch=[big, (features, features)],
        )
        self.dn2[m] = (part, swap(part, "head", 2))

    def inner_weights(self):
        features, hidden = self.features, self.hidden
        self.inner_own, *pair, self.vec_inner = self.run.call(
            inner_weights_kernel, "inner_weights",
            [(features, hidden)] + [(features // PIECES, hidden)] * PIECES + [(2, hidden)],
            (self.fed[0][0], self.fed[1][0], self.fed[0][2], self.fed[1][2]),
        )
        self.inner_pair = swap_near(pair)

    def outer_weights(self):
        features, hidden = self.features, self.hidden
        self.outer_own, *pair, self.vec_outer = self.run.call(
            outer_weights_kernel, "outer_weights",
            [(hidden, features)] + [(hidden // PIECES, features)] * PIECES + [(1, features)],
            (self.fed[0][1], self.fed[1][1], *self.g),
        )
        self.outer_pair = swap_near(pair)

    def feed_out(self):
        (part,) = self.run.call(
            feed_out_kernel, "feed_out", [(self.micros * self.length, self.features)],
            (self.fed[0][1], self.fed[1][1], self.wu, self.wu_pair),
        )
        self.part = (part, swap(part, "head", 2))

    def out_half(self):
        (half,) = self.run.call(
            out_half_kernel, "out_half", [(self.micros * self.length, self.features)],
            (self.fed[0][3], self.fed[1][3], *self.part, self.params),
        )
        self.out = half

    def out_send(self):
        (half,) = self.run.call(copy_kernel, "out_send", [self.out.shape], (self.out,))
        self.out = (half, swap(half, "head", 1))

    def grad_sum(self, m):
        (self.dn2[m],) = self.run.call(add_whole_kernel, "grad_sum", [self.big], self.dn2[m])

    def back(self, m):
        length, width, features = self.length, self.width, self.features
        self.back_of[m] = self.run.call(
            functools.partial(back_kernel, m), "back",
            [self.big, (length, 2 * width), (self.around, 4 * width), (features, width), (features, width), (3, features)],
            (self.dn2[m], self.fed[m][3], self.g[m], self.params, self.wo_here, self.mix_inner[m], self.mix_outer[m], self.q, self.kv,
             self.kv_edge, self.p_inner, self.p_outer[m]),
            scratch=self.key_scratch + self.key_scratch[1:] + [(length, 2 * width)] * 2 + [(features, 2 * width)],
        )

    def pick(self, number):
        return [v[number] for v in self.back_of]

    def project_back(self):
        features, micros = self.features, self.micros
        (dq_0, dq_1), (dkv_0, dkv_1) = self.pick(1), self.pick(2)
        part, pair, beyond, self.vec_first = self.run.call(
            project_back_kernel, "project_back",
            [(micros * self.length, features)] + [(micros, BEFORE, features)] * 2 + [(2, features)],
            (dq_0, dkv_0, dq_1, dkv_1, self.xhat, self.xhat_edge, self.w_all), scratch=[(self.around, features)],
        )
        self.edges_back = (part, swap(pair, "head", 1), swap_edges(beyond, True))

    def edge_add(self):
        part = self.edges_back[0]
        (part,) = self.run.call(edge_add_kernel, "edge_add", [part.shape], self.edges_back)
        self.dn1 = (part, swap(part, "head", 2))

    def project_weights(self):
        features, width = self.features, self.width
        *self.heads_own, self.rows, a, b = self.run.call(
            project_weights_kernel, "project_weights",
            [(features // 2, 4 * width)] * 2 + [(8, features), (features // 2 + 8, 4 * width), (features // 2, 4 * width)],
            (self.normed, self.normed_edge, *self.pick(1), *self.pick(2), *self.pick(3), *self.pick(4), *self.pick(5),
             self.vec_first, self.vec_outer, self.vec_inner),
            scratch=[(features, 4 * width), (features, 6 * width), (1, 6 * width)],
        )
        self.heads_pair = swap_near((a, b))

    def begin(self, name):
        if name == "heads":
            a, b = self.heads_pair
            return SumsOverTm(self.run, self.heads_own, ((a,), (b,)), self.rows)
        return SumsOverTm(self.run, (self.outer_own, self.inner_own), (self.outer_pair, self.inner_pair))

    def sum(self, name):
        if name not in self.sums:
            self.sums[name] = self.begin(name)
        elif not self.sums[name].joined:
            self.sums[name].step()

    def ffn(self):
        self.sum("ffn")

    def heads(self):
        self.sum("heads")

    def ffn_last(self, number):
        self.sums["ffn"].join_one(number)

    def heads_last(self, number):
        self.sums["heads"].join_one(number)

    def frames_back(self):
        (half,) = self.run.call(
            frames_back_kernel, "frames_back", [(self.micros * self.length, self.features)],
            (*self.dn1, self.xhat, self.rate, *self.pick(0), self.params),
        )
        self.grad = (half, swap(half, "head", 1))

    def place(self, name, halves):
        (out,) = self.run.call(
            place_kernel, name, [(self.micros, 2 * self.length, self.features)], halves, copies=2 * self.micros, far_outs=[0]
        )
        return out

    def place_out(self):
        self.layer_output = self.place("place_out", self.out)

    def place_frames(self):
        self.frames_grad = self.place("place_frames", self.grad)

    def join(self, name, number, shape):
        bit, parts = self.sums["ffn"].halves(number)
        (out,) = self.run.call(
            functools.partial(join_out_kernel, bit), name, [shape], parts, copies=2, far_outs=[0]
        )
        return out

    def settle(self, *names):
        while not all(self.sums[name].joined for name in names):
            for name in names:
                self.sum(name)

    def join_outer(self):
        self.settle("ffn", "heads")
        self.outer_grad = self.join("join_outer", 0, self.weights[1].shape)

    def join_inner(self):
        self.inner_grad = self.join("join_inner", 1, self.weights[0].shape)

    def finish(self):
        features, width, hidden = self.features, self.width, self.hidden
        sums = self.sums["heads"]
        rows = sums.rows[0]
        bits, parts = zip(*(sums.halves(i) for i in range(2)), strict=True)
        out = self.run.call(
            functools.partial(finish_kernel, list(bits)), "finish",
            [(1, features)] * 6 + [(1, width)] * 2 + [(1, hidden)] + [(features, width)] * 3 + [(width, features)],
            (rows, swap(rows, "head", 2), *parts[0], *parts[1]),
        )
        bo, g2, s2, g1, s1, bu, bq, bv, bi = (v.reshape(v.shape[1]) for v in out[:9])
        wq, wk, wv, wo = out[9:]
        return (
            self.layer_output, self.frames_grad, wq, bq, wk, wv, bv, wo, bo, g1, s1, g2, s2, self.inner_grad, bi,
            self.outer_grad, bu,
        )


def per_device(*args):
    layer = Layer(*args)
    for step, us in ORDER:
        layer.run.us = us
        name = step.rstrip("0123456789")
        result = getattr(layer, name)(*(int(digit) for digit in step[len(name) :]))
    return result


def solution(mesh):
    in_specs = (
        P(None, "tm", None),
        P(None, "tm", None),
        P(),
        P(None, "head"),
        P("head"),
        P(None, "head"),
        P(None, "head"),
        P("head"),
        P("head", None),
        P(),
        P(),
        P(),
        P(),
        P(),
        P(None, "head"),
        P("head"),
        P("head", None),
        P(),
    )
    out_specs = (
        P(None, "tm", None),
        P(None, "tm", None),
        P(None, "head"),
        P("head"),
        P(None, "head"),
        P(None, "head"),
        P("head"),
        P("head", None),
        P(),
        P(),
        P(),
        P(),
        P(),
        P(None, "head"),
        P("head"),
        P("head", None),
        P(),
    )
    return jax.shard_map(
        per_device, mesh=mesh, in_specs=in_specs, out_specs=out_specs, check_vma=False
    )
```

```python
import functools

import jax
import jax.numpy as jnp
from jax import lax
from jax.experimental import pallas as pl
from jax.experimental.pallas import tpu as pltpu
from jax.sharding import PartitionSpec as P

HEAD_DIM = 64
SEG = 16
RC = 4
LC = 30
MEM = 4

EPSILON = 1e-05
MASKED = -1e30
F32 = jnp.float32

BEFORE = MEM * SEG
AHEAD = 8
CACHE = 32
SUMS = 8
BLOCK = 64
WIN = CACHE + BLOCK + AHEAD
SWIN = 16
KEYS = 128
FIRST_GAIN, FIRST_SHIFT, SECOND_GAIN, SECOND_SHIFT, OUT_BIAS, INNER_BIAS, OUTER_BIAS = range(7)
PAIR = 2 * HEAD_DIM
MIB = 1 << 20


def mm(left, right, left_dim=1, right_dim=0):
    return lax.dot_general(
        left,
        right,
        (((left_dim,), (right_dim,)), ((), ())),
        precision=lax.Precision.HIGH,
        preferred_element_type=F32,
    )


def normalise(values):
    centred = values - jnp.mean(values, axis=-1, keepdims=True)
    variance = jnp.mean(centred * centred, axis=-1, keepdims=True)
    rate = lax.rsqrt(variance + EPSILON)
    return centred * rate, rate


def norm_back(grad, gain, xhat, rate):
    scaled = grad * gain
    first = jnp.mean(scaled, axis=-1, keepdims=True)
    second = jnp.mean(scaled * xhat, axis=-1, keepdims=True)
    return rate * (scaled - first - xhat * second)


def column_sums(values):
    return jnp.sum(values, axis=0, keepdims=True)


def seg_means(values):
    rows, width = values.shape
    return jnp.sum(values.reshape(rows // SEG, SEG, width), axis=1) * (1.0 / SEG)


def near_bit():
    return lax.axis_index("head") % 2


def far_bit():
    return lax.axis_index("head") // 2


def my_rows(rows):
    half = rows // 2
    return pl.ds(pl.multiple_of(near_bit() * half, half), half)


def lanes_of(place, width, start=0):
    at = place + near_bit() - 2 * place * near_bit()
    return pl.ds(pl.multiple_of(start + at * width, width), width)


def half_rows(place, half):
    return pl.ds(pl.multiple_of(place * half, half), half)


def full(shape):
    return pl.BlockSpec(shape, lambda *_: (0,) * len(shape))


class Steps:
    def __init__(self):
        self.held = []
        self.us = 0.1

    def call(self, kernel, name, outs, args, specs=None, scratch=(), vmem=32, copies=0, far=(), far_outs=()):
        specs = dict(specs or {})
        given, made, held = len(args), len(outs), tuple(self.held)
        token = bool(far_outs)
        somewhere = pl.BlockSpec(memory_space=pl.ANY)
        in_hbm = pl.BlockSpec(memory_space=pltpu.HBM)

        def body(*refs):
            ins, rest = refs[:given], refs[given + len(held) :]
            if token:
                rest[made][...] = jnp.zeros(rest[made].shape, F32)
            kernel(*ins, *rest[:made], *rest[made + token :])

        args = [pltpu.with_memory_space_constraint(a, pltpu.HBM) if i in far else a for i, a in enumerate(args)]
        out_specs = [in_hbm if i in far_outs else full(shape) for i, shape in enumerate(outs)]
        out_shape = [
            pltpu.HBM(shape, F32) if i in far_outs else jax.ShapeDtypeStruct(shape, F32) for i, shape in enumerate(outs)
        ]
        if token:
            out_specs.append(full((1, 128)))
            out_shape.append(jax.ShapeDtypeStruct((1, 128), F32))
        out = pl.pallas_call(
            body,
            name=name,
            grid=(1,),
            in_specs=[in_hbm if i in far else specs.get(i, full(a.shape)) for i, a in enumerate(args)]
            + [somewhere] * len(held),
            out_specs=out_specs,
            out_shape=out_shape,
            scratch_shapes=[pltpu.VMEM(shape, F32) for shape in scratch]
            + ([pltpu.SemaphoreType.DMA((copies,))] if copies else []),
            compiler_params=pltpu.CompilerParams(vmem_limit_bytes=vmem * MIB),
            cost_estimate=pl.CostEstimate(flops=int(self.us * 5.18e8), bytes_accessed=0, transcendentals=0),
        )(*args, *held)
        self.held = [out[-1]]
        return out[:made]


def copy_all(pairs, sems):
    copies = [pltpu.make_async_copy(a, b, sems.at[i]) for i, (a, b) in enumerate(pairs)]
    for copy in copies:
        copy.start()
    return copies


def pack_kernel(wq, wk, wv, wo, bq, bv, bi, frames, out, edge, sems):
    rows, width = wq.shape
    out[rows:] = jnp.zeros((out.shape[0] - rows, out.shape[1]), F32)
    pairs = [(w, out.at[pl.ds(0, rows), pl.ds(i * width, width)]) for i, w in enumerate((wq, wk, wv))]
    for at in range(0, wo.shape[1], width):
        pairs.append((wo.at[:, pl.ds(at, width)], out.at[pl.ds(at, width), pl.ds(3 * width, width)]))
    pairs += [(b, out.at[pl.ds(rows, 1), pl.ds(i * width, width)]) for i, b in ((0, bq), (2, bv))]
    pairs.append((bi, out.at[pl.ds(rows + 1, 1), pl.ds(0, bi.shape[1])]))
    start = pl.multiple_of((1 - near_bit()) * (frames.shape[1] - BEFORE), BEFORE)
    pairs += [(frames.at[m, pl.ds(start, BEFORE)], edge.at[m]) for m in range(frames.shape[0])]
    for copy in copy_all(pairs, sems):
        copy.wait()


def norm_kernel(
    frames, gain, shift, wi, wu, wo, cotangent,
    x_ref, xhat_ref, rate_ref, normed_ref, wi_ref, wu_ref, wo_ref, g_0, g_1, before, ahead, params, sems,
):
    micros, half, _ = x_ref.shape
    rows = frames.shape[1]
    pairs = [(gain, params.at[pl.ds(0, 1)]), (shift, params.at[pl.ds(8, 1)])]
    pairs += [(frames.at[m, my_rows(rows)], x_ref.at[m]) for m in range(micros)]
    pairs += [(frames.at[m, pl.ds(half - BEFORE, BEFORE)], before.at[m]) for m in range(micros)]
    pairs += [(frames.at[m, pl.ds(half, AHEAD)], ahead.at[m]) for m in range(micros)]
    pairs += [(wo, wo_ref), (wi, wi_ref), (wu, wu_ref)]
    pairs += [(cotangent.at[m, my_rows(rows)], g) for m, g in enumerate((g_0, g_1))]
    copies = copy_all(pairs, sems)
    for copy in copies[:2]:
        copy.wait()
    for micro in range(micros):
        copies[2 + micro].wait()
        xhat, rate = normalise(x_ref[micro])
        xhat_ref[micro] = xhat
        normed_ref[micro] = xhat * params[0:1] + params[8:9]
        rate_ref[micro] = jnp.broadcast_to(rate, (half, rate_ref.shape[2]))
    for copy in copies[2 + micros :]:
        copy.wait()


def project_kernel(normed, own, pair, g1, s1, g2, s2, bo, bi, bu, q_ref, kv_ref, w_ref, bias, rows_ref, sems):
    micros, half, wide = q_ref.shape
    features = normed.shape[2]
    width = own.shape[1] // 4
    copies = copy_all([(v, rows_ref.at[i]) for i, v in enumerate((g1, s1, g2, s2, bo, bi, bu))], sems)
    for number in range(3):
        at = slice(number * width, (number + 1) * width)
        for place, source in enumerate((own, pair)):
            lanes = lanes_of(place, width, 2 * number * width)
            w_ref[:, lanes] = source[:features, at]
            bias[:, lanes] = source[features : features + 1, at]
    for micro in range(micros):
        out = mm(normed[micro], w_ref[...]) + bias[...]
        q_ref[micro] = out[:, :wide]
        kv_ref[micro] = out[:, wide:]
    for copy in copies:
        copy.wait()


def edges_kernel(edge, before, ahead, params, w_ref, bias, xhat_ref, normed_ref, kv_ref):
    near = near_bit()
    wide = w_ref.shape[1] // 3
    for micro in range(edge.shape[0]):
        first = jnp.where(near == 0, edge[micro], before[micro])
        last = jnp.where(near == 0, ahead[micro], edge[micro, :AHEAD])
        xhat, _ = normalise(jnp.concatenate([first, last], axis=0))
        normed = xhat * params[FIRST_GAIN] + params[FIRST_SHIFT]
        xhat_ref[micro] = xhat
        normed_ref[micro] = normed
        kv_ref[micro] = mm(normed, w_ref[:, wide:]) + bias[:, wide:]


def fill_keys(kv, edge, kx, sx):
    length = kv.shape[0]
    kx[BEFORE : BEFORE + length] = kv
    segs = length // SEG
    sx[SUMS : SUMS + segs] = seg_means(kv)
    if edge is not None:
        kx[:BEFORE] = edge[:BEFORE]
        kx[BEFORE + length :] = edge[BEFORE:]
        sx[: SUMS - MEM] = jnp.zeros((SUMS - MEM, kv.shape[1]), F32)
        sx[SUMS - MEM : SUMS] = seg_means(edge[:BEFORE])
        sx[SUMS + segs :] = jnp.zeros((sx.shape[0] - SUMS - segs, kv.shape[1]), F32)


def summary_start(block):
    return (block * (BLOCK // SEG) + SUMS - MEM) // SUMS * SUMS


def frame_rows(block):
    start = BEFORE - CACHE + block * BLOCK
    return slice(start, start + WIN)


def key_window(kx, sx, block, lanes):
    start = summary_start(block)
    rows = [kx[frame_rows(block), lanes], sx[start : start + SWIN, lanes]]
    return jnp.concatenate(rows + [jnp.zeros((KEYS - WIN - SWIN, PAIR), F32)], axis=0)


def by_head(values):
    first = lax.broadcasted_iota(jnp.int32, values.shape, 1) < HEAD_DIM
    return jnp.concatenate([jnp.where(first, values, 0.0), jnp.where(first, 0.0, values)], axis=0)


def side_by_side(values):
    rows = values.shape[0] // 2
    first = lax.broadcasted_iota(jnp.int32, (rows, values.shape[1]), 1) < HEAD_DIM
    return jnp.where(first, values[:rows], values[rows:])


def owner_of(segment, bounds):
    owner = jnp.where(segment < 0, -1, 0)
    for bound in bounds:
        owner = owner + (segment >= bound).astype(jnp.int32)
    return owner


def visible(block, base, bounds):
    row = lax.broadcasted_iota(jnp.int32, (2 * BLOCK, 1), 0) % BLOCK
    column = lax.broadcasted_iota(jnp.int32, (1, KEYS), 1)
    query_seg = block * (BLOCK // SEG) + row // SEG
    frame = block * BLOCK - CACHE + column
    is_frame = column < WIN
    summary = summary_start(block) - SUMS + column - WIN
    key_seg = jnp.where(is_frame, (frame + CACHE) // SEG - CACHE // SEG, summary)
    key_seg = jnp.where(column < WIN + SWIN, key_seg, -(1 << 20))
    inside = (frame >= query_seg * SEG - LC) & (frame < query_seg * SEG + SEG + RC)
    near = (key_seg >= query_seg - MEM) & (key_seg < query_seg)
    seen = (is_frame & inside) | ((column >= WIN) & near)
    return seen & (owner_of(key_seg + base, bounds) == owner_of(query_seg + base, bounds))


def bounds_of(counts, micro):
    bounds, total = [], 0
    for utterance in range(counts.shape[1]):
        total = total + counts[micro, utterance]
        bounds.append(total)
    return bounds


def first_segment(length):
    return (lax.axis_index("tm") * 2 + near_bit()) * (length // SEG)


def block_rows(block):
    return slice(block * BLOCK, (block + 1) * BLOCK)


def attend_block(block, seen, query, kx, sx, keep, put):
    width = query.shape[1]
    for pair in range(width // PAIR):
        lanes = slice(pair * PAIR, (pair + 1) * PAIR)
        value_lanes = slice(width + pair * PAIR, width + (pair + 1) * PAIR)
        scores = mm(by_head(query[:, lanes] * HEAD_DIM ** (-0.5)), key_window(kx, sx, block, lanes), 1, 1)
        scores = jnp.where(seen, scores, MASKED)
        weights = jnp.exp(scores - jnp.max(scores, axis=-1, keepdims=True))
        weights = weights / jnp.sum(weights, axis=-1, keepdims=True)
        keep(pair, weights)
        put(lanes, side_by_side(mm(weights, key_window(kx, sx, block, value_lanes))))


def attend_inner_kernel(counts, q_ref, kv_ref, mix_0, mix_1, p_ref, kx, sx):
    _, length, _ = q_ref.shape
    base = first_segment(length)
    for micro, mix_ref in enumerate((mix_0, mix_1)):
        fill_keys(kv_ref[micro], None, kx, sx)
        bounds = bounds_of(counts, micro)
        for number, block in enumerate(range(1, length // BLOCK - 1)):
            def keep(pair, weights):
                p_ref[micro, number, pair] = weights

            def put(lanes, values):
                mix_ref[block_rows(number), lanes] = values

            seen = visible(block, base, bounds)
            attend_block(block, seen, q_ref[micro, block_rows(block)], kx, sx, keep, put)


def attend_outer_kernel(micro, counts, q_ref, kv_ref, edge, mix_ref, p_ref, kx, sx):
    _, length, _ = q_ref.shape
    base = first_segment(length)
    fill_keys(kv_ref[micro], edge[micro], kx, sx)
    bounds = bounds_of(counts, micro)
    for number, block in enumerate((0, length // BLOCK - 1)):
        def keep(pair, weights):
            p_ref[number, pair] = weights

        def put(lanes, values):
            mix_ref[block_rows(number), lanes] = values

        seen = visible(block, base, bounds)
        attend_block(block, seen, q_ref[micro, block_rows(block)], kx, sx, keep, put)


def fill_rows(target, lanes, inner, outer):
    length = inner.shape[0] + outer.shape[0]
    target[:BLOCK, lanes] = outer[:BLOCK]
    target[BLOCK : length - BLOCK, lanes] = inner[...]
    target[length - BLOCK : length, lanes] = outer[BLOCK:]


def back_kernel(
    micro, grad_ref, mid_ref, g_ref, params, wo_here, mix_inner, mix_outer, q_ref, kv_ref, edge, p_inner, p_outer,
    dmid_ref, dq_ref, dkv_ref, dwo_own, dwo_pair, vec_ref,
    kx, sx, dsx, dmix, mix, dwo,
):
    _, length, width = q_ref.shape
    near_width = dwo_own.shape[1]
    grad = grad_ref[...]
    xhat, rate = normalise(mid_ref[...])
    dmid = g_ref[...] + norm_back(grad, params[SECOND_GAIN], xhat, rate)
    dmid_ref[...] = dmid
    vec_ref[0:1] = column_sums(dmid)
    vec_ref[1:2] = column_sums(grad * xhat)
    vec_ref[2:3] = column_sums(grad)
    dmix[...] = mm(dmid, wo_here[...], 1, 1)
    fill_rows(mix, slice(None), mix_inner, mix_outer)
    dwo[...] = mm(dmid, mix[...], 0, 0)
    dwo_own[...] = dwo[:, lanes_of(0, near_width)]
    dwo_pair[...] = dwo[:, lanes_of(1, near_width)]
    fill_keys(kv_ref[micro], edge[micro], kx, sx)
    dkv_ref[...] = jnp.zeros_like(dkv_ref)
    dsx[...] = jnp.zeros_like(dsx)
    for block in range(length // BLOCK):
        start = summary_start(block)
        rows, frames, sums = block_rows(block), frame_rows(block), slice(start, start + SWIN)
        for pair in range(width // PAIR):
            lanes = slice(pair * PAIR, (pair + 1) * PAIR)
            value_lanes = slice(width + pair * PAIR, width + (pair + 1) * PAIR)
            inside = 0 < block < length // BLOCK - 1
            weights = p_inner[micro, block - 1, pair] if inside else p_outer[min(block, 1), pair]
            grad = by_head(dmix[rows, lanes])
            dweights = mm(grad, key_window(kx, sx, block, value_lanes), 1, 1)
            dscores = weights * (dweights - jnp.sum(dweights * weights, axis=-1, keepdims=True))
            dquery = side_by_side(mm(dscores, key_window(kx, sx, block, lanes)))
            dq_ref[rows, lanes] = dquery * HEAD_DIM ** (-0.5)
            dkeys = mm(dscores, by_head(q_ref[micro, rows, lanes] * HEAD_DIM ** (-0.5)), 0, 0)
            dvalues = mm(weights, grad, 0, 0)
            dkv_ref[frames, lanes] += dkeys[:WIN]
            dkv_ref[frames, value_lanes] += dvalues[:WIN]
            dsx[sums, lanes] += dkeys[WIN : WIN + SWIN]
            dsx[sums, value_lanes] += dvalues[WIN : WIN + SWIN]
    count = BEFORE + length
    segs = count // SEG
    spread = dsx[SUMS - MEM : SUMS - MEM + segs] * (1.0 / SEG)
    spread = jnp.broadcast_to(spread[:, None, :], (segs, SEG, 2 * width))
    dkv_ref[:count] += spread.reshape(count, 2 * width)


def feed_kernel(
    micro, own_inner, own_outer, far_inner, far_outer, wo_here, wo_far, wo_far_pair, x_ref, g_ref, params, pair, wi_own, wi_pair, wu_own, wu_pair,
    n2_ref, h_ref, dpre_ref, mid_ref, part_ref,
    mix, wo,
):
    width = own_inner.shape[1] // 2
    features, hidden = wi_own.shape
    far = far_bit()
    here = pl.multiple_of(far * 2 * width, 2 * width)
    there = pl.multiple_of((1 - far) * 2 * width, 2 * width)
    fill_rows(mix, pl.ds(here, 2 * width), own_inner, own_outer)
    fill_rows(mix, pl.ds(there, 2 * width), far_inner, far_outer)
    wo[pl.ds(here, 2 * width)] = wo_here[...]
    wo[lanes_of(0, width, there)] = wo_far[...]
    wo[lanes_of(1, width, there)] = wo_far_pair[...]
    middle = x_ref[micro] + mm(mix[...], wo[...]) + params[OUT_BIAS]
    mid_ref[...] = middle
    xhat, _ = normalise(middle)
    normed = xhat * params[SECOND_GAIN] + params[SECOND_SHIFT]
    n2_ref[...] = normed
    part = None
    for place, (wi, wu, bias) in enumerate(((wi_own, wu_own, params[INNER_BIAS][:, :hidden]), (wi_pair, wu_pair, pair[features + 1 : features + 2, :hidden]))):
        at = slice(place * hidden, (place + 1) * hidden)
        pre = mm(normed, wi[...]) + bias
        phi = 0.5 + 0.5 * lax.erf(pre * (0.5**0.5))
        h_ref[:, at] = pre * phi
        slope = phi + pre * (jnp.exp(-0.5 * pre * pre) * 0.3989422804014327)
        dpre = mm(g_ref[...], wu[...], 1, 1) * slope
        dpre_ref[:, at] = dpre
        step = mm(dpre, wi[...], 1, 1)
        part = step if part is None else part + step
    part_ref[...] = part


def put_rows(value, outs):
    at = 0
    for out in outs:
        count = out.shape[0]
        out[...] = value[at : at + count]
        at += count


def inner_weights_kernel(n2_0, n2_1, d_0, d_1, own_ref, *rest):
    *pair, vec_ref = rest
    hidden = own_ref.shape[1]
    for place, outs in enumerate(((own_ref,), pair)):
        at = slice(place * hidden, (place + 1) * hidden)
        put_rows(mm(n2_0[...], d_0[:, at], 0, 0) + mm(n2_1[...], d_1[:, at], 0, 0), outs)
        vec_ref[place : place + 1] = column_sums(d_0[:, at]) + column_sums(d_1[:, at])


def outer_weights_kernel(h_0, h_1, g_0, g_1, own_ref, *rest):
    *pair, vec_ref = rest
    hidden = own_ref.shape[0]
    for place, outs in enumerate(((own_ref,), pair)):
        at = slice(place * hidden, (place + 1) * hidden)
        value = mm(h_0[:, at], g_0[...], 0, 0) + mm(h_1[:, at], g_1[...], 0, 0)
        for out_ref in outs:
            out_ref[:hidden] = value
            if out_ref.shape[0] > hidden:
                out_ref[hidden:] = jnp.zeros((out_ref.shape[0] - hidden, value.shape[1]), F32)
    vec_ref[...] = column_sums(g_0[...]) + column_sums(g_1[...])


def feed_out_kernel(h_0, h_1, wu_own, wu_pair, out_ref):
    hidden = wu_own.shape[0]
    rows = h_0.shape[0]
    for micro, h_ref in enumerate((h_0, h_1)):
        part = mm(h_ref[:, :hidden], wu_own[...]) + mm(h_ref[:, hidden:], wu_pair[...])
        out_ref[micro * rows : (micro + 1) * rows] = part


def out_half_kernel(mid_0, mid_1, part, far, params, out):
    rows = mid_0.shape[0]
    for micro, mid_ref in enumerate((mid_0, mid_1)):
        at = slice(micro * rows, (micro + 1) * rows)
        out[at] = mid_ref[...] + (part[at] + far[at]) + params[OUTER_BIAS]


def project_back_kernel(
    dq_0, dkv_0, dq_1, dkv_1, xhat, xhat_edge, w_ref, part_ref, pair_ref, beyond_ref, vec_ref, work
):
    near = near_bit()
    length, wide = dq_0.shape
    own = slice(BEFORE, BEFORE + length)
    gain, shift = 0.0, 0.0
    for micro, (dq, dkv) in enumerate(((dq_0, dkv_0), (dq_1, dkv_1))):
        work[...] = mm(dkv[...], w_ref[:, wide:], 1, 1)
        work[own] += mm(dq[...], w_ref[:, :wide], 1, 1)
        part_ref[micro * length : (micro + 1) * length] = work[own]
        before = work[:BEFORE]
        ahead = jnp.concatenate([work[BEFORE + length :], jnp.zeros((BEFORE - AHEAD, work.shape[1]), F32)], axis=0)
        pair_ref[micro] = jnp.where(near == 0, ahead, before)
        beyond_ref[micro] = jnp.where(near == 0, before, ahead)
        gain = gain + column_sums(work[own] * xhat[micro]) + column_sums(work[:BEFORE] * xhat_edge[micro, :BEFORE])
        gain = gain + column_sums(work[BEFORE + length :] * xhat_edge[micro, BEFORE:])
        shift = shift + column_sums(work[...])
    vec_ref[0:1] = gain
    vec_ref[1:2] = shift


def edge_add_kernel(part, pair, beyond, out):
    out[...] = part[...]
    near = near_bit()
    micros = pair.shape[0]
    length = part.shape[0] // micros
    for micro in range(micros):
        end = (micro + 1) * length
        out[end - BEFORE : end] += jnp.where(near == 0, pair[micro], beyond[micro])
        out[end - length : end - length + AHEAD] += jnp.where(near == 0, beyond[micro, :AHEAD], pair[micro, :AHEAD])


def project_weights_kernel(
    normed, normed_edge, dq_0, dq_1, dkv_0, dkv_1, wo_own_0, wo_own_1, wo_pair_0, wo_pair_1, mid_0, mid_1, first, vec_outer, vec_inner,
    own_ref, rows_ref, pair_0, pair_1, sums, row,
):
    features = normed.shape[2]
    width = wo_own_0.shape[1]
    hidden = vec_inner.shape[1]
    length, wide = dq_0.shape
    own, after = slice(BEFORE, BEFORE + length), slice(BEFORE + length, None)
    edges = jnp.concatenate([dkv_0[:BEFORE], dkv_0[after], dkv_1[:BEFORE], dkv_1[after]], axis=0)
    normed_edges = jnp.concatenate([normed_edge[0], normed_edge[1]], axis=0)
    queries = mm(normed[0], dq_0[...], 0, 0) + mm(normed[1], dq_1[...], 0, 0)
    keyvals = mm(normed[0], dkv_0[own], 0, 0) + mm(normed[1], dkv_1[own], 0, 0) + mm(normed_edges, edges, 0, 0)
    sums[:, :wide] = queries
    sums[:, wide:] = keyvals
    row[:, :wide] = column_sums(dq_0[...]) + column_sums(dq_1[...])
    row[:, wide:] = column_sums(dkv_0[...]) + column_sums(dkv_1[...])
    rows_ref[0:3] = (mid_0[...] + mid_1[...]) * 0.5
    rows_ref[3:5] = first[...]
    rows_ref[5:6] = vec_outer[...] * 0.5
    rows_ref[6:] = jnp.zeros((2, features), F32)
    half = pair_0.shape[0]
    pair_1[half : half + 6] = rows_ref[0:6]
    pair_1[half + 6 :] = jnp.zeros((2, features), F32)
    for place, (out_ref, at) in enumerate(((rows_ref, 6), (pair_1, half + 6))):
        for number in range(3):
            lanes = slice(number * width, (number + 1) * width)
            out_ref[at : at + 1, lanes] = row[:, lanes_of(place, width, 2 * number * width)]
        out_ref[at + 1 : at + 2, :hidden] = vec_inner[place : place + 1]
    shares = (((own_ref, slice(None)),), ((pair_0, slice(half)), (pair_1, slice(half, features))))
    for place, (share, wo_0, wo_1) in enumerate(((shares[0], wo_own_0, wo_own_1), (shares[1], wo_pair_0, wo_pair_1))):
        for out_ref, rows in share:
            count = half if place else features
            for number in range(3):
                lanes = slice(number * width, (number + 1) * width)
                out_ref[:count, lanes] = sums[rows, lanes_of(place, width, 2 * number * width)]
            out_ref[:count, 3 * width :] = wo_0[rows] + wo_1[rows]


def frames_back_kernel(a_ref, b_ref, xhat, rate, dmid_0, dmid_1, params, out):
    rows = dmid_0.shape[0]
    for micro, dmid_ref in enumerate((dmid_0, dmid_1)):
        at = slice(micro * rows, (micro + 1) * rows)
        grad = norm_back(a_ref[at] + b_ref[at], params[FIRST_GAIN], xhat[micro], rate[micro, :, :1])
        out[at] = dmid_ref[...] + grad


def place_kernel(own, pair, out, sems):
    micros, half = out.shape[0], out.shape[1] // 2
    near = near_bit()
    pairs = []
    for micro in range(micros):
        rows = pl.ds(micro * half, half)
        pairs.append((own.at[rows], out.at[micro, half_rows(near, half)]))
        pairs.append((pair.at[rows], out.at[micro, half_rows(1 - near, half)]))
    for copy in copy_all(pairs, sems):
        copy.wait()


def place_of(bit):
    return lax.axis_index("tm") // bit % 2


def add_pieces(out, a_ref, pieces, rows_ref=None, new_rows=None):
    count, at = a_ref.shape[0], 0
    if not pieces:
        out[...] = a_ref[...]
        if new_rows is not None:
            new_rows[...] = rows_ref[...]
    for piece in pieces:
        take = min(piece.shape[0], count - at)
        if take:
            out[at : at + take] = a_ref[at : at + take] + piece[:take]
        if take < piece.shape[0] and new_rows is not None:
            new_rows[...] = rows_ref[...] + piece[take:]
        at += take


def add_split_kernel(bits, counts, rows, *refs):
    total = len(bits)
    values, refs = refs[:total], refs[total:]
    rows_ref, refs = (refs[0], refs[1:]) if rows else (None, refs)
    pieces = []
    for count in counts:
        pieces.append(refs[:count])
        refs = refs[count:]
    kept, sent, refs = refs[:total], refs[total : 2 * total], refs[2 * total :]
    new_rows, work = (refs[0], refs[1]) if rows else (None, refs[0])
    for number, bit in enumerate(bits):
        small = (rows_ref, new_rows) if rows and number == 0 else ()
        half = kept[number].shape[0]
        add_pieces(work, values[number], pieces[number], *small)
        place = place_of(bit)
        kept[number][...] = work[half_rows(place, half)]
        sent[number][:half] = work[half_rows(1 - place, half)]
        if small:
            sent[number][half:] = new_rows[...]


def last_kernel(rows, a_ref, *refs):
    rows_ref, refs = (refs[0], refs[1:]) if rows else (None, refs)
    b_ref, out_ref = refs
    half = a_ref.shape[0]
    out_ref[:half] = a_ref[...] + b_ref[:half]
    if rows:
        out_ref[half:] = rows_ref[...] + b_ref[half:]


def add_cut_kernel(bit, a_ref, rows_ref, *refs):
    *pieces, kept, sent_0, sent_1, new_rows, work = refs
    half, cut = kept.shape[0], sent_0.shape[0]
    add_pieces(work, a_ref, pieces, rows_ref, new_rows)
    place = place_of(bit)
    kept[...] = work[half_rows(place, half)]
    sent = work[half_rows(1 - place, half)]
    sent_0[...] = sent[:cut]
    sent_1[: half - cut] = sent[cut:]
    sent_1[half - cut :] = new_rows[...]


def stack_kernel(rows, a_0, a_1, *refs):
    rows_ref, refs = (refs[0], refs[1:]) if rows else (None, refs)
    b_0, b_1, out_ref = refs
    half = a_0.shape[0]
    out_ref[:half] = a_0[...] + b_0[:half]
    out_ref[half : 2 * half] = a_1[...] + b_1[...]
    if rows:
        out_ref[2 * half :] = rows_ref[...] + b_0[half:]


def add_whole_kernel(a_ref, b_ref, *outs):
    at = 0
    for out in outs:
        count = out.shape[0]
        out[...] = a_ref[at : at + count] + b_ref[at : at + count]
        at += count


def join_kernel(bits, *refs):
    total = len(bits)
    for bit, mine, theirs, out in zip(bits, refs[:total], refs[total : 2 * total], refs[2 * total :], strict=True):
        half = mine.shape[0]
        place = place_of(bit)
        out[half_rows(place, half)] = mine[...]
        out[half_rows(1 - place, half)] = theirs[...]


def join_out_kernel(bit, mine, theirs, out, sems):
    half = mine.shape[0]
    place = place_of(bit)
    for copy in copy_all([(mine, out.at[half_rows(place, half)]), (theirs, out.at[half_rows(1 - place, half)])], sems):
        copy.wait()


def join_heads_kernel(bits, *refs):
    *parts, wq, wk, wv, wo, work = refs
    width = wq.shape[1]
    count = parts[0].shape[0] // 2
    first, second = (place_of(bit) for bit in bits)
    for number in range(2):
        place = first if number else second
        for where, part in ((place, parts[2 * number]), (1 - place, parts[2 * number + 1])):
            for joined in range(2):
                start = where * 4 * count + joined * 2 * count + count if number else joined * 4 * count + where * 2 * count
                rows = pl.ds(pl.multiple_of(start, count), count)
                here = slice(joined * count, (joined + 1) * count)
                for heads, out in enumerate((wq, wk, wv, work)):
                    out[rows, :] = part[here, heads * width : (heads + 1) * width]
    wo[...] = work[...].T


def small_kernel(rows, far, outs):
    width = outs[-3].shape[1]
    for number, out in enumerate(outs[:6]):
        out[...] = rows[number : number + 1] + far[number : number + 1]
    outs[6][...] = rows[6:7, :width]
    outs[7][...] = rows[6:7, 2 * width : 3 * width]
    outs[8][...] = rows[7:8, : outs[8].shape[1]]


def finish_kernel(bits, rows, far, *refs):
    count = 2 * len(bits)
    small_kernel(rows, far, refs[count : count + 9])
    join_heads_kernel(bits, *refs[:count], *refs[count + 9 :])


def swap(value, axis, bit):
    size = lax.axis_size(axis)
    return lax.ppermute(value, axis, [(i, i ^ bit) for i in range(size)])


def swap_near(parts):
    return [swap(part, "head", 1) for part in parts]


def swap_edges(value, back):
    size, group = lax.axis_size("tm"), lax.axis_size("head")
    pairs = []
    for source in range(size):
        for place in range(group):
            target = source + (1 - 2 * (place % 2)) * (-1 if back else 1)
            if 0 <= target < size:
                pairs.append((source * group + place, target * group + (place ^ 1 if back else place)))
    return lax.ppermute(value, ("tm", "head"), pairs)


class SumsOverTm:
    def __init__(self, run, a, b, rows=None):
        bits = [1 << i for i in range(lax.axis_size("tm").bit_length() - 1)]
        self.run, self.values, self.got, self.ones = run, list(a), [list(v) for v in b], []
        self.rows = [] if rows is None else [rows]
        self.apart = [(bits[1], bits[0]), (bits[0], bits[1])]
        self.together, self.last = bits[2:-1], bits[-1]
        if len(a) == 1:
            self.todo = [("cut", bits[0])] + [("split", (bit,)) for bit in bits[1:-1]] + [("last",)]
        else:
            self.todo = [("split", pair) for pair in self.apart]
            self.todo.append(("stack",))
            self.todo += [("split", (bit,)) for bit in self.together] + [("last",)] * bool(self.together)
        self.todo.append(("add",))
        self.todo += [("join", (bit,)) for bit in reversed(self.together)] + [("part",)] * bool(self.together)
        self.todo.append(("join", self.apart[1]))
        self.step()

    def step(self):
        run, values = self.run, self.values
        kind, *rest = self.todo.pop(0)
        features = values[0].shape[1]
        count = values[0].shape[0]
        more = sum(v.shape[0] for v in self.rows)
        has_rows = bool(self.rows)
        shape = lambda rows: (rows, features)
        got = [piece for pieces in self.got for piece in pieces]
        if kind == "cut":
            half = count // 2
            (value, *sent, rows) = run.call(
                functools.partial(add_cut_kernel, rest[0]), "add_cut",
                [shape(half), shape(half // 2), shape(half // 2 + more), self.rows[0].shape], (*values, *self.rows, *got),
                scratch=[shape(count)],
            )
            self.values, self.rows, self.got = [value], [rows], [[swap(v, "tm", rest[0]) for v in sent]]
            return
        if kind == "split":
            (bits,) = rest
            half = count // 2
            extra = [more] + [0] * (len(bits) - 1)
            out = run.call(
                functools.partial(add_split_kernel, bits, [len(v) for v in self.got], has_rows), "add_split",
                [shape(half)] * len(bits) + [shape(half + e) for e in extra] + [v.shape for v in self.rows],
                (*values, *self.rows, *got), scratch=[shape(count)],
            )
            self.values, messages, self.rows = out[: len(bits)], out[len(bits) : 2 * len(bits)], out[2 * len(bits) :]
            self.got = [[swap(v, "tm", bit)] for v, bit in zip(messages, bits, strict=True)]
            return
        if kind in ("stack", "last"):
            if kind == "stack":
                (value,) = run.call(
                    functools.partial(stack_kernel, has_rows), "stack", [shape(2 * count + more)], (*values, *self.rows, *got)
                )
                count = 2 * count
            else:
                (value,) = run.call(
                    functools.partial(last_kernel, has_rows), "stack", [shape(count + more)], (*values, *self.rows, *got)
                )
            if kind == "stack" and self.together:
                self.values, self.rows = [value[:count]], [value[count:]] * has_rows
                self.values, self.got = self.values, [[]]
                return self.step()
            self.values, self.count = [value], count
            self.got = [[swap(value, "tm", self.last)]]
            return
        if kind == "add":
            parts = [self.count] if self.together else [self.count // 2] * 2
            out = run.call(
                add_whole_kernel, "add", [shape(n) for n in parts] + [v.shape for v in self.rows], (*values, *got)
            )
            self.values, self.rows = out[: len(parts)], out[len(parts) :]
        elif kind == "join":
            (bits,) = rest
            self.values = run.call(
                functools.partial(join_kernel, bits), "join", [shape(2 * count)] * len(bits), (*values, *got)
            )
        elif kind == "part":
            self.values = [values[0][: count // 2], values[0][count // 2 :]]
        following = self.todo[0] if self.todo else ("join", self.apart[0])
        if following[0] == "part":
            return self.step()
        self.got = [[swap(v, "tm", bit)] for v, bit in zip(self.values, following[1], strict=True)]

    def join_one(self, number):
        if len(self.todo) != 1:
            return
        bits = self.todo[0][1]
        value = self.values[number]
        values, got = list(self.values), list(self.got)
        (values[number],) = self.run.call(
            functools.partial(join_kernel, bits[number : number + 1]), "join", [(2 * value.shape[0], value.shape[1])],
            (value, *got[number]),
        )
        got[number] = [swap(values[number], "tm", self.apart[0][number])]
        self.values, self.got = values, got
        self.ones.append(number)
        if len(self.ones) == 2:
            self.todo.pop()

    @property
    def joined(self):
        return not self.todo

    def halves(self, number):
        return self.apart[0][number], (self.values[number], *self.got[number])


ORDER = (
    ("pack", 8), ("norm", 4.8), ("project", 2.2), ("attend_inner", 11), ("edges", 1), ("hand_on", 0.5),
    ("attend_outer0", 24), ("attend_outer1", 1), ("feed0", 18), ("feed1", 14), ("outer_weights", 6),
    ("inner_weights", 11), ("feed_out", 0.6), ("grad_sum0", 18), ("ffn", 11), ("back0", 6), ("grad_sum1", 18),
    ("back1", 0.5), ("ffn", 0.1), ("project_back", 1.8), ("project_weights", 2), ("ffn", 0.1), ("edge_add", 5),
    ("out_half", 5), ("out_send", 6), ("heads", 20), ("place_out", 1.3), ("heads", 0.1), ("ffn", 0.1), ("heads", 3),
    ("frames_back", 0.6), ("ffn_last0", 0.1), ("ffn_last1", 20), ("place_frames", 0.1), ("heads", 0.1),
    ("heads", 0.1), ("join_outer", 0.1), ("join_inner", 0.1), ("finish", 1.3),
)
PIECES = 1


def copy_kernel(source, target):
    target[...] = source[...]


def hand_on_kernel(own, pair, far, here, far_copy):
    far_copy[...] = far[...]
    width = far.shape[0]
    for near, source in enumerate((own, pair)):
        for at in range(0, far.shape[1], width):
            lanes = slice(3 * width, 4 * width)
            here[lanes_of(near, width), at : at + width] = source[at : at + width, lanes]


class Layer:
    def __init__(
        self, frames, cotangent, seg_counts, query_weight, query_bias, key_weight, value_weight, value_bias,
        out_weight, out_bias, first_gain, first_shift, second_gain, second_shift,
        inner_weight, inner_bias, outer_weight, outer_bias,
    ):
        self.frames, self.cotangent, self.counts = frames, cotangent, seg_counts
        self.projections = (query_weight, key_weight, value_weight)
        self.weights = (inner_weight, outer_weight, out_weight)
        row = lambda v: v.reshape(1, v.shape[0])
        self.bq, self.bv, self.bo, self.bi, self.bu = map(row, (query_bias, value_bias, out_bias, inner_bias, outer_bias))
        self.g1, self.s1, self.g2, self.s2 = map(row, (first_gain, first_shift, second_gain, second_shift))
        micros, shard, features = frames.shape
        self.micros, self.features = micros, features
        self.width, self.hidden = query_weight.shape[1], inner_weight.shape[1]
        self.length = shard // 2
        self.segs, self.blocks, self.pairs = self.length // SEG, self.length // BLOCK, 2 * self.width // PAIR
        self.big = (self.length, features)
        self.each = (micros, self.length)
        self.quarter = (self.length // 2, features)
        self.square = (2 * BLOCK, KEYS)
        self.around = BEFORE + self.length + AHEAD
        self.key_scratch = [(self.around, 4 * self.width), (SUMS + self.segs + SUMS, 4 * self.width)]
        self.run = Steps()
        self.smem = pl.BlockSpec(memory_space=pltpu.SMEM)
        pairs = [None] * micros
        self.mix_outer, self.far_outer, self.p_outer, self.fed, self.dn2 = (list(pairs) for _ in range(5))
        self.back_of = list(pairs)
        self.sums = {}

    def pack(self):
        args = (*self.projections, self.weights[2], self.bq, self.bv, self.bi, self.frames)
        self.own, edge = self.run.call(
            pack_kernel, "pack", [(self.features + 8, 4 * self.width), (self.micros, BEFORE, self.features)], args,
            copies=6 + self.features // self.width + self.micros, far=range(8),
        )
        self.pair = swap(self.own, "head", 1)
        self.edge = swap_edges(edge, False)

    def norm(self):
        each, features, micros = self.each, self.features, self.micros
        wi, wu, wo = self.weights
        (self.x, self.xhat, self.rate, self.normed, self.wi, self.wu, self.wo, *self.g, self.before, self.ahead) = self.run.call(
            norm_kernel, "norm",
            [each + (features,)] * 2 + [each + (128,), each + (features,), wi.shape, wu.shape, wo.shape, self.big, self.big,
             (micros, BEFORE, features), (micros, AHEAD, features)],
            (self.frames, self.g1, self.s1, wi, wu, wo, self.cotangent),
            scratch=[(16, features)], copies=4 * micros + 5, far=range(7),
        )
        self.wo_far = swap(self.wo, "head", 2)
        self.wi_pair, self.wu_pair = (swap(v, "head", 1) for v in (self.wi, self.wu))

    def project(self):
        each, features, width = self.each, self.features, self.width
        args = (self.normed, self.own, self.pair, self.g1, self.s1, self.g2, self.s2, self.bo, self.bi, self.bu)
        self.q, self.kv, self.w_all, self.bias, self.params = self.run.call(
            project_kernel, "project",
            [each + (2 * width,), each + (4 * width,), (features, 6 * width), (1, 6 * width), (7, 1, features)],
            args, copies=7, far=range(3, 10),
        )

    def edges(self):
        shape = (self.micros, BEFORE + AHEAD)
        self.xhat_edge, self.normed_edge, self.kv_edge = self.run.call(
            edges_kernel, "edges", [shape + (self.features,)] * 2 + [shape + (4 * self.width,)],
            (self.edge, self.before, self.ahead, self.params, self.w_all, self.bias),
        )

    def attend_inner(self):
        *self.mix_inner, self.p_inner = self.run.call(
            attend_inner_kernel, "attend_inner",
            [(self.length - 2 * BLOCK, 2 * self.width)] * 2 + [(self.micros, self.blocks - 2, self.pairs) + self.square],
            (self.counts, self.q, self.kv), {0: self.smem}, self.key_scratch,
        )
        self.far_inner = [swap(v, "head", 2) for v in self.mix_inner]

    def attend_outer(self, m):
        if m:
            self.run.held.append(self.far_inner[0])
        self.mix_outer[m], self.p_outer[m] = self.run.call(
            functools.partial(attend_outer_kernel, m), "attend_outer",
            [(2 * BLOCK, 2 * self.width), (2, self.pairs) + self.square],
            (self.counts, self.q, self.kv, self.kv_edge),
            {0: self.smem}, self.key_scratch,
        )
        self.far_outer[m] = swap(self.mix_outer[m], "head", 2)

    def hand_on(self):
        shape = self.wo_far.shape
        self.wo_here, far = self.run.call(
            hand_on_kernel, "hand_on", [(2 * shape[0], shape[1]), shape], (self.own, self.pair, self.wo_far)
        )
        self.wo_far_pair = swap(far, "head", 1)

    def feed(self, m):
        big, features, hidden = self.big, self.features, self.hidden
        *self.fed[m], part = self.run.call(
            functools.partial(feed_kernel, m), "feed", [big, (self.length, 2 * hidden), (self.length, 2 * hidden), big, big],
            (self.mix_inner[m], self.mix_outer[m], self.far_inner[m], self.far_outer[m], self.wo_here, self.wo_far, self.wo_far_pair, self.x, self.g[m], self.params,
             self.pair, self.wi, self.wi_pair, self.wu, self.wu_pair),
            scratch=[big, (features, features)],
        )
        self.dn2[m] = (part, swap(part, "head", 2))

    def inner_weights(self):
        features, hidden = self.features, self.hidden
        self.inner_own, *pair, self.vec_inner = self.run.call(
            inner_weights_kernel, "inner_weights",
            [(features, hidden)] + [(features // PIECES, hidden)] * PIECES + [(2, hidden)],
            (self.fed[0][0], self.fed[1][0], self.fed[0][2], self.fed[1][2]),
        )
        self.inner_pair = swap_near(pair)

    def outer_weights(self):
        features, hidden = self.features, self.hidden
        self.outer_own, *pair, self.vec_outer = self.run.call(
            outer_weights_kernel, "outer_weights",
            [(hidden, features), (hidden + 8, features), (1, features)],
            (self.fed[0][1], self.fed[1][1], *self.g),
        )
        self.outer_pair = swap_near(pair)

    def feed_out(self):
        (part,) = self.run.call(
            feed_out_kernel, "feed_out", [(self.micros * self.length, self.features)],
            (self.fed[0][1], self.fed[1][1], self.wu, self.wu_pair),
        )
        self.part = (part, swap(part, "head", 2))

    def out_half(self):
        (half,) = self.run.call(
            out_half_kernel, "out_half", [(self.micros * self.length, self.features)],
            (self.fed[0][3], self.fed[1][3], *self.part, self.params),
        )
        self.out = half

    def out_send(self):
        (half,) = self.run.call(copy_kernel, "out_send", [self.out.shape], (self.out,))
        self.out = (half, swap(half, "head", 1))

    def grad_sum(self, m):
        (self.dn2[m],) = self.run.call(add_whole_kernel, "grad_sum", [self.big], self.dn2[m])

    def back(self, m):
        length, width, features = self.length, self.width, self.features
        self.back_of[m] = self.run.call(
            functools.partial(back_kernel, m), "back",
            [self.big, (length, 2 * width), (self.around, 4 * width), (features, width), (features, width), (3, features)],
            (self.dn2[m], self.fed[m][3], self.g[m], self.params, self.wo_here, self.mix_inner[m], self.mix_outer[m], self.q, self.kv,
             self.kv_edge, self.p_inner, self.p_outer[m]),
            scratch=self.key_scratch + self.key_scratch[1:] + [(length, 2 * width)] * 2 + [(features, 2 * width)],
        )

    def pick(self, number):
        return [v[number] for v in self.back_of]

    def project_back(self):
        features, micros = self.features, self.micros
        (dq_0, dq_1), (dkv_0, dkv_1) = self.pick(1), self.pick(2)
        part, pair, beyond, self.vec_first = self.run.call(
            project_back_kernel, "project_back",
            [(micros * self.length, features)] + [(micros, BEFORE, features)] * 2 + [(2, features)],
            (dq_0, dkv_0, dq_1, dkv_1, self.xhat, self.xhat_edge, self.w_all), scratch=[(self.around, features)],
        )
        self.edges_back = (part, swap(pair, "head", 1), swap_edges(beyond, True))

    def edge_add(self):
        part = self.edges_back[0]
        (part,) = self.run.call(edge_add_kernel, "edge_add", [part.shape], self.edges_back)
        self.dn1 = (part, swap(part, "head", 2))

    def project_weights(self):
        features, width = self.features, self.width
        self.heads_own, self.rows, *pair = self.run.call(
            project_weights_kernel, "project_weights",
            [(features, 4 * width), (8, features), (features // 2, 4 * width), (features // 2 + 8, 4 * width)],
            (self.normed, self.normed_edge, *self.pick(1), *self.pick(2), *self.pick(3), *self.pick(4), *self.pick(5),
             self.vec_first, self.vec_outer, self.vec_inner),
            scratch=[(features, 6 * width), (1, 6 * width)],
        )
        self.heads_pair = tuple(swap(v, "head", 1) for v in pair)

    def begin(self, name):
        if name == "heads":
            return SumsOverTm(self.run, (self.heads_own,), (self.heads_pair,), self.rows)
        return SumsOverTm(self.run, (self.outer_own, self.inner_own), (self.outer_pair, self.inner_pair))

    def sum(self, name):
        if name not in self.sums:
            self.sums[name] = self.begin(name)
        elif not self.sums[name].joined:
            self.sums[name].step()

    def ffn(self):
        self.sum("ffn")

    def heads(self):
        self.sum("heads")

    def ffn_last(self, number):
        self.sums["ffn"].join_one(number)

    def heads_last(self, number):
        self.sums["heads"].join_one(number)

    def frames_back(self):
        (half,) = self.run.call(
            frames_back_kernel, "frames_back", [(self.micros * self.length, self.features)],
            (*self.dn1, self.xhat, self.rate, *self.pick(0), self.params),
        )
        self.grad = (half, swap(half, "head", 1))

    def place(self, name, halves):
        (out,) = self.run.call(
            place_kernel, name, [(self.micros, 2 * self.length, self.features)], halves, copies=2 * self.micros, far_outs=[0]
        )
        return out

    def place_out(self):
        self.layer_output = self.place("place_out", self.out)

    def place_frames(self):
        self.frames_grad = self.place("place_frames", self.grad)

    def join(self, name, number, shape):
        bit, parts = self.sums["ffn"].halves(number)
        (out,) = self.run.call(
            functools.partial(join_out_kernel, bit), name, [shape], parts, copies=2, far_outs=[0]
        )
        return out

    def settle(self, *names):
        while not all(self.sums[name].joined for name in names):
            for name in names:
                self.sum(name)

    def join_outer(self):
        self.settle("ffn", "heads")
        self.outer_grad = self.join("join_outer", 0, self.weights[1].shape)

    def join_inner(self):
        self.inner_grad = self.join("join_inner", 1, self.weights[0].shape)

    def finish(self):
        features, width, hidden = self.features, self.width, self.hidden
        sums = self.sums["heads"]
        rows = sums.rows[0]
        bits, parts = sums.apart[1], [sums.halves(i)[1] for i in range(2)]
        out = self.run.call(
            functools.partial(finish_kernel, bits), "finish",
            [(1, features)] * 6 + [(1, width)] * 2 + [(1, hidden)] + [(features, width)] * 3 + [(width, features)],
            (rows, swap(rows, "head", 2), *parts[0], *parts[1]), scratch=[(features, width)],
        )
        bo, g2, s2, g1, s1, bu, bq, bv, bi = (v.reshape(v.shape[1]) for v in out[:9])
        wq, wk, wv, wo = out[9:]
        return (
            self.layer_output, self.frames_grad, wq, bq, wk, wv, bv, wo, bo, g1, s1, g2, s2, self.inner_grad, bi,
            self.outer_grad, bu,
        )


def per_device(*args):
    layer = Layer(*args)
    for step, us in ORDER:
        layer.run.us = us
        name = step.rstrip("0123456789")
        result = getattr(layer, name)(*(int(digit) for digit in step[len(name) :]))
    return result


def solution(mesh):
    in_specs = (
        P(None, "tm", None),
        P(None, "tm", None),
        P(),
        P(None, "head"),
        P("head"),
        P(None, "head"),
        P(None, "head"),
        P("head"),
        P("head", None),
        P(),
        P(),
        P(),
        P(),
        P(),
        P(None, "head"),
        P("head"),
        P("head", None),
        P(),
    )
    out_specs = (
        P(None, "tm", None),
        P(None, "tm", None),
        P(None, "head"),
        P("head"),
        P(None, "head"),
        P(None, "head"),
        P("head"),
        P("head", None),
        P(),
        P(),
        P(),
        P(),
        P(),
        P(None, "head"),
        P("head"),
        P("head", None),
        P(),
    )
    return jax.shard_map(
        per_device, mesh=mesh, in_specs=in_specs, out_specs=out_specs, check_vma=False
    )
```

```python
import functools

import jax
import jax.numpy as jnp
from jax import lax
from jax.experimental import pallas as pl
from jax.experimental.pallas import tpu as pltpu
from jax.sharding import PartitionSpec as P

HEAD_DIM = 64
SEG = 16
RC = 4
LC = 30
MEM = 4

EPSILON = 1e-05
MASKED = -1e30
F32 = jnp.float32

BEFORE = MEM * SEG
AHEAD = 8
CACHE = 32
SUMS = 8
BLOCK = 64
WIN = CACHE + BLOCK + AHEAD
SWIN = 16
KEYS = 128
FIRST_GAIN, FIRST_SHIFT, SECOND_GAIN, SECOND_SHIFT, OUT_BIAS, INNER_BIAS, OUTER_BIAS = range(7)
PAIR = 2 * HEAD_DIM
MIB = 1 << 20


def mm(left, right, left_dim=1, right_dim=0):
    return lax.dot_general(
        left,
        right,
        (((left_dim,), (right_dim,)), ((), ())),
        precision=lax.Precision.HIGH,
        preferred_element_type=F32,
    )


def normalise(values):
    centred = values - jnp.mean(values, axis=-1, keepdims=True)
    variance = jnp.mean(centred * centred, axis=-1, keepdims=True)
    rate = lax.rsqrt(variance + EPSILON)
    return centred * rate, rate


def norm_back(grad, gain, xhat, rate):
    scaled = grad * gain
    first = jnp.mean(scaled, axis=-1, keepdims=True)
    second = jnp.mean(scaled * xhat, axis=-1, keepdims=True)
    return rate * (scaled - first - xhat * second)


def column_sums(values):
    return jnp.sum(values, axis=0, keepdims=True)


def seg_means(values):
    rows, width = values.shape
    return jnp.sum(values.reshape(rows // SEG, SEG, width), axis=1) * (1.0 / SEG)


def near_bit():
    return lax.axis_index("head") % 2


def far_bit():
    return lax.axis_index("head") // 2


def my_rows(rows):
    half = rows // 2
    return pl.ds(pl.multiple_of(near_bit() * half, half), half)


def lanes_of(place, width, start=0):
    at = place + near_bit() - 2 * place * near_bit()
    return pl.ds(pl.multiple_of(start + at * width, width), width)


def half_rows(place, half):
    return pl.ds(pl.multiple_of(place * half, half), half)


def full(shape):
    return pl.BlockSpec(shape, lambda *_: (0,) * len(shape))


class Steps:
    def __init__(self):
        self.held = []
        self.us = 0.1

    def call(self, kernel, name, outs, args, specs=None, scratch=(), vmem=32, copies=0, far=(), far_outs=()):
        specs = dict(specs or {})
        given, made, held = len(args), len(outs), tuple(self.held)
        token = bool(far_outs)
        somewhere = pl.BlockSpec(memory_space=pl.ANY)
        in_hbm = pl.BlockSpec(memory_space=pltpu.HBM)

        def body(*refs):
            ins, rest = refs[:given], refs[given + len(held) :]
            if token:
                rest[made][...] = jnp.zeros(rest[made].shape, F32)
            kernel(*ins, *rest[:made], *rest[made + token :])

        args = [pltpu.with_memory_space_constraint(a, pltpu.HBM) if i in far else a for i, a in enumerate(args)]
        out_specs = [in_hbm if i in far_outs else full(shape) for i, shape in enumerate(outs)]
        out_shape = [
            pltpu.HBM(shape, F32) if i in far_outs else jax.ShapeDtypeStruct(shape, F32) for i, shape in enumerate(outs)
        ]
        if token:
            out_specs.append(full((1, 128)))
            out_shape.append(jax.ShapeDtypeStruct((1, 128), F32))
        out = pl.pallas_call(
            body,
            name=name,
            grid=(1,),
            in_specs=[in_hbm if i in far else specs.get(i, full(a.shape)) for i, a in enumerate(args)]
            + [somewhere] * len(held),
            out_specs=out_specs,
            out_shape=out_shape,
            scratch_shapes=[pltpu.VMEM(shape, F32) for shape in scratch]
            + ([pltpu.SemaphoreType.DMA((copies,))] if copies else []),
            compiler_params=pltpu.CompilerParams(vmem_limit_bytes=vmem * MIB),
            cost_estimate=pl.CostEstimate(flops=int(self.us * 5.18e8), bytes_accessed=0, transcendentals=0),
        )(*args, *held)
        self.held = [out[-1]]
        return out[:made]


def copy_all(pairs, sems):
    copies = [pltpu.make_async_copy(a, b, sems.at[i]) for i, (a, b) in enumerate(pairs)]
    for copy in copies:
        copy.start()
    return copies


def pack_kernel(wq, wk, wv, wo, bq, bv, bi, frames, out, edge, sems):
    rows, width = wq.shape
    out[rows:] = jnp.zeros((out.shape[0] - rows, out.shape[1]), F32)
    pairs = [(w, out.at[pl.ds(0, rows), pl.ds(i * width, width)]) for i, w in enumerate((wq, wk, wv))]
    for at in range(0, wo.shape[1], width):
        pairs.append((wo.at[:, pl.ds(at, width)], out.at[pl.ds(at, width), pl.ds(3 * width, width)]))
    pairs += [(b, out.at[pl.ds(rows, 1), pl.ds(i * width, width)]) for i, b in ((0, bq), (2, bv))]
    pairs.append((bi, out.at[pl.ds(rows + 1, 1), pl.ds(0, bi.shape[1])]))
    start = pl.multiple_of((1 - near_bit()) * (frames.shape[1] - BEFORE), BEFORE)
    pairs += [(frames.at[m, pl.ds(start, BEFORE)], edge.at[m]) for m in range(frames.shape[0])]
    for copy in copy_all(pairs, sems):
        copy.wait()


def norm_kernel(
    frames, gain, shift, wi, wu, wo, cotangent,
    x_ref, xhat_ref, rate_ref, normed_ref, wi_ref, wu_ref, wo_ref, g_0, g_1, before, ahead, params, sems,
):
    micros, half, _ = x_ref.shape
    rows = frames.shape[1]
    pairs = [(gain, params.at[pl.ds(0, 1)]), (shift, params.at[pl.ds(8, 1)])]
    pairs += [(frames.at[m, my_rows(rows)], x_ref.at[m]) for m in range(micros)]
    pairs += [(frames.at[m, pl.ds(half - BEFORE, BEFORE)], before.at[m]) for m in range(micros)]
    pairs += [(frames.at[m, pl.ds(half, AHEAD)], ahead.at[m]) for m in range(micros)]
    pairs += [(wo, wo_ref), (wi, wi_ref), (wu, wu_ref)]
    pairs += [(cotangent.at[m, my_rows(rows)], g) for m, g in enumerate((g_0, g_1))]
    copies = copy_all(pairs, sems)
    for copy in copies[:2]:
        copy.wait()
    for micro in range(micros):
        copies[2 + micro].wait()
        xhat, rate = normalise(x_ref[micro])
        xhat_ref[micro] = xhat
        normed_ref[micro] = xhat * params[0:1] + params[8:9]
        rate_ref[micro] = jnp.broadcast_to(rate, (half, rate_ref.shape[2]))
    for copy in copies[2 + micros :]:
        copy.wait()


def project_kernel(normed, own, pair, g1, s1, g2, s2, bo, bi, bu, q_ref, kv_ref, w_ref, bias, rows_ref, sems):
    micros, half, wide = q_ref.shape
    features = normed.shape[2]
    width = own.shape[1] // 4
    copies = copy_all([(v, rows_ref.at[i]) for i, v in enumerate((g1, s1, g2, s2, bo, bi, bu))], sems)
    for number in range(3):
        at = slice(number * width, (number + 1) * width)
        for place, source in enumerate((own, pair)):
            lanes = lanes_of(place, width, 2 * number * width)
            w_ref[:, lanes] = source[:features, at]
            bias[:, lanes] = source[features : features + 1, at]
    for micro in range(micros):
        out = mm(normed[micro], w_ref[...]) + bias[...]
        q_ref[micro] = out[:, :wide]
        kv_ref[micro] = out[:, wide:]
    for copy in copies:
        copy.wait()


def edges_kernel(edge, before, ahead, params, w_ref, bias, xhat_ref, normed_ref, kv_ref):
    near = near_bit()
    wide = w_ref.shape[1] // 3
    for micro in range(edge.shape[0]):
        first = jnp.where(near == 0, edge[micro], before[micro])
        last = jnp.where(near == 0, ahead[micro], edge[micro, :AHEAD])
        xhat, _ = normalise(jnp.concatenate([first, last], axis=0))
        normed = xhat * params[FIRST_GAIN] + params[FIRST_SHIFT]
        xhat_ref[micro] = xhat
        normed_ref[micro] = normed
        kv_ref[micro] = mm(normed, w_ref[:, wide:]) + bias[:, wide:]


def fill_keys(kv, edge, kx, sx):
    length = kv.shape[0]
    kx[BEFORE : BEFORE + length] = kv
    segs = length // SEG
    sx[SUMS : SUMS + segs] = seg_means(kv)
    if edge is not None:
        kx[:BEFORE] = edge[:BEFORE]
        kx[BEFORE + length :] = edge[BEFORE:]
        sx[: SUMS - MEM] = jnp.zeros((SUMS - MEM, kv.shape[1]), F32)
        sx[SUMS - MEM : SUMS] = seg_means(edge[:BEFORE])
        sx[SUMS + segs :] = jnp.zeros((sx.shape[0] - SUMS - segs, kv.shape[1]), F32)


def summary_start(block):
    return (block * (BLOCK // SEG) + SUMS - MEM) // SUMS * SUMS


def frame_rows(block):
    start = BEFORE - CACHE + block * BLOCK
    return slice(start, start + WIN)


def key_window(kx, sx, block, lanes):
    start = summary_start(block)
    rows = [kx[frame_rows(block), lanes], sx[start : start + SWIN, lanes]]
    return jnp.concatenate(rows + [jnp.zeros((KEYS - WIN - SWIN, PAIR), F32)], axis=0)


def by_head(values):
    first = lax.broadcasted_iota(jnp.int32, values.shape, 1) < HEAD_DIM
    return jnp.concatenate([jnp.where(first, values, 0.0), jnp.where(first, 0.0, values)], axis=0)


def side_by_side(values):
    rows = values.shape[0] // 2
    first = lax.broadcasted_iota(jnp.int32, (rows, values.shape[1]), 1) < HEAD_DIM
    return jnp.where(first, values[:rows], values[rows:])


def owner_of(segment, bounds):
    owner = jnp.where(segment < 0, -1, 0)
    for bound in bounds:
        owner = owner + (segment >= bound).astype(jnp.int32)
    return owner


def visible(block, base, bounds):
    row = lax.broadcasted_iota(jnp.int32, (2 * BLOCK, 1), 0) % BLOCK
    column = lax.broadcasted_iota(jnp.int32, (1, KEYS), 1)
    query_seg = block * (BLOCK // SEG) + row // SEG
    frame = block * BLOCK - CACHE + column
    is_frame = column < WIN
    summary = summary_start(block) - SUMS + column - WIN
    key_seg = jnp.where(is_frame, (frame + CACHE) // SEG - CACHE // SEG, summary)
    key_seg = jnp.where(column < WIN + SWIN, key_seg, -(1 << 20))
    inside = (frame >= query_seg * SEG - LC) & (frame < query_seg * SEG + SEG + RC)
    near = (key_seg >= query_seg - MEM) & (key_seg < query_seg)
    seen = (is_frame & inside) | ((column >= WIN) & near)
    return seen & (owner_of(key_seg + base, bounds) == owner_of(query_seg + base, bounds))


def bounds_of(counts, micro):
    bounds, total = [], 0
    for utterance in range(counts.shape[1]):
        total = total + counts[micro, utterance]
        bounds.append(total)
    return bounds


def first_segment(length):
    return (lax.axis_index("tm") * 2 + near_bit()) * (length // SEG)


def block_rows(block):
    return slice(block * BLOCK, (block + 1) * BLOCK)


def attend_block(block, seen, query, kx, sx, keep, put):
    width = query.shape[1]
    for pair in range(width // PAIR):
        lanes = slice(pair * PAIR, (pair + 1) * PAIR)
        value_lanes = slice(width + pair * PAIR, width + (pair + 1) * PAIR)
        scores = mm(by_head(query[:, lanes] * HEAD_DIM ** (-0.5)), key_window(kx, sx, block, lanes), 1, 1)
        scores = jnp.where(seen, scores, MASKED)
        weights = jnp.exp(scores - jnp.max(scores, axis=-1, keepdims=True))
        weights = weights / jnp.sum(weights, axis=-1, keepdims=True)
        keep(pair, weights)
        put(lanes, side_by_side(mm(weights, key_window(kx, sx, block, value_lanes))))


def attend_inner_kernel(counts, q_ref, kv_ref, mix_0, mix_1, p_ref, kx, sx):
    _, length, _ = q_ref.shape
    base = first_segment(length)
    for micro, mix_ref in enumerate((mix_0, mix_1)):
        fill_keys(kv_ref[micro], None, kx, sx)
        bounds = bounds_of(counts, micro)
        for number, block in enumerate(range(1, length // BLOCK - 1)):
            def keep(pair, weights):
                p_ref[micro, number, pair] = weights

            def put(lanes, values):
                mix_ref[block_rows(number), lanes] = values

            seen = visible(block, base, bounds)
            attend_block(block, seen, q_ref[micro, block_rows(block)], kx, sx, keep, put)


def attend_outer_kernel(micro, counts, q_ref, kv_ref, edge, mix_ref, p_ref, kx, sx):
    _, length, _ = q_ref.shape
    base = first_segment(length)
    fill_keys(kv_ref[micro], edge[micro], kx, sx)
    bounds = bounds_of(counts, micro)
    for number, block in enumerate((0, length // BLOCK - 1)):
        def keep(pair, weights):
            p_ref[number, pair] = weights

        def put(lanes, values):
            mix_ref[block_rows(number), lanes] = values

        seen = visible(block, base, bounds)
        attend_block(block, seen, q_ref[micro, block_rows(block)], kx, sx, keep, put)


def fill_rows(target, lanes, inner, outer):
    length = inner.shape[0] + outer.shape[0]
    target[:BLOCK, lanes] = outer[:BLOCK]
    target[BLOCK : length - BLOCK, lanes] = inner[...]
    target[length - BLOCK : length, lanes] = outer[BLOCK:]


def back_kernel(
    micro, grad_ref, mid_ref, g_ref, params, wo_here, mix_inner, mix_outer, q_ref, kv_ref, edge, p_inner, p_outer,
    dmid_ref, dq_ref, dkv_ref, dwo_own, dwo_pair, vec_ref,
    kx, sx, dsx, dmix, mix, dwo,
):
    _, length, width = q_ref.shape
    near_width = dwo_own.shape[1]
    grad = grad_ref[...]
    xhat, rate = normalise(mid_ref[...])
    dmid = g_ref[...] + norm_back(grad, params[SECOND_GAIN], xhat, rate)
    dmid_ref[...] = dmid
    vec_ref[0:1] = column_sums(dmid)
    vec_ref[1:2] = column_sums(grad * xhat)
    vec_ref[2:3] = column_sums(grad)
    dmix[...] = mm(dmid, wo_here[...], 1, 1)
    fill_rows(mix, slice(None), mix_inner, mix_outer)
    dwo[...] = mm(dmid, mix[...], 0, 0)
    dwo_own[...] = dwo[:, lanes_of(0, near_width)]
    dwo_pair[...] = dwo[:, lanes_of(1, near_width)]
    fill_keys(kv_ref[micro], edge[micro], kx, sx)
    dkv_ref[...] = jnp.zeros_like(dkv_ref)
    dsx[...] = jnp.zeros_like(dsx)
    for block in range(length // BLOCK):
        start = summary_start(block)
        rows, frames, sums = block_rows(block), frame_rows(block), slice(start, start + SWIN)
        for pair in range(width // PAIR):
            lanes = slice(pair * PAIR, (pair + 1) * PAIR)
            value_lanes = slice(width + pair * PAIR, width + (pair + 1) * PAIR)
            inside = 0 < block < length // BLOCK - 1
            weights = p_inner[micro, block - 1, pair] if inside else p_outer[min(block, 1), pair]
            grad = by_head(dmix[rows, lanes])
            dweights = mm(grad, key_window(kx, sx, block, value_lanes), 1, 1)
            dscores = weights * (dweights - jnp.sum(dweights * weights, axis=-1, keepdims=True))
            dquery = side_by_side(mm(dscores, key_window(kx, sx, block, lanes)))
            dq_ref[rows, lanes] = dquery * HEAD_DIM ** (-0.5)
            dkeys = mm(dscores, by_head(q_ref[micro, rows, lanes] * HEAD_DIM ** (-0.5)), 0, 0)
            dvalues = mm(weights, grad, 0, 0)
            dkv_ref[frames, lanes] += dkeys[:WIN]
            dkv_ref[frames, value_lanes] += dvalues[:WIN]
            dsx[sums, lanes] += dkeys[WIN : WIN + SWIN]
            dsx[sums, value_lanes] += dvalues[WIN : WIN + SWIN]
    count = BEFORE + length
    segs = count // SEG
    spread = dsx[SUMS - MEM : SUMS - MEM + segs] * (1.0 / SEG)
    spread = jnp.broadcast_to(spread[:, None, :], (segs, SEG, 2 * width))
    dkv_ref[:count] += spread.reshape(count, 2 * width)


def feed_kernel(
    micro, own_inner, own_outer, far_inner, far_outer, wo_here, wo_far, wo_far_pair, x_ref, g_ref, params, pair, wi_own, wi_pair, wu_own, wu_pair,
    n2_ref, h_ref, dpre_ref, mid_ref, part_ref,
    mix, wo,
):
    width = own_inner.shape[1] // 2
    features, hidden = wi_own.shape
    far = far_bit()
    here = pl.multiple_of(far * 2 * width, 2 * width)
    there = pl.multiple_of((1 - far) * 2 * width, 2 * width)
    fill_rows(mix, pl.ds(here, 2 * width), own_inner, own_outer)
    fill_rows(mix, pl.ds(there, 2 * width), far_inner, far_outer)
    wo[pl.ds(here, 2 * width)] = wo_here[...]
    wo[lanes_of(0, width, there)] = wo_far[...]
    wo[lanes_of(1, width, there)] = wo_far_pair[...]
    middle = x_ref[micro] + mm(mix[...], wo[...]) + params[OUT_BIAS]
    mid_ref[...] = middle
    xhat, _ = normalise(middle)
    normed = xhat * params[SECOND_GAIN] + params[SECOND_SHIFT]
    n2_ref[...] = normed
    part = None
    for place, (wi, wu, bias) in enumerate(((wi_own, wu_own, params[INNER_BIAS][:, :hidden]), (wi_pair, wu_pair, pair[features + 1 : features + 2, :hidden]))):
        at = slice(place * hidden, (place + 1) * hidden)
        pre = mm(normed, wi[...]) + bias
        phi = 0.5 + 0.5 * lax.erf(pre * (0.5**0.5))
        h_ref[:, at] = pre * phi
        slope = phi + pre * (jnp.exp(-0.5 * pre * pre) * 0.3989422804014327)
        dpre = mm(g_ref[...], wu[...], 1, 1) * slope
        dpre_ref[:, at] = dpre
        step = mm(dpre, wi[...], 1, 1)
        part = step if part is None else part + step
    part_ref[...] = part


def put_rows(value, outs):
    at = 0
    for out in outs:
        count = out.shape[0]
        out[...] = value[at : at + count]
        at += count


def inner_weights_kernel(n2_0, n2_1, d_0, d_1, own_ref, *rest):
    *pair, vec_ref = rest
    hidden = own_ref.shape[1]
    for place, outs in enumerate(((own_ref,), pair)):
        at = slice(place * hidden, (place + 1) * hidden)
        put_rows(mm(n2_0[...], d_0[:, at], 0, 0) + mm(n2_1[...], d_1[:, at], 0, 0), outs)
        vec_ref[place : place + 1] = column_sums(d_0[:, at]) + column_sums(d_1[:, at])


def outer_weights_kernel(h_0, h_1, g_0, g_1, own_ref, *rest):
    *pair, vec_ref = rest
    hidden = own_ref.shape[0]
    for place, outs in enumerate(((own_ref,), pair)):
        at = slice(place * hidden, (place + 1) * hidden)
        value = mm(h_0[:, at], g_0[...], 0, 0) + mm(h_1[:, at], g_1[...], 0, 0)
        for out_ref in outs:
            out_ref[:hidden] = value
            if out_ref.shape[0] > hidden:
                out_ref[hidden:] = jnp.zeros((out_ref.shape[0] - hidden, value.shape[1]), F32)
    vec_ref[...] = column_sums(g_0[...]) + column_sums(g_1[...])


def feed_out_kernel(h_0, h_1, wu_own, wu_pair, out_ref):
    hidden = wu_own.shape[0]
    rows = h_0.shape[0]
    for micro, h_ref in enumerate((h_0, h_1)):
        part = mm(h_ref[:, :hidden], wu_own[...]) + mm(h_ref[:, hidden:], wu_pair[...])
        out_ref[micro * rows : (micro + 1) * rows] = part


def out_half_kernel(mid_0, mid_1, part, far, params, out):
    rows = mid_0.shape[0]
    for micro, mid_ref in enumerate((mid_0, mid_1)):
        at = slice(micro * rows, (micro + 1) * rows)
        out[at] = mid_ref[...] + (part[at] + far[at]) + params[OUTER_BIAS]


def project_back_kernel(
    dq_0, dkv_0, dq_1, dkv_1, xhat, xhat_edge, w_ref, part_ref, pair_ref, beyond_ref, vec_ref, work
):
    near = near_bit()
    length, wide = dq_0.shape
    own = slice(BEFORE, BEFORE + length)
    gain, shift = 0.0, 0.0
    for micro, (dq, dkv) in enumerate(((dq_0, dkv_0), (dq_1, dkv_1))):
        work[...] = mm(dkv[...], w_ref[:, wide:], 1, 1)
        work[own] += mm(dq[...], w_ref[:, :wide], 1, 1)
        part_ref[micro * length : (micro + 1) * length] = work[own]
        before = work[:BEFORE]
        ahead = jnp.concatenate([work[BEFORE + length :], jnp.zeros((BEFORE - AHEAD, work.shape[1]), F32)], axis=0)
        pair_ref[micro] = jnp.where(near == 0, ahead, before)
        beyond_ref[micro] = jnp.where(near == 0, before, ahead)
        gain = gain + column_sums(work[own] * xhat[micro]) + column_sums(work[:BEFORE] * xhat_edge[micro, :BEFORE])
        gain = gain + column_sums(work[BEFORE + length :] * xhat_edge[micro, BEFORE:])
        shift = shift + column_sums(work[...])
    vec_ref[0:1] = gain
    vec_ref[1:2] = shift


def edge_add_kernel(part, pair, beyond, out):
    out[...] = part[...]
    near = near_bit()
    micros = pair.shape[0]
    length = part.shape[0] // micros
    for micro in range(micros):
        end = (micro + 1) * length
        out[end - BEFORE : end] += jnp.where(near == 0, pair[micro], beyond[micro])
        out[end - length : end - length + AHEAD] += jnp.where(near == 0, beyond[micro, :AHEAD], pair[micro, :AHEAD])


def project_weights_kernel(
    normed, normed_edge, dq_0, dq_1, dkv_0, dkv_1, wo_own_0, wo_own_1, wo_pair_0, wo_pair_1, mid_0, mid_1, first, vec_outer, vec_inner,
    own_0, own_1, rows_ref, pair_0, pair_1, sums, row,
):
    features = normed.shape[2]
    width = wo_own_0.shape[1]
    hidden = vec_inner.shape[1]
    length, wide = dq_0.shape
    own, after = slice(BEFORE, BEFORE + length), slice(BEFORE + length, None)
    edges = jnp.concatenate([dkv_0[:BEFORE], dkv_0[after], dkv_1[:BEFORE], dkv_1[after]], axis=0)
    normed_edges = jnp.concatenate([normed_edge[0], normed_edge[1]], axis=0)
    queries = mm(normed[0], dq_0[...], 0, 0) + mm(normed[1], dq_1[...], 0, 0)
    keyvals = mm(normed[0], dkv_0[own], 0, 0) + mm(normed[1], dkv_1[own], 0, 0) + mm(normed_edges, edges, 0, 0)
    sums[:, :wide] = queries
    sums[:, wide:] = keyvals
    row[:, :wide] = column_sums(dq_0[...]) + column_sums(dq_1[...])
    row[:, wide:] = column_sums(dkv_0[...]) + column_sums(dkv_1[...])
    rows_ref[0:3] = (mid_0[...] + mid_1[...]) * 0.5
    rows_ref[3:5] = first[...]
    rows_ref[5:6] = vec_outer[...] * 0.5
    rows_ref[6:] = jnp.zeros((2, features), F32)
    half = pair_0.shape[0]
    pair_1[half : half + 6] = rows_ref[0:6]
    pair_1[half + 6 :] = jnp.zeros((2, features), F32)
    for place, (out_ref, at) in enumerate(((rows_ref, 6), (pair_1, half + 6))):
        for number in range(3):
            lanes = slice(number * width, (number + 1) * width)
            out_ref[at : at + 1, lanes] = row[:, lanes_of(place, width, 2 * number * width)]
        out_ref[at + 1 : at + 2, :hidden] = vec_inner[place : place + 1]
    for place, (outs, wo_0, wo_1) in enumerate((((own_0, own_1), wo_own_0, wo_own_1), ((pair_0, pair_1), wo_pair_0, wo_pair_1))):
        for out_ref, rows in zip(outs, (slice(half), slice(half, features)), strict=True):
            for number in range(3):
                lanes = slice(number * width, (number + 1) * width)
                out_ref[:half, lanes] = sums[rows, lanes_of(place, width, 2 * number * width)]
            out_ref[:half, 3 * width :] = wo_0[rows] + wo_1[rows]


def frames_back_kernel(a_ref, b_ref, xhat, rate, dmid_0, dmid_1, params, out):
    rows = dmid_0.shape[0]
    for micro, dmid_ref in enumerate((dmid_0, dmid_1)):
        at = slice(micro * rows, (micro + 1) * rows)
        grad = norm_back(a_ref[at] + b_ref[at], params[FIRST_GAIN], xhat[micro], rate[micro, :, :1])
        out[at] = dmid_ref[...] + grad


def place_kernel(own, pair, out, sems):
    micros, half = out.shape[0], out.shape[1] // 2
    near = near_bit()
    pairs = []
    for micro in range(micros):
        rows = pl.ds(micro * half, half)
        pairs.append((own.at[rows], out.at[micro, half_rows(near, half)]))
        pairs.append((pair.at[rows], out.at[micro, half_rows(1 - near, half)]))
    for copy in copy_all(pairs, sems):
        copy.wait()


def place_of(bit):
    return lax.axis_index("tm") // bit % 2


def add_pieces(out, a_ref, pieces, rows_ref=None, new_rows=None):
    count, at = a_ref.shape[0], 0
    if not pieces:
        out[...] = a_ref[...]
        if new_rows is not None:
            new_rows[...] = rows_ref[...]
    for piece in pieces:
        take = min(piece.shape[0], count - at)
        if take:
            out[at : at + take] = a_ref[at : at + take] + piece[:take]
        if take < piece.shape[0] and new_rows is not None:
            new_rows[...] = rows_ref[...] + piece[take:]
        at += take


def add_split_kernel(bits, counts, rows, *refs):
    total = len(bits)
    values, refs = refs[:total], refs[total:]
    rows_ref, refs = (refs[0], refs[1:]) if rows else (None, refs)
    pieces = []
    for count in counts:
        pieces.append(refs[:count])
        refs = refs[count:]
    kept, sent, refs = refs[:total], refs[total : 2 * total], refs[2 * total :]
    new_rows, work = (refs[0], refs[1]) if rows else (None, refs[0])
    for number, bit in enumerate(bits):
        small = (rows_ref, new_rows) if rows and number == 0 else ()
        half = kept[number].shape[0]
        add_pieces(work, values[number], pieces[number], *small)
        place = place_of(bit)
        kept[number][...] = work[half_rows(place, half)]
        sent[number][:half] = work[half_rows(1 - place, half)]
        if small:
            sent[number][half:] = new_rows[...]


def last_kernel(rows, a_ref, *refs):
    rows_ref, refs = (refs[0], refs[1:]) if rows else (None, refs)
    b_ref, out_ref = refs
    half = a_ref.shape[0]
    out_ref[:half] = a_ref[...] + b_ref[:half]
    if rows:
        out_ref[half:] = rows_ref[...] + b_ref[half:]


def stack_kernel(rows, a_0, a_1, *refs):
    rows_ref, refs = (refs[0], refs[1:]) if rows else (None, refs)
    b_0, b_1, out_ref = refs
    half = a_0.shape[0]
    out_ref[:half] = a_0[...] + b_0[:half]
    out_ref[half : 2 * half] = a_1[...] + b_1[...]
    if rows:
        out_ref[2 * half :] = rows_ref[...] + b_0[half:]


def add_whole_kernel(a_ref, b_ref, *outs):
    at = 0
    for out in outs:
        count = out.shape[0]
        out[...] = a_ref[at : at + count] + b_ref[at : at + count]
        at += count


def join_kernel(bits, *refs):
    total = len(bits)
    for bit, mine, theirs, out in zip(bits, refs[:total], refs[total : 2 * total], refs[2 * total :], strict=True):
        half = mine.shape[0]
        place = place_of(bit)
        out[half_rows(place, half)] = mine[...]
        out[half_rows(1 - place, half)] = theirs[...]


def join_out_kernel(bit, mine, theirs, out, sems):
    half = mine.shape[0]
    place = place_of(bit)
    for copy in copy_all([(mine, out.at[half_rows(place, half)]), (theirs, out.at[half_rows(1 - place, half)])], sems):
        copy.wait()


def join_heads_kernel(bits, *refs):
    *parts, wq, wk, wv, wo, work = refs
    width = wq.shape[1]
    half = parts[0].shape[0]
    place = place_of(bits[0])
    for number in range(2):
        for where, part in zip((place, 1 - place), parts[2 * number : 2 * number + 2], strict=True):
            rows = pl.ds(pl.multiple_of(2 * number * half + where * half, half), half)
            for heads, out in enumerate((wq, wk, wv, work)):
                out[rows, :] = part[:, heads * width : (heads + 1) * width]
    wo[...] = work[...].T


def small_kernel(rows, far, outs):
    width = outs[-3].shape[1]
    for number, out in enumerate(outs[:6]):
        out[...] = rows[number : number + 1] + far[number : number + 1]
    outs[6][...] = rows[6:7, :width]
    outs[7][...] = rows[6:7, 2 * width : 3 * width]
    outs[8][...] = rows[7:8, : outs[8].shape[1]]


def finish_kernel(bits, rows, far, *refs):
    count = 2 * len(bits)
    small_kernel(rows, far, refs[count : count + 9])
    join_heads_kernel(bits, *refs[:count], *refs[count + 9 :])


def swap(value, axis, bit):
    size = lax.axis_size(axis)
    return lax.ppermute(value, axis, [(i, i ^ bit) for i in range(size)])


def swap_near(parts):
    return [swap(part, "head", 1) for part in parts]


def swap_edges(value, back):
    size, group = lax.axis_size("tm"), lax.axis_size("head")
    pairs = []
    for source in range(size):
        for place in range(group):
            target = source + (1 - 2 * (place % 2)) * (-1 if back else 1)
            if 0 <= target < size:
                pairs.append((source * group + place, target * group + (place ^ 1 if back else place)))
    return lax.ppermute(value, ("tm", "head"), pairs)


class SumsOverTm:
    def __init__(self, run, a, b, rows=None, joins=None):
        bits = [1 << i for i in range(lax.axis_size("tm").bit_length() - 1)]
        self.run, self.values, self.got, self.ones = run, list(a), [list(v) for v in b], []
        self.rows = [] if rows is None else [rows]
        self.apart = [(bits[1], bits[0]), (bits[0], bits[1])]
        self.together, self.last = bits[2:-1], bits[-1]
        self.joins = joins
        if len(a) == 1:
            self.todo = [("split", (bit,)) for bit in bits[:-1]] + [("last",), ("add",)]
            self.todo += [("join", (bit,)) for bit in (*reversed(self.together), joins[0])]
            self.step()
            return
        self.todo = [("split", pair) for pair in self.apart]
        self.todo.append(("stack",))
        self.todo += [("split", (bit,)) for bit in self.together] + [("last",)] * bool(self.together)
        self.todo.append(("add",))
        self.todo += [("join", (bit,)) for bit in reversed(self.together)] + [("part",)] * bool(self.together)
        self.todo.append(("join", self.apart[1]))
        self.step()

    def step(self):
        run, values = self.run, self.values
        kind, *rest = self.todo.pop(0)
        features = values[0].shape[1]
        count = values[0].shape[0]
        more = sum(v.shape[0] for v in self.rows)
        has_rows = bool(self.rows)
        shape = lambda rows: (rows, features)
        got = [piece for pieces in self.got for piece in pieces]
        if kind == "split":
            (bits,) = rest
            half = count // 2
            extra = [more] + [0] * (len(bits) - 1)
            out = run.call(
                functools.partial(add_split_kernel, bits, [len(v) for v in self.got], has_rows), "add_split",
                [shape(half)] * len(bits) + [shape(half + e) for e in extra] + [v.shape for v in self.rows],
                (*values, *self.rows, *got), scratch=[shape(count)],
            )
            self.values, messages, self.rows = out[: len(bits)], out[len(bits) : 2 * len(bits)], out[2 * len(bits) :]
            self.got = [[swap(v, "tm", bit)] for v, bit in zip(messages, bits, strict=True)]
            return
        if kind in ("stack", "last"):
            if kind == "stack":
                (value,) = run.call(
                    functools.partial(stack_kernel, has_rows), "stack", [shape(2 * count + more)], (*values, *self.rows, *got)
                )
                count = 2 * count
            else:
                (value,) = run.call(
                    functools.partial(last_kernel, has_rows), "stack", [shape(count + more)], (*values, *self.rows, *got)
                )
            if kind == "stack" and self.together:
                self.values, self.rows = [value[:count]], [value[count:]] * has_rows
                self.values, self.got = self.values, [[]]
                return self.step()
            self.values, self.count = [value], count
            self.got = [[swap(value, "tm", self.last)]]
            return
        if kind == "add":
            parts = [self.count] if self.together or self.joins else [self.count // 2] * 2
            out = run.call(
                add_whole_kernel, "add", [shape(n) for n in parts] + [v.shape for v in self.rows], (*values, *got)
            )
            self.values, self.rows = out[: len(parts)], out[len(parts) :]
        elif kind == "join":
            (bits,) = rest
            self.values = run.call(
                functools.partial(join_kernel, bits), "join", [shape(2 * count)] * len(bits), (*values, *got)
            )
        elif kind == "part":
            self.values = [values[0][: count // 2], values[0][count // 2 :]]
        following = self.todo[0] if self.todo else ("join", self.joins[1:] if self.joins else self.apart[0])
        if following[0] == "part":
            return self.step()
        self.got = [[swap(v, "tm", bit)] for v, bit in zip(self.values, following[1], strict=True)]

    def join_one(self, number):
        if len(self.todo) != 1:
            return
        bits = self.todo[0][1]
        value = self.values[number]
        values, got = list(self.values), list(self.got)
        (values[number],) = self.run.call(
            functools.partial(join_kernel, bits[number : number + 1]), "join", [(2 * value.shape[0], value.shape[1])],
            (value, *got[number]),
        )
        got[number] = [swap(values[number], "tm", self.apart[0][number])]
        self.values, self.got = values, got
        self.ones.append(number)
        if len(self.ones) == 2:
            self.todo.pop()

    @property
    def joined(self):
        return not self.todo

    def halves(self, number):
        return self.apart[0][number], (self.values[number], *self.got[number])


ORDER = (
    ("pack", 8), ("norm", 4.8), ("project", 2.2), ("attend_inner", 11), ("edges", 1), ("hand_on", 0.5),
    ("attend_outer0", 24), ("attend_outer1", 1), ("feed0", 18), ("feed1", 14), ("outer_weights", 6),
    ("inner_weights", 11), ("feed_out", 0.6), ("grad_sum0", 18), ("ffn", 11), ("back0", 6), ("grad_sum1", 2),
    ("back1", 0.5), ("ffn", 0.1), ("project_back", 1.8), ("project_weights", 2), ("ffn", 0.1), ("edge_add", 5),
    ("out_half", 5), ("heads0", 20), ("out_send", 20), ("heads1", 20), ("place_out", 1), ("heads0", 0.1),
    ("heads1", 0.1), ("heads0", 0.1), ("ffn", 0.1), ("frames_back", 0.1), ("heads1", 3), ("ffn_last1", 4),
    ("heads0", 16), ("heads1", 1), ("ffn_last0", 16), ("heads0", 16), ("place_frames", 0.1), ("heads1", 2),
    ("join_inner", 0.1), ("join_outer", 3), ("finish", 0.1),
)
PIECES = 1


def copy_kernel(source, target):
    target[...] = source[...]


def hand_on_kernel(own, pair, far, here, far_copy):
    far_copy[...] = far[...]
    width = far.shape[0]
    for near, source in enumerate((own, pair)):
        for at in range(0, far.shape[1], width):
            lanes = slice(3 * width, 4 * width)
            here[lanes_of(near, width), at : at + width] = source[at : at + width, lanes]


class Layer:
    def __init__(
        self, frames, cotangent, seg_counts, query_weight, query_bias, key_weight, value_weight, value_bias,
        out_weight, out_bias, first_gain, first_shift, second_gain, second_shift,
        inner_weight, inner_bias, outer_weight, outer_bias,
    ):
        self.frames, self.cotangent, self.counts = frames, cotangent, seg_counts
        self.projections = (query_weight, key_weight, value_weight)
        self.weights = (inner_weight, outer_weight, out_weight)
        row = lambda v: v.reshape(1, v.shape[0])
        self.bq, self.bv, self.bo, self.bi, self.bu = map(row, (query_bias, value_bias, out_bias, inner_bias, outer_bias))
        self.g1, self.s1, self.g2, self.s2 = map(row, (first_gain, first_shift, second_gain, second_shift))
        micros, shard, features = frames.shape
        self.micros, self.features = micros, features
        self.width, self.hidden = query_weight.shape[1], inner_weight.shape[1]
        self.length = shard // 2
        self.segs, self.blocks, self.pairs = self.length // SEG, self.length // BLOCK, 2 * self.width // PAIR
        self.big = (self.length, features)
        self.each = (micros, self.length)
        self.quarter = (self.length // 2, features)
        self.square = (2 * BLOCK, KEYS)
        self.around = BEFORE + self.length + AHEAD
        self.key_scratch = [(self.around, 4 * self.width), (SUMS + self.segs + SUMS, 4 * self.width)]
        self.run = Steps()
        self.smem = pl.BlockSpec(memory_space=pltpu.SMEM)
        pairs = [None] * micros
        self.mix_outer, self.far_outer, self.p_outer, self.fed, self.dn2 = (list(pairs) for _ in range(5))
        self.back_of = list(pairs)
        self.sums = {}
        self.heads_names = ("heads0", "heads1")

    def pack(self):
        args = (*self.projections, self.weights[2], self.bq, self.bv, self.bi, self.frames)
        self.own, edge = self.run.call(
            pack_kernel, "pack", [(self.features + 8, 4 * self.width), (self.micros, BEFORE, self.features)], args,
            copies=6 + self.features // self.width + self.micros, far=range(8),
        )
        self.pair = swap(self.own, "head", 1)
        self.edge = swap_edges(edge, False)

    def norm(self):
        each, features, micros = self.each, self.features, self.micros
        wi, wu, wo = self.weights
        (self.x, self.xhat, self.rate, self.normed, self.wi, self.wu, self.wo, *self.g, self.before, self.ahead) = self.run.call(
            norm_kernel, "norm",
            [each + (features,)] * 2 + [each + (128,), each + (features,), wi.shape, wu.shape, wo.shape, self.big, self.big,
             (micros, BEFORE, features), (micros, AHEAD, features)],
            (self.frames, self.g1, self.s1, wi, wu, wo, self.cotangent),
            scratch=[(16, features)], copies=4 * micros + 5, far=range(7),
        )
        self.wo_far = swap(self.wo, "head", 2)
        self.wi_pair, self.wu_pair = (swap(v, "head", 1) for v in (self.wi, self.wu))

    def project(self):
        each, features, width = self.each, self.features, self.width
        args = (self.normed, self.own, self.pair, self.g1, self.s1, self.g2, self.s2, self.bo, self.bi, self.bu)
        self.q, self.kv, self.w_all, self.bias, self.params = self.run.call(
            project_kernel, "project",
            [each + (2 * width,), each + (4 * width,), (features, 6 * width), (1, 6 * width), (7, 1, features)],
            args, copies=7, far=range(3, 10),
        )

    def edges(self):
        shape = (self.micros, BEFORE + AHEAD)
        self.xhat_edge, self.normed_edge, self.kv_edge = self.run.call(
            edges_kernel, "edges", [shape + (self.features,)] * 2 + [shape + (4 * self.width,)],
            (self.edge, self.before, self.ahead, self.params, self.w_all, self.bias),
        )

    def attend_inner(self):
        *self.mix_inner, self.p_inner = self.run.call(
            attend_inner_kernel, "attend_inner",
            [(self.length - 2 * BLOCK, 2 * self.width)] * 2 + [(self.micros, self.blocks - 2, self.pairs) + self.square],
            (self.counts, self.q, self.kv), {0: self.smem}, self.key_scratch,
        )
        self.far_inner = [swap(v, "head", 2) for v in self.mix_inner]

    def attend_outer(self, m):
        if m:
            self.run.held.append(self.far_inner[0])
        self.mix_outer[m], self.p_outer[m] = self.run.call(
            functools.partial(attend_outer_kernel, m), "attend_outer",
            [(2 * BLOCK, 2 * self.width), (2, self.pairs) + self.square],
            (self.counts, self.q, self.kv, self.kv_edge),
            {0: self.smem}, self.key_scratch,
        )
        self.far_outer[m] = swap(self.mix_outer[m], "head", 2)

    def hand_on(self):
        shape = self.wo_far.shape
        self.wo_here, far = self.run.call(
            hand_on_kernel, "hand_on", [(2 * shape[0], shape[1]), shape], (self.own, self.pair, self.wo_far)
        )
        self.wo_far_pair = swap(far, "head", 1)

    def feed(self, m):
        big, features, hidden = self.big, self.features, self.hidden
        *self.fed[m], part = self.run.call(
            functools.partial(feed_kernel, m), "feed", [big, (self.length, 2 * hidden), (self.length, 2 * hidden), big, big],
            (self.mix_inner[m], self.mix_outer[m], self.far_inner[m], self.far_outer[m], self.wo_here, self.wo_far, self.wo_far_pair, self.x, self.g[m], self.params,
             self.pair, self.wi, self.wi_pair, self.wu, self.wu_pair),
            scratch=[big, (features, features)],
        )
        self.dn2[m] = (part, swap(part, "head", 2))

    def inner_weights(self):
        features, hidden = self.features, self.hidden
        self.inner_own, *pair, self.vec_inner = self.run.call(
            inner_weights_kernel, "inner_weights",
            [(features, hidden)] + [(features // PIECES, hidden)] * PIECES + [(2, hidden)],
            (self.fed[0][0], self.fed[1][0], self.fed[0][2], self.fed[1][2]),
        )
        self.inner_pair = swap_near(pair)

    def outer_weights(self):
        features, hidden = self.features, self.hidden
        self.outer_own, *pair, self.vec_outer = self.run.call(
            outer_weights_kernel, "outer_weights",
            [(hidden, features), (hidden + 8, features), (1, features)],
            (self.fed[0][1], self.fed[1][1], *self.g),
        )
        self.outer_pair = swap_near(pair)

    def feed_out(self):
        (part,) = self.run.call(
            feed_out_kernel, "feed_out", [(self.micros * self.length, self.features)],
            (self.fed[0][1], self.fed[1][1], self.wu, self.wu_pair),
        )
        self.part = (part, swap(part, "head", 2))

    def out_half(self):
        (half,) = self.run.call(
            out_half_kernel, "out_half", [(self.micros * self.length, self.features)],
            (self.fed[0][3], self.fed[1][3], *self.part, self.params),
        )
        self.out = half

    def out_send(self):
        (half,) = self.run.call(copy_kernel, "out_send", [self.out.shape], (self.out,))
        self.out = (half, swap(half, "head", 1))

    def grad_sum(self, m):
        (self.dn2[m],) = self.run.call(add_whole_kernel, "grad_sum", [self.big], self.dn2[m])

    def back(self, m):
        length, width, features = self.length, self.width, self.features
        self.back_of[m] = self.run.call(
            functools.partial(back_kernel, m), "back",
            [self.big, (length, 2 * width), (self.around, 4 * width), (features, width), (features, width), (3, features)],
            (self.dn2[m], self.fed[m][3], self.g[m], self.params, self.wo_here, self.mix_inner[m], self.mix_outer[m], self.q, self.kv,
             self.kv_edge, self.p_inner, self.p_outer[m]),
            scratch=self.key_scratch + self.key_scratch[1:] + [(length, 2 * width)] * 2 + [(features, 2 * width)],
        )

    def pick(self, number):
        return [v[number] for v in self.back_of]

    def project_back(self):
        features, micros = self.features, self.micros
        (dq_0, dq_1), (dkv_0, dkv_1) = self.pick(1), self.pick(2)
        part, pair, beyond, self.vec_first = self.run.call(
            project_back_kernel, "project_back",
            [(micros * self.length, features)] + [(micros, BEFORE, features)] * 2 + [(2, features)],
            (dq_0, dkv_0, dq_1, dkv_1, self.xhat, self.xhat_edge, self.w_all), scratch=[(self.around, features)],
        )
        self.edges_back = (part, swap(pair, "head", 1), swap_edges(beyond, True))

    def edge_add(self):
        part = self.edges_back[0]
        (part,) = self.run.call(edge_add_kernel, "edge_add", [part.shape], self.edges_back)
        self.dn1 = (part, swap(part, "head", 2))

    def project_weights(self):
        features, width = self.features, self.width
        *self.heads_own, self.rows, a, b = self.run.call(
            project_weights_kernel, "project_weights",
            [(features // 2, 4 * width)] * 2 + [(8, features), (features // 2, 4 * width), (features // 2 + 8, 4 * width)],
            (self.normed, self.normed_edge, *self.pick(1), *self.pick(2), *self.pick(3), *self.pick(4), *self.pick(5),
             self.vec_first, self.vec_outer, self.vec_inner),
            scratch=[(features, 6 * width), (1, 6 * width)],
        )
        self.heads_pair = swap_near((a, b))

    def begin(self, name):
        if name in self.heads_names:
            number = self.heads_names.index(name)
            a, b = self.heads_own[number], self.heads_pair[number]
            return SumsOverTm(self.run, (a,), ((b,),), self.rows if number else None, (2, 1))
        return SumsOverTm(self.run, (self.outer_own, self.inner_own), (self.outer_pair, self.inner_pair))

    def sum(self, name):
        if name not in self.sums:
            self.sums[name] = self.begin(name)
        elif not self.sums[name].joined:
            self.sums[name].step()

    def ffn(self):
        self.sum("ffn")

    def heads(self, number):
        self.sum(self.heads_names[number])

    def ffn_last(self, number):
        self.sums["ffn"].join_one(number)

    def frames_back(self):
        (half,) = self.run.call(
            frames_back_kernel, "frames_back", [(self.micros * self.length, self.features)],
            (*self.dn1, self.xhat, self.rate, *self.pick(0), self.params),
        )
        self.grad = (half, swap(half, "head", 1))

    def place(self, name, halves):
        (out,) = self.run.call(
            place_kernel, name, [(self.micros, 2 * self.length, self.features)], halves, copies=2 * self.micros, far_outs=[0]
        )
        return out

    def place_out(self):
        self.layer_output = self.place("place_out", self.out)

    def place_frames(self):
        self.frames_grad = self.place("place_frames", self.grad)

    def join(self, name, number, shape):
        bit, parts = self.sums["ffn"].halves(number)
        (out,) = self.run.call(
            functools.partial(join_out_kernel, bit), name, [shape], parts, copies=2, far_outs=[0]
        )
        return out

    def settle(self, *names):
        while not all(self.sums[name].joined for name in names):
            for name in names:
                self.sum(name)

    def join_outer(self):
        self.settle("ffn", *self.heads_names)
        self.outer_grad = self.join("join_outer", 0, self.weights[1].shape)

    def join_inner(self):
        self.settle("ffn", *self.heads_names)
        self.inner_grad = self.join("join_inner", 1, self.weights[0].shape)

    def finish(self):
        features, width, hidden = self.features, self.width, self.hidden
        both = [self.sums[name] for name in self.heads_names]
        rows = both[1].rows[0]
        bits, parts = both[0].joins[::-1], [sums.halves(0)[1] for sums in both]
        out = self.run.call(
            functools.partial(finish_kernel, bits), "finish",
            [(1, features)] * 6 + [(1, width)] * 2 + [(1, hidden)] + [(features, width)] * 3 + [(width, features)],
            (rows, swap(rows, "head", 2), *parts[0], *parts[1]), scratch=[(features, width)],
        )
        bo, g2, s2, g1, s1, bu, bq, bv, bi = (v.reshape(v.shape[1]) for v in out[:9])
        wq, wk, wv, wo = out[9:]
        return (
            self.layer_output, self.frames_grad, wq, bq, wk, wv, bv, wo, bo, g1, s1, g2, s2, self.inner_grad, bi,
            self.outer_grad, bu,
        )


def per_device(*args):
    layer = Layer(*args)
    for step, us in ORDER:
        layer.run.us = us
        name = step.rstrip("0123456789")
        result = getattr(layer, name)(*(int(digit) for digit in step[len(name) :]))
    return result


def solution(mesh):
    in_specs = (
        P(None, "tm", None),
        P(None, "tm", None),
        P(),
        P(None, "head"),
        P("head"),
        P(None, "head"),
        P(None, "head"),
        P("head"),
        P("head", None),
        P(),
        P(),
        P(),
        P(),
        P(),
        P(None, "head"),
        P("head"),
        P("head", None),
        P(),
    )
    out_specs = (
        P(None, "tm", None),
        P(None, "tm", None),
        P(None, "head"),
        P("head"),
        P(None, "head"),
        P(None, "head"),
        P("head"),
        P("head", None),
        P(),
        P(),
        P(),
        P(),
        P(),
        P(None, "head"),
        P("head"),
        P("head", None),
        P(),
    )
    return jax.shard_map(
        per_device, mesh=mesh, in_specs=in_specs, out_specs=out_specs, check_vma=False
    )
```

```python
import functools

import jax
import jax.numpy as jnp
from jax import lax
from jax.experimental import pallas as pl
from jax.experimental.pallas import tpu as pltpu
from jax.sharding import PartitionSpec as P

HEAD_DIM = 64
SEG = 16
RC = 4
LC = 30
MEM = 4

EPSILON = 1e-05
MASKED = -1e30
F32 = jnp.float32

BEFORE = MEM * SEG
AHEAD = 8
CACHE = 32
SUMS = 8
BLOCK = 64
WIN = CACHE + BLOCK + AHEAD
SWIN = 16
KEYS = 128
FIRST_GAIN, FIRST_SHIFT, SECOND_GAIN, SECOND_SHIFT, OUT_BIAS, INNER_BIAS, OUTER_BIAS = range(7)
PAIR = 2 * HEAD_DIM
MIB = 1 << 20


def mm(left, right, left_dim=1, right_dim=0):
    return lax.dot_general(
        left,
        right,
        (((left_dim,), (right_dim,)), ((), ())),
        precision=lax.Precision.HIGH,
        preferred_element_type=F32,
    )


def normalise(values):
    centred = values - jnp.mean(values, axis=-1, keepdims=True)
    variance = jnp.mean(centred * centred, axis=-1, keepdims=True)
    rate = lax.rsqrt(variance + EPSILON)
    return centred * rate, rate


def norm_back(grad, gain, xhat, rate):
    scaled = grad * gain
    first = jnp.mean(scaled, axis=-1, keepdims=True)
    second = jnp.mean(scaled * xhat, axis=-1, keepdims=True)
    return rate * (scaled - first - xhat * second)


def column_sums(values):
    return jnp.sum(values, axis=0, keepdims=True)


def seg_means(values):
    rows, width = values.shape
    return jnp.sum(values.reshape(rows // SEG, SEG, width), axis=1) * (1.0 / SEG)


def near_bit():
    return lax.axis_index("head") % 2


def far_bit():
    return lax.axis_index("head") // 2


def my_rows(rows):
    half = rows // 2
    return pl.ds(pl.multiple_of(near_bit() * half, half), half)


def lanes_of(place, width, start=0):
    at = place + near_bit() - 2 * place * near_bit()
    return pl.ds(pl.multiple_of(start + at * width, width), width)


def half_rows(place, half):
    return pl.ds(pl.multiple_of(place * half, half), half)


def full(shape):
    return pl.BlockSpec(shape, lambda *_: (0,) * len(shape))


class Steps:
    def __init__(self):
        self.held = []
        self.us = 0.1

    def call(self, kernel, name, outs, args, specs=None, scratch=(), vmem=32, copies=0, far=(), far_outs=()):
        specs = dict(specs or {})
        given, made, held = len(args), len(outs), tuple(self.held)
        token = bool(far_outs)
        somewhere = pl.BlockSpec(memory_space=pl.ANY)
        in_hbm = pl.BlockSpec(memory_space=pltpu.HBM)

        def body(*refs):
            ins, rest = refs[:given], refs[given + len(held) :]
            if token:
                rest[made][...] = jnp.zeros(rest[made].shape, F32)
            kernel(*ins, *rest[:made], *rest[made + token :])

        args = [pltpu.with_memory_space_constraint(a, pltpu.HBM) if i in far else a for i, a in enumerate(args)]
        out_specs = [in_hbm if i in far_outs else full(shape) for i, shape in enumerate(outs)]
        out_shape = [
            pltpu.HBM(shape, F32) if i in far_outs else jax.ShapeDtypeStruct(shape, F32) for i, shape in enumerate(outs)
        ]
        if token:
            out_specs.append(full((1, 128)))
            out_shape.append(jax.ShapeDtypeStruct((1, 128), F32))
        out = pl.pallas_call(
            body,
            name=name,
            grid=(1,),
            in_specs=[in_hbm if i in far else specs.get(i, full(a.shape)) for i, a in enumerate(args)]
            + [somewhere] * len(held),
            out_specs=out_specs,
            out_shape=out_shape,
            scratch_shapes=[pltpu.VMEM(shape, F32) for shape in scratch]
            + ([pltpu.SemaphoreType.DMA((copies,))] if copies else []),
            compiler_params=pltpu.CompilerParams(vmem_limit_bytes=vmem * MIB),
            cost_estimate=pl.CostEstimate(flops=int(self.us * 5.18e8), bytes_accessed=0, transcendentals=0),
        )(*args, *held)
        self.held = [out[-1]]
        return out[:made]


def copy_all(pairs, sems):
    copies = [pltpu.make_async_copy(a, b, sems.at[i]) for i, (a, b) in enumerate(pairs)]
    for copy in copies:
        copy.start()
    return copies


def pack_kernel(wq, wk, wv, wo, bq, bv, bi, frames, out, edge, sems):
    rows, width = wq.shape
    out[rows:] = jnp.zeros((out.shape[0] - rows, out.shape[1]), F32)
    pairs = [(w, out.at[pl.ds(0, rows), pl.ds(i * width, width)]) for i, w in enumerate((wq, wk, wv))]
    for at in range(0, wo.shape[1], width):
        pairs.append((wo.at[:, pl.ds(at, width)], out.at[pl.ds(at, width), pl.ds(3 * width, width)]))
    pairs += [(b, out.at[pl.ds(rows, 1), pl.ds(i * width, width)]) for i, b in ((0, bq), (2, bv))]
    pairs.append((bi, out.at[pl.ds(rows + 1, 1), pl.ds(0, bi.shape[1])]))
    start = pl.multiple_of((1 - near_bit()) * (frames.shape[1] - BEFORE), BEFORE)
    pairs += [(frames.at[m, pl.ds(start, BEFORE)], edge.at[m]) for m in range(frames.shape[0])]
    for copy in copy_all(pairs, sems):
        copy.wait()


def norm_kernel(
    frames, gain, shift, wi, wu, wo, cotangent,
    x_ref, xhat_ref, rate_ref, normed_ref, wi_ref, wu_ref, wo_ref, g_0, g_1, before, ahead, params, sems,
):
    micros, half, _ = x_ref.shape
    rows = frames.shape[1]
    pairs = [(gain, params.at[pl.ds(0, 1)]), (shift, params.at[pl.ds(8, 1)])]
    pairs += [(frames.at[m, my_rows(rows)], x_ref.at[m]) for m in range(micros)]
    pairs += [(frames.at[m, pl.ds(half - BEFORE, BEFORE)], before.at[m]) for m in range(micros)]
    pairs += [(frames.at[m, pl.ds(half, AHEAD)], ahead.at[m]) for m in range(micros)]
    pairs += [(wo, wo_ref), (wi, wi_ref), (wu, wu_ref)]
    pairs += [(cotangent.at[m, my_rows(rows)], g) for m, g in enumerate((g_0, g_1))]
    copies = copy_all(pairs, sems)
    for copy in copies[:2]:
        copy.wait()
    for micro in range(micros):
        copies[2 + micro].wait()
        xhat, rate = normalise(x_ref[micro])
        xhat_ref[micro] = xhat
        normed_ref[micro] = xhat * params[0:1] + params[8:9]
        rate_ref[micro] = jnp.broadcast_to(rate, (half, rate_ref.shape[2]))
    for copy in copies[2 + micros :]:
        copy.wait()


def project_kernel(normed, own, pair, g1, s1, g2, s2, bo, bi, bu, q_ref, kv_ref, w_ref, bias, rows_ref, sems):
    micros, half, wide = q_ref.shape
    features = normed.shape[2]
    width = own.shape[1] // 4
    copies = copy_all([(v, rows_ref.at[i]) for i, v in enumerate((g1, s1, g2, s2, bo, bi, bu))], sems)
    for number in range(3):
        at = slice(number * width, (number + 1) * width)
        for place, source in enumerate((own, pair)):
            lanes = lanes_of(place, width, 2 * number * width)
            w_ref[:, lanes] = source[:features, at]
            bias[:, lanes] = source[features : features + 1, at]
    for micro in range(micros):
        out = mm(normed[micro], w_ref[...]) + bias[...]
        q_ref[micro] = out[:, :wide]
        kv_ref[micro] = out[:, wide:]
    for copy in copies:
        copy.wait()


def edges_kernel(edge, before, ahead, params, w_ref, bias, xhat_ref, normed_ref, kv_ref):
    near = near_bit()
    wide = w_ref.shape[1] // 3
    for micro in range(edge.shape[0]):
        first = jnp.where(near == 0, edge[micro], before[micro])
        last = jnp.where(near == 0, ahead[micro], edge[micro, :AHEAD])
        xhat, _ = normalise(jnp.concatenate([first, last], axis=0))
        normed = xhat * params[FIRST_GAIN] + params[FIRST_SHIFT]
        xhat_ref[micro] = xhat
        normed_ref[micro] = normed
        kv_ref[micro] = mm(normed, w_ref[:, wide:]) + bias[:, wide:]


def fill_keys(kv, edge, kx, sx):
    length = kv.shape[0]
    kx[BEFORE : BEFORE + length] = kv
    segs = length // SEG
    sx[SUMS : SUMS + segs] = seg_means(kv)
    if edge is not None:
        kx[:BEFORE] = edge[:BEFORE]
        kx[BEFORE + length :] = edge[BEFORE:]
        sx[: SUMS - MEM] = jnp.zeros((SUMS - MEM, kv.shape[1]), F32)
        sx[SUMS - MEM : SUMS] = seg_means(edge[:BEFORE])
        sx[SUMS + segs :] = jnp.zeros((sx.shape[0] - SUMS - segs, kv.shape[1]), F32)


def summary_start(block):
    return (block * (BLOCK // SEG) + SUMS - MEM) // SUMS * SUMS


def frame_rows(block):
    start = BEFORE - CACHE + block * BLOCK
    return slice(start, start + WIN)


def key_window(kx, sx, block, lanes):
    start = summary_start(block)
    rows = [kx[frame_rows(block), lanes], sx[start : start + SWIN, lanes]]
    return jnp.concatenate(rows + [jnp.zeros((KEYS - WIN - SWIN, PAIR), F32)], axis=0)


def by_head(values):
    first = lax.broadcasted_iota(jnp.int32, values.shape, 1) < HEAD_DIM
    return jnp.concatenate([jnp.where(first, values, 0.0), jnp.where(first, 0.0, values)], axis=0)


def side_by_side(values):
    rows = values.shape[0] // 2
    first = lax.broadcasted_iota(jnp.int32, (rows, values.shape[1]), 1) < HEAD_DIM
    return jnp.where(first, values[:rows], values[rows:])


def owner_of(segment, bounds):
    owner = jnp.where(segment < 0, -1, 0)
    for bound in bounds:
        owner = owner + (segment >= bound).astype(jnp.int32)
    return owner


def visible(block, base, bounds):
    row = lax.broadcasted_iota(jnp.int32, (2 * BLOCK, 1), 0) % BLOCK
    column = lax.broadcasted_iota(jnp.int32, (1, KEYS), 1)
    query_seg = block * (BLOCK // SEG) + row // SEG
    frame = block * BLOCK - CACHE + column
    is_frame = column < WIN
    summary = summary_start(block) - SUMS + column - WIN
    key_seg = jnp.where(is_frame, (frame + CACHE) // SEG - CACHE // SEG, summary)
    key_seg = jnp.where(column < WIN + SWIN, key_seg, -(1 << 20))
    inside = (frame >= query_seg * SEG - LC) & (frame < query_seg * SEG + SEG + RC)
    near = (key_seg >= query_seg - MEM) & (key_seg < query_seg)
    seen = (is_frame & inside) | ((column >= WIN) & near)
    return seen & (owner_of(key_seg + base, bounds) == owner_of(query_seg + base, bounds))


def bounds_of(counts, micro):
    bounds, total = [], 0
    for utterance in range(counts.shape[1]):
        total = total + counts[micro, utterance]
        bounds.append(total)
    return bounds


def first_segment(length):
    return (lax.axis_index("tm") * 2 + near_bit()) * (length // SEG)


def block_rows(block):
    return slice(block * BLOCK, (block + 1) * BLOCK)


def attend_block(block, seen, query, kx, sx, keep, put):
    width = query.shape[1]
    for pair in range(width // PAIR):
        lanes = slice(pair * PAIR, (pair + 1) * PAIR)
        value_lanes = slice(width + pair * PAIR, width + (pair + 1) * PAIR)
        scores = mm(by_head(query[:, lanes] * HEAD_DIM ** (-0.5)), key_window(kx, sx, block, lanes), 1, 1)
        scores = jnp.where(seen, scores, MASKED)
        weights = jnp.exp(scores - jnp.max(scores, axis=-1, keepdims=True))
        weights = weights / jnp.sum(weights, axis=-1, keepdims=True)
        keep(pair, weights)
        put(lanes, side_by_side(mm(weights, key_window(kx, sx, block, value_lanes))))


def attend_inner_kernel(counts, q_ref, kv_ref, mix_0, mix_1, p_ref, kx, sx):
    _, length, _ = q_ref.shape
    base = first_segment(length)
    for micro, mix_ref in enumerate((mix_0, mix_1)):
        fill_keys(kv_ref[micro], None, kx, sx)
        bounds = bounds_of(counts, micro)
        for number, block in enumerate(range(1, length // BLOCK - 1)):
            def keep(pair, weights):
                p_ref[micro, number, pair] = weights

            def put(lanes, values):
                mix_ref[block_rows(number), lanes] = values

            seen = visible(block, base, bounds)
            attend_block(block, seen, q_ref[micro, block_rows(block)], kx, sx, keep, put)


def attend_outer_kernel(micro, counts, q_ref, kv_ref, edge, mix_ref, p_ref, kx, sx):
    _, length, _ = q_ref.shape
    base = first_segment(length)
    fill_keys(kv_ref[micro], edge[micro], kx, sx)
    bounds = bounds_of(counts, micro)
    for number, block in enumerate((0, length // BLOCK - 1)):
        def keep(pair, weights):
            p_ref[number, pair] = weights

        def put(lanes, values):
            mix_ref[block_rows(number), lanes] = values

        seen = visible(block, base, bounds)
        attend_block(block, seen, q_ref[micro, block_rows(block)], kx, sx, keep, put)


def fill_rows(target, lanes, inner, outer):
    length = inner.shape[0] + outer.shape[0]
    target[:BLOCK, lanes] = outer[:BLOCK]
    target[BLOCK : length - BLOCK, lanes] = inner[...]
    target[length - BLOCK : length, lanes] = outer[BLOCK:]


def back_kernel(
    micro, grad_ref, mid_ref, g_ref, params, wo_here, mix_inner, mix_outer, q_ref, kv_ref, edge, p_inner, p_outer,
    dmid_ref, dq_ref, dkv_ref, dwo_own, dwo_pair, vec_ref,
    kx, sx, dsx, dmix, mix, dwo,
):
    _, length, width = q_ref.shape
    near_width = dwo_own.shape[1]
    grad = grad_ref[...]
    xhat, rate = normalise(mid_ref[...])
    dmid = g_ref[...] + norm_back(grad, params[SECOND_GAIN], xhat, rate)
    dmid_ref[...] = dmid
    vec_ref[0:1] = column_sums(dmid)
    vec_ref[1:2] = column_sums(grad * xhat)
    vec_ref[2:3] = column_sums(grad)
    dmix[...] = mm(dmid, wo_here[...], 1, 1)
    fill_rows(mix, slice(None), mix_inner, mix_outer)
    dwo[...] = mm(dmid, mix[...], 0, 0)
    dwo_own[...] = dwo[:, lanes_of(0, near_width)]
    dwo_pair[...] = dwo[:, lanes_of(1, near_width)]
    fill_keys(kv_ref[micro], edge[micro], kx, sx)
    dkv_ref[...] = jnp.zeros_like(dkv_ref)
    dsx[...] = jnp.zeros_like(dsx)
    for block in range(length // BLOCK):
        start = summary_start(block)
        rows, frames, sums = block_rows(block), frame_rows(block), slice(start, start + SWIN)
        for pair in range(width // PAIR):
            lanes = slice(pair * PAIR, (pair + 1) * PAIR)
            value_lanes = slice(width + pair * PAIR, width + (pair + 1) * PAIR)
            inside = 0 < block < length // BLOCK - 1
            weights = p_inner[micro, block - 1, pair] if inside else p_outer[min(block, 1), pair]
            grad = by_head(dmix[rows, lanes])
            dweights = mm(grad, key_window(kx, sx, block, value_lanes), 1, 1)
            dscores = weights * (dweights - jnp.sum(dweights * weights, axis=-1, keepdims=True))
            dquery = side_by_side(mm(dscores, key_window(kx, sx, block, lanes)))
            dq_ref[rows, lanes] = dquery * HEAD_DIM ** (-0.5)
            dkeys = mm(dscores, by_head(q_ref[micro, rows, lanes] * HEAD_DIM ** (-0.5)), 0, 0)
            dvalues = mm(weights, grad, 0, 0)
            dkv_ref[frames, lanes] += dkeys[:WIN]
            dkv_ref[frames, value_lanes] += dvalues[:WIN]
            dsx[sums, lanes] += dkeys[WIN : WIN + SWIN]
            dsx[sums, value_lanes] += dvalues[WIN : WIN + SWIN]
    count = BEFORE + length
    segs = count // SEG
    spread = dsx[SUMS - MEM : SUMS - MEM + segs] * (1.0 / SEG)
    spread = jnp.broadcast_to(spread[:, None, :], (segs, SEG, 2 * width))
    dkv_ref[:count] += spread.reshape(count, 2 * width)


def feed_kernel(
    micro, own_inner, own_outer, far_inner, far_outer, wo_here, wo_far, wo_far_pair, x_ref, g_ref, params, pair, wi_own, wi_pair, wu_own, wu_pair,
    n2_ref, h_ref, dpre_ref, mid_ref, part_ref,
    mix, wo,
):
    width = own_inner.shape[1] // 2
    features, hidden = wi_own.shape
    far = far_bit()
    here = pl.multiple_of(far * 2 * width, 2 * width)
    there = pl.multiple_of((1 - far) * 2 * width, 2 * width)
    fill_rows(mix, pl.ds(here, 2 * width), own_inner, own_outer)
    fill_rows(mix, pl.ds(there, 2 * width), far_inner, far_outer)
    wo[pl.ds(here, 2 * width)] = wo_here[...]
    wo[lanes_of(0, width, there)] = wo_far[...]
    wo[lanes_of(1, width, there)] = wo_far_pair[...]
    middle = x_ref[micro] + mm(mix[...], wo[...]) + params[OUT_BIAS]
    mid_ref[...] = middle
    xhat, _ = normalise(middle)
    normed = xhat * params[SECOND_GAIN] + params[SECOND_SHIFT]
    n2_ref[...] = normed
    part = None
    for place, (wi, wu, bias) in enumerate(((wi_own, wu_own, params[INNER_BIAS][:, :hidden]), (wi_pair, wu_pair, pair[features + 1 : features + 2, :hidden]))):
        at = slice(place * hidden, (place + 1) * hidden)
        pre = mm(normed, wi[...]) + bias
        phi = 0.5 + 0.5 * lax.erf(pre * (0.5**0.5))
        h_ref[:, at] = pre * phi
        slope = phi + pre * (jnp.exp(-0.5 * pre * pre) * 0.3989422804014327)
        dpre = mm(g_ref[...], wu[...], 1, 1) * slope
        dpre_ref[:, at] = dpre
        step = mm(dpre, wi[...], 1, 1)
        part = step if part is None else part + step
    part_ref[...] = part


def put_rows(value, outs):
    at = 0
    for out in outs:
        count = out.shape[0]
        out[...] = value[at : at + count]
        at += count


def inner_weights_kernel(n2_0, n2_1, d_0, d_1, own_ref, *rest):
    *pair, vec_ref = rest
    hidden = own_ref.shape[1]
    for place, outs in enumerate(((own_ref,), pair)):
        at = slice(place * hidden, (place + 1) * hidden)
        put_rows(mm(n2_0[...], d_0[:, at], 0, 0) + mm(n2_1[...], d_1[:, at], 0, 0), outs)
        vec_ref[place : place + 1] = column_sums(d_0[:, at]) + column_sums(d_1[:, at])


def outer_weights_kernel(h_0, h_1, g_0, g_1, own_ref, *rest):
    *pair, vec_ref = rest
    hidden = own_ref.shape[0]
    for place, outs in enumerate(((own_ref,), pair)):
        at = slice(place * hidden, (place + 1) * hidden)
        value = mm(h_0[:, at], g_0[...], 0, 0) + mm(h_1[:, at], g_1[...], 0, 0)
        for out_ref in outs:
            out_ref[:hidden] = value
            if out_ref.shape[0] > hidden:
                out_ref[hidden:] = jnp.zeros((out_ref.shape[0] - hidden, value.shape[1]), F32)
    vec_ref[...] = column_sums(g_0[...]) + column_sums(g_1[...])


def feed_out_kernel(h_0, h_1, wu_own, wu_pair, out_ref):
    hidden = wu_own.shape[0]
    rows = h_0.shape[0]
    for micro, h_ref in enumerate((h_0, h_1)):
        part = mm(h_ref[:, :hidden], wu_own[...]) + mm(h_ref[:, hidden:], wu_pair[...])
        out_ref[micro * rows : (micro + 1) * rows] = part


def out_half_kernel(mid_0, mid_1, part, far, params, out):
    rows = mid_0.shape[0]
    for micro, mid_ref in enumerate((mid_0, mid_1)):
        at = slice(micro * rows, (micro + 1) * rows)
        out[at] = mid_ref[...] + (part[at] + far[at]) + params[OUTER_BIAS]


def project_back_kernel(
    dq_0, dkv_0, dq_1, dkv_1, xhat, xhat_edge, w_ref, part_ref, pair_ref, beyond_ref, vec_ref, work
):
    near = near_bit()
    length, wide = dq_0.shape
    own = slice(BEFORE, BEFORE + length)
    gain, shift = 0.0, 0.0
    for micro, (dq, dkv) in enumerate(((dq_0, dkv_0), (dq_1, dkv_1))):
        work[...] = mm(dkv[...], w_ref[:, wide:], 1, 1)
        work[own] += mm(dq[...], w_ref[:, :wide], 1, 1)
        part_ref[micro * length : (micro + 1) * length] = work[own]
        before = work[:BEFORE]
        ahead = jnp.concatenate([work[BEFORE + length :], jnp.zeros((BEFORE - AHEAD, work.shape[1]), F32)], axis=0)
        pair_ref[micro] = jnp.where(near == 0, ahead, before)
        beyond_ref[micro] = jnp.where(near == 0, before, ahead)
        gain = gain + column_sums(work[own] * xhat[micro]) + column_sums(work[:BEFORE] * xhat_edge[micro, :BEFORE])
        gain = gain + column_sums(work[BEFORE + length :] * xhat_edge[micro, BEFORE:])
        shift = shift + column_sums(work[...])
    vec_ref[0:1] = gain
    vec_ref[1:2] = shift


def edge_add_kernel(part, pair, beyond, out):
    out[...] = part[...]
    near = near_bit()
    micros = pair.shape[0]
    length = part.shape[0] // micros
    for micro in range(micros):
        end = (micro + 1) * length
        out[end - BEFORE : end] += jnp.where(near == 0, pair[micro], beyond[micro])
        out[end - length : end - length + AHEAD] += jnp.where(near == 0, beyond[micro, :AHEAD], pair[micro, :AHEAD])


def project_weights_kernel(
    normed, normed_edge, dq_0, dq_1, dkv_0, dkv_1, wo_own_0, wo_own_1, wo_pair_0, wo_pair_1, mid_0, mid_1, first, vec_outer, vec_inner,
    own_0, own_1, rows_ref, pair_0, pair_1, sums, row,
):
    features = normed.shape[2]
    width = wo_own_0.shape[1]
    hidden = vec_inner.shape[1]
    length, wide = dq_0.shape
    own, after = slice(BEFORE, BEFORE + length), slice(BEFORE + length, None)
    edges = jnp.concatenate([dkv_0[:BEFORE], dkv_0[after], dkv_1[:BEFORE], dkv_1[after]], axis=0)
    normed_edges = jnp.concatenate([normed_edge[0], normed_edge[1]], axis=0)
    queries = mm(normed[0], dq_0[...], 0, 0) + mm(normed[1], dq_1[...], 0, 0)
    keyvals = mm(normed[0], dkv_0[own], 0, 0) + mm(normed[1], dkv_1[own], 0, 0) + mm(normed_edges, edges, 0, 0)
    sums[:, :wide] = queries
    sums[:, wide:] = keyvals
    row[:, :wide] = column_sums(dq_0[...]) + column_sums(dq_1[...])
    row[:, wide:] = column_sums(dkv_0[...]) + column_sums(dkv_1[...])
    rows_ref[0:3] = (mid_0[...] + mid_1[...]) * 0.5
    rows_ref[3:5] = first[...]
    rows_ref[5:6] = vec_outer[...] * 0.5
    rows_ref[6:] = jnp.zeros((2, features), F32)
    half = pair_0.shape[0]
    pair_1[half : half + 6] = rows_ref[0:6]
    pair_1[half + 6 :] = jnp.zeros((2, features), F32)
    for place, (out_ref, at) in enumerate(((rows_ref, 6), (pair_1, half + 6))):
        for number in range(3):
            lanes = slice(number * width, (number + 1) * width)
            out_ref[at : at + 1, lanes] = row[:, lanes_of(place, width, 2 * number * width)]
        out_ref[at + 1 : at + 2, :hidden] = vec_inner[place : place + 1]
    for place, (outs, wo_0, wo_1) in enumerate((((own_0, own_1), wo_own_0, wo_own_1), ((pair_0, pair_1), wo_pair_0, wo_pair_1))):
        for out_ref, rows in zip(outs, (slice(half), slice(half, features)), strict=True):
            for number in range(3):
                lanes = slice(number * width, (number + 1) * width)
                out_ref[:half, lanes] = sums[rows, lanes_of(place, width, 2 * number * width)]
            out_ref[:half, 3 * width :] = wo_0[rows] + wo_1[rows]


def frames_back_kernel(a_ref, b_ref, xhat, rate, dmid_0, dmid_1, params, out):
    rows = dmid_0.shape[0]
    for micro, dmid_ref in enumerate((dmid_0, dmid_1)):
        at = slice(micro * rows, (micro + 1) * rows)
        grad = norm_back(a_ref[at] + b_ref[at], params[FIRST_GAIN], xhat[micro], rate[micro, :, :1])
        out[at] = dmid_ref[...] + grad


def place_kernel(own, pair, out, sems):
    micros, half = out.shape[0], out.shape[1] // 2
    near = near_bit()
    pairs = []
    for micro in range(micros):
        rows = pl.ds(micro * half, half)
        pairs.append((own.at[rows], out.at[micro, half_rows(near, half)]))
        pairs.append((pair.at[rows], out.at[micro, half_rows(1 - near, half)]))
    for copy in copy_all(pairs, sems):
        copy.wait()


def place_of(bit):
    return lax.axis_index("tm") // bit % 2


def add_pieces(out, a_ref, pieces, rows_ref=None, new_rows=None):
    count, at = a_ref.shape[0], 0
    if not pieces:
        out[...] = a_ref[...]
        if new_rows is not None:
            new_rows[...] = rows_ref[...]
    for piece in pieces:
        take = min(piece.shape[0], count - at)
        if take:
            out[at : at + take] = a_ref[at : at + take] + piece[:take]
        if take < piece.shape[0] and new_rows is not None:
            new_rows[...] = rows_ref[...] + piece[take:]
        at += take


def add_split_kernel(bits, counts, rows, *refs):
    total = len(bits)
    values, refs = refs[:total], refs[total:]
    rows_ref, refs = (refs[0], refs[1:]) if rows else (None, refs)
    pieces = []
    for count in counts:
        pieces.append(refs[:count])
        refs = refs[count:]
    kept, sent, refs = refs[:total], refs[total : 2 * total], refs[2 * total :]
    new_rows, work = (refs[0], refs[1]) if rows else (None, refs[0])
    for number, bit in enumerate(bits):
        small = (rows_ref, new_rows) if rows and number == 0 else ()
        half = kept[number].shape[0]
        add_pieces(work, values[number], pieces[number], *small)
        place = place_of(bit)
        kept[number][...] = work[half_rows(place, half)]
        sent[number][:half] = work[half_rows(1 - place, half)]
        if small:
            sent[number][half:] = new_rows[...]


def last_kernel(rows, a_ref, *refs):
    rows_ref, refs = (refs[0], refs[1:]) if rows else (None, refs)
    b_ref, out_ref = refs
    half = a_ref.shape[0]
    out_ref[:half] = a_ref[...] + b_ref[:half]
    if rows:
        out_ref[half:] = rows_ref[...] + b_ref[half:]


def stack_kernel(rows, a_0, a_1, *refs):
    rows_ref, refs = (refs[0], refs[1:]) if rows else (None, refs)
    b_0, b_1, out_ref = refs
    half = a_0.shape[0]
    out_ref[:half] = a_0[...] + b_0[:half]
    out_ref[half : 2 * half] = a_1[...] + b_1[...]
    if rows:
        out_ref[2 * half :] = rows_ref[...] + b_0[half:]


def add_whole_kernel(a_ref, b_ref, *outs):
    at = 0
    for out in outs:
        count = out.shape[0]
        out[...] = a_ref[at : at + count] + b_ref[at : at + count]
        at += count


def join_kernel(bits, *refs):
    total = len(bits)
    for bit, mine, theirs, out in zip(bits, refs[:total], refs[total : 2 * total], refs[2 * total :], strict=True):
        half = mine.shape[0]
        place = place_of(bit)
        out[half_rows(place, half)] = mine[...]
        out[half_rows(1 - place, half)] = theirs[...]


def join_out_kernel(bit, mine, theirs, out, sems):
    half = mine.shape[0]
    place = place_of(bit)
    for copy in copy_all([(mine, out.at[half_rows(place, half)]), (theirs, out.at[half_rows(1 - place, half)])], sems):
        copy.wait()


def join_heads_kernel(bits, *refs):
    *parts, wq, wk, wv, wo, work = refs
    width = wq.shape[1]
    half = parts[0].shape[0]
    place = place_of(bits[0])
    for number in range(2):
        for where, part in zip((place, 1 - place), parts[2 * number : 2 * number + 2], strict=True):
            rows = pl.ds(pl.multiple_of(2 * number * half + where * half, half), half)
            for heads, out in enumerate((wq, wk, wv, work)):
                out[rows, :] = part[:, heads * width : (heads + 1) * width]
    wo[...] = work[...].T


def small_kernel(rows, far, outs):
    width = outs[-3].shape[1]
    for number, out in enumerate(outs[:6]):
        out[...] = rows[number : number + 1] + far[number : number + 1]
    outs[6][...] = rows[6:7, :width]
    outs[7][...] = rows[6:7, 2 * width : 3 * width]
    outs[8][...] = rows[7:8, : outs[8].shape[1]]


def finish_kernel(bits, rows, far, *refs):
    count = 2 * len(bits)
    small_kernel(rows, far, refs[count : count + 9])
    join_heads_kernel(bits, *refs[:count], *refs[count + 9 :])


def swap(value, axis, bit):
    size = lax.axis_size(axis)
    return lax.ppermute(value, axis, [(i, i ^ bit) for i in range(size)])


def swap_near(parts):
    return [swap(part, "head", 1) for part in parts]


def swap_edges(value, back):
    size, group = lax.axis_size("tm"), lax.axis_size("head")
    pairs = []
    for source in range(size):
        for place in range(group):
            target = source + (1 - 2 * (place % 2)) * (-1 if back else 1)
            if 0 <= target < size:
                pairs.append((source * group + place, target * group + (place ^ 1 if back else place)))
    return lax.ppermute(value, ("tm", "head"), pairs)


class SumsOverTm:
    def __init__(self, run, a, b, rows=None, joins=None):
        bits = [1 << i for i in range(lax.axis_size("tm").bit_length() - 1)]
        self.run, self.values, self.got, self.ones = run, list(a), [list(v) for v in b], []
        self.rows = [] if rows is None else [rows]
        self.apart = [(bits[1], bits[0]), (bits[0], bits[1])]
        self.together, self.last = bits[2:-1], bits[-1]
        self.joins = joins
        if len(a) == 1:
            self.todo = [("split", (bit,)) for bit in bits[:-1]] + [("last",), ("add",)]
            self.todo += [("join", (bit,)) for bit in (*reversed(self.together), joins[0])]
            self.step()
            return
        self.todo = [("split", pair) for pair in self.apart]
        self.todo.append(("stack",))
        self.todo += [("split", (bit,)) for bit in self.together] + [("last",)] * bool(self.together)
        self.todo.append(("add",))
        self.todo += [("join", (bit,)) for bit in reversed(self.together)] + [("part",)] * bool(self.together)
        self.todo.append(("join", self.apart[1]))
        self.step()

    def step(self):
        run, values = self.run, self.values
        kind, *rest = self.todo.pop(0)
        features = values[0].shape[1]
        count = values[0].shape[0]
        more = sum(v.shape[0] for v in self.rows)
        has_rows = bool(self.rows)
        shape = lambda rows: (rows, features)
        got = [piece for pieces in self.got for piece in pieces]
        if kind == "split":
            (bits,) = rest
            half = count // 2
            extra = [more] + [0] * (len(bits) - 1)
            out = run.call(
                functools.partial(add_split_kernel, bits, [len(v) for v in self.got], has_rows), "add_split",
                [shape(half)] * len(bits) + [shape(half + e) for e in extra] + [v.shape for v in self.rows],
                (*values, *self.rows, *got), scratch=[shape(count)],
            )
            self.values, messages, self.rows = out[: len(bits)], out[len(bits) : 2 * len(bits)], out[2 * len(bits) :]
            self.got = [[swap(v, "tm", bit)] for v, bit in zip(messages, bits, strict=True)]
            return
        if kind in ("stack", "last"):
            if kind == "stack":
                (value,) = run.call(
                    functools.partial(stack_kernel, has_rows), "stack", [shape(2 * count + more)], (*values, *self.rows, *got)
                )
                count = 2 * count
            else:
                (value,) = run.call(
                    functools.partial(last_kernel, has_rows), "stack", [shape(count + more)], (*values, *self.rows, *got)
                )
            if kind == "stack" and self.together:
                self.values, self.rows = [value[:count]], [value[count:]] * has_rows
                self.values, self.got = self.values, [[]]
                return self.step()
            self.values, self.count = [value], count
            self.got = [[swap(value, "tm", self.last)]]
            return
        if kind == "add":
            parts = [self.count] if self.together or self.joins else [self.count // 2] * 2
            out = run.call(
                add_whole_kernel, "add", [shape(n) for n in parts] + [v.shape for v in self.rows], (*values, *got)
            )
            self.values, self.rows = out[: len(parts)], out[len(parts) :]
        elif kind == "join":
            (bits,) = rest
            self.values = run.call(
                functools.partial(join_kernel, bits), "join", [shape(2 * count)] * len(bits), (*values, *got)
            )
        elif kind == "part":
            self.values = [values[0][: count // 2], values[0][count // 2 :]]
        following = self.todo[0] if self.todo else ("join", self.joins[1:] if self.joins else self.apart[0])
        if following[0] == "part":
            return self.step()
        self.got = [[swap(v, "tm", bit)] for v, bit in zip(self.values, following[1], strict=True)]

    def join_one(self, number):
        if len(self.todo) != 1:
            return
        bits = self.todo[0][1]
        value = self.values[number]
        values, got = list(self.values), list(self.got)
        (values[number],) = self.run.call(
            functools.partial(join_kernel, bits[number : number + 1]), "join", [(2 * value.shape[0], value.shape[1])],
            (value, *got[number]),
        )
        got[number] = [swap(values[number], "tm", self.apart[0][number])]
        self.values, self.got = values, got
        self.ones.append(number)
        if len(self.ones) == 2:
            self.todo.pop()

    @property
    def joined(self):
        return not self.todo

    def halves(self, number):
        return self.apart[0][number], (self.values[number], *self.got[number])


ORDER = (
    ("pack", 8), ("norm", 4.8), ("project", 2.2), ("attend_inner", 11), ("edges", 1), ("hand_on", 0.5),
    ("attend_outer0", 24), ("attend_outer1", 1), ("feed0", 18), ("feed1", 14), ("outer_weights", 6),
    ("inner_weights", 11), ("feed_out", 0.6), ("grad_sum0", 18), ("ffn", 11), ("back0", 6), ("grad_sum1", 2),
    ("back1", 0.5), ("ffn", 0.1), ("project_back", 1.8), ("project_weights", 2), ("ffn", 0.1), ("edge_add", 5),
    ("out_half", 5), ("heads0", 20), ("out_send", 20), ("heads1", 20), ("place_out", 1), ("heads0", 1),
    ("heads1", 0.1), ("ffn", 0.1), ("heads0", 0.1), ("heads1", 3), ("frames_back", 0.6), ("ffn_last1", 20),
    ("heads0", 3), ("heads1", 0.1), ("ffn_last0", 12), ("place_frames", 0.1), ("heads0", 9), ("heads1", 2),
    ("join_inner", 0.1), ("join_outer", 0.1), ("finish", 1.3),
)
PIECES = 1


def copy_kernel(source, target):
    target[...] = source[...]


def hand_on_kernel(own, pair, far, here, far_copy):
    far_copy[...] = far[...]
    width = far.shape[0]
    for near, source in enumerate((own, pair)):
        for at in range(0, far.shape[1], width):
            lanes = slice(3 * width, 4 * width)
            here[lanes_of(near, width), at : at + width] = source[at : at + width, lanes]


class Layer:
    def __init__(
        self, frames, cotangent, seg_counts, query_weight, query_bias, key_weight, value_weight, value_bias,
        out_weight, out_bias, first_gain, first_shift, second_gain, second_shift,
        inner_weight, inner_bias, outer_weight, outer_bias,
    ):
        self.frames, self.cotangent, self.counts = frames, cotangent, seg_counts
        self.projections = (query_weight, key_weight, value_weight)
        self.weights = (inner_weight, outer_weight, out_weight)
        row = lambda v: v.reshape(1, v.shape[0])
        self.bq, self.bv, self.bo, self.bi, self.bu = map(row, (query_bias, value_bias, out_bias, inner_bias, outer_bias))
        self.g1, self.s1, self.g2, self.s2 = map(row, (first_gain, first_shift, second_gain, second_shift))
        micros, shard, features = frames.shape
        self.micros, self.features = micros, features
        self.width, self.hidden = query_weight.shape[1], inner_weight.shape[1]
        self.length = shard // 2
        self.segs, self.blocks, self.pairs = self.length // SEG, self.length // BLOCK, 2 * self.width // PAIR
        self.big = (self.length, features)
        self.each = (micros, self.length)
        self.quarter = (self.length // 2, features)
        self.square = (2 * BLOCK, KEYS)
        self.around = BEFORE + self.length + AHEAD
        self.key_scratch = [(self.around, 4 * self.width), (SUMS + self.segs + SUMS, 4 * self.width)]
        self.run = Steps()
        self.smem = pl.BlockSpec(memory_space=pltpu.SMEM)
        pairs = [None] * micros
        self.mix_outer, self.far_outer, self.p_outer, self.fed, self.dn2 = (list(pairs) for _ in range(5))
        self.back_of = list(pairs)
        self.sums = {}
        self.heads_names = ("heads0", "heads1")

    def pack(self):
        args = (*self.projections, self.weights[2], self.bq, self.bv, self.bi, self.frames)
        self.own, edge = self.run.call(
            pack_kernel, "pack", [(self.features + 8, 4 * self.width), (self.micros, BEFORE, self.features)], args,
            copies=6 + self.features // self.width + self.micros, far=range(8),
        )
        self.pair = swap(self.own, "head", 1)
        self.edge = swap_edges(edge, False)

    def norm(self):
        each, features, micros = self.each, self.features, self.micros
        wi, wu, wo = self.weights
        (self.x, self.xhat, self.rate, self.normed, self.wi, self.wu, self.wo, *self.g, self.before, self.ahead) = self.run.call(
            norm_kernel, "norm",
            [each + (features,)] * 2 + [each + (128,), each + (features,), wi.shape, wu.shape, wo.shape, self.big, self.big,
             (micros, BEFORE, features), (micros, AHEAD, features)],
            (self.frames, self.g1, self.s1, wi, wu, wo, self.cotangent),
            scratch=[(16, features)], copies=4 * micros + 5, far=range(7),
        )
        self.wo_far = swap(self.wo, "head", 2)
        self.wi_pair, self.wu_pair = (swap(v, "head", 1) for v in (self.wi, self.wu))

    def project(self):
        each, features, width = self.each, self.features, self.width
        args = (self.normed, self.own, self.pair, self.g1, self.s1, self.g2, self.s2, self.bo, self.bi, self.bu)
        self.q, self.kv, self.w_all, self.bias, self.params = self.run.call(
            project_kernel, "project",
            [each + (2 * width,), each + (4 * width,), (features, 6 * width), (1, 6 * width), (7, 1, features)],
            args, copies=7, far=range(3, 10),
        )

    def edges(self):
        shape = (self.micros, BEFORE + AHEAD)
        self.xhat_edge, self.normed_edge, self.kv_edge = self.run.call(
            edges_kernel, "edges", [shape + (self.features,)] * 2 + [shape + (4 * self.width,)],
            (self.edge, self.before, self.ahead, self.params, self.w_all, self.bias),
        )

    def attend_inner(self):
        *self.mix_inner, self.p_inner = self.run.call(
            attend_inner_kernel, "attend_inner",
            [(self.length - 2 * BLOCK, 2 * self.width)] * 2 + [(self.micros, self.blocks - 2, self.pairs) + self.square],
            (self.counts, self.q, self.kv), {0: self.smem}, self.key_scratch,
        )
        self.far_inner = [swap(v, "head", 2) for v in self.mix_inner]

    def attend_outer(self, m):
        if m:
            self.run.held.append(self.far_inner[0])
        self.mix_outer[m], self.p_outer[m] = self.run.call(
            functools.partial(attend_outer_kernel, m), "attend_outer",
            [(2 * BLOCK, 2 * self.width), (2, self.pairs) + self.square],
            (self.counts, self.q, self.kv, self.kv_edge),
            {0: self.smem}, self.key_scratch,
        )
        self.far_outer[m] = swap(self.mix_outer[m], "head", 2)

    def hand_on(self):
        shape = self.wo_far.shape
        self.wo_here, far = self.run.call(
            hand_on_kernel, "hand_on", [(2 * shape[0], shape[1]), shape], (self.own, self.pair, self.wo_far)
        )
        self.wo_far_pair = swap(far, "head", 1)

    def feed(self, m):
        big, features, hidden = self.big, self.features, self.hidden
        *self.fed[m], part = self.run.call(
            functools.partial(feed_kernel, m), "feed", [big, (self.length, 2 * hidden), (self.length, 2 * hidden), big, big],
            (self.mix_inner[m], self.mix_outer[m], self.far_inner[m], self.far_outer[m], self.wo_here, self.wo_far, self.wo_far_pair, self.x, self.g[m], self.params,
             self.pair, self.wi, self.wi_pair, self.wu, self.wu_pair),
            scratch=[big, (features, features)],
        )
        self.dn2[m] = (part, swap(part, "head", 2))

    def inner_weights(self):
        features, hidden = self.features, self.hidden
        self.inner_own, *pair, self.vec_inner = self.run.call(
            inner_weights_kernel, "inner_weights",
            [(features, hidden)] + [(features // PIECES, hidden)] * PIECES + [(2, hidden)],
            (self.fed[0][0], self.fed[1][0], self.fed[0][2], self.fed[1][2]),
        )
        self.inner_pair = swap_near(pair)

    def outer_weights(self):
        features, hidden = self.features, self.hidden
        self.outer_own, *pair, self.vec_outer = self.run.call(
            outer_weights_kernel, "outer_weights",
            [(hidden, features), (hidden + 8, features), (1, features)],
            (self.fed[0][1], self.fed[1][1], *self.g),
        )
        self.outer_pair = swap_near(pair)

    def feed_out(self):
        (part,) = self.run.call(
            feed_out_kernel, "feed_out", [(self.micros * self.length, self.features)],
            (self.fed[0][1], self.fed[1][1], self.wu, self.wu_pair),
        )
        self.part = (part, swap(part, "head", 2))

    def out_half(self):
        (half,) = self.run.call(
            out_half_kernel, "out_half", [(self.micros * self.length, self.features)],
            (self.fed[0][3], self.fed[1][3], *self.part, self.params),
        )
        self.out = half

    def out_send(self):
        (half,) = self.run.call(copy_kernel, "out_send", [self.out.shape], (self.out,))
        self.out = (half, swap(half, "head", 1))

    def grad_sum(self, m):
        (self.dn2[m],) = self.run.call(add_whole_kernel, "grad_sum", [self.big], self.dn2[m])

    def back(self, m):
        length, width, features = self.length, self.width, self.features
        self.back_of[m] = self.run.call(
            functools.partial(back_kernel, m), "back",
            [self.big, (length, 2 * width), (self.around, 4 * width), (features, width), (features, width), (3, features)],
            (self.dn2[m], self.fed[m][3], self.g[m], self.params, self.wo_here, self.mix_inner[m], self.mix_outer[m], self.q, self.kv,
             self.kv_edge, self.p_inner, self.p_outer[m]),
            scratch=self.key_scratch + self.key_scratch[1:] + [(length, 2 * width)] * 2 + [(features, 2 * width)],
        )

    def pick(self, number):
        return [v[number] for v in self.back_of]

    def project_back(self):
        features, micros = self.features, self.micros
        (dq_0, dq_1), (dkv_0, dkv_1) = self.pick(1), self.pick(2)
        part, pair, beyond, self.vec_first = self.run.call(
            project_back_kernel, "project_back",
            [(micros * self.length, features)] + [(micros, BEFORE, features)] * 2 + [(2, features)],
            (dq_0, dkv_0, dq_1, dkv_1, self.xhat, self.xhat_edge, self.w_all), scratch=[(self.around, features)],
        )
        self.edges_back = (part, swap(pair, "head", 1), swap_edges(beyond, True))

    def edge_add(self):
        part = self.edges_back[0]
        (part,) = self.run.call(edge_add_kernel, "edge_add", [part.shape], self.edges_back)
        self.dn1 = (part, swap(part, "head", 2))

    def project_weights(self):
        features, width = self.features, self.width
        *self.heads_own, self.rows, a, b = self.run.call(
            project_weights_kernel, "project_weights",
            [(features // 2, 4 * width)] * 2 + [(8, features), (features // 2, 4 * width), (features // 2 + 8, 4 * width)],
            (self.normed, self.normed_edge, *self.pick(1), *self.pick(2), *self.pick(3), *self.pick(4), *self.pick(5),
             self.vec_first, self.vec_outer, self.vec_inner),
            scratch=[(features, 6 * width), (1, 6 * width)],
        )
        self.heads_pair = swap_near((a, b))

    def begin(self, name):
        if name in self.heads_names:
            number = self.heads_names.index(name)
            a, b = self.heads_own[number], self.heads_pair[number]
            return SumsOverTm(self.run, (a,), ((b,),), self.rows if number else None, (2, 1))
        return SumsOverTm(self.run, (self.outer_own, self.inner_own), (self.outer_pair, self.inner_pair))

    def sum(self, name):
        if name not in self.sums:
            self.sums[name] = self.begin(name)
        elif not self.sums[name].joined:
            self.sums[name].step()

    def ffn(self):
        self.sum("ffn")

    def heads(self, number):
        self.sum(self.heads_names[number])

    def ffn_last(self, number):
        self.sums["ffn"].join_one(number)

    def frames_back(self):
        (half,) = self.run.call(
            frames_back_kernel, "frames_back", [(self.micros * self.length, self.features)],
            (*self.dn1, self.xhat, self.rate, *self.pick(0), self.params),
        )
        self.grad = (half, swap(half, "head", 1))

    def place(self, name, halves):
        (out,) = self.run.call(
            place_kernel, name, [(self.micros, 2 * self.length, self.features)], halves, copies=2 * self.micros, far_outs=[0]
        )
        return out

    def place_out(self):
        self.layer_output = self.place("place_out", self.out)

    def place_frames(self):
        self.frames_grad = self.place("place_frames", self.grad)

    def join(self, name, number, shape):
        bit, parts = self.sums["ffn"].halves(number)
        (out,) = self.run.call(
            functools.partial(join_out_kernel, bit), name, [shape], parts, copies=2, far_outs=[0]
        )
        return out

    def settle(self, *names):
        while not all(self.sums[name].joined for name in names):
            for name in names:
                self.sum(name)

    def join_outer(self):
        self.settle("ffn", *self.heads_names)
        self.outer_grad = self.join("join_outer", 0, self.weights[1].shape)

    def join_inner(self):
        self.settle("ffn", *self.heads_names)
        self.inner_grad = self.join("join_inner", 1, self.weights[0].shape)

    def finish(self):
        features, width, hidden = self.features, self.width, self.hidden
        both = [self.sums[name] for name in self.heads_names]
        rows = both[1].rows[0]
        bits, parts = both[0].joins[::-1], [sums.halves(0)[1] for sums in both]
        out = self.run.call(
            functools.partial(finish_kernel, bits), "finish",
            [(1, features)] * 6 + [(1, width)] * 2 + [(1, hidden)] + [(features, width)] * 3 + [(width, features)],
            (rows, swap(rows, "head", 2), *parts[0], *parts[1]), scratch=[(features, width)],
        )
        bo, g2, s2, g1, s1, bu, bq, bv, bi = (v.reshape(v.shape[1]) for v in out[:9])
        wq, wk, wv, wo = out[9:]
        return (
            self.layer_output, self.frames_grad, wq, bq, wk, wv, bv, wo, bo, g1, s1, g2, s2, self.inner_grad, bi,
            self.outer_grad, bu,
        )


def per_device(*args):
    layer = Layer(*args)
    for step, us in ORDER:
        layer.run.us = us
        name = step.rstrip("0123456789")
        result = getattr(layer, name)(*(int(digit) for digit in step[len(name) :]))
    return result


def solution(mesh):
    in_specs = (
        P(None, "tm", None),
        P(None, "tm", None),
        P(),
        P(None, "head"),
        P("head"),
        P(None, "head"),
        P(None, "head"),
        P("head"),
        P("head", None),
        P(),
        P(),
        P(),
        P(),
        P(),
        P(None, "head"),
        P("head"),
        P("head", None),
        P(),
    )
    out_specs = (
        P(None, "tm", None),
        P(None, "tm", None),
        P(None, "head"),
        P("head"),
        P(None, "head"),
        P(None, "head"),
        P("head"),
        P("head", None),
        P(),
        P(),
        P(),
        P(),
        P(),
        P(None, "head"),
        P("head"),
        P("head", None),
        P(),
    )
    return jax.shard_map(
        per_device, mesh=mesh, in_specs=in_specs, out_specs=out_specs, check_vma=False
    )
```
